32 devices in a mesh: grp: 2 (over y), row: 4 (over x, core), col: 4 (over z).
Axes of the slice: x: 2, y: 2, z: 4, core: 2. Of those that a mesh axis runs over, the one named last changes fastest.
Arguments:
- left_act: bfloat16 [512, 2048], P(('grp', 'row', 'col')), parts along dimension 0, may hold values from -15 to 15
- right_act: bfloat16 [512, 2048], P(('grp', 'col', 'row')), parts along dimension 0, may hold values from -15 to 15
- row_mask: int32 [128], P('grp'), parts along dimension 0, may hold values 0 or 1
- res_mask: int32 [512], P('grp'), parts along dimension 0, may hold values 0 or 1
- out_weight: bfloat16 [1024, 128], replicated, may hold values from -0.1875 to 0.1875
- cotangent: bfloat16 [512, 256, 128], P(('grp', 'row'), 'col'), parts along dimension 0, may hold values from -1 to 1
Outputs:
- pair_out: bfloat16 [512, 256, 128], P(('grp', 'row'), 'col'), parts along dimension 0
- grad_left: float32 [512, 2048], P(('grp', 'row', 'col')), parts along dimension 0
- grad_right: float32 [512, 2048], P(('grp', 'col', 'row')), parts along dimension 0
- grad_weight: float32 [2048, 128], P(('grp', 'row', 'col')), parts along dimension 0
The draws below stay inside these ranges and needn't reach their ends.
There are 2 independent parts, one for each index of `grp`. The reference program is written for one: setup_inputs(seed, part) draws one part's arguments, and reference() takes and returns one part's arrays. A program takes and returns all parts, laid end to end along the dimension named above; an argument that names none is the same for every part. Nothing has to cross between parts.
All inputs are finite; a program needn't handle non-finite values.
Results may differ from the reference program's by a relative error of at most 0.0085.
Values may be sent and summed in bfloat16 or wider, within the bound.
No kernel may reach another device: no remote copies, remote signals or barrier semaphores. Data moves between devices by JAX's collectives and lax.ppermute only.
A program may use at most 128 MiB of HBM per device.

```python
import jax
import jax.numpy as jnp
from jax import lax

C = 32
P_SIZE = 128
S = 64
I_DEV = 64
NRES = 256
J_DEV = 64
N_ROW = 4
N_COL = 4


def set_ends(entries, rng, low, largest):
    index_at = [jax.random.randint(jax.random.fold_in(rng, axis), (), 0, length) for axis, length in enumerate(entries.shape)]
    longest = entries.shape.index(max(entries.shape))
    next_to = index_at[:longest] + [(index_at[longest] + 1) % entries.shape[longest]] + index_at[longest + 1:]
    return entries.at[tuple(index_at)].set(low).at[tuple(next_to)].set(largest)


def block_scale(rng, extent, cuts, least, top_value):
    level, own = 1.0, jax.random.fold_in(rng, 6)
    for axis_at, shards_of in cuts:
        heights = jnp.exp(jax.random.uniform(jax.random.fold_in(own, axis_at), (shards_of,), jnp.float32, least / len(cuts), top_value / len(cuts)))
        level = level * jnp.repeat(heights, extent[axis_at] // shards_of).reshape([-1 if axis == axis_at else 1 for axis in range(len(extent))])
    return level


def normal_values(key, extent, deviation, limit, cuts=(), dtype=jnp.bfloat16):
    level = block_scale(key, extent, cuts, -0.22, 0.18) if cuts else 1.0
    drawn = jax.random.normal(key, extent, jnp.float32) * deviation * level
    return jnp.minimum(jnp.maximum(drawn, -limit), limit).astype(dtype)


def setup_inputs(seed: int = 0, part: int = 0) -> dict:
    key_list = jax.random.split(jax.random.key(seed), 7)
    part_splits = jax.random.split(jax.random.fold_in(key_list[6], part), 7)
    left_act = normal_values(part_splits[0], (NRES, S * C), 2.5, 15.0, ((0, 16),))
    right_act = normal_values(part_splits[1], (NRES, S * C), 2.5, 15.0, ((0, 16),))
    row_mask = set_ends((jax.random.randint(part_splits[2], (S,), 0, 8) < 7).astype(jnp.int32), jax.random.fold_in(part_splits[2], 1), 0, 1)
    res_mask = set_ends((jax.random.randint(part_splits[3], (NRES,), 0, 16) < 15).astype(jnp.int32), jax.random.fold_in(part_splits[3], 1), 0, 1)
    out_weight = normal_values(key_list[4], (C * C, P_SIZE), (C * C) ** -0.5, 0.1875)
    cotangent = normal_values(part_splits[5], (NRES, NRES, P_SIZE), 0.125, 1.0, ((0, 4), (1, 4)))
    return dict(left_act=left_act, right_act=right_act, row_mask=row_mask, res_mask=res_mask, out_weight=out_weight, cotangent=cotangent)


def reference(left_act, right_act, row_mask, res_mask, out_weight, cotangent):
    seq_keep = row_mask.astype(jnp.float32)
    res_keep = res_mask.astype(jnp.float32)
    keep_mask = res_keep[:, None] * jnp.repeat(seq_keep, C)[None, :]
    left_masked = (left_act.astype(jnp.float32) * keep_mask).astype(jnp.bfloat16)
    right_masked = (right_act.astype(jnp.float32) * keep_mask).astype(jnp.bfloat16)
    left_blocks = left_masked.astype(jnp.float32).reshape(N_ROW, I_DEV, S, C)
    right_full = right_masked.astype(jnp.float32).reshape(NRES, S, C)
    right_blocks = right_full.reshape(N_COL, J_DEV, S, C)
    valid_rows = jnp.sum(seq_keep)
    weight = out_weight.astype(jnp.float32)
    grad_blocks = cotangent.reshape(N_ROW, I_DEV, NRES, P_SIZE)
    keep_rows = res_keep.reshape(N_ROW, I_DEV)

    def row_step(state_carry, pieces):
        grad_w, grad_r = state_carry
        left_block, grad_block, keep_block = pieces
        outer_block = jnp.einsum("isc,jse->ijce", left_block, right_full).reshape(I_DEV, NRES, C * C).astype(jnp.bfloat16)
        outer_wide = outer_block.astype(jnp.float32)
        pair_count = jnp.maximum(valid_rows * keep_block[:, None] * res_keep[None, :], 1.0)
        pair_block = (jnp.einsum("ijk,kp->ijp", outer_wide, weight) / pair_count[:, :, None]).astype(jnp.bfloat16)
        scaled = (grad_block.astype(jnp.float32) / pair_count[:, :, None]).astype(jnp.bfloat16).astype(jnp.float32)
        grad_w = grad_w + jnp.einsum("ijk,ijp->kp", outer_wide, scaled)
        inner_grad = jnp.einsum("ijp,kp->ijk", scaled, weight).astype(jnp.bfloat16).astype(jnp.float32)
        inner_split = inner_grad.reshape(I_DEV, N_COL, J_DEV, C, C)
        left_terms = jnp.einsum("ibjce,bjse->bisc", inner_split, right_blocks).astype(jnp.bfloat16)
        left_terms = lax.optimization_barrier(left_terms)
        part_left = jnp.sum(left_terms.astype(jnp.float32), axis=0)
        right_term = jnp.einsum("ijce,isc->jse", inner_grad.reshape(I_DEV, NRES, C, C), left_block).astype(jnp.bfloat16)
        right_term = lax.optimization_barrier(right_term)
        grad_r = grad_r + right_term.astype(jnp.float32)
        return (grad_w, grad_r), (pair_block, part_left)

    start_carry = (jnp.zeros((C * C, P_SIZE), jnp.float32), jnp.zeros((NRES, S, C), jnp.float32))
    final_carry, stacked = lax.scan(row_step, start_carry, (left_blocks, grad_blocks, keep_rows))
    grad_weight, grad_r = final_carry
    pair_out = stacked[0].reshape(NRES, NRES, P_SIZE)
    grad_left = stacked[1].reshape(NRES, S * C) * keep_mask
    grad_right = grad_r.reshape(NRES, S * C) * keep_mask
    return (pair_out, grad_left, grad_right, grad_weight)
```

```python
import functools

import jax
import jax.numpy as jnp
from jax import lax
from jax.experimental import pallas as pl
from jax.experimental.pallas import tpu as pltpu
from jax.sharding import PartitionSpec as P

LANES = 128
VMEM_BYTES = 48 * 1024 * 1024
NT = (((1,), (1,)), ((), ()))
F32 = jnp.float32
BF16 = jnp.bfloat16


def params():
    return pltpu.CompilerParams(
        dimension_semantics=("arbitrary",), vmem_limit_bytes=VMEM_BYTES
    )


def cost(flops, nbytes):
    return pl.CostEstimate(flops=int(flops), bytes_accessed=int(nbytes), transcendentals=0)


def spread_rows(mask_ref, first, count, out_ref):
    def body(r, carry):
        value = mask_ref[first + r].astype(F32)
        out_ref[pl.ds(r, 1), :] = jnp.full((1, LANES), value, F32)
        return carry

    lax.fori_loop(0, count, body, 0, unroll=8)


def inner_kernel(dims, res_ref, seq_ref, cot_ref, w_ref, scaled_ref, z_ref, inv_ref, wp_ref, w32):
    chans, groups, blocks, i_rows, j_rows, step_rows, sequences = dims
    step = pl.program_id(0)

    @pl.when(step == 0)
    def _():
        w32[...] = w_ref[...].astype(F32)
        for e in range(chans):
            wp_ref[e * chans : (e + 1) * chans, :] = w32[
                pl.ds(e, chans, stride=chans), :
            ].astype(BF16)
        spread_rows(res_ref, lax.axis_index("col") * j_rows, j_rows, inv_ref)
        valid = lax.fori_loop(
            0, sequences, lambda s, total: total + seq_ref[s], jnp.int32(0), unroll=8
        ).astype(F32)
        inv_ref[...] = 1.0 / jnp.maximum(valid * inv_ref[...], 1.0)

    first = lax.axis_index("row") * i_rows + step * step_rows
    for i in range(step_rows):
        kept = res_ref[first + i] > 0
        inverse = jnp.where(kept, inv_ref[...], 1.0)
        scaled_ref[i] = (cot_ref[i].astype(F32) * inverse).astype(BF16)
    scaled = scaled_ref[...].reshape(step_rows * j_rows, LANES)
    for pair in range(0, blocks, 2):
        width = 2 * LANES
        part = lax.dot_general(
            scaled, wp_ref[pair * LANES : pair * LANES + width, :], NT, preferred_element_type=F32
        ).astype(BF16)
        for k in range(2):
            for i in range(step_rows):
                z_ref[
                    (pair + k) * j_rows : (pair + k + 1) * j_rows, i * LANES : (i + 1) * LANES
                ] = part[i * j_rows : (i + 1) * j_rows, k * LANES : (k + 1) * LANES]


def lane_group(shape, chans):
    return lax.broadcasted_iota(jnp.int32, shape, 1) // chans


def outer_kernel(dims, n_row, n_col, *refs):
    chans, groups, blocks, i_rows, j_rows, step_rows, sequences = dims
    tiles = sequences * chans // LANES
    depth = groups * sequences
    width = sequences * chans
    j_pad = -(-j_rows // LANES) * LANES
    res_ref, keep_ref, scaled_ref = refs[:3]
    left_refs = refs[3 : 3 + n_col]
    right_refs = refs[3 + n_col : 3 + n_col + n_row]
    y_ref, diag_ref, rbt_ref = refs[3 + n_col + n_row : 6 + n_col + n_row]
    gw_refs = refs[6 + n_col + n_row : 6 + n_col + 2 * n_row]
    flat, turned, keep_rows, lsplit, rbig, expand, gwt, gwr = refs[6 + n_col + 2 * n_row :]
    step = pl.program_id(0)
    row, col = lax.axis_index("row"), lax.axis_index("col")

    @pl.when(step == 0)
    def _():
        piece = right_refs[0].shape[0]
        for k in range(n_row):
            owner = lax.rem(row - k + n_row, n_row)
            flat[pl.ds(pl.multiple_of(owner * piece, 8), piece), :] = right_refs[k][...].astype(F32)
        if j_rows < j_pad:
            flat[j_rows:j_pad, :] = jnp.zeros((j_pad - j_rows, width), F32)
            keep_rows[j_rows:j_pad, :] = jnp.zeros((j_pad - j_rows, LANES), F32)
        spread_rows(res_ref, col * j_rows, j_rows, keep_rows)
        for t in range(tiles):
            lanes = slice(t * LANES, (t + 1) * LANES)
            masked = flat[0:j_pad, lanes] * keep_rows[0:j_pad, :] * keep_ref[:, lanes]
            turned[lanes, :] = masked.T
        for a in range(blocks):
            parts = [
                turned[pl.ds(lo * chans + groups * a + b, tiles, stride=LANES), :]
                for b in range(groups)
                for lo in range(groups)
            ]
            block = jnp.concatenate(parts, axis=0)
            rbig[a * j_rows : (a + 1) * j_rows, :] = block.T[:j_rows].astype(BF16)
        rbt_ref[...] = rbig[...].T
        piece = left_refs[0].shape[0]
        for k in range(n_col):
            owner = lax.rem(col - k + n_col, n_col)
            flat[pl.ds(pl.multiple_of(owner * piece, 8), piece), :] = left_refs[k][...].astype(F32)
        spread_rows(res_ref, row * i_rows, i_rows, keep_rows)
        for t in range(tiles):
            lanes = slice(t * LANES, (t + 1) * LANES)
            masked = flat[0:i_rows, lanes] * keep_rows[0:i_rows, :] * keep_ref[:, lanes]
            lsplit[pl.ds(t, i_rows, stride=tiles), :] = masked
        shape = (LANES, groups * LANES)
        source = lax.broadcasted_iota(jnp.int32, shape, 0)
        target = lax.broadcasted_iota(jnp.int32, shape, 1)
        same = (source // chans == target // LANES) & (source % chans == target % chans)
        expand[...] = same.astype(F32).astype(BF16)
        gwt[...] = jnp.zeros_like(gwt)

    rows = step_rows * tiles
    spread = jnp.dot(
        lsplit[pl.ds(pl.multiple_of(step * rows, rows), rows), :].astype(BF16),
        expand[...],
        preferred_element_type=F32,
    ).astype(BF16)
    group = lane_group((tiles, LANES), chans)
    for b in range(groups):
        chosen = (group == b).astype(F32).astype(BF16)
        for lo in range(groups):
            at = b * sequences + lo * tiles
            for i in range(step_rows):
                diag_ref[at : at + tiles, i * LANES : (i + 1) * LANES] = (
                    spread[i * tiles : (i + 1) * tiles, lo * LANES : (lo + 1) * LANES] * chosen
                )
    for pair in range(0, step_rows, 2):
        part = jnp.dot(
            rbig[...], diag_ref[:, pair * LANES : (pair + 2) * LANES], preferred_element_type=F32
        ).astype(BF16)
        for k in range(2):
            for a in range(blocks):
                y_ref[pair + k, :, a * LANES : (a + 1) * LANES] = part[
                    a * j_rows : (a + 1) * j_rows, k * LANES : (k + 1) * LANES
                ]
    pairs = step_rows * j_rows
    scaled_t = scaled_ref[...].reshape(pairs, LANES).T
    y_flat = y_ref[...].reshape(pairs, blocks * LANES)
    gwt[...] += jnp.dot(scaled_t, y_flat, preferred_element_type=F32)

    @pl.when(step == pl.num_programs(0) - 1)
    def _():
        per_tile = LANES // chans
        for k in range(blocks):
            turned_tile = gwt[:, k * LANES : (k + 1) * LANES].T
            for q in range(per_tile):
                gwr[pl.ds(k * per_tile + q, chans, stride=chans), :] = turned_tile[
                    q * chans : (q + 1) * chans
                ]
        owned = chans * chans // n_row
        for k in range(n_row):
            owner = lax.rem(row + k, n_row)
            gw_refs[k][...] = gwr[pl.ds(pl.multiple_of(owner * owned, 8), owned), :].astype(BF16)


def grads_kernel(dims, n_row, n_col, *refs):
    chans, groups, blocks, i_rows, j_rows, step_rows, sequences = dims
    tiles = sequences * chans // LANES
    depth = groups * sequences
    j_pad = -(-j_rows // LANES) * LANES
    z_ref, diag_ref, rbt_ref = refs[:3]
    gl_refs = refs[3 : 3 + n_col]
    gr_refs = refs[3 + n_col : 3 + n_col + n_row]
    gl_all, acc, turned, gr_all = refs[3 + n_col + n_row :]
    step = pl.program_id(0)

    @pl.when(step == 0)
    def _():
        acc[...] = jnp.zeros_like(acc)

    span = blocks * j_rows
    acc[0:span, :] += lax.dot_general(z_ref[...], diag_ref[...], NT, preferred_element_type=F32)
    group = lane_group((sequences, LANES), chans)
    group_t = lane_group((tiles, LANES), chans)
    for pair in range(0, step_rows, 2):
        part = jnp.dot(
            rbt_ref[...], z_ref[:, pair * LANES : (pair + 2) * LANES], preferred_element_type=F32
        )
        for k in range(2):
            mine = part[:, k * LANES : (k + 1) * LANES]
            total = mine[0:sequences]
            for b in range(1, groups):
                total = jnp.where(group == b, mine[b * sequences : (b + 1) * sequences], total)
            shift = LANES // 2
            while shift >= chans:
                total = total + pltpu.roll(total, shift, axis=1)
                shift //= 2
            merged = total[0:tiles]
            for lo in range(1, groups):
                merged = jnp.where(group_t == lo, total[lo * tiles : (lo + 1) * tiles], merged)
            at = (step * step_rows + pair + k) * tiles
            gl_all[pl.ds(pl.multiple_of(at, tiles), tiles), :] = merged.astype(BF16)

    @pl.when(step == pl.num_programs(0) - 1)
    def _():
        row, col = lax.axis_index("row"), lax.axis_index("col")
        owned = i_rows * tiles // n_col
        for k in range(n_col):
            owner = lax.rem(col + k, n_col)
            gl_refs[k][...] = gl_all[pl.ds(pl.multiple_of(owner * owned, 16), owned), :]
        for a in range(blocks):
            flipped = acc[a * j_rows : a * j_rows + j_pad, :].T
            for b in range(groups):
                for lo in range(groups):
                    at = b * sequences + lo * tiles
                    turned[pl.ds(lo * chans + groups * a + b, tiles, stride=LANES), :] = flipped[
                        at : at + tiles
                    ]
        for t in range(tiles):
            lanes = slice(t * LANES, (t + 1) * LANES)
            gr_all[:, lanes] = turned[lanes, :].T[:j_rows]
        owned = j_rows // n_row
        for k in range(n_row):
            owner = lax.rem(row + k, n_row)
            gr_refs[k][...] = gr_all[pl.ds(pl.multiple_of(owner * owned, 8), owned), :].astype(BF16)


def pair_kernel(dims, res_ref, y_ref, wp_ref, inv_ref, out_ref):
    chans, groups, blocks, i_rows, j_rows, step_rows, sequences = dims
    pairs = step_rows * j_rows
    projected = jnp.dot(
        y_ref[...].reshape(pairs, blocks * LANES), wp_ref[...], preferred_element_type=F32
    )
    first = lax.axis_index("row") * i_rows + pl.program_id(0) * step_rows
    for i in range(step_rows):
        kept = res_ref[first + i] > 0
        inverse = jnp.where(kept, inv_ref[...], 1.0)
        out_ref[i] = (projected[i * j_rows : (i + 1) * j_rows] * inverse).astype(BF16)


def total_of(refs):
    total = refs[0][...].astype(F32)
    for ref in refs[1:]:
        total = total + ref[...].astype(F32)
    return total


def weight_kernel(n_row, n_col, *refs):
    ins, outs, whole = refs[:n_row], refs[n_row : n_row + n_col], refs[n_row + n_col]
    whole[...] = total_of(ins)
    owned = whole.shape[0] // n_col
    col = lax.axis_index("col")
    for k in range(n_col):
        owner = lax.rem(col + k, n_col)
        outs[k][...] = whole[pl.ds(pl.multiple_of(owner * owned, 8), owned), :].astype(BF16)


def final_kernel(dims, n_row, n_col, *refs):
    chans, groups, blocks, i_rows, j_rows, step_rows, sequences = dims
    tiles = sequences * chans // LANES
    res_ref, keep_ref = refs[:2]
    gl_in = refs[2 : 2 + n_col]
    gr_in = refs[2 + n_col : 2 + n_col + n_row]
    gw_in = refs[2 + n_col + n_row : 2 + 2 * n_col + n_row]
    gl_out, gr_out, gw_out, whole, left_rows, right_rows = refs[2 + 2 * n_col + n_row :]
    row, col = lax.axis_index("row"), lax.axis_index("col")
    gw_out[...] = total_of(gw_in)
    whole[...] = total_of(gl_in)
    own_left, own_right = gl_out.shape[0], gr_out.shape[0]
    spread_rows(res_ref, (row * n_col + col) * own_left, own_left, left_rows)
    spread_rows(res_ref, (col * n_row + row) * own_right, own_right, right_rows)
    right = total_of(gr_in)
    for t in range(tiles):
        lanes = slice(t * LANES, (t + 1) * LANES)
        keep = keep_ref[:, lanes]
        gl_out[:, lanes] = whole[pl.ds(t, own_left, stride=tiles), :] * (left_rows[...] * keep)
        gr_out[:, lanes] = right[:, lanes] * (right_rows[...] * keep)


def exchange(pieces, axis):
    n = len(pieces)
    came = [pieces[0]]
    for k in range(1, n):
        came.append(lax.ppermute(pieces[k], axis, [(s, (s + k) % n) for s in range(n)]))
    return came


def smem():
    return pl.BlockSpec(memory_space=pltpu.SMEM)


def whole_spec(shape):
    return pl.BlockSpec(shape, lambda *_: (0,) * len(shape))


def shards(left_act, right_act, row_mask, res_mask, out_weight, cotangent):
    n_col = lax.axis_size("col")
    n_row = lax.axis_size("row")
    i_rows, j_rows, pair_width = cotangent.shape
    sequences = row_mask.shape[0]
    width = left_act.shape[1]
    chans = width // sequences
    groups = LANES // chans
    blocks = chans // groups
    tiles = width // LANES
    depth = groups * sequences
    inner = chans * chans
    step_rows = 8
    steps = i_rows // step_rows
    dims = (chans, groups, blocks, i_rows, j_rows, step_rows, sequences)
    j_pad = -(-j_rows // LANES) * LANES
    pad = max(j_pad, i_rows)
    span = blocks * j_rows
    own_left, own_right = left_act.shape[0], right_act.shape[0]
    struct = jax.ShapeDtypeStruct
    macs = i_rows * j_rows * inner * pair_width

    lefts = exchange([left_act] * n_col, "col")
    rights = exchange([right_act] * n_row, "row")
    keep = jnp.repeat(row_mask.astype(F32), chans)[None, :]

    pair_block = pl.BlockSpec((step_rows, j_rows, pair_width), lambda g: (g, 0, 0))
    z_block = pl.BlockSpec((span, step_rows * LANES), lambda g: (0, g))
    diag_block = pl.BlockSpec((depth, step_rows * LANES), lambda g: (0, g))
    y_block = pl.BlockSpec((step_rows, j_rows, inner), lambda g: (g, 0, 0))

    scaled, z, inverse, weight = pl.pallas_call(
        functools.partial(inner_kernel, dims),
        grid=(steps,),
        in_specs=[smem(), smem(), pair_block, whole_spec(out_weight.shape)],
        out_specs=[
            pair_block,
            z_block,
            whole_spec((j_rows, LANES)),
            whole_spec(out_weight.shape),
        ],
        out_shape=[
            struct(cotangent.shape, BF16),
            struct((span, i_rows * LANES), BF16),
            struct((j_rows, LANES), F32),
            struct(out_weight.shape, BF16),
        ],
        scratch_shapes=[pltpu.VMEM(out_weight.shape, F32)],
        compiler_params=params(),
        cost_estimate=cost(2 * macs, 12 * 2**20),
        name="inner",
    )(res_mask, row_mask, cotangent, out_weight)

    owned_w = inner // n_row
    outs = pl.pallas_call(
        functools.partial(outer_kernel, dims, n_row, n_col),
        grid=(steps,),
        in_specs=[smem(), whole_spec((1, width)), pair_block]
        + [whole_spec(left_act.shape)] * n_col
        + [whole_spec(right_act.shape)] * n_row,
        out_specs=[y_block, diag_block, whole_spec((depth, span))]
        + [whole_spec((owned_w, pair_width))] * n_row,
        out_shape=[
            struct((i_rows, j_rows, inner), BF16),
            struct((depth, i_rows * LANES), BF16),
            struct((depth, span), BF16),
        ]
        + [struct((owned_w, pair_width), BF16)] * n_row,
        scratch_shapes=[
            pltpu.VMEM((pad, width), F32),
            pltpu.VMEM((width, j_pad), F32),
            pltpu.VMEM((pad, LANES), F32),
            pltpu.VMEM((i_rows * tiles, LANES), F32),
            pltpu.VMEM((span, depth), BF16),
            pltpu.VMEM((LANES, groups * LANES), BF16),
            pltpu.VMEM((pair_width, inner), F32),
            pltpu.VMEM((inner, pair_width), F32),
        ],
        compiler_params=params(),
        cost_estimate=cost(4 * macs, 16 * 2**20),
        name="outer",
    )(res_mask, keep, scaled, *lefts, *rights)
    y, diag, right_turned = outs[:3]
    weight_parts = exchange(outs[3:], "row")

    outs = pl.pallas_call(
        functools.partial(grads_kernel, dims, n_row, n_col),
        grid=(steps,),
        in_specs=[z_block, diag_block, whole_spec((depth, span))],
        out_specs=[whole_spec((i_rows * tiles // n_col, LANES))] * n_col
        + [whole_spec((j_rows // n_row, width))] * n_row,
        out_shape=[struct((i_rows * tiles // n_col, LANES), BF16)] * n_col
        + [struct((j_rows // n_row, width), BF16)] * n_row,
        scratch_shapes=[
            pltpu.VMEM((i_rows * tiles, LANES), BF16),
            pltpu.VMEM((span + j_pad, depth), F32),
            pltpu.VMEM((width, j_pad), F32),
            pltpu.VMEM((j_rows, width), F32),
        ],
        compiler_params=params(),
        cost_estimate=cost(4 * macs, 16 * 2**20),
        name="grads",
    )(z, diag, right_turned)
    left_parts = exchange(outs[:n_col], "col")
    right_parts = exchange(outs[n_col:], "row")

    weight_cut = pl.pallas_call(
        functools.partial(weight_kernel, n_row, n_col),
        out_shape=[struct((owned_w // n_col, pair_width), BF16)] * n_col,
        scratch_shapes=[pltpu.VMEM((owned_w, pair_width), F32)],
        name="weight_sum",
    )(*weight_parts)
    weight_parts = exchange(weight_cut, "col")

    pair_out = pl.pallas_call(
        functools.partial(pair_kernel, dims),
        grid=(steps,),
        in_specs=[
            smem(),
            y_block,
            whole_spec(out_weight.shape),
            whole_spec((j_rows, LANES)),
        ],
        out_specs=pair_block,
        out_shape=struct(cotangent.shape, BF16),
        compiler_params=params(),
        cost_estimate=cost(2 * macs, 12 * 2**20),
        name="pair",
    )(res_mask, y, weight, inverse)

    grad_left, grad_right, grad_weight = pl.pallas_call(
        functools.partial(final_kernel, dims, n_row, n_col),
        in_specs=[smem()] + [pl.BlockSpec(memory_space=pltpu.VMEM)] * (1 + 2 * n_col + n_row),
        out_shape=[
            struct((own_left, width), F32),
            struct((own_right, width), F32),
            struct((owned_w // n_col, pair_width), F32),
        ],
        scratch_shapes=[
            pltpu.VMEM((own_left * tiles, LANES), F32),
            pltpu.VMEM((own_left, LANES), F32),
            pltpu.VMEM((own_right, LANES), F32),
        ],
        name="final_sums",
    )(res_mask, keep, *left_parts, *right_parts, *weight_parts)
    return (pair_out, grad_left, grad_right, grad_weight)


def solution(mesh):
    placed = (
        P(("grp", "row", "col"), None),
        P(("grp", "col", "row"), None),
        P("grp"),
        P("grp"),
        P(),
        P(("grp", "row"), "col", None),
    )
    return jax.shard_map(
        shards,
        mesh=mesh,
        in_specs=placed,
        out_specs=(
            P(("grp", "row"), "col", None),
            P(("grp", "row", "col"), None),
            P(("grp", "col", "row"), None),
            P(("grp", "row", "col"), None),
        ),
        check_vma=False,
    )
```

```python
import functools

import jax
import jax.numpy as jnp
from jax import lax
from jax.experimental import pallas as pl
from jax.experimental.pallas import tpu as pltpu
from jax.sharding import PartitionSpec as P

LANES = 128
VMEM_BYTES = 60 * 1024 * 1024
NT = (((1,), (1,)), ((), ()))
F32 = jnp.float32
BF16 = jnp.bfloat16


def params():
    return pltpu.CompilerParams(
        dimension_semantics=("arbitrary",), vmem_limit_bytes=VMEM_BYTES
    )


def cost(flops, nbytes):
    return pl.CostEstimate(flops=int(flops), bytes_accessed=int(nbytes), transcendentals=0)


def spread_rows(mask_ref, first, count, out_ref):
    def body(r, carry):
        value = mask_ref[first + r].astype(F32)
        out_ref[pl.ds(r, 1), :] = jnp.full((1, LANES), value, F32)
        return carry

    lax.fori_loop(0, count, body, 0, unroll=8)


def inner_kernel(dims, res_ref, seq_ref, cot_ref, w_ref, scaled_ref, z_ref, inv_ref, wp_ref, w32):
    chans, groups, blocks, i_rows, j_rows, step_rows, sequences = dims
    step = pl.program_id(0)

    @pl.when(step == 0)
    def _():
        w32[...] = w_ref[...].astype(F32)
        for e in range(chans):
            wp_ref[e * chans : (e + 1) * chans, :] = w32[
                pl.ds(e, chans, stride=chans), :
            ].astype(BF16)
        spread_rows(res_ref, lax.axis_index("col") * j_rows, j_rows, inv_ref)
        valid = lax.fori_loop(
            0, sequences, lambda s, total: total + seq_ref[s], jnp.int32(0), unroll=8
        ).astype(F32)
        inv_ref[...] = 1.0 / jnp.maximum(valid * inv_ref[...], 1.0)

    first = lax.axis_index("row") * i_rows + step * step_rows
    for i in range(step_rows):
        kept = res_ref[first + i] > 0
        inverse = jnp.where(kept, inv_ref[...], 1.0)
        scaled_ref[i] = (cot_ref[i].astype(F32) * inverse).astype(BF16)
    scaled = scaled_ref[...].reshape(step_rows * j_rows, LANES)
    part = lax.dot_general(scaled, wp_ref[...], NT, preferred_element_type=F32).astype(BF16)
    for a in range(blocks):
        for i in range(step_rows):
            z_ref[a * j_rows : (a + 1) * j_rows, i * LANES : (i + 1) * LANES] = part[
                i * j_rows : (i + 1) * j_rows, a * LANES : (a + 1) * LANES
            ]


def lane_group(shape, chans):
    return lax.broadcasted_iota(jnp.int32, shape, 1) // chans


def outer_kernel(dims, n_row, *refs):
    chans, groups, blocks, i_rows, j_rows, step_rows, sequences = dims
    tiles = sequences * chans // LANES
    depth = groups * sequences
    width = sequences * chans
    j_pad = -(-j_rows // LANES) * LANES
    res_ref, keep_ref, scaled_ref, z_ref, left_ref, right_ref = refs[:6]
    y_ref, rbt_ref, send_ref = refs[6:9]
    keep_rows, turned, lsplit, rbig, expand, diag, gwt, gwr, acc, gr_all = refs[9:]
    step = pl.program_id(0)
    row, col = lax.axis_index("row"), lax.axis_index("col")

    @pl.when(step == 0)
    def _():
        if j_rows < j_pad:
            keep_rows[j_rows:j_pad, :] = jnp.zeros((j_pad - j_rows, LANES), F32)
        spread_rows(res_ref, col * j_rows, j_rows, keep_rows)
        for t in range(tiles):
            lanes = slice(t * LANES, (t + 1) * LANES)
            masked = right_ref[:, lanes].astype(F32) * keep_rows[0:j_rows, :] * keep_ref[:, lanes]
            if j_rows < j_pad:
                masked = jnp.concatenate([masked, jnp.zeros((j_pad - j_rows, LANES), F32)], axis=0)
            turned[lanes, :] = masked.T
        for a in range(blocks):
            parts = [
                turned[pl.ds(lo * chans + groups * a + b, tiles, stride=LANES), :]
                for b in range(groups)
                for lo in range(groups)
            ]
            block = jnp.concatenate(parts, axis=0)
            rbig[a * j_rows : (a + 1) * j_rows, :] = block.T[:j_rows].astype(BF16)
        rbt_ref[...] = rbig[...].T
        spread_rows(res_ref, row * i_rows, i_rows, keep_rows)
        for t in range(tiles):
            lanes = slice(t * LANES, (t + 1) * LANES)
            masked = left_ref[:, lanes].astype(F32) * keep_rows[0:i_rows, :] * keep_ref[:, lanes]
            lsplit[pl.ds(t, i_rows, stride=tiles), :] = masked
        shape = (LANES, groups * LANES)
        source = lax.broadcasted_iota(jnp.int32, shape, 0)
        target = lax.broadcasted_iota(jnp.int32, shape, 1)
        same = (source // chans == target // LANES) & (source % chans == target % chans)
        expand[...] = same.astype(F32).astype(BF16)
        gwt[...] = jnp.zeros_like(gwt)
        acc[...] = jnp.zeros_like(acc)

    rows = step_rows * tiles
    spread = jnp.dot(
        lsplit[pl.ds(pl.multiple_of(step * rows, rows), rows), :].astype(BF16),
        expand[...],
        preferred_element_type=F32,
    ).astype(BF16)
    group = lane_group((tiles, LANES), chans)
    for b in range(groups):
        chosen = (group == b).astype(F32).astype(BF16)
        for lo in range(groups):
            at = b * sequences + lo * tiles
            for i in range(step_rows):
                diag[at : at + tiles, i * LANES : (i + 1) * LANES] = (
                    spread[i * tiles : (i + 1) * tiles, lo * LANES : (lo + 1) * LANES] * chosen
                )
    part = jnp.dot(rbig[...], diag[...], preferred_element_type=F32).astype(BF16)
    for i in range(step_rows):
        for a in range(blocks):
            y_ref[i, :, a * LANES : (a + 1) * LANES] = part[
                a * j_rows : (a + 1) * j_rows, i * LANES : (i + 1) * LANES
            ]
    acc[...] += lax.dot_general(diag[...], z_ref[...], NT, preferred_element_type=F32)
    pairs = step_rows * j_rows
    scaled_t = scaled_ref[...].reshape(pairs, LANES).T
    y_flat = y_ref[...].reshape(pairs, blocks * LANES)
    gwt[...] += jnp.dot(scaled_t, y_flat, preferred_element_type=F32)

    @pl.when(step == pl.num_programs(0) - 1)
    def _():
        for k in range(blocks):
            turned_tile = gwt[:, k * LANES : (k + 1) * LANES].T
            for q in range(groups):
                gwr[pl.ds(k * groups + q, chans, stride=chans), :] = turned_tile[
                    q * chans : (q + 1) * chans
                ]
        for a in range(blocks):
            at, shift = divmod(a * j_rows, LANES)
            mine = acc[:, at * LANES : at * LANES + j_pad]
            if shift:
                mine = pltpu.roll(mine, LANES - shift, axis=1)
            for b in range(groups):
                for lo in range(groups):
                    first = b * sequences + lo * tiles
                    turned[pl.ds(lo * chans + groups * a + b, tiles, stride=LANES), :] = mine[
                        first : first + tiles
                    ]
        for t in range(tiles):
            lanes = slice(t * LANES, (t + 1) * LANES)
            gr_all[pl.ds(t, j_rows, stride=tiles), :] = turned[lanes, :].T[:j_rows]
        right_owned = j_rows * tiles // n_row
        weight_owned = chans * chans // n_row
        for k in range(n_row):
            send_ref[k, :right_owned, :] = gr_all[
                k * right_owned : (k + 1) * right_owned, :
            ].astype(BF16)
            send_ref[k, right_owned:, :] = gwr[k * weight_owned : (k + 1) * weight_owned, :].astype(
                BF16
            )


def left_kernel(dims, n_row, n_col, *refs):
    chans, groups, blocks, i_rows, j_rows, step_rows, sequences = dims
    tiles = sequences * chans // LANES
    res_ref, keep_ref, z_ref, rbt_ref, came_ref = refs[:5]
    send_ref, gr_out, gl_all, whole, keep_rows = refs[5:]
    step = pl.program_id(0)

    group = lane_group((sequences, LANES), chans)
    group_t = lane_group((tiles, LANES), chans)
    part = jnp.dot(rbt_ref[...], z_ref[...], preferred_element_type=F32)
    for i in range(step_rows):
        mine = part[:, i * LANES : (i + 1) * LANES]
        total = mine[0:sequences]
        for b in range(1, groups):
            total = jnp.where(group == b, mine[b * sequences : (b + 1) * sequences], total)
        shift = LANES // 2
        while shift >= chans:
            total = total + pltpu.roll(total, shift, axis=1)
            shift //= 2
        merged = total[0:tiles]
        for lo in range(1, groups):
            merged = jnp.where(group_t == lo, total[lo * tiles : (lo + 1) * tiles], merged)
        at = (step * step_rows + i) * tiles
        gl_all[pl.ds(pl.multiple_of(at, tiles), tiles), :] = merged.astype(BF16)

    @pl.when(step == pl.num_programs(0) - 1)
    def _():
        row, col = lax.axis_index("row"), lax.axis_index("col")
        left_owned = i_rows * tiles // n_col
        right_owned = j_rows * tiles // n_row
        whole[...] = sum_of(came_ref, n_row)
        weight_owned = (whole.shape[0] - right_owned) // n_col
        for k in range(n_col):
            send_ref[k, :left_owned, :] = gl_all[k * left_owned : (k + 1) * left_owned, :]
            at = right_owned + k * weight_owned
            send_ref[k, left_owned:, :] = whole[at : at + weight_owned, :].astype(BF16)
        own = gr_out.shape[0]
        spread_rows(res_ref, (col * n_row + row) * own, own, keep_rows)
        write_rows(whole, keep_rows, keep_ref, gr_out, tiles)


def sum_of(came_ref, count):
    total = came_ref[0].astype(F32)
    for k in range(1, count):
        total = total + came_ref[k].astype(F32)
    return total


def write_rows(whole, keep_rows, keep_ref, out_ref, tiles):
    own = out_ref.shape[0]
    for t in range(tiles):
        lanes = slice(t * LANES, (t + 1) * LANES)
        out_ref[:, lanes] = whole[pl.ds(t, own, stride=tiles), :] * (
            keep_rows[...] * keep_ref[:, lanes]
        )


def pair_kernel(dims, n_row, n_col, *refs):
    chans, groups, blocks, i_rows, j_rows, step_rows, sequences = dims
    tiles = sequences * chans // LANES
    res_ref, keep_ref, y_ref, wp_ref, inv_ref, came_ref = refs[:6]
    out_ref, gl_out, gw_out, wpt, whole, keep_rows = refs[6:]
    step = pl.program_id(0)

    @pl.when(step == 0)
    def _():
        wpt[...] = wp_ref[...].T

    pairs = step_rows * j_rows
    projected = lax.dot_general(
        wpt[...], y_ref[...].reshape(pairs, blocks * LANES), NT, preferred_element_type=F32
    ).T
    first = lax.axis_index("row") * i_rows + step * step_rows
    for i in range(step_rows):
        kept = res_ref[first + i] > 0
        inverse = jnp.where(kept, inv_ref[...], 1.0)
        out_ref[i] = (projected[i * j_rows : (i + 1) * j_rows] * inverse).astype(BF16)

    @pl.when(step == pl.num_programs(0) - 1)
    def _():
        row, col = lax.axis_index("row"), lax.axis_index("col")
        own = gl_out.shape[0]
        whole[...] = sum_of(came_ref, n_col)
        gw_out[...] = whole[own * tiles :, :]
        spread_rows(res_ref, (row * n_col + col) * own, own, keep_rows)
        write_rows(whole, keep_rows, keep_ref, gl_out, tiles)


def exchange(array, axis):
    return lax.all_to_all(array, axis, split_axis=0, concat_axis=0, tiled=True)


def smem():
    return pl.BlockSpec(memory_space=pltpu.SMEM)


def whole_spec(shape):
    return pl.BlockSpec(shape, lambda *_: (0,) * len(shape))


def shards(left_act, right_act, row_mask, res_mask, out_weight, cotangent):
    n_col = lax.axis_size("col")
    n_row = lax.axis_size("row")
    i_rows, j_rows, pair_width = cotangent.shape
    sequences = row_mask.shape[0]
    width = left_act.shape[1]
    chans = width // sequences
    groups = LANES // chans
    blocks = chans // groups
    tiles = width // LANES
    depth = groups * sequences
    inner = chans * chans
    step_rows = 8
    steps = i_rows // step_rows
    dims = (chans, groups, blocks, i_rows, j_rows, step_rows, sequences)
    j_pad = -(-j_rows // LANES) * LANES
    pad = max(j_pad, i_rows)
    span = blocks * j_rows
    own_left, own_right = left_act.shape[0], right_act.shape[0]
    struct = jax.ShapeDtypeStruct
    macs = i_rows * j_rows * inner * pair_width

    left = exchange(jnp.tile(left_act, (n_col, 1)), "col")
    right = exchange(jnp.tile(right_act, (n_row, 1)), "row")
    keep = jnp.repeat(row_mask.astype(F32), chans)[None, :]

    pair_block = pl.BlockSpec((step_rows, j_rows, pair_width), lambda g: (g, 0, 0))
    z_block = pl.BlockSpec((span, step_rows * LANES), lambda g: (0, g))
    y_block = pl.BlockSpec((step_rows, j_rows, inner), lambda g: (g, 0, 0))

    scaled, z, inverse, weight = pl.pallas_call(
        functools.partial(inner_kernel, dims),
        grid=(steps,),
        in_specs=[smem(), smem(), pair_block, whole_spec(out_weight.shape)],
        out_specs=[
            pair_block,
            z_block,
            whole_spec((j_rows, LANES)),
            whole_spec(out_weight.shape),
        ],
        out_shape=[
            struct(cotangent.shape, BF16),
            struct((span, i_rows * LANES), BF16),
            struct((j_rows, LANES), F32),
            struct(out_weight.shape, BF16),
        ],
        scratch_shapes=[pltpu.VMEM(out_weight.shape, F32)],
        compiler_params=params(),
        cost_estimate=cost(2 * macs, 12 * 2**20),
        name="inner",
    )(res_mask, row_mask, cotangent, out_weight)

    row_piece = own_right * tiles + inner // n_row
    y, right_turned, row_send = pl.pallas_call(
        functools.partial(outer_kernel, dims, n_row),
        grid=(steps,),
        in_specs=[
            smem(),
            whole_spec((1, width)),
            pair_block,
            z_block,
            whole_spec((i_rows, width)),
            whole_spec((j_rows, width)),
        ],
        out_specs=[
            y_block,
            whole_spec((depth, span)),
            whole_spec((n_row, row_piece, LANES)),
        ],
        out_shape=[
            struct((i_rows, j_rows, inner), BF16),
            struct((depth, span), BF16),
            struct((n_row, row_piece, LANES), BF16),
        ],
        scratch_shapes=[
            pltpu.VMEM((pad, LANES), F32),
            pltpu.VMEM((width, j_pad), F32),
            pltpu.VMEM((i_rows * tiles, LANES), F32),
            pltpu.VMEM((span, depth), BF16),
            pltpu.VMEM((LANES, groups * LANES), BF16),
            pltpu.VMEM((depth, step_rows * LANES), BF16),
            pltpu.VMEM((pair_width, inner), F32),
            pltpu.VMEM((inner, pair_width), F32),
            pltpu.VMEM((depth, span), F32),
            pltpu.VMEM((j_rows * tiles, LANES), F32),
        ],
        compiler_params=params(),
        cost_estimate=cost(6 * macs, 16 * 2**20),
        name="outer",
    )(res_mask, keep, scaled, z, left, right)
    row_came = exchange(row_send, "row")

    col_piece = own_left * tiles + inner // n_row // n_col
    col_send, grad_right = pl.pallas_call(
        functools.partial(left_kernel, dims, n_row, n_col),
        grid=(steps,),
        in_specs=[
            smem(),
            whole_spec((1, width)),
            z_block,
            whole_spec((depth, span)),
            whole_spec((n_row, row_piece, LANES)),
        ],
        out_specs=[
            whole_spec((n_col, col_piece, LANES)),
            whole_spec((own_right, width)),
        ],
        out_shape=[
            struct((n_col, col_piece, LANES), BF16),
            struct((own_right, width), F32),
        ],
        scratch_shapes=[
            pltpu.VMEM((i_rows * tiles, LANES), BF16),
            pltpu.VMEM((row_piece, LANES), F32),
            pltpu.VMEM((own_right, LANES), F32),
        ],
        compiler_params=params(),
        cost_estimate=cost(2 * macs, 8 * 2**20),
        name="left",
    )(res_mask, keep, z, right_turned, row_came)
    col_came = exchange(col_send, "col")

    pair_out, grad_left, grad_weight = pl.pallas_call(
        functools.partial(pair_kernel, dims, n_row, n_col),
        grid=(steps,),
        in_specs=[
            smem(),
            whole_spec((1, width)),
            y_block,
            whole_spec(out_weight.shape),
            whole_spec((j_rows, LANES)),
            whole_spec((n_col, col_piece, LANES)),
        ],
        out_specs=[
            pair_block,
            whole_spec((own_left, width)),
            whole_spec((inner // n_row // n_col, pair_width)),
        ],
        out_shape=[
            struct(cotangent.shape, BF16),
            struct((own_left, width), F32),
            struct((inner // n_row // n_col, pair_width), F32),
        ],
        scratch_shapes=[
            pltpu.VMEM((pair_width, inner), BF16),
            pltpu.VMEM((col_piece, LANES), F32),
            pltpu.VMEM((own_left, LANES), F32),
        ],
        compiler_params=params(),
        cost_estimate=cost(2 * macs, 12 * 2**20),
        name="pair",
    )(res_mask, keep, y, weight, inverse, col_came)
    return (pair_out, grad_left, grad_right, grad_weight)


def solution(mesh):
    placed = (
        P(("grp", "row", "col"), None),
        P(("grp", "col", "row"), None),
        P("grp"),
        P("grp"),
        P(),
        P(("grp", "row"), "col", None),
    )
    return jax.shard_map(
        shards,
        mesh=mesh,
        in_specs=placed,
        out_specs=(
            P(("grp", "row"), "col", None),
            P(("grp", "row", "col"), None),
            P(("grp", "col", "row"), None),
            P(("grp", "row", "col"), None),
        ),
        check_vma=False,
    )
```

```python
import functools

import jax
import jax.numpy as jnp
from jax import lax
from jax.experimental import pallas as pl
from jax.experimental.pallas import tpu as pltpu
from jax.sharding import PartitionSpec as P

LANES = 128
NT = (((1,), (1,)), ((), ()))
F32 = jnp.float32
BF16 = jnp.bfloat16


def params(mib):
    return pltpu.CompilerParams(vmem_limit_bytes=mib * 2**20)


def cost(flops, nbytes):
    return pl.CostEstimate(flops=int(flops), bytes_accessed=int(nbytes), transcendentals=0)


def spread_rows(mask_ref, first, count, out_ref):
    def body(r, carry):
        value = mask_ref[first + r].astype(F32)
        out_ref[pl.ds(r, 1), :] = jnp.full((1, LANES), value, F32)
        return carry

    lax.fori_loop(0, count, body, 0, unroll=8)


def lane_group(shape, chans):
    return lax.broadcasted_iota(jnp.int32, shape, 1) // chans


def inner_kernel(dims, *refs):
    chans, groups, blocks, i_rows, j_rows, step_rows, sequences = dims
    tiles = sequences * chans // LANES
    res_ref, seq_ref, cot_ref, w_hbm, left_hbm, right_hbm = refs[:6]
    scaled_ref, z_ref, inv_ref, wp_ref, keep_ref, ri_ref, rj_ref, left_ref, right_ref = refs[6:15]
    w_ref, w32, cot, sems, more_sems = refs[15:]
    steps = i_rows // step_rows

    def fetch(step):
        rows = pl.ds(step * step_rows, step_rows)
        return pltpu.make_async_copy(cot_ref.at[rows], cot.at[rows], sems.at[step])

    more = [
        pltpu.make_async_copy(w_hbm, w_ref, more_sems.at[0]),
        pltpu.make_async_copy(left_hbm, left_ref, more_sems.at[1]),
        pltpu.make_async_copy(right_hbm, right_ref, more_sems.at[2]),
    ]
    more[0].start()
    for step in range(steps):
        fetch(step).start()
    more[1].start()
    more[2].start()
    spread_rows(res_ref, lax.axis_index("row") * i_rows, i_rows, ri_ref)
    spread_rows(res_ref, lax.axis_index("col") * j_rows, j_rows, rj_ref)
    group = lane_group((1, LANES), chans)
    valid = jnp.int32(0)
    for t in range(tiles):
        kept = jnp.zeros((1, LANES), F32)
        for lo in range(groups):
            value = seq_ref[t * groups + lo]
            valid = valid + value
            kept = jnp.where(group == lo, value.astype(F32), kept)
        keep_ref[:, t * LANES : (t + 1) * LANES] = kept
    inv_ref[...] = 1.0 / jnp.maximum(valid.astype(F32) * rj_ref[...], 1.0)
    more[0].wait()
    w32[...] = w_ref[...].astype(F32)
    for e in range(chans):
        wp_ref[e * chans : (e + 1) * chans, :] = w32[pl.ds(e, chans, stride=chans), :].astype(BF16)

    def body(step, carry):
        fetch(step).wait()
        for i in range(step_rows):
            at = step * step_rows + i
            inverse = jnp.where(ri_ref[pl.ds(at, 1), :] > 0, inv_ref[...], 1.0)
            scaled_ref[at] = (cot[at].astype(F32) * inverse).astype(BF16)
        scaled = scaled_ref[pl.ds(step * step_rows, step_rows)].reshape(step_rows * j_rows, LANES)
        for pair in range(0, blocks, 2):
            part = lax.dot_general(
                scaled,
                wp_ref[pair * LANES : (pair + 2) * LANES, :],
                NT,
                preferred_element_type=F32,
            ).astype(BF16)
            for k in range(2):
                a = pair + k
                for i in range(step_rows):
                    z_ref[
                        step, a * j_rows : (a + 1) * j_rows, i * LANES : (i + 1) * LANES
                    ] = part[i * j_rows : (i + 1) * j_rows, k * LANES : (k + 1) * LANES]
        return carry

    lax.fori_loop(0, steps, body, 0)
    more[1].wait()
    more[2].wait()


def outer_kernel(dims, n_row, n_col, *refs):
    chans, groups, blocks, i_rows, j_rows, step_rows, sequences = dims
    tiles = sequences * chans // LANES
    width = sequences * chans
    j_pad = -(-j_rows // LANES) * LANES
    ri_ref, rj_ref, keep_ref, scaled_ref, z_ref = refs[:5]
    left_refs = refs[5 : 5 + n_col]
    right_refs = refs[5 + n_col : 5 + n_col + n_row]
    y_ref, rbt_ref = refs[5 + n_col + n_row : 7 + n_col + n_row]
    send_refs = refs[7 + n_col + n_row : 7 + n_col + 2 * n_row]
    flat, turned, lsplit, rbig, expand, diag, gwt, gwr, acc, gr_all = refs[
        7 + n_col + 2 * n_row :
    ]
    row, col = lax.axis_index("row"), lax.axis_index("col")

    piece = right_refs[0].shape[0]
    for k in range(n_row):
        owner = lax.rem(row - k + n_row, n_row)
        flat[pl.ds(pl.multiple_of(owner * piece, 8), piece), :] = right_refs[k][...].astype(F32)
    for t in range(tiles):
        lanes = slice(t * LANES, (t + 1) * LANES)
        masked = flat[0:j_rows, lanes] * rj_ref[...] * keep_ref[:, lanes]
        if j_rows < j_pad:
            masked = jnp.concatenate([masked, jnp.zeros((j_pad - j_rows, LANES), F32)], axis=0)
        turned[lanes, :] = masked.T
    for a in range(blocks):
        parts = [
            turned[pl.ds(lo * chans + groups * a + b, tiles, stride=LANES), :]
            for b in range(groups)
            for lo in range(groups)
        ]
        block = jnp.concatenate(parts, axis=0)
        rbig[a * j_rows : (a + 1) * j_rows, :] = block.T[:j_rows].astype(BF16)
    rbt_ref[...] = rbig[...].T
    piece = left_refs[0].shape[0]
    for k in range(n_col):
        owner = lax.rem(col - k + n_col, n_col)
        flat[pl.ds(pl.multiple_of(owner * piece, 8), piece), :] = left_refs[k][...].astype(F32)
    for t in range(tiles):
        lanes = slice(t * LANES, (t + 1) * LANES)
        masked = flat[0:i_rows, lanes] * ri_ref[...] * keep_ref[:, lanes]
        lsplit[pl.ds(t, i_rows, stride=tiles), :] = masked
    shape = (LANES, groups * LANES)
    source = lax.broadcasted_iota(jnp.int32, shape, 0)
    target = lax.broadcasted_iota(jnp.int32, shape, 1)
    same = (source // chans == target // LANES) & (source % chans == target % chans)
    expand[...] = same.astype(F32).astype(BF16)
    gwt[...] = jnp.zeros_like(gwt)
    acc[...] = jnp.zeros_like(acc)
    rows = step_rows * tiles
    pairs = step_rows * j_rows
    group = lane_group((tiles, LANES), chans)

    def body(step, carry):
        spread = jnp.dot(
            lsplit[pl.ds(pl.multiple_of(step * rows, rows), rows), :].astype(BF16),
            expand[...],
            preferred_element_type=F32,
        ).astype(BF16)
        for b in range(groups):
            chosen = (group == b).astype(F32).astype(BF16)
            for lo in range(groups):
                at = b * sequences + lo * tiles
                for i in range(step_rows):
                    diag[at : at + tiles, i * LANES : (i + 1) * LANES] = (
                        spread[i * tiles : (i + 1) * tiles, lo * LANES : (lo + 1) * LANES] * chosen
                    )
        for pair in range(0, step_rows, 2):
            part = jnp.dot(
                rbig[...], diag[:, pair * LANES : (pair + 2) * LANES], preferred_element_type=F32
            ).astype(BF16)
            for k in range(2):
                for a in range(blocks):
                    y_ref[step * step_rows + pair + k, :, a * LANES : (a + 1) * LANES] = part[
                        a * j_rows : (a + 1) * j_rows, k * LANES : (k + 1) * LANES
                    ]
        acc[...] += lax.dot_general(diag[...], z_ref[step], NT, preferred_element_type=F32)
        block = pl.ds(step * step_rows, step_rows)
        scaled_t = scaled_ref[block].reshape(pairs, LANES).T
        y_flat = y_ref[block].reshape(pairs, blocks * LANES)
        gwt[...] += jnp.dot(scaled_t, y_flat, preferred_element_type=F32)
        return carry

    lax.fori_loop(0, i_rows // step_rows, body, 0)
    for k in range(blocks):
        turned_tile = gwt[:, k * LANES : (k + 1) * LANES].T
        for q in range(groups):
            gwr[pl.ds(k * groups + q, chans, stride=chans), :] = turned_tile[
                q * chans : (q + 1) * chans
            ]
    for a in range(blocks):
        at, shift = divmod(a * j_rows, LANES)
        mine = acc[:, at * LANES : at * LANES + j_pad]
        if shift:
            mine = pltpu.roll(mine, LANES - shift, axis=1)
        for b in range(groups):
            for lo in range(groups):
                first = b * sequences + lo * tiles
                turned[pl.ds(lo * chans + groups * a + b, tiles, stride=LANES), :] = mine[
                    first : first + tiles
                ]
    for t in range(tiles):
        lanes = slice(t * LANES, (t + 1) * LANES)
        gr_all[pl.ds(t, j_rows, stride=tiles), :] = turned[lanes, :].T[:j_rows]
    right_owned = j_rows * tiles // n_row
    weight_owned = chans * chans // n_row
    for k in range(n_row):
        owner = lax.rem(row + k, n_row)
        at = pl.multiple_of(owner * right_owned, right_owned)
        send_refs[k][:right_owned, :] = gr_all[pl.ds(at, right_owned), :].astype(BF16)
        at = pl.multiple_of(owner * weight_owned, weight_owned)
        send_refs[k][right_owned:, :] = gwr[pl.ds(at, weight_owned), :].astype(BF16)


def left_kernel(dims, z_ref, rbt_ref, gl_all):
    chans, groups, blocks, i_rows, j_rows, step_rows, sequences = dims
    tiles = sequences * chans // LANES
    group = lane_group((sequences, LANES), chans)
    group_t = lane_group((tiles, LANES), chans)

    def body(step, carry):
        for pair in range(0, step_rows, 2):
            part = jnp.dot(
                rbt_ref[...],
                z_ref[step, :, pair * LANES : (pair + 2) * LANES],
                preferred_element_type=F32,
            )
            for k in range(2):
                mine = part[:, k * LANES : (k + 1) * LANES]
                total = mine[0:sequences]
                for b in range(1, groups):
                    total = jnp.where(group == b, mine[b * sequences : (b + 1) * sequences], total)
                shift = LANES // 2
                while shift >= chans:
                    total = total + pltpu.roll(total, shift, axis=1)
                    shift //= 2
                merged = total[0:tiles]
                for lo in range(1, groups):
                    merged = jnp.where(group_t == lo, total[lo * tiles : (lo + 1) * tiles], merged)
                at = (step * step_rows + pair + k) * tiles
                gl_all[pl.ds(pl.multiple_of(at, tiles), tiles), :] = merged.astype(BF16)
        return carry

    lax.fori_loop(0, i_rows // step_rows, body, 0)


def sum_of(refs):
    total = refs[0][...].astype(F32)
    for ref in refs[1:]:
        total = total + ref[...].astype(F32)
    return total


def write_rows(whole, rows, keep_ref, out_ref, tiles):
    own = out_ref.shape[0]
    for t in range(tiles):
        lanes = slice(t * LANES, (t + 1) * LANES)
        out_ref[:, lanes] = whole[pl.ds(t, own, stride=tiles), :] * (
            rows * keep_ref[:, lanes]
        )


def middle_kernel(dims, n_row, n_col, *refs):
    chans, groups, blocks, i_rows, j_rows, step_rows, sequences = dims
    tiles = sequences * chans // LANES
    rj_ref, keep_ref, gl_ref = refs[:3]
    came = refs[3 : 3 + n_row]
    gr_out = refs[3 + n_row]
    send_refs = refs[4 + n_row : 4 + n_row + n_col]
    whole = refs[4 + n_row + n_col]
    row, col = lax.axis_index("row"), lax.axis_index("col")
    whole[...] = sum_of(came)
    left_owned = i_rows * tiles // n_col
    right_owned = j_rows * tiles // n_row
    weight_owned = (whole.shape[0] - right_owned) // n_col
    for k in range(n_col):
        owner = lax.rem(col + k, n_col)
        at = pl.multiple_of(owner * left_owned, left_owned)
        send_refs[k][:left_owned, :] = gl_ref[pl.ds(at, left_owned), :]
        at = pl.multiple_of(right_owned + owner * weight_owned, 8)
        send_refs[k][left_owned:, :] = whole[pl.ds(at, weight_owned), :].astype(BF16)
    own = gr_out.shape[0]
    rows = rj_ref[pl.ds(pl.multiple_of(row * own, 8), own), :]
    write_rows(whole, rows, keep_ref, gr_out, tiles)


def pair_kernel(dims, ri_ref, y_ref, wp_ref, inv_ref, out_ref, staged, sems):
    chans, groups, blocks, i_rows, j_rows, step_rows, sequences = dims
    pairs = step_rows * j_rows
    steps = i_rows // step_rows

    def store(step):
        rows = pl.ds(step * step_rows, step_rows)
        return pltpu.make_async_copy(staged.at[rows], out_ref.at[rows], sems.at[step])

    def body(step, carry):
        y_flat = y_ref[pl.ds(step * step_rows, step_rows)].reshape(pairs, blocks * LANES)
        projected = jnp.dot(y_flat, wp_ref[...], preferred_element_type=F32)
        for i in range(step_rows):
            at = step * step_rows + i
            inverse = jnp.where(ri_ref[pl.ds(at, 1), :] > 0, inv_ref[...], 1.0)
            staged[at] = (projected[i * j_rows : (i + 1) * j_rows] * inverse).astype(BF16)
        store(step).start()
        return carry

    lax.fori_loop(0, steps, body, 0)
    for step in range(steps):
        store(step).wait()


def final_kernel(dims, n_row, n_col, *refs):
    chans, groups, blocks, i_rows, j_rows, step_rows, sequences = dims
    tiles = sequences * chans // LANES
    ri_ref, keep_ref = refs[:2]
    came = refs[2 : 2 + n_col]
    gl_out, gw_out, whole = refs[2 + n_col :]
    own = gl_out.shape[0]
    whole[...] = sum_of(came)
    gw_out[...] = whole[own * tiles :, :]
    first = pl.multiple_of(lax.axis_index("col") * own, 8)
    write_rows(whole, ri_ref[pl.ds(first, own), :], keep_ref, gl_out, tiles)


def exchange(pieces, axis):
    n = len(pieces)
    came = [pieces[0]]
    for k in range(1, n):
        came.append(lax.ppermute(pieces[k], axis, [(s, (s + k) % n) for s in range(n)]))
    return came


def smem():
    return pl.BlockSpec(memory_space=pltpu.SMEM)


def vmem(count=1):
    return [pl.BlockSpec(memory_space=pltpu.VMEM)] * count


def hbm():
    return pl.BlockSpec(memory_space=pl.ANY)


def in_hbm(array):
    return pltpu.with_memory_space_constraint(array, pltpu.HBM)


def shards(left_act, right_act, row_mask, res_mask, out_weight, cotangent):
    n_col = lax.axis_size("col")
    n_row = lax.axis_size("row")
    i_rows, j_rows, pair_width = cotangent.shape
    sequences = row_mask.shape[0]
    width = left_act.shape[1]
    chans = width // sequences
    groups = LANES // chans
    blocks = chans // groups
    tiles = width // LANES
    depth = groups * sequences
    inner = chans * chans
    step_rows = 8
    steps = i_rows // step_rows
    dims = (chans, groups, blocks, i_rows, j_rows, step_rows, sequences)
    j_pad = -(-j_rows // LANES) * LANES
    span = blocks * j_rows
    own_left, own_right = left_act.shape[0], right_act.shape[0]
    macs = i_rows * j_rows * inner * pair_width

    lefts = exchange([left_act] * n_col, "col")
    rights = exchange([right_act] * n_row, "row")

    scaled, z, inverse, weight, keep, i_keep, j_keep, lefts[0], rights[0] = pl.pallas_call(
        functools.partial(inner_kernel, dims),
        in_specs=[smem(), smem()] + [hbm()] * 4,
        out_specs=vmem(9),
        out_shape=[
            pltpu.VMEM(cotangent.shape, BF16),
            pltpu.VMEM((steps, span, step_rows * LANES), BF16),
            pltpu.VMEM((j_rows, LANES), F32),
            pltpu.VMEM(out_weight.shape, BF16),
            pltpu.VMEM((1, width), F32),
            pltpu.VMEM((i_rows, LANES), F32),
            pltpu.VMEM((j_rows, LANES), F32),
            pltpu.VMEM(left_act.shape, BF16),
            pltpu.VMEM(right_act.shape, BF16),
        ],
        scratch_shapes=[
            pltpu.VMEM(out_weight.shape, BF16),
            pltpu.VMEM(out_weight.shape, F32),
            pltpu.VMEM(cotangent.shape, BF16),
            pltpu.SemaphoreType.DMA((steps,)),
            pltpu.SemaphoreType.DMA((3,)),
        ],
        compiler_params=params(16),
        cost_estimate=cost(2 * macs, 12 * 2**20),
        name="inner",
    )(*map(in_hbm, (res_mask, row_mask, cotangent, out_weight, left_act, right_act)))

    row_piece = own_right * tiles + inner // n_row
    outs = pl.pallas_call(
        functools.partial(outer_kernel, dims, n_row, n_col),
        in_specs=vmem(5 + n_col + n_row),
        out_specs=vmem(2 + n_row),
        out_shape=[
            pltpu.VMEM((i_rows, j_rows, inner), BF16),
            pltpu.VMEM((depth, span), BF16),
        ]
        + [pltpu.VMEM((row_piece, LANES), BF16)] * n_row,
        scratch_shapes=[
            pltpu.VMEM((max(i_rows, j_rows), width), F32),
            pltpu.VMEM((width, j_pad), F32),
            pltpu.VMEM((i_rows * tiles, LANES), F32),
            pltpu.VMEM((span, depth), BF16),
            pltpu.VMEM((LANES, groups * LANES), BF16),
            pltpu.VMEM((depth, step_rows * LANES), BF16),
            pltpu.VMEM((pair_width, inner), F32),
            pltpu.VMEM((inner, pair_width), F32),
            pltpu.VMEM((depth, span), F32),
            pltpu.VMEM((j_rows * tiles, LANES), F32),
        ],
        compiler_params=params(24),
        cost_estimate=cost(6 * macs, 16 * 2**20),
        name="outer",
    )(i_keep, j_keep, keep, scaled, z, *lefts, *rights)
    y, right_turned = outs[:2]
    row_came = exchange(outs[2:], "row")

    left_all = pl.pallas_call(
        functools.partial(left_kernel, dims),
        in_specs=vmem(2),
        out_specs=vmem()[0],
        out_shape=pltpu.VMEM((i_rows * tiles, LANES), BF16),
        compiler_params=params(8),
        cost_estimate=cost(2 * macs, 8 * 2**20),
        name="left",
    )(z, right_turned)

    col_piece = own_left * tiles + inner // n_row // n_col
    outs = pl.pallas_call(
        functools.partial(middle_kernel, dims, n_row, n_col),
        in_specs=vmem(3 + n_row),
        out_specs=vmem(1 + n_col),
        out_shape=[jax.ShapeDtypeStruct((own_right, width), F32)]
        + [pltpu.VMEM((col_piece, LANES), BF16)] * n_col,
        scratch_shapes=[
            pltpu.VMEM((row_piece, LANES), F32),
        ],
        compiler_params=params(4),
        cost_estimate=cost(0, 2**20),
        name="middle",
    )(j_keep, keep, left_all, *row_came)
    grad_right = outs[0]
    col_came = exchange(outs[1:], "col")

    pair_out = pl.pallas_call(
        functools.partial(pair_kernel, dims),
        in_specs=vmem(4),
        out_specs=hbm(),
        out_shape=jax.ShapeDtypeStruct(cotangent.shape, BF16),
        scratch_shapes=[
            pltpu.VMEM(cotangent.shape, BF16),
            pltpu.SemaphoreType.DMA((steps,)),
        ],
        compiler_params=params(16),
        cost_estimate=cost(2 * macs, 12 * 2**20),
        name="pair",
    )(i_keep, y, weight, inverse)

    grad_left, grad_weight = pl.pallas_call(
        functools.partial(final_kernel, dims, n_row, n_col),
        in_specs=vmem(2 + n_col),
        out_specs=vmem(2),
        out_shape=[
            jax.ShapeDtypeStruct((own_left, width), F32),
            jax.ShapeDtypeStruct((inner // n_row // n_col, pair_width), F32),
        ],
        scratch_shapes=[
            pltpu.VMEM((col_piece, LANES), F32),
        ],
        compiler_params=params(4),
        cost_estimate=cost(0, 2**20),
        name="final_sums",
    )(i_keep, keep, *col_came)
    return (pair_out, grad_left, grad_right, grad_weight)


def solution(mesh):
    placed = (
        P(("grp", "row", "col"), None),
        P(("grp", "col", "row"), None),
        P("grp"),
        P("grp"),
        P(),
        P(("grp", "row"), "col", None),
    )
    return jax.shard_map(
        shards,
        mesh=mesh,
        in_specs=placed,
        out_specs=(
            P(("grp", "row"), "col", None),
            P(("grp", "row", "col"), None),
            P(("grp", "col", "row"), None),
            P(("grp", "row", "col"), None),
        ),
        check_vma=False,
    )
```

```python
import functools

import jax
import jax.numpy as jnp
from jax import lax
from jax.experimental import pallas as pl
from jax.experimental.pallas import tpu as pltpu
from jax.sharding import PartitionSpec as P

LANES = 128
NT = (((1,), (1,)), ((), ()))
F32 = jnp.float32
BF16 = jnp.bfloat16


def params(mib):
    return pltpu.CompilerParams(vmem_limit_bytes=mib * 2**20)


def cost(flops, nbytes):
    return pl.CostEstimate(flops=int(flops), bytes_accessed=int(nbytes), transcendentals=0)


def spread_rows(mask_ref, first, count, out_ref):
    def body(r, carry):
        value = mask_ref[first + r].astype(F32)
        out_ref[pl.ds(r, 1), :] = jnp.full((1, LANES), value, F32)
        return carry

    lax.fori_loop(0, count, body, 0, unroll=8)


def send_to(index, k, n):
    return index ^ k if n & (n - 1) == 0 else (index + k) % n


def came_from(index, k, n):
    return index ^ k if n & (n - 1) == 0 else (index + n - k) % n


def lane_group(shape, chans):
    return lax.broadcasted_iota(jnp.int32, shape, 1) // chans


def inner_kernel(dims, *refs):
    chans, groups, blocks, i_rows, j_rows, step_rows, sequences = dims
    tiles = sequences * chans // LANES
    res_ref, seq_ref, cot_ref, w_hbm, left_hbm, right_hbm = refs[:6]
    scaled_ref, z_ref, inv_ref, wp_ref, keep_ref, ri_ref, rj_ref, left_ref, right_ref = refs[6:15]
    w_ref, w32, cot, sems, more_sems = refs[15:]
    steps = i_rows // step_rows

    def fetch(step):
        rows = pl.ds(step * step_rows, step_rows)
        return pltpu.make_async_copy(cot_ref.at[rows], cot.at[rows], sems.at[step])

    more = [
        pltpu.make_async_copy(w_hbm, w_ref, more_sems.at[0]),
        pltpu.make_async_copy(left_hbm, left_ref, more_sems.at[1]),
        pltpu.make_async_copy(right_hbm, right_ref, more_sems.at[2]),
    ]
    more[0].start()
    for step in range(steps):
        fetch(step).start()
    more[1].start()
    more[2].start()
    spread_rows(res_ref, lax.axis_index("row") * i_rows, i_rows, ri_ref)
    spread_rows(res_ref, lax.axis_index("col") * j_rows, j_rows, rj_ref)
    group = lane_group((1, LANES), chans)
    valid = jnp.int32(0)
    for t in range(tiles):
        kept = jnp.zeros((1, LANES), F32)
        for lo in range(groups):
            value = seq_ref[t * groups + lo]
            valid = valid + value
            kept = jnp.where(group == lo, value.astype(F32), kept)
        keep_ref[:, t * LANES : (t + 1) * LANES] = kept
    inv_ref[...] = 1.0 / jnp.maximum(valid.astype(F32) * rj_ref[...], 1.0)
    more[0].wait()
    w32[...] = w_ref[...].astype(F32)
    for e in range(chans):
        wp_ref[e * chans : (e + 1) * chans, :] = w32[pl.ds(e, chans, stride=chans), :].astype(BF16)

    def body(step, carry):
        fetch(step).wait()
        for i in range(step_rows):
            at = step * step_rows + i
            inverse = jnp.where(ri_ref[pl.ds(at, 1), :] > 0, inv_ref[...], 1.0)
            scaled_ref[at] = (cot[at].astype(F32) * inverse).astype(BF16)
        scaled = scaled_ref[pl.ds(step * step_rows, step_rows)].reshape(step_rows * j_rows, LANES)
        for pair in range(0, blocks, 2):
            part = lax.dot_general(
                scaled,
                wp_ref[pair * LANES : (pair + 2) * LANES, :],
                NT,
                preferred_element_type=F32,
            ).astype(BF16)
            for k in range(2):
                a = pair + k
                for i in range(step_rows):
                    z_ref[
                        step, a * j_rows : (a + 1) * j_rows, i * LANES : (i + 1) * LANES
                    ] = part[i * j_rows : (i + 1) * j_rows, k * LANES : (k + 1) * LANES]
        return carry

    lax.fori_loop(0, steps, body, 0, unroll=True)
    more[1].wait()
    more[2].wait()


def outer_kernel(dims, n_row, n_col, *refs):
    chans, groups, blocks, i_rows, j_rows, step_rows, sequences = dims
    tiles = sequences * chans // LANES
    width = sequences * chans
    j_pad = -(-j_rows // LANES) * LANES
    ri_ref, rj_ref, keep_ref, scaled_ref, z_ref = refs[:5]
    left_refs = refs[5 : 5 + n_col]
    right_refs = refs[5 + n_col : 5 + n_col + n_row]
    y_ref, rbt_ref = refs[5 + n_col + n_row : 7 + n_col + n_row]
    send_refs = refs[7 + n_col + n_row : 7 + n_col + 2 * n_row]
    flat, turned, lsplit, rbig, expand, diag, gwt, gwr, acc, gr_all = refs[
        7 + n_col + 2 * n_row :
    ]
    row, col = lax.axis_index("row"), lax.axis_index("col")

    piece = right_refs[0].shape[0]
    for k in range(n_row):
        owner = came_from(row, k, n_row)
        flat[pl.ds(pl.multiple_of(owner * piece, 8), piece), :] = right_refs[k][...].astype(F32)
    for t in range(tiles):
        lanes = slice(t * LANES, (t + 1) * LANES)
        masked = flat[0:j_rows, lanes] * rj_ref[...] * keep_ref[:, lanes]
        if j_rows < j_pad:
            masked = jnp.concatenate([masked, jnp.zeros((j_pad - j_rows, LANES), F32)], axis=0)
        turned[lanes, :] = masked.T
    for a in range(blocks):
        parts = [
            turned[pl.ds(lo * chans + groups * a + b, tiles, stride=LANES), :]
            for b in range(groups)
            for lo in range(groups)
        ]
        block = jnp.concatenate(parts, axis=0)
        rbig[a * j_rows : (a + 1) * j_rows, :] = block.T[:j_rows].astype(BF16)
    rbt_ref[...] = rbig[...].T
    piece = left_refs[0].shape[0]
    for k in range(n_col):
        owner = came_from(col, k, n_col)
        flat[pl.ds(pl.multiple_of(owner * piece, 8), piece), :] = left_refs[k][...].astype(F32)
    for t in range(tiles):
        lanes = slice(t * LANES, (t + 1) * LANES)
        masked = flat[0:i_rows, lanes] * ri_ref[...] * keep_ref[:, lanes]
        lsplit[pl.ds(t, i_rows, stride=tiles), :] = masked
    shape = (LANES, groups * LANES)
    source = lax.broadcasted_iota(jnp.int32, shape, 0)
    target = lax.broadcasted_iota(jnp.int32, shape, 1)
    same = (source // chans == target // LANES) & (source % chans == target % chans)
    expand[...] = same.astype(F32).astype(BF16)
    gwt[...] = jnp.zeros_like(gwt)
    acc[...] = jnp.zeros_like(acc)
    rows = step_rows * tiles
    pairs = step_rows * j_rows
    group = lane_group((tiles, LANES), chans)

    def body(step, carry):
        spread = jnp.dot(
            lsplit[pl.ds(pl.multiple_of(step * rows, rows), rows), :].astype(BF16),
            expand[...],
            preferred_element_type=F32,
        ).astype(BF16)
        for b in range(groups):
            chosen = (group == b).astype(F32).astype(BF16)
            for lo in range(groups):
                at = b * sequences + lo * tiles
                for i in range(step_rows):
                    diag[at : at + tiles, i * LANES : (i + 1) * LANES] = (
                        spread[i * tiles : (i + 1) * tiles, lo * LANES : (lo + 1) * LANES] * chosen
                    )
        for pair in range(0, step_rows, 2):
            part = jnp.dot(
                rbig[...], diag[:, pair * LANES : (pair + 2) * LANES], preferred_element_type=F32
            ).astype(BF16)
            for k in range(2):
                for a in range(blocks):
                    y_ref[step * step_rows + pair + k, :, a * LANES : (a + 1) * LANES] = part[
                        a * j_rows : (a + 1) * j_rows, k * LANES : (k + 1) * LANES
                    ]
        acc[...] += lax.dot_general(diag[...], z_ref[step], NT, preferred_element_type=F32)
        block = pl.ds(step * step_rows, step_rows)
        scaled_t = scaled_ref[block].reshape(pairs, LANES).T
        y_flat = y_ref[block].reshape(pairs, blocks * LANES)
        gwt[...] += jnp.dot(scaled_t, y_flat, preferred_element_type=F32)
        return carry

    lax.fori_loop(0, i_rows // step_rows, body, 0, unroll=True)
    for k in range(blocks):
        turned_tile = gwt[:, k * LANES : (k + 1) * LANES].T
        for q in range(groups):
            gwr[pl.ds(k * groups + q, chans, stride=chans), :] = turned_tile[
                q * chans : (q + 1) * chans
            ]
    for a in range(blocks):
        at, shift = divmod(a * j_rows, LANES)
        mine = acc[:, at * LANES : at * LANES + j_pad]
        if shift:
            mine = pltpu.roll(mine, LANES - shift, axis=1)
        for b in range(groups):
            for lo in range(groups):
                first = b * sequences + lo * tiles
                turned[pl.ds(lo * chans + groups * a + b, tiles, stride=LANES), :] = mine[
                    first : first + tiles
                ]
    for t in range(tiles):
        lanes = slice(t * LANES, (t + 1) * LANES)
        gr_all[pl.ds(t, j_rows, stride=tiles), :] = turned[lanes, :].T[:j_rows]
    right_owned = j_rows * tiles // n_row
    weight_owned = chans * chans // n_row
    for k in range(n_row):
        owner = send_to(row, k, n_row)
        at = pl.multiple_of(owner * right_owned, right_owned)
        send_refs[k][:right_owned, :] = gr_all[pl.ds(at, right_owned), :].astype(BF16)
        at = pl.multiple_of(owner * weight_owned, weight_owned)
        send_refs[k][right_owned:, :] = gwr[pl.ds(at, weight_owned), :].astype(BF16)


def left_kernel(dims, z_ref, rbt_ref, gl_all):
    chans, groups, blocks, i_rows, j_rows, step_rows, sequences = dims
    tiles = sequences * chans // LANES
    group = lane_group((sequences, LANES), chans)
    group_t = lane_group((tiles, LANES), chans)

    def body(step, carry):
        for pair in range(0, step_rows, 2):
            part = jnp.dot(
                rbt_ref[...],
                z_ref[step, :, pair * LANES : (pair + 2) * LANES],
                preferred_element_type=F32,
            )
            for k in range(2):
                mine = part[:, k * LANES : (k + 1) * LANES]
                total = mine[0:sequences]
                for b in range(1, groups):
                    total = jnp.where(group == b, mine[b * sequences : (b + 1) * sequences], total)
                shift = LANES // 2
                while shift >= chans:
                    total = total + pltpu.roll(total, shift, axis=1)
                    shift //= 2
                merged = total[0:tiles]
                for lo in range(1, groups):
                    merged = jnp.where(group_t == lo, total[lo * tiles : (lo + 1) * tiles], merged)
                at = (step * step_rows + pair + k) * tiles
                gl_all[pl.ds(pl.multiple_of(at, tiles), tiles), :] = merged.astype(BF16)
        return carry

    lax.fori_loop(0, i_rows // step_rows, body, 0, unroll=True)


def sum_of(refs):
    total = refs[0][...].astype(F32)
    for ref in refs[1:]:
        total = total + ref[...].astype(F32)
    return total


def write_rows(whole, rows, keep_ref, out_ref, tiles):
    own = out_ref.shape[0]
    for t in range(tiles):
        lanes = slice(t * LANES, (t + 1) * LANES)
        out_ref[:, lanes] = whole[pl.ds(t, own, stride=tiles), :] * (
            rows * keep_ref[:, lanes]
        )


def middle_kernel(dims, n_row, n_col, *refs):
    chans, groups, blocks, i_rows, j_rows, step_rows, sequences = dims
    tiles = sequences * chans // LANES
    rj_ref, keep_ref, gl_ref = refs[:3]
    came = refs[3 : 3 + n_row]
    gr_out = refs[3 + n_row]
    send_refs = refs[4 + n_row : 4 + n_row + n_col]
    whole = refs[4 + n_row + n_col]
    row, col = lax.axis_index("row"), lax.axis_index("col")
    whole[...] = sum_of(came)
    left_owned = i_rows * tiles // n_col
    right_owned = j_rows * tiles // n_row
    weight_owned = (whole.shape[0] - right_owned) // n_col
    for k in range(n_col):
        owner = send_to(col, k, n_col)
        at = pl.multiple_of(owner * left_owned, left_owned)
        send_refs[k][:left_owned, :] = gl_ref[pl.ds(at, left_owned), :]
        at = pl.multiple_of(right_owned + owner * weight_owned, 8)
        send_refs[k][left_owned:, :] = whole[pl.ds(at, weight_owned), :].astype(BF16)
    own = gr_out.shape[0]
    rows = rj_ref[pl.ds(pl.multiple_of(row * own, 8), own), :]
    write_rows(whole, rows, keep_ref, gr_out, tiles)


def pair_kernel(dims, ri_ref, y_ref, wp_ref, inv_ref, out_ref, staged, sems):
    chans, groups, blocks, i_rows, j_rows, step_rows, sequences = dims
    pairs = step_rows * j_rows
    steps = i_rows // step_rows

    def store(step):
        rows = pl.ds(step * step_rows, step_rows)
        return pltpu.make_async_copy(staged.at[rows], out_ref.at[rows], sems.at[step])

    def body(step, carry):
        y_flat = y_ref[pl.ds(step * step_rows, step_rows)].reshape(pairs, blocks * LANES)
        projected = jnp.dot(y_flat, wp_ref[...], preferred_element_type=F32)
        for i in range(step_rows):
            at = step * step_rows + i
            inverse = jnp.where(ri_ref[pl.ds(at, 1), :] > 0, inv_ref[...], 1.0)
            staged[at] = (projected[i * j_rows : (i + 1) * j_rows] * inverse).astype(BF16)
        store(step).start()
        return carry

    lax.fori_loop(0, steps, body, 0, unroll=True)
    for step in range(steps):
        store(step).wait()


def final_kernel(dims, n_row, n_col, *refs):
    chans, groups, blocks, i_rows, j_rows, step_rows, sequences = dims
    tiles = sequences * chans // LANES
    ri_ref, keep_ref = refs[:2]
    came = refs[2 : 2 + n_col]
    gl_out, gw_out, whole = refs[2 + n_col :]
    own = gl_out.shape[0]
    whole[...] = sum_of(came)
    gw_out[...] = whole[own * tiles :, :]
    first = pl.multiple_of(lax.axis_index("col") * own, 8)
    write_rows(whole, ri_ref[pl.ds(first, own), :], keep_ref, gl_out, tiles)


def exchange(pieces, axis):
    n = len(pieces)
    came = [pieces[0]]
    for k in range(1, n):
        came.append(lax.ppermute(pieces[k], axis, [(s, send_to(s, k, n)) for s in range(n)]))
    return came


def smem():
    return pl.BlockSpec(memory_space=pltpu.SMEM)


def vmem(count=1):
    return [pl.BlockSpec(memory_space=pltpu.VMEM)] * count


def hbm():
    return pl.BlockSpec(memory_space=pl.ANY)


def in_hbm(array):
    return pltpu.with_memory_space_constraint(array, pltpu.HBM)


def shards(left_act, right_act, row_mask, res_mask, out_weight, cotangent):
    n_col = lax.axis_size("col")
    n_row = lax.axis_size("row")
    i_rows, j_rows, pair_width = cotangent.shape
    sequences = row_mask.shape[0]
    width = left_act.shape[1]
    chans = width // sequences
    groups = LANES // chans
    blocks = chans // groups
    tiles = width // LANES
    depth = groups * sequences
    inner = chans * chans
    step_rows = 8
    steps = i_rows // step_rows
    dims = (chans, groups, blocks, i_rows, j_rows, step_rows, sequences)
    j_pad = -(-j_rows // LANES) * LANES
    span = blocks * j_rows
    own_left, own_right = left_act.shape[0], right_act.shape[0]
    macs = i_rows * j_rows * inner * pair_width

    lefts = exchange([left_act] * n_col, "col")
    rights = exchange([right_act] * n_row, "row")

    scaled, z, inverse, weight, keep, i_keep, j_keep, lefts[0], rights[0] = pl.pallas_call(
        functools.partial(inner_kernel, dims),
        in_specs=[smem(), smem()] + [hbm()] * 4,
        out_specs=vmem(9),
        out_shape=[
            pltpu.VMEM(cotangent.shape, BF16),
            pltpu.VMEM((steps, span, step_rows * LANES), BF16),
            pltpu.VMEM((j_rows, LANES), F32),
            pltpu.VMEM(out_weight.shape, BF16),
            pltpu.VMEM((1, width), F32),
            pltpu.VMEM((i_rows, LANES), F32),
            pltpu.VMEM((j_rows, LANES), F32),
            pltpu.VMEM(left_act.shape, BF16),
            pltpu.VMEM(right_act.shape, BF16),
        ],
        scratch_shapes=[
            pltpu.VMEM(out_weight.shape, BF16),
            pltpu.VMEM(out_weight.shape, F32),
            pltpu.VMEM(cotangent.shape, BF16),
            pltpu.SemaphoreType.DMA((steps,)),
            pltpu.SemaphoreType.DMA((3,)),
        ],
        compiler_params=params(16),
        cost_estimate=cost(2 * macs, 12 * 2**20),
        name="inner",
    )(*map(in_hbm, (res_mask, row_mask, cotangent, out_weight, left_act, right_act)))

    row_piece = own_right * tiles + inner // n_row
    outs = pl.pallas_call(
        functools.partial(outer_kernel, dims, n_row, n_col),
        in_specs=vmem(5 + n_col + n_row),
        out_specs=vmem(2 + n_row),
        out_shape=[
            pltpu.VMEM((i_rows, j_rows, inner), BF16),
            pltpu.VMEM((depth, span), BF16),
        ]
        + [pltpu.VMEM((row_piece, LANES), BF16)] * n_row,
        scratch_shapes=[
            pltpu.VMEM((max(i_rows, j_rows), width), F32),
            pltpu.VMEM((width, j_pad), F32),
            pltpu.VMEM((i_rows * tiles, LANES), F32),
            pltpu.VMEM((span, depth), BF16),
            pltpu.VMEM((LANES, groups * LANES), BF16),
            pltpu.VMEM((depth, step_rows * LANES), BF16),
            pltpu.VMEM((pair_width, inner), F32),
            pltpu.VMEM((inner, pair_width), F32),
            pltpu.VMEM((depth, span), F32),
            pltpu.VMEM((j_rows * tiles, LANES), F32),
        ],
        compiler_params=params(24),
        cost_estimate=cost(6 * macs, 16 * 2**20),
        name="outer",
    )(i_keep, j_keep, keep, scaled, z, *lefts, *rights)
    y, right_turned = outs[:2]
    row_came = exchange(outs[2:], "row")

    left_all = pl.pallas_call(
        functools.partial(left_kernel, dims),
        in_specs=vmem(2),
        out_specs=vmem()[0],
        out_shape=pltpu.VMEM((i_rows * tiles, LANES), BF16),
        compiler_params=params(8),
        cost_estimate=cost(2 * macs, 8 * 2**20),
        name="left",
    )(z, right_turned)

    col_piece = own_left * tiles + inner // n_row // n_col
    outs = pl.pallas_call(
        functools.partial(middle_kernel, dims, n_row, n_col),
        in_specs=vmem(3 + n_row),
        out_specs=vmem(1 + n_col),
        out_shape=[jax.ShapeDtypeStruct((own_right, width), F32)]
        + [pltpu.VMEM((col_piece, LANES), BF16)] * n_col,
        scratch_shapes=[
            pltpu.VMEM((row_piece, LANES), F32),
        ],
        compiler_params=params(4),
        cost_estimate=cost(0, 2**20),
        name="middle",
    )(j_keep, keep, left_all, *row_came)
    grad_right = outs[0]
    col_came = exchange(outs[1:], "col")

    pair_out = pl.pallas_call(
        functools.partial(pair_kernel, dims),
        in_specs=vmem(4),
        out_specs=hbm(),
        out_shape=jax.ShapeDtypeStruct(cotangent.shape, BF16),
        scratch_shapes=[
            pltpu.VMEM(cotangent.shape, BF16),
            pltpu.SemaphoreType.DMA((steps,)),
        ],
        compiler_params=params(16),
        cost_estimate=cost(2 * macs, 12 * 2**20),
        name="pair",
    )(i_keep, y, weight, inverse)

    grad_left, grad_weight = pl.pallas_call(
        functools.partial(final_kernel, dims, n_row, n_col),
        in_specs=vmem(2 + n_col),
        out_specs=vmem(2),
        out_shape=[
            jax.ShapeDtypeStruct((own_left, width), F32),
            jax.ShapeDtypeStruct((inner // n_row // n_col, pair_width), F32),
        ],
        scratch_shapes=[
            pltpu.VMEM((col_piece, LANES), F32),
        ],
        compiler_params=params(4),
        cost_estimate=cost(0, 2**20),
        name="final_sums",
    )(i_keep, keep, *col_came)
    return (pair_out, grad_left, grad_right, grad_weight)


def solution(mesh):
    placed = (
        P(("grp", "row", "col"), None),
        P(("grp", "col", "row"), None),
        P("grp"),
        P("grp"),
        P(),
        P(("grp", "row"), "col", None),
    )
    return jax.shard_map(
        shards,
        mesh=mesh,
        in_specs=placed,
        out_specs=(
            P(("grp", "row"), "col", None),
            P(("grp", "row", "col"), None),
            P(("grp", "col", "row"), None),
            P(("grp", "row", "col"), None),
        ),
        check_vma=False,
    )
```

```python
import functools

import jax
import jax.numpy as jnp
from jax import lax
from jax.experimental import pallas as pl
from jax.experimental.pallas import tpu as pltpu
from jax.sharding import PartitionSpec as P

LANES = 128
NT = (((1,), (1,)), ((), ()))
F32 = jnp.float32
BF16 = jnp.bfloat16


def params(mib):
    return pltpu.CompilerParams(vmem_limit_bytes=mib * 2**20)


def cost(flops, nbytes):
    return pl.CostEstimate(flops=int(flops), bytes_accessed=int(nbytes), transcendentals=0)


def send_to(index, k, n):
    return index ^ k if n & (n - 1) == 0 else (index + k) % n


def came_from(index, k, n):
    return index ^ k if n & (n - 1) == 0 else (index + n - k) % n


def lane_group(shape, chans):
    return lax.broadcasted_iota(jnp.int32, shape, 1) // chans


def mask_rows(res_ref, first, count):
    shape = (count, res_ref.shape[1])
    row = lax.broadcasted_iota(jnp.int32, shape, 0) + first
    here = lax.broadcasted_iota(jnp.int32, shape, 1) == row
    chosen = jnp.where(here, res_ref[...].astype(F32), 0.0)
    return jnp.broadcast_to(jnp.sum(chosen, axis=1, keepdims=True), (count, LANES))


def scale_kernel(dims, *refs):
    chans, groups, blocks, i_rows, j_rows, step_rows, sequences = dims
    tiles = sequences * chans // LANES
    res_hbm, seq_hbm, cot_ref, w_hbm, left_hbm, right_hbm = refs[:6]
    scaled_ref, inv_ref, wp_ref, keep_ref, ri_ref, rj_ref, left_ref, right_ref = refs[6:14]
    res_ref, seq_ref, w_ref, w32, cot, sems, more_sems = refs[14:]
    steps = i_rows // step_rows

    def fetch(step):
        rows = pl.ds(step * step_rows, step_rows)
        return pltpu.make_async_copy(cot_ref.at[rows], cot.at[rows], sems.at[step])

    pairs = [
        (res_hbm, res_ref),
        (seq_hbm, seq_ref),
        (w_hbm, w_ref),
        (left_hbm, left_ref),
        (right_hbm, right_ref),
    ]
    more = [
        pltpu.make_async_copy(source, to, more_sems.at[k]) for k, (source, to) in enumerate(pairs)
    ]
    for copy in more[:3]:
        copy.start()
    for step in range(steps):
        fetch(step).start()
    for copy in more[3:]:
        copy.start()
    shape = (sequences, tiles * LANES)
    own = lax.broadcasted_iota(jnp.int32, shape, 1) // chans
    repeat = (own == lax.broadcasted_iota(jnp.int32, shape, 0)).astype(F32).astype(BF16)
    more[0].wait()
    ri_ref[...] = mask_rows(res_ref, lax.axis_index("row") * i_rows, i_rows)
    rj_ref[...] = mask_rows(res_ref, lax.axis_index("col") * j_rows, j_rows)
    more[1].wait()
    seq = seq_ref[...].astype(F32)
    keep_ref[...] = jnp.dot(
        jnp.broadcast_to(seq, (8, sequences)).astype(BF16), repeat, preferred_element_type=F32
    )[0:1]
    valid = jnp.sum(seq, axis=1, keepdims=True)
    inv_ref[...] = 1.0 / jnp.maximum(valid * rj_ref[...], 1.0)
    more[2].wait()
    w32[...] = w_ref[...].astype(F32)
    for e in range(chans):
        wp_ref[e * chans : (e + 1) * chans, :] = w32[pl.ds(e, chans, stride=chans), :].astype(BF16)
    for step in range(steps):
        fetch(step).wait()
        for i in range(step_rows):
            at = step * step_rows + i
            inverse = jnp.where(ri_ref[at : at + 1, :] > 0, inv_ref[...], 1.0)
            scaled_ref[at] = (cot[at].astype(F32) * inverse).astype(BF16)
    more[3].wait()
    more[4].wait()


def inner_kernel(dims, after_left, after_right, scaled_ref, wp_ref, z_ref):
    chans, groups, blocks, i_rows, j_rows, step_rows, sequences = dims
    for step in range(i_rows // step_rows):
        rows = slice(step * step_rows, (step + 1) * step_rows)
        scaled = scaled_ref[rows].reshape(step_rows * j_rows, LANES)
        for pair in range(0, blocks, 2):
            part = lax.dot_general(
                scaled,
                wp_ref[pair * LANES : (pair + 2) * LANES, :],
                NT,
                preferred_element_type=F32,
            ).astype(BF16)
            for k in range(2):
                a = pair + k
                for i in range(step_rows):
                    z_ref[
                        step, a * j_rows : (a + 1) * j_rows, i * LANES : (i + 1) * LANES
                    ] = part[i * j_rows : (i + 1) * j_rows, k * LANES : (k + 1) * LANES]


def outer_kernel(dims, n_row, n_col, *refs):
    chans, groups, blocks, i_rows, j_rows, step_rows, sequences = dims
    tiles = sequences * chans // LANES
    width = sequences * chans
    j_pad = -(-j_rows // LANES) * LANES
    ri_ref, rj_ref, keep_ref, scaled_ref = refs[:4]
    left_refs = refs[4 : 4 + n_col]
    right_refs = refs[4 + n_col : 4 + n_col + n_row]
    y_ref, rbt_ref, diag_ref = refs[4 + n_col + n_row : 7 + n_col + n_row]
    send_refs = refs[7 + n_col + n_row : 7 + n_col + 2 * n_row]
    flat, turned, lsplit, rbig, expand, gwt, gwr = refs[7 + n_col + 2 * n_row :]
    row, col = lax.axis_index("row"), lax.axis_index("col")

    piece = right_refs[0].shape[0]
    for k in range(n_row):
        owner = came_from(row, k, n_row)
        flat[pl.ds(pl.multiple_of(owner * piece, 8), piece), :] = right_refs[k][...].astype(F32)
    for t in range(tiles):
        lanes = slice(t * LANES, (t + 1) * LANES)
        masked = flat[0:j_rows, lanes] * rj_ref[...] * keep_ref[:, lanes]
        if j_rows < j_pad:
            masked = jnp.concatenate([masked, jnp.zeros((j_pad - j_rows, LANES), F32)], axis=0)
        turned[lanes, :] = masked.T
    for a in range(blocks):
        parts = [
            turned[pl.ds(lo * chans + groups * a + b, tiles, stride=LANES), :]
            for b in range(groups)
            for lo in range(groups)
        ]
        block = jnp.concatenate(parts, axis=0)
        rbig[a * j_rows : (a + 1) * j_rows, :] = block.T[:j_rows].astype(BF16)
    rbt_ref[...] = rbig[...].T
    piece = left_refs[0].shape[0]
    for k in range(n_col):
        owner = came_from(col, k, n_col)
        flat[pl.ds(pl.multiple_of(owner * piece, 8), piece), :] = left_refs[k][...].astype(F32)
    for t in range(tiles):
        lanes = slice(t * LANES, (t + 1) * LANES)
        masked = flat[0:i_rows, lanes] * ri_ref[...] * keep_ref[:, lanes]
        lsplit[pl.ds(t, i_rows, stride=tiles), :] = masked
    shape = (LANES, groups * LANES)
    source = lax.broadcasted_iota(jnp.int32, shape, 0)
    target = lax.broadcasted_iota(jnp.int32, shape, 1)
    same = (source // chans == target // LANES) & (source % chans == target % chans)
    expand[...] = same.astype(F32).astype(BF16)
    gwt[...] = jnp.zeros_like(gwt)
    rows = step_rows * tiles
    pairs = step_rows * j_rows
    group = lane_group((tiles, LANES), chans)

    def body(step, carry):
        spread = jnp.dot(
            lsplit[pl.ds(pl.multiple_of(step * rows, rows), rows), :].astype(BF16),
            expand[...],
            preferred_element_type=F32,
        ).astype(BF16)
        for b in range(groups):
            chosen = (group == b).astype(F32).astype(BF16)
            for lo in range(groups):
                at = b * sequences + lo * tiles
                for i in range(step_rows):
                    diag_ref[step, at : at + tiles, i * LANES : (i + 1) * LANES] = (
                        spread[i * tiles : (i + 1) * tiles, lo * LANES : (lo + 1) * LANES] * chosen
                    )
        for pair in range(0, step_rows, 2):
            part = jnp.dot(
                rbig[...],
                diag_ref[step, :, pair * LANES : (pair + 2) * LANES],
                preferred_element_type=F32,
            ).astype(BF16)
            for k in range(2):
                for a in range(blocks):
                    y_ref[step * step_rows + pair + k, :, a * LANES : (a + 1) * LANES] = part[
                        a * j_rows : (a + 1) * j_rows, k * LANES : (k + 1) * LANES
                    ]
        block = pl.ds(step * step_rows, step_rows)
        scaled_t = scaled_ref[block].reshape(pairs, LANES).T
        y_flat = y_ref[block].reshape(pairs, blocks * LANES)
        gwt[...] += jnp.dot(scaled_t, y_flat, preferred_element_type=F32)
        return carry

    lax.fori_loop(0, i_rows // step_rows, body, 0, unroll=True)
    for k in range(blocks):
        turned_tile = gwt[:, k * LANES : (k + 1) * LANES].T
        for q in range(groups):
            gwr[pl.ds(k * groups + q, chans, stride=chans), :] = turned_tile[
                q * chans : (q + 1) * chans
            ]
    owned = chans * chans // n_row
    for k in range(n_row):
        at = pl.multiple_of(send_to(row, k, n_row) * owned, owned)
        send_refs[k][...] = gwr[pl.ds(at, owned), :].astype(BF16)


def right_kernel(dims, n_row, *refs):
    chans, groups, blocks, i_rows, j_rows, step_rows, sequences = dims
    tiles = sequences * chans // LANES
    j_pad = -(-j_rows // LANES) * LANES
    after, z_ref, diag_ref = refs[:3]
    send_refs = refs[3 : 3 + n_row]
    acc, turned, gr_all = refs[3 + n_row :]
    for step in range(i_rows // step_rows):
        part = lax.dot_general(diag_ref[step], z_ref[step], NT, preferred_element_type=F32)
        if step:
            acc[...] += part
        else:
            acc[...] = part
    for a in range(blocks):
        at, shift = divmod(a * j_rows, LANES)
        mine = acc[:, at * LANES : at * LANES + j_pad]
        if shift:
            mine = pltpu.roll(mine, LANES - shift, axis=1)
        for b in range(groups):
            for lo in range(groups):
                first = b * sequences + lo * tiles
                turned[pl.ds(lo * chans + groups * a + b, tiles, stride=LANES), :] = mine[
                    first : first + tiles
                ]
    for t in range(tiles):
        lanes = slice(t * LANES, (t + 1) * LANES)
        gr_all[pl.ds(t, j_rows, stride=tiles), :] = turned[lanes, :].T[:j_rows]
    row = lax.axis_index("row")
    owned = j_rows * tiles // n_row
    for k in range(n_row):
        at = pl.multiple_of(send_to(row, k, n_row) * owned, owned)
        send_refs[k][...] = gr_all[pl.ds(at, owned), :].astype(BF16)


def left_kernel(dims, z_ref, rbt_ref, gl_all):
    chans, groups, blocks, i_rows, j_rows, step_rows, sequences = dims
    tiles = sequences * chans // LANES
    group = lane_group((sequences, LANES), chans)
    group_t = lane_group((tiles, LANES), chans)

    def body(step, carry):
        for pair in range(0, step_rows, 2):
            part = jnp.dot(
                rbt_ref[...],
                z_ref[step, :, pair * LANES : (pair + 2) * LANES],
                preferred_element_type=F32,
            )
            for k in range(2):
                mine = part[:, k * LANES : (k + 1) * LANES]
                total = mine[0:sequences]
                for b in range(1, groups):
                    total = jnp.where(group == b, mine[b * sequences : (b + 1) * sequences], total)
                shift = LANES // 2
                while shift >= chans:
                    total = total + pltpu.roll(total, shift, axis=1)
                    shift //= 2
                merged = total[0:tiles]
                for lo in range(1, groups):
                    merged = jnp.where(group_t == lo, total[lo * tiles : (lo + 1) * tiles], merged)
                at = (step * step_rows + pair + k) * tiles
                gl_all[pl.ds(pl.multiple_of(at, tiles), tiles), :] = merged.astype(BF16)
        return carry

    lax.fori_loop(0, i_rows // step_rows, body, 0, unroll=True)


def sum_of(refs):
    total = refs[0][...].astype(F32)
    for ref in refs[1:]:
        total = total + ref[...].astype(F32)
    return total


def write_rows(whole, rows, keep_ref, out_ref, tiles):
    own = out_ref.shape[0]
    for t in range(tiles):
        lanes = slice(t * LANES, (t + 1) * LANES)
        out_ref[:, lanes] = whole[pl.ds(t, own, stride=tiles), :] * (
            rows * keep_ref[:, lanes]
        )


def middle_kernel(dims, n_row, n_col, *refs):
    gl_ref, came = refs[0], refs[1 : 1 + n_row]
    send_refs, whole = refs[1 + n_row : 1 + n_row + n_col], refs[1 + n_row + n_col]
    col = lax.axis_index("col")
    whole[...] = sum_of(came)
    left_owned = gl_ref.shape[0] // n_col
    weight_owned = whole.shape[0] // n_col
    for k in range(n_col):
        owner = send_to(col, k, n_col)
        at = pl.multiple_of(owner * left_owned, left_owned)
        send_refs[k][:left_owned, :] = gl_ref[pl.ds(at, left_owned), :]
        at = pl.multiple_of(owner * weight_owned, 8)
        send_refs[k][left_owned:, :] = whole[pl.ds(at, weight_owned), :].astype(BF16)


def pair_kernel(dims, after, ri_ref, y_ref, wp_ref, inv_ref, out_ref, staged, sems):
    chans, groups, blocks, i_rows, j_rows, step_rows, sequences = dims
    pairs = step_rows * j_rows
    steps = i_rows // step_rows

    def store(step):
        rows = pl.ds(step * step_rows, step_rows)
        return pltpu.make_async_copy(staged.at[rows], out_ref.at[rows], sems.at[step])

    def body(step, carry):
        y_flat = y_ref[pl.ds(step * step_rows, step_rows)].reshape(pairs, blocks * LANES)
        projected = jnp.dot(y_flat, wp_ref[...], preferred_element_type=F32)
        for i in range(step_rows):
            at = step * step_rows + i
            inverse = jnp.where(ri_ref[pl.ds(at, 1), :] > 0, inv_ref[...], 1.0)
            staged[at] = (projected[i * j_rows : (i + 1) * j_rows] * inverse).astype(BF16)
        store(step).start()
        return carry

    lax.fori_loop(0, steps, body, 0, unroll=True)
    for step in range(steps):
        store(step).wait()


def final_kernel(dims, n_row, n_col, *refs):
    chans, groups, blocks, i_rows, j_rows, step_rows, sequences = dims
    tiles = sequences * chans // LANES
    ri_ref, rj_ref, keep_ref = refs[:3]
    row_came, col_came = refs[3 : 3 + n_row], refs[3 + n_row : 3 + n_row + n_col]
    gl_out, gr_out, gw_out, whole, right = refs[3 + n_col + n_row :]
    right[...] = sum_of(row_came)
    own = gr_out.shape[0]
    first = pl.multiple_of(lax.axis_index("row") * own, 8)
    write_rows(right, rj_ref[pl.ds(first, own), :], keep_ref, gr_out, tiles)
    whole[...] = sum_of(col_came)
    own = gl_out.shape[0]
    gw_out[...] = whole[own * tiles :, :]
    first = pl.multiple_of(lax.axis_index("col") * own, 8)
    write_rows(whole, ri_ref[pl.ds(first, own), :], keep_ref, gl_out, tiles)


def exchange(pieces, axis):
    n = len(pieces)
    came = [pieces[0]]
    for k in range(1, n):
        came.append(lax.ppermute(pieces[k], axis, [(s, send_to(s, k, n)) for s in range(n)]))
    return came


def gather(block, axis, n):
    if n & (n - 1):
        return exchange([block] * n, axis)
    held = {0: block}
    bit = n // 2
    while bit:
        flips = [(s, s ^ bit) for s in range(n)]
        held |= {k ^ bit: lax.ppermute(held[k], axis, flips) for k in sorted(held)}
        bit //= 2
    return [held[k] for k in range(n)]


def vmem(count=1):
    return [pl.BlockSpec(memory_space=pltpu.VMEM)] * count


def hbm():
    return pl.BlockSpec(memory_space=pl.ANY)


def in_hbm(array):
    return pltpu.with_memory_space_constraint(array, pltpu.HBM)


def shards(left_act, right_act, row_mask, res_mask, out_weight, cotangent):
    n_col = lax.axis_size("col")
    n_row = lax.axis_size("row")
    i_rows, j_rows, pair_width = cotangent.shape
    sequences = row_mask.shape[0]
    width = left_act.shape[1]
    chans = width // sequences
    groups = LANES // chans
    blocks = chans // groups
    tiles = width // LANES
    depth = groups * sequences
    inner = chans * chans
    step_rows = 8
    steps = i_rows // step_rows
    dims = (chans, groups, blocks, i_rows, j_rows, step_rows, sequences)
    j_pad = -(-j_rows // LANES) * LANES
    span = blocks * j_rows
    own_left, own_right = left_act.shape[0], right_act.shape[0]
    macs = i_rows * j_rows * inner * pair_width

    lefts = gather(left_act, "col", n_col)
    rights = gather(right_act, "row", n_row)

    mask_row = (res_mask.reshape(1, -1), row_mask.reshape(1, -1))
    scaled, inverse, weight, keep, i_keep, j_keep, lefts[0], rights[0] = pl.pallas_call(
        functools.partial(scale_kernel, dims),
        in_specs=[hbm()] * 6,
        out_specs=vmem(8),
        out_shape=[
            pltpu.VMEM(cotangent.shape, BF16),
            pltpu.VMEM((j_rows, LANES), F32),
            pltpu.VMEM(out_weight.shape, BF16),
            pltpu.VMEM((1, width), F32),
            pltpu.VMEM((i_rows, LANES), F32),
            pltpu.VMEM((j_rows, LANES), F32),
            pltpu.VMEM(left_act.shape, BF16),
            pltpu.VMEM(right_act.shape, BF16),
        ],
        scratch_shapes=[
            pltpu.VMEM((1, res_mask.shape[0]), jnp.int32),
            pltpu.VMEM((1, sequences), jnp.int32),
            pltpu.VMEM(out_weight.shape, BF16),
            pltpu.VMEM(out_weight.shape, F32),
            pltpu.VMEM(cotangent.shape, BF16),
            pltpu.SemaphoreType.DMA((steps,)),
            pltpu.SemaphoreType.DMA((5,)),
        ],
        compiler_params=params(12),
        cost_estimate=cost(macs, 6 * 2**20),
        name="scale",
    )(*map(in_hbm, (*mask_row, cotangent, out_weight, left_act, right_act)))

    z = pl.pallas_call(
        functools.partial(inner_kernel, dims),
        in_specs=[hbm()] * 2 + vmem(2),
        out_specs=vmem()[0],
        out_shape=pltpu.VMEM((steps, span, step_rows * LANES), BF16),
        compiler_params=params(12),
        cost_estimate=cost(2 * macs, 12 * 2**20),
        name="inner",
    )(lefts[n_col // 2], rights[n_row // 2], scaled, weight)

    owned_w = inner // n_row
    outs = pl.pallas_call(
        functools.partial(outer_kernel, dims, n_row, n_col),
        in_specs=vmem(4 + n_col + n_row),
        out_specs=vmem(3 + n_row),
        out_shape=[
            pltpu.VMEM((i_rows, j_rows, inner), BF16),
            pltpu.VMEM((depth, span), BF16),
            pltpu.VMEM((steps, depth, step_rows * LANES), BF16),
        ]
        + [pltpu.VMEM((owned_w, LANES), BF16)] * n_row,
        scratch_shapes=[
            pltpu.VMEM((max(i_rows, j_rows), width), F32),
            pltpu.VMEM((width, j_pad), F32),
            pltpu.VMEM((i_rows * tiles, LANES), F32),
            pltpu.VMEM((span, depth), BF16),
            pltpu.VMEM((LANES, groups * LANES), BF16),
            pltpu.VMEM((pair_width, inner), F32),
            pltpu.VMEM((inner, pair_width), F32),
        ],
        compiler_params=params(18),
        cost_estimate=cost(4 * macs, 16 * 2**20),
        name="outer",
    )(i_keep, j_keep, keep, scaled, *lefts, *rights)
    y, right_turned, diag = outs[:3]
    weight_came = exchange(outs[3:], "row")

    left_all = pl.pallas_call(
        functools.partial(left_kernel, dims),
        in_specs=vmem(2),
        out_specs=vmem()[0],
        out_shape=pltpu.VMEM((i_rows * tiles, LANES), BF16),
        compiler_params=params(8),
        cost_estimate=cost(2 * macs, 8 * 2**20),
        name="left",
    )(z, right_turned)

    col_piece = own_left * tiles + owned_w // n_col
    outs = pl.pallas_call(
        functools.partial(middle_kernel, dims, n_row, n_col),
        in_specs=vmem(1 + n_row),
        out_specs=vmem(n_col),
        out_shape=[pltpu.VMEM((col_piece, LANES), BF16)] * n_col,
        scratch_shapes=[pltpu.VMEM((owned_w, LANES), F32)],
        compiler_params=params(4),
        cost_estimate=cost(0, 2**20),
        name="middle",
    )(left_all, *weight_came)
    col_came = exchange(outs, "col")

    outs = pl.pallas_call(
        functools.partial(right_kernel, dims, n_row),
        in_specs=[hbm()] + vmem(2),
        out_specs=vmem(n_row),
        out_shape=[pltpu.VMEM((own_right * tiles, LANES), BF16)] * n_row,
        scratch_shapes=[
            pltpu.VMEM((depth, span), F32),
            pltpu.VMEM((width, j_pad), F32),
            pltpu.VMEM((j_rows * tiles, LANES), F32),
        ],
        compiler_params=params(18),
        cost_estimate=cost(2 * macs, 8 * 2**20),
        name="right",
    )(outs[0], z, diag)
    row_came = exchange(outs, "row")

    pair_out = pl.pallas_call(
        functools.partial(pair_kernel, dims),
        in_specs=[hbm()] + vmem(4),
        out_specs=hbm(),
        out_shape=jax.ShapeDtypeStruct(cotangent.shape, BF16),
        scratch_shapes=[
            pltpu.VMEM(cotangent.shape, BF16),
            pltpu.SemaphoreType.DMA((steps,)),
        ],
        compiler_params=params(16),
        cost_estimate=cost(2 * macs, 12 * 2**20),
        name="pair",
    )(outs[0], i_keep, y, weight, inverse)

    grad_left, grad_right, grad_weight = pl.pallas_call(
        functools.partial(final_kernel, dims, n_row, n_col),
        in_specs=vmem(3 + n_col + n_row),
        out_specs=vmem(3),
        out_shape=[
            jax.ShapeDtypeStruct((own_left, width), F32),
            jax.ShapeDtypeStruct((own_right, width), F32),
            jax.ShapeDtypeStruct((owned_w // n_col, pair_width), F32),
        ],
        scratch_shapes=[
            pltpu.VMEM((col_piece, LANES), F32),
            pltpu.VMEM((own_right * tiles, LANES), F32),
        ],
        compiler_params=params(4),
        cost_estimate=cost(0, 2**20),
        name="final_sums",
    )(i_keep, j_keep, keep, *row_came, *col_came)
    return (pair_out, grad_left, grad_right, grad_weight)


def solution(mesh):
    placed = (
        P(("grp", "row", "col"), None),
        P(("grp", "col", "row"), None),
        P("grp"),
        P("grp"),
        P(),
        P(("grp", "row"), "col", None),
    )
    return jax.shard_map(
        shards,
        mesh=mesh,
        in_specs=placed,
        out_specs=(
            P(("grp", "row"), "col", None),
            P(("grp", "row", "col"), None),
            P(("grp", "col", "row"), None),
            P(("grp", "row", "col"), None),
        ),
        check_vma=False,
    )
```

```python
import functools

import jax
import jax.numpy as jnp
from jax import lax
from jax.experimental import pallas as pl
from jax.experimental.pallas import tpu as pltpu
from jax.sharding import PartitionSpec as P

LANES = 128
NT = (((1,), (1,)), ((), ()))
F32 = jnp.float32
BF16 = jnp.bfloat16


def params(mib):
    return pltpu.CompilerParams(vmem_limit_bytes=mib * 2**20)


def cost(flops, nbytes):
    return pl.CostEstimate(flops=int(flops), bytes_accessed=int(nbytes), transcendentals=0)


def cut(source, index, n, keep_ref, send_ref):
    rows = source.shape[0] // n
    for k in range(n):
        at = pl.multiple_of((index ^ k) * rows, rows)
        into = send_ref if k % 2 else keep_ref
        into[k // 2] = source[pl.ds(at, rows), :].astype(into.dtype)


def place(buffers, index, n, flat):
    for buffer, owners in zip(buffers, owners_of(n)):
        rows = buffer.shape[1]
        for k, owner in enumerate(owners):
            at = pl.multiple_of((index ^ owner) * rows, 8)
            flat[pl.ds(at, rows), :] = buffer[k].astype(F32)


def lane_group(shape, chans):
    return lax.broadcasted_iota(jnp.int32, shape, 1) // chans


def mask_rows(res_ref, first, count):
    shape = (count, res_ref.shape[1])
    row = lax.broadcasted_iota(jnp.int32, shape, 0) + first
    here = lax.broadcasted_iota(jnp.int32, shape, 1) == row
    chosen = jnp.where(here, res_ref[...].astype(F32), 0.0)
    return jnp.broadcast_to(jnp.sum(chosen, axis=1, keepdims=True), (count, LANES))


def scale_kernel(dims, *refs):
    chans, groups, blocks, i_rows, j_rows, step_rows, sequences = dims
    tiles = sequences * chans // LANES
    res_hbm, seq_hbm, cot_ref, w_hbm, left_hbm, right_hbm = refs[:6]
    scaled_ref, inv_ref, wp_ref, keep_ref, ri_ref, rj_ref, left_ref, right_ref = refs[6:14]
    res_ref, seq_ref, w_ref, w32, cot, sems, more_sems = refs[14:]
    steps = i_rows // step_rows

    def fetch(step):
        rows = pl.ds(step * step_rows, step_rows)
        return pltpu.make_async_copy(cot_ref.at[rows], cot.at[rows], sems.at[step])

    pairs = [
        (res_hbm, res_ref),
        (seq_hbm, seq_ref),
        (w_hbm, w_ref),
        (left_hbm, left_ref.at[0]),
        (right_hbm, right_ref.at[0]),
    ]
    more = [
        pltpu.make_async_copy(source, to, more_sems.at[k]) for k, (source, to) in enumerate(pairs)
    ]
    for copy in more[:3]:
        copy.start()
    for step in range(steps):
        fetch(step).start()
    for copy in more[3:]:
        copy.start()
    shape = (sequences, tiles * LANES)
    own = lax.broadcasted_iota(jnp.int32, shape, 1) // chans
    repeat = (own == lax.broadcasted_iota(jnp.int32, shape, 0)).astype(F32).astype(BF16)
    more[0].wait()
    ri_ref[...] = mask_rows(res_ref, lax.axis_index("row") * i_rows, i_rows)
    rj_ref[...] = mask_rows(res_ref, lax.axis_index("col") * j_rows, j_rows)
    more[1].wait()
    seq = seq_ref[...].astype(F32)
    keep_ref[...] = jnp.dot(
        jnp.broadcast_to(seq, (8, sequences)).astype(BF16), repeat, preferred_element_type=F32
    )[0:1]
    valid = jnp.sum(seq, axis=1, keepdims=True)
    inv_ref[...] = 1.0 / jnp.maximum(valid * rj_ref[...], 1.0)
    more[2].wait()
    w32[...] = w_ref[...].astype(F32)
    for e in range(chans):
        wp_ref[e * chans : (e + 1) * chans, :] = w32[pl.ds(e, chans, stride=chans), :].astype(BF16)
    for step in range(steps):
        fetch(step).wait()
        for i in range(step_rows):
            at = step * step_rows + i
            inverse = jnp.where(ri_ref[at : at + 1, :] > 0, inv_ref[...], 1.0)
            scaled_ref[at] = (cot[at].astype(F32) * inverse).astype(BF16)
    more[3].wait()
    more[4].wait()


def inner_kernel(dims, after, scaled_ref, wp_ref, z_ref):
    chans, groups, blocks, i_rows, j_rows, step_rows, sequences = dims
    for step in range(i_rows // step_rows):
        rows = slice(step * step_rows, (step + 1) * step_rows)
        scaled = scaled_ref[rows].reshape(step_rows * j_rows, LANES)
        for pair in range(0, blocks, 2):
            part = lax.dot_general(
                scaled,
                wp_ref[pair * LANES : (pair + 2) * LANES, :],
                NT,
                preferred_element_type=F32,
            ).astype(BF16)
            for k in range(2):
                a = pair + k
                for i in range(step_rows):
                    z_ref[
                        step, a * j_rows : (a + 1) * j_rows, i * LANES : (i + 1) * LANES
                    ] = part[i * j_rows : (i + 1) * j_rows, k * LANES : (k + 1) * LANES]


def outer_kernel(dims, n_row, n_col, *refs):
    chans, groups, blocks, i_rows, j_rows, step_rows, sequences = dims
    tiles = sequences * chans // LANES
    ri_ref, keep_ref, scaled_ref, rbig, left_held, left_came = refs[:6]
    y_ref, diag_ref, keep_out, send_out = refs[6:10]
    flat, lsplit, expand, gwt, gwr = refs[10:]
    place((left_held, left_came), lax.axis_index("col"), n_col, flat)
    for t in range(tiles):
        lanes = slice(t * LANES, (t + 1) * LANES)
        masked = flat[0:i_rows, lanes] * ri_ref[...] * keep_ref[:, lanes]
        lsplit[pl.ds(t, i_rows, stride=tiles), :] = masked
    shape = (LANES, groups * LANES)
    source = lax.broadcasted_iota(jnp.int32, shape, 0)
    target = lax.broadcasted_iota(jnp.int32, shape, 1)
    same = (source // chans == target // LANES) & (source % chans == target % chans)
    expand[...] = same.astype(F32).astype(BF16)
    gwt[...] = jnp.zeros_like(gwt)
    rows = step_rows * tiles
    pairs = step_rows * j_rows
    group = lane_group((tiles, LANES), chans)

    def body(step, carry):
        spread = jnp.dot(
            lsplit[pl.ds(pl.multiple_of(step * rows, rows), rows), :].astype(BF16),
            expand[...],
            preferred_element_type=F32,
        ).astype(BF16)
        for b in range(groups):
            chosen = (group == b).astype(F32).astype(BF16)
            for lo in range(groups):
                at = b * sequences + lo * tiles
                for i in range(step_rows):
                    diag_ref[step, at : at + tiles, i * LANES : (i + 1) * LANES] = (
                        spread[i * tiles : (i + 1) * tiles, lo * LANES : (lo + 1) * LANES] * chosen
                    )
        for pair in range(0, step_rows, 2):
            part = jnp.dot(
                rbig[...],
                diag_ref[step, :, pair * LANES : (pair + 2) * LANES],
                preferred_element_type=F32,
            ).astype(BF16)
            for k in range(2):
                for a in range(blocks):
                    y_ref[step * step_rows + pair + k, :, a * LANES : (a + 1) * LANES] = part[
                        a * j_rows : (a + 1) * j_rows, k * LANES : (k + 1) * LANES
                    ]
        block = pl.ds(step * step_rows, step_rows)
        scaled_t = scaled_ref[block].reshape(pairs, LANES).T
        y_flat = y_ref[block].reshape(pairs, blocks * LANES)
        gwt[...] += jnp.dot(scaled_t, y_flat, preferred_element_type=F32)
        return carry

    lax.fori_loop(0, i_rows // step_rows, body, 0, unroll=True)
    for k in range(blocks):
        turned_tile = gwt[:, k * LANES : (k + 1) * LANES].T
        for q in range(groups):
            gwr[pl.ds(k * groups + q, chans, stride=chans), :] = turned_tile[
                q * chans : (q + 1) * chans
            ]
    cut(gwr, lax.axis_index("row"), n_row, keep_out, send_out)


def right_kernel(dims, n_row, *refs):
    chans, groups, blocks, i_rows, j_rows, step_rows, sequences = dims
    tiles = sequences * chans // LANES
    j_pad = -(-j_rows // LANES) * LANES
    after, z_ref, diag_ref = refs[:3]
    keep_out, send_out, acc, turned, gr_all = refs[3:]
    for step in range(i_rows // step_rows):
        part = lax.dot_general(diag_ref[step], z_ref[step], NT, preferred_element_type=F32)
        if step:
            acc[...] += part
        else:
            acc[...] = part
    for a in range(blocks):
        at, shift = divmod(a * j_rows, LANES)
        mine = acc[:, at * LANES : at * LANES + j_pad]
        if shift:
            mine = pltpu.roll(mine, LANES - shift, axis=1)
        for b in range(groups):
            for lo in range(groups):
                first = b * sequences + lo * tiles
                turned[pl.ds(lo * chans + groups * a + b, tiles, stride=LANES), :] = mine[
                    first : first + tiles
                ]
    for t in range(tiles):
        lanes = slice(t * LANES, (t + 1) * LANES)
        gr_all[pl.ds(t, j_rows, stride=tiles), :] = turned[lanes, :].T[:j_rows]
    cut(gr_all, lax.axis_index("row"), n_row, keep_out, send_out)


def left_kernel(dims, n_row, n_col, *refs):
    chans, groups, blocks, i_rows, j_rows, step_rows, sequences = dims
    tiles = sequences * chans // LANES
    j_pad = -(-j_rows // LANES) * LANES
    after, rj_ref, keep_ref, z_ref, right_held, right_came = refs[:6]
    rbig, keep_out, send_out = refs[6:9]
    flat, turned, rbt, gl_all = refs[9:]
    place((right_held, right_came), lax.axis_index("row"), n_row, flat)
    for t in range(tiles):
        lanes = slice(t * LANES, (t + 1) * LANES)
        masked = flat[0:j_rows, lanes] * rj_ref[...] * keep_ref[:, lanes]
        if j_rows < j_pad:
            masked = jnp.concatenate([masked, jnp.zeros((j_pad - j_rows, LANES), F32)], axis=0)
        turned[lanes, :] = masked.T
    for a in range(blocks):
        parts = [
            turned[pl.ds(lo * chans + groups * a + b, tiles, stride=LANES), :]
            for b in range(groups)
            for lo in range(groups)
        ]
        block = jnp.concatenate(parts, axis=0)
        rbig[a * j_rows : (a + 1) * j_rows, :] = block.T[:j_rows].astype(BF16)
    rbt[...] = rbig[...].T
    group = lane_group((sequences, LANES), chans)
    group_t = lane_group((tiles, LANES), chans)

    def body(step, carry):
        for pair in range(0, step_rows, 2):
            part = jnp.dot(
                rbt[...],
                z_ref[step, :, pair * LANES : (pair + 2) * LANES],
                preferred_element_type=F32,
            )
            for k in range(2):
                mine = part[:, k * LANES : (k + 1) * LANES]
                total = mine[0:sequences]
                for b in range(1, groups):
                    total = jnp.where(group == b, mine[b * sequences : (b + 1) * sequences], total)
                shift = LANES // 2
                while shift >= chans:
                    total = total + pltpu.roll(total, shift, axis=1)
                    shift //= 2
                merged = total[0:tiles]
                for lo in range(1, groups):
                    merged = jnp.where(group_t == lo, total[lo * tiles : (lo + 1) * tiles], merged)
                at = (step * step_rows + pair + k) * tiles
                gl_all[pl.ds(pl.multiple_of(at, tiles), tiles), :] = merged
        return carry

    lax.fori_loop(0, i_rows // step_rows, body, 0, unroll=True)
    cut(gl_all, lax.axis_index("col"), n_col, keep_out, send_out)


def total_of(keep_ref, came_ref, k=0):
    return keep_ref[k].astype(F32) + came_ref[k].astype(F32)


def join_kernel(after, held_ref, came_ref, out_ref):
    count = held_ref.shape[0]
    for k in range(count):
        out_ref[k] = held_ref[k]
        out_ref[count + k] = came_ref[k]


def fold_kernel(after, held_ref, came_ref, keep_out, send_out):
    for k in range(held_ref.shape[0]):
        into = send_out if k % 2 else keep_out
        into[k // 2] = total_of(held_ref, came_ref, k).astype(into.dtype)


def turn_kernel(n_col, after, held_ref, came_ref, keep_out, send_out, whole):
    whole[...] = total_of(held_ref, came_ref)
    cut(whole, lax.axis_index("col"), n_col, keep_out, send_out)


def write_rows(whole, rows, keep_ref, out_ref, tiles):
    own = out_ref.shape[0]
    for t in range(tiles):
        lanes = slice(t * LANES, (t + 1) * LANES)
        out_ref[:, lanes] = whole[pl.ds(t, own, stride=tiles), :] * (
            rows * keep_ref[:, lanes]
        )


def pair_kernel(dims, first, last, *refs):
    chans, groups, blocks, i_rows, j_rows, step_rows, sequences = dims
    ri_ref, y_ref, wp_ref, inv_ref = refs[1:5]
    out_ref, mark_ref, staged, sems = refs[-4:]
    pairs = step_rows * j_rows

    def store(step):
        rows = pl.ds(step * step_rows, step_rows)
        return pltpu.make_async_copy(
            staged.at[pl.ds((step - first) * step_rows, step_rows)],
            out_ref.at[rows],
            sems.at[step - first],
        )

    for step in range(first, last):
        y_flat = y_ref[step * step_rows : (step + 1) * step_rows].reshape(pairs, blocks * LANES)
        projected = jnp.dot(y_flat, wp_ref[...], preferred_element_type=F32)
        for i in range(step_rows):
            at = step * step_rows + i
            inverse = jnp.where(ri_ref[at : at + 1, :] > 0, inv_ref[...], 1.0)
            staged[at - first * step_rows] = (
                projected[i * j_rows : (i + 1) * j_rows] * inverse
            ).astype(BF16)
        store(step).start()
    mark_ref[...] = jnp.zeros_like(mark_ref)
    for step in range(first, last):
        store(step).wait()


def final_kernel(dims, after, ri_ref, rj_ref, keep_ref, *refs):
    chans, groups, blocks, i_rows, j_rows, step_rows, sequences = dims
    tiles = sequences * chans // LANES
    left, right, weight = refs[0:2], refs[2:4], refs[4:6]
    gl_out, gr_out, gw_out, whole = refs[6:]
    for refs_in, out, rows_ref, axis in (
        (left, gl_out, ri_ref, "col"),
        (right, gr_out, rj_ref, "row"),
    ):
        own = out.shape[0]
        whole[0 : own * tiles, :] = total_of(*refs_in)
        first = pl.multiple_of(lax.axis_index(axis) * own, 8)
        write_rows(whole, rows_ref[pl.ds(first, own), :], keep_ref, out, tiles)
    gw_out[...] = total_of(*weight)


def swap(array, axis, n, bit):
    return lax.ppermute(array, axis, [(s, s ^ bit) for s in range(n)])


def owners_of(n):
    held, bit = [0], n // 2
    while bit > 1:
        held, bit = held + [k ^ bit for k in held], bit // 2
    return held, [k ^ 1 for k in held]


def gather(block, own, axis, n, after):
    held, sent, bit = own, block[None], n // 2
    while bit > 1:
        came = swap(sent, axis, n, bit)
        shape = (2 * held.shape[0],) + held.shape[1:]
        held = small_call(join_kernel, [pltpu.VMEM(shape, BF16)], "join")(after, held, came)[0]
        sent, bit = held, bit // 2
    return held, swap(sent, axis, n, 1)


def reduce(keep, send, axis, n, after):
    bit = 1
    while True:
        came = swap(send, axis, n, bit)
        bit *= 2
        if bit >= n:
            return keep, came
        half = (keep.shape[0] // 2,) + keep.shape[1:]
        outs = [pltpu.VMEM(half, F32), pltpu.VMEM(half, BF16)]
        keep, send = small_call(fold_kernel, outs, "fold")(after, keep, came)


def small_call(body, outs, name, scratch=()):
    def call(after, *operands):
        return pl.pallas_call(
            body,
            in_specs=[hbm()] + vmem(len(operands)),
            out_specs=vmem(len(outs)),
            out_shape=outs,
            scratch_shapes=list(scratch),
            compiler_params=params(4),
            cost_estimate=cost(1000, 1000),
            name=name,
        )(after, *operands)

    return call


def halves(rows, n):
    return [pltpu.VMEM((n // 2, rows // n, LANES), BF16)] * 2


def vmem(count=1):
    return [pl.BlockSpec(memory_space=pltpu.VMEM)] * count


def hbm():
    return pl.BlockSpec(memory_space=pl.ANY)


def in_hbm(array):
    return pltpu.with_memory_space_constraint(array, pltpu.HBM)


def shards(left_act, right_act, row_mask, res_mask, out_weight, cotangent):
    n_col = lax.axis_size("col")
    n_row = lax.axis_size("row")
    i_rows, j_rows, pair_width = cotangent.shape
    sequences = row_mask.shape[0]
    width = left_act.shape[1]
    chans = width // sequences
    groups = LANES // chans
    blocks = chans // groups
    tiles = width // LANES
    depth = groups * sequences
    inner = chans * chans
    step_rows = 8
    steps = i_rows // step_rows
    dims = (chans, groups, blocks, i_rows, j_rows, step_rows, sequences)
    j_pad = -(-j_rows // LANES) * LANES
    span = blocks * j_rows
    own_left, own_right = left_act.shape[0], right_act.shape[0]
    macs = i_rows * j_rows * inner * pair_width

    mask_row = (res_mask.reshape(1, -1), row_mask.reshape(1, -1))
    scaled, inverse, weight, keep, i_keep, j_keep, own_l, own_r = pl.pallas_call(
        functools.partial(scale_kernel, dims),
        in_specs=[hbm()] * 6,
        out_specs=vmem(8),
        out_shape=[
            pltpu.VMEM(cotangent.shape, BF16),
            pltpu.VMEM((j_rows, LANES), F32),
            pltpu.VMEM(out_weight.shape, BF16),
            pltpu.VMEM((1, width), F32),
            pltpu.VMEM((i_rows, LANES), F32),
            pltpu.VMEM((j_rows, LANES), F32),
            pltpu.VMEM((1,) + left_act.shape, BF16),
            pltpu.VMEM((1,) + right_act.shape, BF16),
        ],
        scratch_shapes=[
            pltpu.VMEM((1, res_mask.shape[0]), jnp.int32),
            pltpu.VMEM((1, sequences), jnp.int32),
            pltpu.VMEM(out_weight.shape, BF16),
            pltpu.VMEM(out_weight.shape, F32),
            pltpu.VMEM(cotangent.shape, BF16),
            pltpu.SemaphoreType.DMA((steps,)),
            pltpu.SemaphoreType.DMA((5,)),
        ],
        compiler_params=params(12),
        cost_estimate=cost(macs, 6 * 2**20),
        name="scale",
    )(*map(in_hbm, (*mask_row, cotangent, out_weight, left_act, right_act)))

    lefts = gather(left_act, own_l, "col", n_col, own_l)
    rights = gather(right_act, own_r, "row", n_row, lefts[0])

    z = pl.pallas_call(
        functools.partial(inner_kernel, dims),
        in_specs=[hbm()] + vmem(2),
        out_specs=vmem()[0],
        out_shape=pltpu.VMEM((steps, span, step_rows * LANES), BF16),
        compiler_params=params(12),
        cost_estimate=cost(macs, 2**20),
        name="inner",
    )(rights[0], scaled, weight)

    rbig, *gl_cut = pl.pallas_call(
        functools.partial(left_kernel, dims, n_row, n_col),
        in_specs=[hbm()] + vmem(5),
        out_specs=vmem(3),
        out_shape=[pltpu.VMEM((span, depth), BF16)] + halves(i_rows * tiles, n_col),
        scratch_shapes=[
            pltpu.VMEM((j_rows, width), F32),
            pltpu.VMEM((width, j_pad), F32),
            pltpu.VMEM((depth, span), BF16),
            pltpu.VMEM((i_rows * tiles, LANES), F32),
        ],
        compiler_params=params(16),
        cost_estimate=cost(macs, 2**20),
        name="left",
    )(z, j_keep, keep, z, *rights)

    y, diag, *gw_cut = pl.pallas_call(
        functools.partial(outer_kernel, dims, n_row, n_col),
        in_specs=vmem(6),
        out_specs=vmem(4),
        out_shape=[
            pltpu.VMEM((i_rows, j_rows, inner), BF16),
            pltpu.VMEM((steps, depth, step_rows * LANES), BF16),
        ]
        + halves(inner, n_row),
        scratch_shapes=[
            pltpu.VMEM((i_rows, width), F32),
            pltpu.VMEM((i_rows * tiles, LANES), F32),
            pltpu.VMEM((LANES, groups * LANES), BF16),
            pltpu.VMEM((pair_width, inner), F32),
            pltpu.VMEM((inner, pair_width), F32),
        ],
        compiler_params=params(16),
        cost_estimate=cost(2 * macs, 2**20),
        name="outer",
    )(i_keep, keep, scaled, rbig, *lefts)
    gl_last = reduce(*gl_cut, "col", n_col, gw_cut[0])

    gr_cut = pl.pallas_call(
        functools.partial(right_kernel, dims, n_row),
        in_specs=[hbm()] + vmem(2),
        out_specs=vmem(2),
        out_shape=halves(j_rows * tiles, n_row),
        scratch_shapes=[
            pltpu.VMEM((depth, span), F32),
            pltpu.VMEM((width, j_pad), F32),
            pltpu.VMEM((j_rows * tiles, LANES), F32),
        ],
        compiler_params=params(18),
        cost_estimate=cost(macs, 2**20),
        name="right",
    )(gl_last[0], z, diag)
    gw_row = reduce(*gw_cut, "row", n_row, gr_cut[0])

    def pair_part(first, last, so_far, after):
        done = [] if so_far is None else [so_far]
        return pl.pallas_call(
            functools.partial(pair_kernel, dims, first, last),
            in_specs=[hbm()] + vmem(4) + [hbm()] * len(done),
            out_specs=[hbm()] + vmem(),
            out_shape=[jax.ShapeDtypeStruct(cotangent.shape, BF16), pltpu.VMEM((8, LANES), F32)],
            scratch_shapes=[
                pltpu.VMEM(((last - first) * step_rows, j_rows, pair_width), BF16),
                pltpu.SemaphoreType.DMA((last - first,)),
            ],
            input_output_aliases={5: 0} if done else {},
            compiler_params=params(12),
            cost_estimate=cost(macs // 2, 2**20),
            name="pair",
        )(after, i_keep, y, weight, inverse, *done)

    ends = (3 * steps // 8, 6 * steps // 8, steps)
    pair_out, mark = pair_part(0, ends[0], None, gw_row[0])
    gr_last = reduce(*gr_cut, "row", n_row, mark)
    gw_cut = small_call(
        functools.partial(turn_kernel, n_col),
        halves(inner // n_row, n_col),
        "turn",
        [pltpu.VMEM((inner // n_row, pair_width), F32)],
    )(mark, *gw_row)
    pair_out, mark = pair_part(ends[0], ends[1], pair_out, gw_cut[0])
    gw_last = reduce(*gw_cut, "col", n_col, mark)
    pair_out, mark = pair_part(ends[1], ends[2], pair_out, gw_last[0])

    grad_left, grad_right, grad_weight = pl.pallas_call(
        functools.partial(final_kernel, dims),
        in_specs=[hbm()] + vmem(9),
        out_specs=vmem(3),
        out_shape=[
            jax.ShapeDtypeStruct((own_left, width), F32),
            jax.ShapeDtypeStruct((own_right, width), F32),
            jax.ShapeDtypeStruct((inner // n_row // n_col, pair_width), F32),
        ],
        scratch_shapes=[pltpu.VMEM((max(own_left, own_right) * tiles, LANES), F32)],
        compiler_params=params(4),
        cost_estimate=cost(1000, 1000),
        name="final_sums",
    )(mark, i_keep, j_keep, keep, *gl_last, *gr_last, *gw_last)
    return (pair_out, grad_left, grad_right, grad_weight)


def solution(mesh):
    placed = (
        P(("grp", "row", "col"), None),
        P(("grp", "col", "row"), None),
        P("grp"),
        P("grp"),
        P(),
        P(("grp", "row"), "col", None),
    )
    return jax.shard_map(
        shards,
        mesh=mesh,
        in_specs=placed,
        out_specs=(
            P(("grp", "row"), "col", None),
            P(("grp", "row", "col"), None),
            P(("grp", "col", "row"), None),
            P(("grp", "row", "col"), None),
        ),
        check_vma=False,
    )
```

```python
import functools

import jax
import jax.numpy as jnp
from jax import lax
from jax.experimental import pallas as pl
from jax.experimental.pallas import tpu as pltpu
from jax.sharding import PartitionSpec as P

LANES = 128
NT = (((1,), (1,)), ((), ()))
F32 = jnp.float32
BF16 = jnp.bfloat16


def params(mib):
    return pltpu.CompilerParams(vmem_limit_bytes=mib * 2**20)


def cost(flops, nbytes):
    return pl.CostEstimate(flops=int(flops), bytes_accessed=int(nbytes), transcendentals=0)


def cut(source, index, n, keep_ref, send_ref):
    rows = source.shape[0] // n
    for k in range(n):
        at = pl.multiple_of((index ^ k) * rows, rows)
        into = send_ref if k % 2 else keep_ref
        into[k // 2] = source[pl.ds(at, rows), :].astype(into.dtype)


def place(buffers, index, n, flat):
    for buffer, owners in zip(buffers, owners_of(n)):
        rows = buffer.shape[1]
        for k, owner in enumerate(owners):
            at = pl.multiple_of((index ^ owner) * rows, 8)
            flat[pl.ds(at, rows), :] = buffer[k].astype(F32)


def lane_group(shape, chans):
    return lax.broadcasted_iota(jnp.int32, shape, 1) // chans


def mask_rows(res_ref, first, count):
    shape = (count, res_ref.shape[1])
    row = lax.broadcasted_iota(jnp.int32, shape, 0) + first
    here = lax.broadcasted_iota(jnp.int32, shape, 1) == row
    chosen = jnp.where(here, res_ref[...].astype(F32), 0.0)
    return jnp.broadcast_to(jnp.sum(chosen, axis=1, keepdims=True), (count, LANES))


def scale_kernel(dims, *refs):
    chans, groups, blocks, i_rows, j_rows, step_rows, sequences = dims
    tiles = sequences * chans // LANES
    res_hbm, seq_hbm, cot_ref, w_hbm, left_hbm, right_hbm = refs[:6]
    scaled_ref, inv_ref, wp_ref, keep_ref, ri_ref, rj_ref, left_ref, right_ref = refs[6:14]
    res_ref, seq_ref, w_ref, w32, cot, sems, more_sems = refs[14:]
    steps = i_rows // step_rows

    def fetch(step):
        rows = pl.ds(step * step_rows, step_rows)
        return pltpu.make_async_copy(cot_ref.at[rows], cot.at[rows], sems.at[step])

    pairs = [
        (res_hbm, res_ref),
        (seq_hbm, seq_ref),
        (w_hbm, w_ref),
        (left_hbm, left_ref.at[0]),
        (right_hbm, right_ref.at[0]),
    ]
    more = [
        pltpu.make_async_copy(source, to, more_sems.at[k]) for k, (source, to) in enumerate(pairs)
    ]
    for copy in more[:3]:
        copy.start()
    for step in range(steps):
        fetch(step).start()
    for copy in more[3:]:
        copy.start()
    shape = (sequences, tiles * LANES)
    own = lax.broadcasted_iota(jnp.int32, shape, 1) // chans
    repeat = (own == lax.broadcasted_iota(jnp.int32, shape, 0)).astype(F32).astype(BF16)
    more[0].wait()
    ri_ref[...] = mask_rows(res_ref, lax.axis_index("row") * i_rows, i_rows)
    rj_ref[...] = mask_rows(res_ref, lax.axis_index("col") * j_rows, j_rows)
    more[1].wait()
    seq = seq_ref[...].astype(F32)
    keep_ref[...] = jnp.dot(
        jnp.broadcast_to(seq, (8, sequences)).astype(BF16), repeat, preferred_element_type=F32
    )[0:1]
    valid = jnp.sum(seq, axis=1, keepdims=True)
    inv_ref[...] = 1.0 / jnp.maximum(valid * rj_ref[...], 1.0)
    more[2].wait()
    w32[...] = w_ref[...].astype(F32)
    for e in range(chans):
        wp_ref[e * chans : (e + 1) * chans, :] = w32[pl.ds(e, chans, stride=chans), :].astype(BF16)
    for step in range(steps):
        fetch(step).wait()
        for i in range(step_rows):
            at = step * step_rows + i
            inverse = jnp.where(ri_ref[at : at + 1, :] > 0, inv_ref[...], 1.0)
            scaled_ref[at] = (cot[at].astype(F32) * inverse).astype(BF16)
    more[3].wait()
    more[4].wait()


def inner_kernel(dims, after, scaled_ref, wp_ref, z_ref):
    chans, groups, blocks, i_rows, j_rows, step_rows, sequences = dims
    for step in range(i_rows // step_rows):
        rows = slice(step * step_rows, (step + 1) * step_rows)
        scaled = scaled_ref[rows].reshape(step_rows * j_rows, LANES)
        for pair in range(0, blocks, 2):
            part = lax.dot_general(
                scaled,
                wp_ref[pair * LANES : (pair + 2) * LANES, :],
                NT,
                preferred_element_type=F32,
            ).astype(BF16)
            for k in range(2):
                a = pair + k
                for i in range(step_rows):
                    z_ref[
                        step, a * j_rows : (a + 1) * j_rows, i * LANES : (i + 1) * LANES
                    ] = part[i * j_rows : (i + 1) * j_rows, k * LANES : (k + 1) * LANES]


def outer_kernel(dims, n_row, n_col, *refs):
    chans, groups, blocks, i_rows, j_rows, step_rows, sequences = dims
    tiles = sequences * chans // LANES
    ri_ref, keep_ref, scaled_ref, rbig, left_held, left_came = refs[:6]
    y_ref, diag_ref, keep_out, send_out = refs[6:10]
    flat, lsplit, expand, gwt, gwr = refs[10:]
    place((left_held, left_came), lax.axis_index("col"), n_col, flat)
    for t in range(tiles):
        lanes = slice(t * LANES, (t + 1) * LANES)
        masked = flat[0:i_rows, lanes] * ri_ref[...] * keep_ref[:, lanes]
        lsplit[pl.ds(t, i_rows, stride=tiles), :] = masked
    shape = (LANES, groups * LANES)
    source = lax.broadcasted_iota(jnp.int32, shape, 0)
    target = lax.broadcasted_iota(jnp.int32, shape, 1)
    same = (source // chans == target // LANES) & (source % chans == target % chans)
    expand[...] = same.astype(F32).astype(BF16)
    gwt[...] = jnp.zeros_like(gwt)
    rows = step_rows * tiles
    pairs = step_rows * j_rows
    group = lane_group((tiles, LANES), chans)

    def body(step, carry):
        spread = jnp.dot(
            lsplit[pl.ds(pl.multiple_of(step * rows, rows), rows), :].astype(BF16),
            expand[...],
            preferred_element_type=F32,
        ).astype(BF16)
        for b in range(groups):
            chosen = (group == b).astype(F32).astype(BF16)
            for lo in range(groups):
                at = b * sequences + lo * tiles
                for i in range(step_rows):
                    diag_ref[step, at : at + tiles, i * LANES : (i + 1) * LANES] = (
                        spread[i * tiles : (i + 1) * tiles, lo * LANES : (lo + 1) * LANES] * chosen
                    )
        for pair in range(0, step_rows, 2):
            part = jnp.dot(
                rbig[...],
                diag_ref[step, :, pair * LANES : (pair + 2) * LANES],
                preferred_element_type=F32,
            ).astype(BF16)
            for k in range(2):
                for a in range(blocks):
                    y_ref[step * step_rows + pair + k, :, a * LANES : (a + 1) * LANES] = part[
                        a * j_rows : (a + 1) * j_rows, k * LANES : (k + 1) * LANES
                    ]
        block = pl.ds(step * step_rows, step_rows)
        scaled_t = scaled_ref[block].reshape(pairs, LANES).T
        y_flat = y_ref[block].reshape(pairs, blocks * LANES)
        gwt[...] += jnp.dot(scaled_t, y_flat, preferred_element_type=F32)
        return carry

    lax.fori_loop(0, i_rows // step_rows, body, 0, unroll=True)
    for k in range(blocks):
        turned_tile = gwt[:, k * LANES : (k + 1) * LANES].T
        for q in range(groups):
            gwr[pl.ds(k * groups + q, chans, stride=chans), :] = turned_tile[
                q * chans : (q + 1) * chans
            ]
    cut(gwr, lax.axis_index("row"), n_row, keep_out, send_out)


def right_sum(first, last, z_ref, diag_ref, acc, so_far=None):
    for step in range(first, last):
        part = lax.dot_general(diag_ref[step], z_ref[step], NT, preferred_element_type=F32)
        acc[...] = part if so_far is None else so_far[...] + part
        so_far = acc


def right_first_kernel(steps, after, z_ref, diag_ref, acc):
    right_sum(0, steps // 2, z_ref, diag_ref, acc)


def right_kernel(dims, n_row, *refs):
    chans, groups, blocks, i_rows, j_rows, step_rows, sequences = dims
    tiles = sequences * chans // LANES
    j_pad = -(-j_rows // LANES) * LANES
    after, z_ref, diag_ref, acc_first = refs[:4]
    keep_out, send_out, acc, turned, gr_all = refs[4:]
    steps = i_rows // step_rows
    right_sum(steps // 2, steps, z_ref, diag_ref, acc, acc_first)
    for a in range(blocks):
        at, shift = divmod(a * j_rows, LANES)
        mine = acc[:, at * LANES : at * LANES + j_pad]
        if shift:
            mine = pltpu.roll(mine, LANES - shift, axis=1)
        for b in range(groups):
            for lo in range(groups):
                first = b * sequences + lo * tiles
                turned[pl.ds(lo * chans + groups * a + b, tiles, stride=LANES), :] = mine[
                    first : first + tiles
                ]
    for t in range(tiles):
        lanes = slice(t * LANES, (t + 1) * LANES)
        gr_all[pl.ds(t, j_rows, stride=tiles), :] = turned[lanes, :].T[:j_rows]
    cut(gr_all, lax.axis_index("row"), n_row, keep_out, send_out)


def left_kernel(dims, n_row, n_col, *refs):
    chans, groups, blocks, i_rows, j_rows, step_rows, sequences = dims
    tiles = sequences * chans // LANES
    j_pad = -(-j_rows // LANES) * LANES
    after, rj_ref, keep_ref, z_ref, right_held, right_came = refs[:6]
    rbig, keep_out, send_out = refs[6:9]
    flat, turned, rbt, gl_all = refs[9:]
    place((right_held, right_came), lax.axis_index("row"), n_row, flat)
    for t in range(tiles):
        lanes = slice(t * LANES, (t + 1) * LANES)
        masked = flat[0:j_rows, lanes] * rj_ref[...] * keep_ref[:, lanes]
        if j_rows < j_pad:
            masked = jnp.concatenate([masked, jnp.zeros((j_pad - j_rows, LANES), F32)], axis=0)
        turned[lanes, :] = masked.T
    for a in range(blocks):
        parts = [
            turned[pl.ds(lo * chans + groups * a + b, tiles, stride=LANES), :]
            for b in range(groups)
            for lo in range(groups)
        ]
        block = jnp.concatenate(parts, axis=0)
        rbig[a * j_rows : (a + 1) * j_rows, :] = block.T[:j_rows].astype(BF16)
    rbt[...] = rbig[...].T
    group = lane_group((sequences, LANES), chans)
    group_t = lane_group((tiles, LANES), chans)

    def body(step, carry):
        for pair in range(0, step_rows, 2):
            part = jnp.dot(
                rbt[...],
                z_ref[step, :, pair * LANES : (pair + 2) * LANES],
                preferred_element_type=F32,
            )
            for k in range(2):
                mine = part[:, k * LANES : (k + 1) * LANES]
                total = mine[0:sequences]
                for b in range(1, groups):
                    total = jnp.where(group == b, mine[b * sequences : (b + 1) * sequences], total)
                shift = LANES // 2
                while shift >= chans:
                    total = total + pltpu.roll(total, shift, axis=1)
                    shift //= 2
                merged = total[0:tiles]
                for lo in range(1, groups):
                    merged = jnp.where(group_t == lo, total[lo * tiles : (lo + 1) * tiles], merged)
                at = (step * step_rows + pair + k) * tiles
                gl_all[pl.ds(pl.multiple_of(at, tiles), tiles), :] = merged
        return carry

    lax.fori_loop(0, i_rows // step_rows, body, 0, unroll=True)
    cut(gl_all, lax.axis_index("col"), n_col, keep_out, send_out)


def total_of(keep_ref, came_ref, k=0):
    return keep_ref[k].astype(F32) + came_ref[k].astype(F32)


def join_kernel(after, held_ref, came_ref, out_ref):
    count = held_ref.shape[0]
    for k in range(count):
        out_ref[k] = held_ref[k]
        out_ref[count + k] = came_ref[k]


def fold_kernel(after, held_ref, came_ref, keep_out, send_out):
    for k in range(held_ref.shape[0]):
        into = send_out if k % 2 else keep_out
        into[k // 2] = total_of(held_ref, came_ref, k).astype(into.dtype)


def turn_kernel(n_col, after, held_ref, came_ref, keep_out, send_out, whole):
    whole[...] = total_of(held_ref, came_ref)
    cut(whole, lax.axis_index("col"), n_col, keep_out, send_out)


def write_rows(whole, rows, keep_ref, out_ref, tiles):
    own = out_ref.shape[0]
    for t in range(tiles):
        lanes = slice(t * LANES, (t + 1) * LANES)
        out_ref[:, lanes] = whole[pl.ds(t, own, stride=tiles), :] * (
            rows * keep_ref[:, lanes]
        )


def pair_rows(dims, step, ri_ref, y_ref, wp_ref, inv_ref, out_ref, at):
    chans, groups, blocks, i_rows, j_rows, step_rows, sequences = dims
    pairs = step_rows * j_rows
    y_flat = y_ref[step * step_rows : (step + 1) * step_rows].reshape(pairs, blocks * LANES)
    projected = jnp.dot(y_flat, wp_ref[...], preferred_element_type=F32)
    for i in range(step_rows):
        row = step * step_rows + i
        inverse = jnp.where(ri_ref[row : row + 1, :] > 0, inv_ref[...], 1.0)
        out_ref[at + i] = (projected[i * j_rows : (i + 1) * j_rows] * inverse).astype(BF16)


def pair_first_kernel(dims, steps, after, ri_ref, y_ref, wp_ref, inv_ref, out_ref):
    for step in range(steps):
        pair_rows(dims, step, ri_ref, y_ref, wp_ref, inv_ref, out_ref, step * dims[5])


def pair_kernel(dims, *refs):
    i_rows, j_rows, step_rows = dims[3:6]
    after_left, after_right, ri_ref, y_ref, wp_ref, inv_ref, early = refs[:7]
    out_ref, staged, sems = refs[7:]
    begin = early.shape[0]
    copies = [pltpu.make_async_copy(early, out_ref.at[pl.ds(0, begin)], sems.at[0])]
    copies[0].start()
    for step in range(begin // step_rows, i_rows // step_rows):
        at = step * step_rows - begin
        pair_rows(dims, step, ri_ref, y_ref, wp_ref, inv_ref, staged, at)
        copies.append(
            pltpu.make_async_copy(
                staged.at[pl.ds(at, step_rows)],
                out_ref.at[pl.ds(begin + at, step_rows)],
                sems.at[len(copies)],
            )
        )
        copies[-1].start()
    for copy in copies:
        copy.wait()


def final_kernel(dims, after, ri_ref, rj_ref, keep_ref, *refs):
    chans, groups, blocks, i_rows, j_rows, step_rows, sequences = dims
    tiles = sequences * chans // LANES
    left, right, weight = refs[0:2], refs[2:4], refs[4:6]
    gl_out, gr_out, gw_out, whole = refs[6:]
    for refs_in, out, rows_ref, axis in (
        (left, gl_out, ri_ref, "col"),
        (right, gr_out, rj_ref, "row"),
    ):
        own = out.shape[0]
        whole[0 : own * tiles, :] = total_of(*refs_in)
        first = pl.multiple_of(lax.axis_index(axis) * own, 8)
        write_rows(whole, rows_ref[pl.ds(first, own), :], keep_ref, out, tiles)
    gw_out[...] = total_of(*weight)


def swap(array, axis, n, bit):
    return lax.ppermute(array, axis, [(s, s ^ bit) for s in range(n)])


def owners_of(n):
    held, bit = [0], n // 2
    while bit > 1:
        held, bit = held + [k ^ bit for k in held], bit // 2
    return held, [k ^ 1 for k in held]


def gather(block, own, axis, n, after):
    held, sent, bit = own, block[None], n // 2
    while bit > 1:
        came = swap(sent, axis, n, bit)
        shape = (2 * held.shape[0],) + held.shape[1:]
        held = small_call(join_kernel, [pltpu.VMEM(shape, BF16)], "join")(after, held, came)[0]
        sent, bit = held, bit // 2
    return held, swap(sent, axis, n, 1)


def reduce(keep, send, axis, n, after):
    bit = 1
    while True:
        came = swap(send, axis, n, bit)
        bit *= 2
        if bit >= n:
            return keep, came
        half = (keep.shape[0] // 2,) + keep.shape[1:]
        outs = [pltpu.VMEM(half, F32), pltpu.VMEM(half, BF16)]
        keep, send = small_call(fold_kernel, outs, "fold")(after, keep, came)


def small_call(body, outs, name, scratch=()):
    def call(after, *operands):
        return pl.pallas_call(
            body,
            in_specs=[hbm()] + vmem(len(operands)),
            out_specs=vmem(len(outs)),
            out_shape=outs,
            scratch_shapes=list(scratch),
            compiler_params=params(4),
            cost_estimate=cost(1000, 1000),
            name=name,
        )(after, *operands)

    return call


def halves(rows, n):
    return [pltpu.VMEM((n // 2, rows // n, LANES), BF16)] * 2


def vmem(count=1):
    return [pl.BlockSpec(memory_space=pltpu.VMEM)] * count


def hbm():
    return pl.BlockSpec(memory_space=pl.ANY)


def in_hbm(array):
    return pltpu.with_memory_space_constraint(array, pltpu.HBM)


def shards(left_act, right_act, row_mask, res_mask, out_weight, cotangent):
    n_col = lax.axis_size("col")
    n_row = lax.axis_size("row")
    i_rows, j_rows, pair_width = cotangent.shape
    sequences = row_mask.shape[0]
    width = left_act.shape[1]
    chans = width // sequences
    groups = LANES // chans
    blocks = chans // groups
    tiles = width // LANES
    depth = groups * sequences
    inner = chans * chans
    step_rows = 8
    steps = i_rows // step_rows
    dims = (chans, groups, blocks, i_rows, j_rows, step_rows, sequences)
    j_pad = -(-j_rows // LANES) * LANES
    span = blocks * j_rows
    own_left, own_right = left_act.shape[0], right_act.shape[0]
    macs = i_rows * j_rows * inner * pair_width

    mask_row = (res_mask.reshape(1, -1), row_mask.reshape(1, -1))
    scaled, inverse, weight, keep, i_keep, j_keep, own_l, own_r = pl.pallas_call(
        functools.partial(scale_kernel, dims),
        in_specs=[hbm()] * 6,
        out_specs=vmem(8),
        out_shape=[
            pltpu.VMEM(cotangent.shape, BF16),
            pltpu.VMEM((j_rows, LANES), F32),
            pltpu.VMEM(out_weight.shape, BF16),
            pltpu.VMEM((1, width), F32),
            pltpu.VMEM((i_rows, LANES), F32),
            pltpu.VMEM((j_rows, LANES), F32),
            pltpu.VMEM((1,) + left_act.shape, BF16),
            pltpu.VMEM((1,) + right_act.shape, BF16),
        ],
        scratch_shapes=[
            pltpu.VMEM((1, res_mask.shape[0]), jnp.int32),
            pltpu.VMEM((1, sequences), jnp.int32),
            pltpu.VMEM(out_weight.shape, BF16),
            pltpu.VMEM(out_weight.shape, F32),
            pltpu.VMEM(cotangent.shape, BF16),
            pltpu.SemaphoreType.DMA((steps,)),
            pltpu.SemaphoreType.DMA((5,)),
        ],
        compiler_params=params(12),
        cost_estimate=cost(16 * macs, 2**20),
        name="scale",
    )(*map(in_hbm, (*mask_row, cotangent, out_weight, left_act, right_act)))

    lefts = gather(left_act, own_l, "col", n_col, own_l)
    rights = gather(right_act, own_r, "row", n_row, lefts[0])

    z = pl.pallas_call(
        functools.partial(inner_kernel, dims),
        in_specs=[hbm()] + vmem(2),
        out_specs=vmem()[0],
        out_shape=pltpu.VMEM((steps, span, step_rows * LANES), BF16),
        compiler_params=params(12),
        cost_estimate=cost(16 * macs, 2**20),
        name="inner",
    )(rights[0], scaled, weight)

    rbig, *gl_cut = pl.pallas_call(
        functools.partial(left_kernel, dims, n_row, n_col),
        in_specs=[hbm()] + vmem(5),
        out_specs=vmem(3),
        out_shape=[pltpu.VMEM((span, depth), BF16)] + halves(i_rows * tiles, n_col),
        scratch_shapes=[
            pltpu.VMEM((j_rows, width), F32),
            pltpu.VMEM((width, j_pad), F32),
            pltpu.VMEM((depth, span), BF16),
            pltpu.VMEM((i_rows * tiles, LANES), F32),
        ],
        compiler_params=params(16),
        cost_estimate=cost(16 * macs, 2**20),
        name="left",
    )(z, j_keep, keep, z, *rights)

    y, diag, *gw_cut = pl.pallas_call(
        functools.partial(outer_kernel, dims, n_row, n_col),
        in_specs=vmem(6),
        out_specs=vmem(4),
        out_shape=[
            pltpu.VMEM((i_rows, j_rows, inner), BF16),
            pltpu.VMEM((steps, depth, step_rows * LANES), BF16),
        ]
        + halves(inner, n_row),
        scratch_shapes=[
            pltpu.VMEM((i_rows, width), F32),
            pltpu.VMEM((i_rows * tiles, LANES), F32),
            pltpu.VMEM((LANES, groups * LANES), BF16),
            pltpu.VMEM((pair_width, inner), F32),
            pltpu.VMEM((inner, pair_width), F32),
        ],
        compiler_params=params(16),
        cost_estimate=cost(16 * macs, 2**20),
        name="outer",
    )(i_keep, keep, scaled, rbig, *lefts)
    gl_last = reduce(*gl_cut, "col", n_col, gw_cut[0])

    acc = pl.pallas_call(
        functools.partial(right_first_kernel, steps),
        in_specs=[hbm()] + vmem(2),
        out_specs=vmem()[0],
        out_shape=pltpu.VMEM((depth, span), F32),
        compiler_params=params(12),
        cost_estimate=cost(16 * macs, 2**20),
        name="right_first",
    )(gl_last[0], z, diag)
    gw_row = reduce(*gw_cut, "row", n_row, acc)
    gr_cut = pl.pallas_call(
        functools.partial(right_kernel, dims, n_row),
        in_specs=[hbm()] + vmem(3),
        out_specs=vmem(2),
        out_shape=halves(j_rows * tiles, n_row),
        scratch_shapes=[
            pltpu.VMEM((depth, span), F32),
            pltpu.VMEM((width, j_pad), F32),
            pltpu.VMEM((j_rows * tiles, LANES), F32),
        ],
        compiler_params=params(18),
        cost_estimate=cost(16 * macs, 2**20),
        name="right",
    )(gw_row[0], z, diag, acc)
    gw_cut = small_call(
        functools.partial(turn_kernel, n_col),
        halves(inner // n_row, n_col),
        "turn",
        [pltpu.VMEM((inner // n_row, pair_width), F32)],
    )(gr_cut[0], *gw_row)

    half = steps // 2
    early = pl.pallas_call(
        functools.partial(pair_first_kernel, dims, half),
        in_specs=[hbm()] + vmem(4),
        out_specs=vmem()[0],
        out_shape=pltpu.VMEM((half * step_rows, j_rows, pair_width), BF16),
        compiler_params=params(12),
        cost_estimate=cost(16 * macs, 2**20),
        name="pair_first",
    )(gw_cut[0], i_keep, y, weight, inverse)
    gw_last = reduce(*gw_cut, "col", n_col, early)
    gr_last = reduce(*gr_cut, "row", n_row, gw_last[0])
    pair_out = pl.pallas_call(
        functools.partial(pair_kernel, dims),
        in_specs=[hbm()] * 2 + vmem(5),
        out_specs=hbm(),
        out_shape=jax.ShapeDtypeStruct(cotangent.shape, BF16),
        scratch_shapes=[
            pltpu.VMEM((i_rows - half * step_rows, j_rows, pair_width), BF16),
            pltpu.SemaphoreType.DMA((1 + steps - half,)),
        ],
        compiler_params=params(12),
        cost_estimate=cost(16 * macs, 2**20),
        name="pair",
    )(gl_last[1], gr_last[0], i_keep, y, weight, inverse, early)

    grad_left, grad_right, grad_weight = pl.pallas_call(
        functools.partial(final_kernel, dims),
        in_specs=[hbm()] + vmem(9),
        out_specs=vmem(3),
        out_shape=[
            jax.ShapeDtypeStruct((own_left, width), F32),
            jax.ShapeDtypeStruct((own_right, width), F32),
            jax.ShapeDtypeStruct((inner // n_row // n_col, pair_width), F32),
        ],
        scratch_shapes=[pltpu.VMEM((max(own_left, own_right) * tiles, LANES), F32)],
        compiler_params=params(4),
        cost_estimate=cost(1000, 1000),
        name="final_sums",
    )(in_hbm(pair_out), i_keep, j_keep, keep, *gl_last, *gr_last, *gw_last)
    return (pair_out, grad_left, grad_right, grad_weight)


def solution(mesh):
    placed = (
        P(("grp", "row", "col"), None),
        P(("grp", "col", "row"), None),
        P("grp"),
        P("grp"),
        P(),
        P(("grp", "row"), "col", None),
    )
    return jax.shard_map(
        shards,
        mesh=mesh,
        in_specs=placed,
        out_specs=(
            P(("grp", "row"), "col", None),
            P(("grp", "row", "col"), None),
            P(("grp", "col", "row"), None),
            P(("grp", "row", "col"), None),
        ),
        check_vma=False,
    )
```

```python
import functools

import jax
import jax.numpy as jnp
from jax import lax
from jax.experimental import pallas as pl
from jax.experimental.pallas import tpu as pltpu
from jax.sharding import PartitionSpec as P

LANES = 128
NT = (((1,), (1,)), ((), ()))
F32 = jnp.float32
BF16 = jnp.bfloat16


def params(mib):
    return pltpu.CompilerParams(vmem_limit_bytes=mib * 2**20)


def cost(flops, nbytes):
    return pl.CostEstimate(flops=int(flops), bytes_accessed=int(nbytes), transcendentals=0)


def cut(source, index, n, keep_ref, send_ref):
    rows = source.shape[0] // n
    for k in range(n):
        at = pl.multiple_of((index ^ k) * rows, rows)
        into = send_ref if k % 2 else keep_ref
        into[k // 2] = source[pl.ds(at, rows), :].astype(into.dtype)


def place(buffers, index, n, flat):
    for buffer, owners in zip(buffers, owners_of(n)):
        rows = buffer.shape[1]
        for k, owner in enumerate(owners):
            at = pl.multiple_of((index ^ owner) * rows, 8)
            flat[pl.ds(at, rows), :] = buffer[k].astype(F32)


def lane_group(shape, chans):
    return lax.broadcasted_iota(jnp.int32, shape, 1) // chans


def mask_rows(res_ref, first, count):
    shape = (count, res_ref.shape[1])
    row = lax.broadcasted_iota(jnp.int32, shape, 0) + first
    here = lax.broadcasted_iota(jnp.int32, shape, 1) == row
    chosen = jnp.where(here, res_ref[...].astype(F32), 0.0)
    return jnp.broadcast_to(jnp.sum(chosen, axis=1, keepdims=True), (count, LANES))


def scale_kernel(dims, *refs):
    chans, groups, blocks, i_rows, j_rows, step_rows, sequences = dims
    tiles = sequences * chans // LANES
    res_hbm, seq_hbm, cot_ref, w_hbm, left_hbm, right_hbm = refs[:6]
    scaled_ref, inv_ref, wp_ref, keep_ref, ri_ref, rj_ref, left_ref, right_ref, z_ref = refs[6:15]
    res_ref, seq_ref, w_ref, w32, cot, sems, more_sems = refs[15:]
    steps = i_rows // step_rows

    def fetch(step):
        rows = pl.ds(step * step_rows, step_rows)
        return pltpu.make_async_copy(cot_ref.at[rows], cot.at[rows], sems.at[step])

    pairs = [
        (res_hbm, res_ref),
        (seq_hbm, seq_ref),
        (w_hbm, w_ref),
        (left_hbm, left_ref.at[0]),
        (right_hbm, right_ref.at[0]),
    ]
    more = [
        pltpu.make_async_copy(source, to, more_sems.at[k]) for k, (source, to) in enumerate(pairs)
    ]
    for copy in more[:3]:
        copy.start()
    for step in range(steps):
        fetch(step).start()
    for copy in more[3:]:
        copy.start()
    shape = (sequences, tiles * LANES)
    own = lax.broadcasted_iota(jnp.int32, shape, 1) // chans
    repeat = (own == lax.broadcasted_iota(jnp.int32, shape, 0)).astype(F32).astype(BF16)
    more[0].wait()
    ri_ref[...] = mask_rows(res_ref, lax.axis_index("row") * i_rows, i_rows)
    rj_ref[...] = mask_rows(res_ref, lax.axis_index("col") * j_rows, j_rows)
    more[1].wait()
    seq = seq_ref[...].astype(F32)
    keep_ref[...] = jnp.dot(
        jnp.broadcast_to(seq, (8, sequences)).astype(BF16), repeat, preferred_element_type=F32
    )[0:1]
    valid = jnp.sum(seq, axis=1, keepdims=True)
    inv_ref[...] = 1.0 / jnp.maximum(valid * rj_ref[...], 1.0)
    more[2].wait()
    w32[...] = w_ref[...].astype(F32)
    for e in range(chans):
        wp_ref[e * chans : (e + 1) * chans, :] = w32[pl.ds(e, chans, stride=chans), :].astype(BF16)
    for step in range(steps):
        fetch(step).wait()
        for i in range(step_rows):
            at = step * step_rows + i
            inverse = jnp.where(ri_ref[at : at + 1, :] > 0, inv_ref[...], 1.0)
            scaled_ref[at] = (cot[at].astype(F32) * inverse).astype(BF16)
        if step < z_ref.shape[0]:
            rows = slice(step * step_rows, (step + 1) * step_rows)
            inner_rows(dims, scaled_ref[rows], wp_ref, z_ref, step)
    more[3].wait()
    more[4].wait()


def inner_rows(dims, scaled, wp_ref, z_ref, at):
    chans, groups, blocks, i_rows, j_rows, step_rows, sequences = dims
    for pair in range(0, blocks, 2):
        part = lax.dot_general(
            scaled.reshape(step_rows * j_rows, LANES),
            wp_ref[pair * LANES : (pair + 2) * LANES, :],
            NT,
            preferred_element_type=F32,
        ).astype(BF16)
        for k in range(2):
            a = pair + k
            for i in range(step_rows):
                z_ref[at, a * j_rows : (a + 1) * j_rows, i * LANES : (i + 1) * LANES] = part[
                    i * j_rows : (i + 1) * j_rows, k * LANES : (k + 1) * LANES
                ]


def inner_kernel(dims, first, after, scaled_ref, wp_ref, z_ref):
    step_rows = dims[5]
    for at in range(z_ref.shape[0]):
        rows = slice((first + at) * step_rows, (first + at + 1) * step_rows)
        inner_rows(dims, scaled_ref[rows], wp_ref, z_ref, at)


def at_step(refs, step):
    for ref in refs:
        if step < ref.shape[0]:
            return ref.at[step]
        step -= ref.shape[0]


def outer_kernel(dims, n_row, n_col, *refs):
    chans, groups, blocks, i_rows, j_rows, step_rows, sequences = dims
    tiles = sequences * chans // LANES
    ri_ref, keep_ref, scaled_ref, rbig, left_held, left_came = refs[:6]
    y_ref, diag_ref, keep_out, send_out = refs[6:10]
    flat, lsplit, expand, gwt, gwr = refs[10:]
    place((left_held, left_came), lax.axis_index("col"), n_col, flat)
    for t in range(tiles):
        lanes = slice(t * LANES, (t + 1) * LANES)
        masked = flat[0:i_rows, lanes] * ri_ref[...] * keep_ref[:, lanes]
        lsplit[pl.ds(t, i_rows, stride=tiles), :] = masked
    shape = (LANES, groups * LANES)
    source = lax.broadcasted_iota(jnp.int32, shape, 0)
    target = lax.broadcasted_iota(jnp.int32, shape, 1)
    same = (source // chans == target // LANES) & (source % chans == target % chans)
    expand[...] = same.astype(F32).astype(BF16)
    rows = step_rows * tiles
    pairs = step_rows * j_rows
    group = lane_group((tiles, LANES), chans)

    for step in range(i_rows // step_rows):
        spread = jnp.dot(
            lsplit[step * rows : (step + 1) * rows, :].astype(BF16),
            expand[...],
            preferred_element_type=F32,
        ).astype(BF16)
        for b in range(groups):
            chosen = (group == b).astype(F32).astype(BF16)
            for lo in range(groups):
                at = b * sequences + lo * tiles
                for i in range(step_rows):
                    diag_ref[step, at : at + tiles, i * LANES : (i + 1) * LANES] = (
                        spread[i * tiles : (i + 1) * tiles, lo * LANES : (lo + 1) * LANES] * chosen
                    )
        for pair in range(0, step_rows, 2):
            part = jnp.dot(
                rbig[...],
                diag_ref[step, :, pair * LANES : (pair + 2) * LANES],
                preferred_element_type=F32,
            ).astype(BF16)
            for k in range(2):
                for a in range(blocks):
                    y_ref[step * step_rows + pair + k, :, a * LANES : (a + 1) * LANES] = part[
                        a * j_rows : (a + 1) * j_rows, k * LANES : (k + 1) * LANES
                    ]
        block = slice(step * step_rows, (step + 1) * step_rows)
        scaled_t = scaled_ref[block].reshape(pairs, LANES).T
        y_flat = y_ref[block].reshape(pairs, blocks * LANES)
        part = jnp.dot(scaled_t, y_flat, preferred_element_type=F32)
        gwt[...] = gwt[...] + part if step else part
    for k in range(blocks):
        turned_tile = gwt[:, k * LANES : (k + 1) * LANES].T
        for q in range(groups):
            gwr[pl.ds(k * groups + q, chans, stride=chans), :] = turned_tile[
                q * chans : (q + 1) * chans
            ]
    cut(gwr, lax.axis_index("row"), n_row, keep_out, send_out)


def right_kernel(dims, n_row, after, diag_ref, *refs):
    chans, groups, blocks, i_rows, j_rows, step_rows, sequences = dims
    tiles = sequences * chans // LANES
    j_pad = -(-j_rows // LANES) * LANES
    z_refs, (keep_out, send_out, acc, turned, gr_all) = refs[:-5], refs[-5:]
    for step in range(i_rows // step_rows):
        part = lax.dot_general(
            diag_ref[step], at_step(z_refs, step)[...], NT, preferred_element_type=F32
        )
        acc[...] = acc[...] + part if step else part
    for a in range(blocks):
        at, shift = divmod(a * j_rows, LANES)
        mine = acc[:, at * LANES : at * LANES + j_pad]
        if shift:
            mine = pltpu.roll(mine, LANES - shift, axis=1)
        for b in range(groups):
            for lo in range(groups):
                first = b * sequences + lo * tiles
                turned[pl.ds(lo * chans + groups * a + b, tiles, stride=LANES), :] = mine[
                    first : first + tiles
                ]
    for t in range(tiles):
        lanes = slice(t * LANES, (t + 1) * LANES)
        gr_all[pl.ds(t, j_rows, stride=tiles), :] = turned[lanes, :].T[:j_rows]
    cut(gr_all, lax.axis_index("row"), n_row, keep_out, send_out)


def right_rows_kernel(dims, n_row, after, rj_ref, keep_ref, right_held, right_came, *refs):
    chans, groups, blocks, i_rows, j_rows, step_rows, sequences = dims
    tiles = sequences * chans // LANES
    j_pad = -(-j_rows // LANES) * LANES
    rbig, rbt_ref, flat, turned = refs
    place((right_held, right_came), lax.axis_index("row"), n_row, flat)
    for t in range(tiles):
        lanes = slice(t * LANES, (t + 1) * LANES)
        masked = flat[0:j_rows, lanes] * rj_ref[...] * keep_ref[:, lanes]
        if j_rows < j_pad:
            masked = jnp.concatenate([masked, jnp.zeros((j_pad - j_rows, LANES), F32)], axis=0)
        turned[lanes, :] = masked.T
    for a in range(blocks):
        parts = [
            turned[pl.ds(lo * chans + groups * a + b, tiles, stride=LANES), :]
            for b in range(groups)
            for lo in range(groups)
        ]
        block = jnp.concatenate(parts, axis=0)
        rbig[a * j_rows : (a + 1) * j_rows, :] = block.T[:j_rows].astype(BF16)
    rbt_ref[...] = rbig[...].T


def left_kernel(dims, n_col, after, rbt_ref, *refs):
    chans, groups, blocks, i_rows, j_rows, step_rows, sequences = dims
    tiles = sequences * chans // LANES
    z_refs, (keep_out, send_out, gl_all) = refs[:-3], refs[-3:]
    group = lane_group((sequences, LANES), chans)
    group_t = lane_group((tiles, LANES), chans)

    for step in range(i_rows // step_rows):
        z_ref = at_step(z_refs, step)
        for pair in range(0, step_rows, 2):
            part = jnp.dot(
                rbt_ref[...],
                z_ref[:, pair * LANES : (pair + 2) * LANES],
                preferred_element_type=F32,
            )
            for k in range(2):
                mine = part[:, k * LANES : (k + 1) * LANES]
                total = mine[0:sequences]
                for b in range(1, groups):
                    total = jnp.where(group == b, mine[b * sequences : (b + 1) * sequences], total)
                shift = LANES // 2
                while shift >= chans:
                    total = total + pltpu.roll(total, shift, axis=1)
                    shift //= 2
                merged = total[0:tiles]
                for lo in range(1, groups):
                    merged = jnp.where(group_t == lo, total[lo * tiles : (lo + 1) * tiles], merged)
                at = (step * step_rows + pair + k) * tiles
                gl_all[at : at + tiles, :] = merged
    cut(gl_all, lax.axis_index("col"), n_col, keep_out, send_out)


def total_of(keep_ref, came_ref, k=0):
    return keep_ref[k].astype(F32) + came_ref[k].astype(F32)


def join_kernel(after, held_ref, came_ref, out_ref):
    count = held_ref.shape[0]
    for k in range(count):
        out_ref[k] = held_ref[k]
        out_ref[count + k] = came_ref[k]


def fold_kernel(after, held_ref, came_ref, keep_out, send_out):
    for k in range(held_ref.shape[0]):
        into = send_out if k % 2 else keep_out
        into[k // 2] = total_of(held_ref, came_ref, k).astype(into.dtype)


def turn_kernel(n_col, after, held_ref, came_ref, keep_out, send_out, whole):
    whole[...] = total_of(held_ref, came_ref)
    cut(whole, lax.axis_index("col"), n_col, keep_out, send_out)


def write_rows(whole, rows, keep_ref, out_ref, tiles):
    own = out_ref.shape[0]
    for t in range(tiles):
        lanes = slice(t * LANES, (t + 1) * LANES)
        out_ref[:, lanes] = whole[pl.ds(t, own, stride=tiles), :] * (
            rows * keep_ref[:, lanes]
        )


def pair_rows(dims, step, ri_ref, y_ref, wp_ref, inv_ref, out_ref, at):
    chans, groups, blocks, i_rows, j_rows, step_rows, sequences = dims
    pairs = step_rows * j_rows
    y_flat = y_ref[step * step_rows : (step + 1) * step_rows].reshape(pairs, blocks * LANES)
    projected = jnp.dot(y_flat, wp_ref[...], preferred_element_type=F32)
    for i in range(step_rows):
        row = step * step_rows + i
        inverse = jnp.where(ri_ref[row : row + 1, :] > 0, inv_ref[...], 1.0)
        out_ref[at + i] = (projected[i * j_rows : (i + 1) * j_rows] * inverse).astype(BF16)


def pair_first_kernel(dims, steps, after, ri_ref, y_ref, wp_ref, inv_ref, out_ref):
    for step in range(steps):
        pair_rows(dims, step, ri_ref, y_ref, wp_ref, inv_ref, out_ref, step * dims[5])


def pair_kernel(dims, *refs):
    i_rows, j_rows, step_rows = dims[3:6]
    after_left, after_right, ri_ref, y_ref, wp_ref, inv_ref, early = refs[:7]
    out_ref, staged, sems = refs[7:]
    begin = early.shape[0]
    copies = [pltpu.make_async_copy(early, out_ref.at[pl.ds(0, begin)], sems.at[0])]
    copies[0].start()
    for step in range(begin // step_rows, i_rows // step_rows):
        at = step * step_rows - begin
        pair_rows(dims, step, ri_ref, y_ref, wp_ref, inv_ref, staged, at)
        copies.append(
            pltpu.make_async_copy(
                staged.at[pl.ds(at, step_rows)],
                out_ref.at[pl.ds(begin + at, step_rows)],
                sems.at[len(copies)],
            )
        )
        copies[-1].start()
    for copy in copies:
        copy.wait()


def final_kernel(dims, after, ri_ref, rj_ref, keep_ref, *refs):
    chans, groups, blocks, i_rows, j_rows, step_rows, sequences = dims
    tiles = sequences * chans // LANES
    left, right, weight = refs[0:2], refs[2:4], refs[4:6]
    gl_out, gr_out, gw_out, whole = refs[6:]
    for refs_in, out, rows_ref, axis in (
        (left, gl_out, ri_ref, "col"),
        (right, gr_out, rj_ref, "row"),
    ):
        own = out.shape[0]
        whole[0 : own * tiles, :] = total_of(*refs_in)
        first = pl.multiple_of(lax.axis_index(axis) * own, 8)
        write_rows(whole, rows_ref[pl.ds(first, own), :], keep_ref, out, tiles)
    gw_out[...] = total_of(*weight)


def swap(array, axis, n, bit):
    return lax.ppermute(array, axis, [(s, s ^ bit) for s in range(n)])


def owners_of(n):
    held, bit = [0], n // 2
    while bit > 1:
        held, bit = held + [k ^ bit for k in held], bit // 2
    return held, [k ^ 1 for k in held]


def gather(block, own, axis, n, after):
    held, sent, bit = own, block[None], n // 2
    while bit > 1:
        came = swap(sent, axis, n, bit)
        shape = (2 * held.shape[0],) + held.shape[1:]
        held = small_call(join_kernel, [pltpu.VMEM(shape, BF16)], "join")(after, held, came)[0]
        sent, bit = held, bit // 2
    return held, swap(sent, axis, n, 1)


def reduce(keep, send, axis, n, after):
    bit = 1
    while True:
        came = swap(send, axis, n, bit)
        bit *= 2
        if bit >= n:
            return keep, came
        half = (keep.shape[0] // 2,) + keep.shape[1:]
        outs = [pltpu.VMEM(half, F32), pltpu.VMEM(half, BF16)]
        keep, send = small_call(fold_kernel, outs, "fold")(after, keep, came)


def small_call(body, outs, name, scratch=()):
    def call(after, *operands):
        return pl.pallas_call(
            body,
            in_specs=[hbm()] + vmem(len(operands)),
            out_specs=vmem(len(outs)),
            out_shape=outs,
            scratch_shapes=list(scratch),
            compiler_params=params(4),
            cost_estimate=cost(1000, 1000),
            name=name,
        )(after, *operands)

    return call


def halves(rows, n):
    return [pltpu.VMEM((n // 2, rows // n, LANES), BF16)] * 2


def vmem(count=1):
    return [pl.BlockSpec(memory_space=pltpu.VMEM)] * count


def hbm():
    return pl.BlockSpec(memory_space=pl.ANY)


def in_hbm(array):
    return pltpu.with_memory_space_constraint(array, pltpu.HBM)


def shards(left_act, right_act, row_mask, res_mask, out_weight, cotangent):
    n_col = lax.axis_size("col")
    n_row = lax.axis_size("row")
    i_rows, j_rows, pair_width = cotangent.shape
    sequences = row_mask.shape[0]
    width = left_act.shape[1]
    chans = width // sequences
    groups = LANES // chans
    blocks = chans // groups
    tiles = width // LANES
    depth = groups * sequences
    inner = chans * chans
    step_rows = 16
    steps = i_rows // step_rows
    early_steps = steps // 4
    dims = (chans, groups, blocks, i_rows, j_rows, step_rows, sequences)
    j_pad = -(-j_rows // LANES) * LANES
    span = blocks * j_rows
    own_left, own_right = left_act.shape[0], right_act.shape[0]
    macs = i_rows * j_rows * inner * pair_width

    mask_row = (res_mask.reshape(1, -1), row_mask.reshape(1, -1))
    scaled, inverse, weight, keep, i_keep, j_keep, own_l, own_r, z_first = pl.pallas_call(
        functools.partial(scale_kernel, dims),
        in_specs=[hbm()] * 6,
        out_specs=vmem(9),
        out_shape=[
            pltpu.VMEM(cotangent.shape, BF16),
            pltpu.VMEM((j_rows, LANES), F32),
            pltpu.VMEM(out_weight.shape, BF16),
            pltpu.VMEM((1, width), F32),
            pltpu.VMEM((i_rows, LANES), F32),
            pltpu.VMEM((j_rows, LANES), F32),
            pltpu.VMEM((1,) + left_act.shape, BF16),
            pltpu.VMEM((1,) + right_act.shape, BF16),
            pltpu.VMEM((early_steps, span, step_rows * LANES), BF16),
        ],
        scratch_shapes=[
            pltpu.VMEM((1, res_mask.shape[0]), jnp.int32),
            pltpu.VMEM((1, sequences), jnp.int32),
            pltpu.VMEM(out_weight.shape, BF16),
            pltpu.VMEM(out_weight.shape, F32),
            pltpu.VMEM(cotangent.shape, BF16),
            pltpu.SemaphoreType.DMA((steps,)),
            pltpu.SemaphoreType.DMA((5,)),
        ],
        compiler_params=params(16),
        cost_estimate=cost(16 * macs, 2**20),
        name="scale",
    )(*map(in_hbm, (*mask_row, cotangent, out_weight, left_act, right_act)))

    lefts = gather(left_act, own_l, "col", n_col, own_l)
    rights = gather(right_act, own_r, "row", n_row, lefts[0])

    z_last = pl.pallas_call(
        functools.partial(inner_kernel, dims, early_steps),
        in_specs=[hbm()] + vmem(2),
        out_specs=vmem()[0],
        out_shape=pltpu.VMEM((steps - early_steps, span, step_rows * LANES), BF16),
        compiler_params=params(16),
        cost_estimate=cost(16 * macs, 2**20),
        name="inner",
    )(rights[0], scaled, weight)
    z = (z_first, z_last)

    rbig, right_turned = pl.pallas_call(
        functools.partial(right_rows_kernel, dims, n_row),
        in_specs=[hbm()] + vmem(4),
        out_specs=vmem(2),
        out_shape=[pltpu.VMEM((span, depth), BF16), pltpu.VMEM((depth, span), BF16)],
        scratch_shapes=[pltpu.VMEM((j_rows, width), F32), pltpu.VMEM((width, j_pad), F32)],
        compiler_params=params(12),
        cost_estimate=cost(16 * macs, 2**20),
        name="right_rows",
    )(z_last, j_keep, keep, *rights)

    y, diag, *gw_cut = pl.pallas_call(
        functools.partial(outer_kernel, dims, n_row, n_col),
        in_specs=vmem(6),
        out_specs=vmem(4),
        out_shape=[
            pltpu.VMEM((i_rows, j_rows, inner), BF16),
            pltpu.VMEM((steps, depth, step_rows * LANES), BF16),
        ]
        + halves(inner, n_row),
        scratch_shapes=[
            pltpu.VMEM((i_rows, width), F32),
            pltpu.VMEM((i_rows * tiles, LANES), F32),
            pltpu.VMEM((LANES, groups * LANES), BF16),
            pltpu.VMEM((pair_width, inner), F32),
            pltpu.VMEM((inner, pair_width), F32),
        ],
        compiler_params=params(16),
        cost_estimate=cost(16 * macs, 2**20),
        name="outer",
    )(i_keep, keep, scaled, rbig, *lefts)

    gl_cut = pl.pallas_call(
        functools.partial(left_kernel, dims, n_col),
        in_specs=[hbm()] + vmem(1 + len(z)),
        out_specs=vmem(2),
        out_shape=halves(i_rows * tiles, n_col),
        scratch_shapes=[pltpu.VMEM((i_rows * tiles, LANES), F32)],
        compiler_params=params(16),
        cost_estimate=cost(16 * macs, 2**20),
        name="left",
    )(gw_cut[0], right_turned, *z)
    gw_row = reduce(*gw_cut, "row", n_row, gl_cut[0])

    gr_cut = pl.pallas_call(
        functools.partial(right_kernel, dims, n_row),
        in_specs=[hbm()] + vmem(1 + len(z)),
        out_specs=vmem(2),
        out_shape=halves(j_rows * tiles, n_row),
        scratch_shapes=[
            pltpu.VMEM((depth, span), F32),
            pltpu.VMEM((width, j_pad), F32),
            pltpu.VMEM((j_rows * tiles, LANES), F32),
        ],
        compiler_params=params(20),
        cost_estimate=cost(16 * macs, 2**20),
        name="right",
    )(gw_row[0], diag, *z)
    gw_cut = small_call(
        functools.partial(turn_kernel, n_col),
        halves(inner // n_row, n_col),
        "turn",
        [pltpu.VMEM((inner // n_row, pair_width), F32)],
    )(gr_cut[0], *gw_row)
    gl_last = reduce(*gl_cut, "col", n_col, gw_cut[0])

    half = steps // 2
    early = pl.pallas_call(
        functools.partial(pair_first_kernel, dims, half),
        in_specs=[hbm()] + vmem(4),
        out_specs=vmem()[0],
        out_shape=pltpu.VMEM((half * step_rows, j_rows, pair_width), BF16),
        compiler_params=params(12),
        cost_estimate=cost(16 * macs, 2**20),
        name="pair_first",
    )(gl_last[0], i_keep, y, weight, inverse)
    gw_last = reduce(*gw_cut, "col", n_col, early)
    gr_last = reduce(*gr_cut, "row", n_row, gw_last[0])
    pair_out = pl.pallas_call(
        functools.partial(pair_kernel, dims),
        in_specs=[hbm()] * 2 + vmem(5),
        out_specs=hbm(),
        out_shape=jax.ShapeDtypeStruct(cotangent.shape, BF16),
        scratch_shapes=[
            pltpu.VMEM((i_rows - half * step_rows, j_rows, pair_width), BF16),
            pltpu.SemaphoreType.DMA((1 + steps - half,)),
        ],
        compiler_params=params(12),
        cost_estimate=cost(16 * macs, 2**20),
        name="pair",
    )(gl_last[1], gr_last[0], i_keep, y, weight, inverse, early)

    grad_left, grad_right, grad_weight = pl.pallas_call(
        functools.partial(final_kernel, dims),
        in_specs=[hbm()] + vmem(9),
        out_specs=vmem(3),
        out_shape=[
            jax.ShapeDtypeStruct((own_left, width), F32),
            jax.ShapeDtypeStruct((own_right, width), F32),
            jax.ShapeDtypeStruct((inner // n_row // n_col, pair_width), F32),
        ],
        scratch_shapes=[pltpu.VMEM((max(own_left, own_right) * tiles, LANES), F32)],
        compiler_params=params(4),
        cost_estimate=cost(1000, 1000),
        name="final_sums",
    )(in_hbm(pair_out), i_keep, j_keep, keep, *gl_last, *gr_last, *gw_last)
    return (pair_out, grad_left, grad_right, grad_weight)


def solution(mesh):
    placed = (
        P(("grp", "row", "col"), None),
        P(("grp", "col", "row"), None),
        P("grp"),
        P("grp"),
        P(),
        P(("grp", "row"), "col", None),
    )
    return jax.shard_map(
        shards,
        mesh=mesh,
        in_specs=placed,
        out_specs=(
            P(("grp", "row"), "col", None),
            P(("grp", "row", "col"), None),
            P(("grp", "col", "row"), None),
            P(("grp", "row", "col"), None),
        ),
        check_vma=False,
    )
```

```python
import functools

import jax
import jax.numpy as jnp
from jax import lax
from jax.experimental import pallas as pl
from jax.experimental.pallas import tpu as pltpu
from jax.sharding import PartitionSpec as P

LANES = 128
NT = (((1,), (1,)), ((), ()))
F32 = jnp.float32
BF16 = jnp.bfloat16


def params(mib):
    return pltpu.CompilerParams(vmem_limit_bytes=mib * 2**20)


def cost(flops, nbytes):
    return pl.CostEstimate(flops=int(flops), bytes_accessed=int(nbytes), transcendentals=0)


def cut(source, index, n, keep_ref, send_ref):
    rows = source.shape[0] // n
    for k in range(n):
        at = pl.multiple_of((index ^ k) * rows, rows)
        into = send_ref if k % 2 else keep_ref
        into[k // 2] = source[pl.ds(at, rows), :].astype(into.dtype)


def place(buffers, index, n, flat):
    for buffer, owners in zip(buffers, owners_of(n)):
        rows = buffer.shape[1]
        for k, owner in enumerate(owners):
            at = pl.multiple_of((index ^ owner) * rows, 8)
            flat[pl.ds(at, rows), :] = buffer[k].astype(F32)


def lane_group(shape, chans):
    return lax.broadcasted_iota(jnp.int32, shape, 1) // chans


def mask_rows(res_ref, first, count):
    shape = (count, res_ref.shape[1])
    row = lax.broadcasted_iota(jnp.int32, shape, 0) + first
    here = lax.broadcasted_iota(jnp.int32, shape, 1) == row
    chosen = jnp.where(here, res_ref[...].astype(F32), 0.0)
    return jnp.broadcast_to(jnp.sum(chosen, axis=1, keepdims=True), (count, LANES))


def scale_kernel(dims, *refs):
    chans, groups, blocks, i_rows, j_rows, step_rows, sequences = dims
    tiles = sequences * chans // LANES
    res_hbm, seq_hbm, cot_ref, w_hbm, left_hbm, right_hbm = refs[:6]
    scaled_ref, inv_ref, wp_ref, keep_ref, ri_ref, rj_ref, left_ref, right_ref, z_ref = refs[6:15]
    res_ref, seq_ref, w_ref, w32, cot, sems, more_sems = refs[15:]
    steps = i_rows // step_rows

    def fetch(step):
        rows = pl.ds(step * step_rows, step_rows)
        return pltpu.make_async_copy(cot_ref.at[rows], cot.at[rows], sems.at[step])

    pairs = [
        (res_hbm, res_ref),
        (seq_hbm, seq_ref),
        (w_hbm, w_ref),
        (left_hbm, left_ref.at[0]),
        (right_hbm, right_ref.at[0]),
    ]
    more = [
        pltpu.make_async_copy(source, to, more_sems.at[k]) for k, (source, to) in enumerate(pairs)
    ]
    for copy in more[:3]:
        copy.start()
    for step in range(steps):
        fetch(step).start()
    for copy in more[3:]:
        copy.start()
    shape = (sequences, tiles * LANES)
    own = lax.broadcasted_iota(jnp.int32, shape, 1) // chans
    repeat = (own == lax.broadcasted_iota(jnp.int32, shape, 0)).astype(F32).astype(BF16)
    more[0].wait()
    ri_ref[...] = mask_rows(res_ref, lax.axis_index("row") * i_rows, i_rows)
    rj_ref[...] = mask_rows(res_ref, lax.axis_index("col") * j_rows, j_rows)
    more[1].wait()
    seq = seq_ref[...].astype(F32)
    keep_ref[...] = jnp.dot(
        jnp.broadcast_to(seq, (8, sequences)).astype(BF16), repeat, preferred_element_type=F32
    )[0:1]
    valid = jnp.sum(seq, axis=1, keepdims=True)
    inv_ref[...] = 1.0 / jnp.maximum(valid * rj_ref[...], 1.0)
    more[2].wait()
    w32[...] = w_ref[...].astype(F32)
    for e in range(chans):
        wp_ref[e * chans : (e + 1) * chans, :] = w32[pl.ds(e, chans, stride=chans), :].astype(BF16)
    for step in range(steps):
        fetch(step).wait()
        for i in range(step_rows):
            at = step * step_rows + i
            inverse = jnp.where(ri_ref[at : at + 1, :] > 0, inv_ref[...], 1.0)
            scaled_ref[at] = (cot[at].astype(F32) * inverse).astype(BF16)
        if step < z_ref.shape[0]:
            rows = slice(step * step_rows, (step + 1) * step_rows)
            inner_rows(dims, scaled_ref[rows], wp_ref, z_ref, step)
    more[3].wait()
    more[4].wait()


def inner_rows(dims, scaled, wp_ref, z_ref, at):
    chans, groups, blocks, i_rows, j_rows, step_rows, sequences = dims
    for pair in range(0, blocks, 2):
        part = lax.dot_general(
            scaled.reshape(step_rows * j_rows, LANES),
            wp_ref[pair * LANES : (pair + 2) * LANES, :],
            NT,
            preferred_element_type=F32,
        ).astype(BF16)
        for k in range(2):
            a = pair + k
            for i in range(step_rows):
                z_ref[at, a * j_rows : (a + 1) * j_rows, i * LANES : (i + 1) * LANES] = part[
                    i * j_rows : (i + 1) * j_rows, k * LANES : (k + 1) * LANES
                ]


def inner_kernel(dims, first, after, scaled_ref, wp_ref, z_ref):
    step_rows = dims[5]
    for at in range(z_ref.shape[0]):
        rows = slice((first + at) * step_rows, (first + at + 1) * step_rows)
        inner_rows(dims, scaled_ref[rows], wp_ref, z_ref, at)


def at_step(refs, step):
    for ref in refs:
        if step < ref.shape[0]:
            return ref.at[step]
        step -= ref.shape[0]


def outer_kernel(dims, n_row, n_col, *refs):
    chans, groups, blocks, i_rows, j_rows, step_rows, sequences = dims
    tiles = sequences * chans // LANES
    after, ri_ref, keep_ref, scaled_ref, rbig, left_held, left_came = refs[:7]
    y_ref, diag_ref, keep_out, send_out = refs[7:11]
    flat, lsplit, expand, gwt, gwr = refs[11:]
    place((left_held, left_came), lax.axis_index("col"), n_col, flat)
    for t in range(tiles):
        lanes = slice(t * LANES, (t + 1) * LANES)
        masked = flat[0:i_rows, lanes] * ri_ref[...] * keep_ref[:, lanes]
        lsplit[pl.ds(t, i_rows, stride=tiles), :] = masked
    shape = (LANES, groups * LANES)
    source = lax.broadcasted_iota(jnp.int32, shape, 0)
    target = lax.broadcasted_iota(jnp.int32, shape, 1)
    same = (source // chans == target // LANES) & (source % chans == target % chans)
    expand[...] = same.astype(F32).astype(BF16)
    rows = step_rows * tiles
    pairs = step_rows * j_rows
    group = lane_group((tiles, LANES), chans)

    for step in range(i_rows // step_rows):
        spread = jnp.dot(
            lsplit[step * rows : (step + 1) * rows, :].astype(BF16),
            expand[...],
            preferred_element_type=F32,
        ).astype(BF16)
        for b in range(groups):
            chosen = (group == b).astype(F32).astype(BF16)
            for lo in range(groups):
                at = b * sequences + lo * tiles
                for i in range(step_rows):
                    diag_ref[step, at : at + tiles, i * LANES : (i + 1) * LANES] = (
                        spread[i * tiles : (i + 1) * tiles, lo * LANES : (lo + 1) * LANES] * chosen
                    )
        for pair in range(0, step_rows, 2):
            part = jnp.dot(
                rbig[...],
                diag_ref[step, :, pair * LANES : (pair + 2) * LANES],
                preferred_element_type=F32,
            ).astype(BF16)
            for k in range(2):
                for a in range(blocks):
                    y_ref[step * step_rows + pair + k, :, a * LANES : (a + 1) * LANES] = part[
                        a * j_rows : (a + 1) * j_rows, k * LANES : (k + 1) * LANES
                    ]
        block = slice(step * step_rows, (step + 1) * step_rows)
        scaled_t = scaled_ref[block].reshape(pairs, LANES).T
        y_flat = y_ref[block].reshape(pairs, blocks * LANES)
        part = jnp.dot(scaled_t, y_flat, preferred_element_type=F32)
        gwt[...] = gwt[...] + part if step else part
    for k in range(blocks):
        turned_tile = gwt[:, k * LANES : (k + 1) * LANES].T
        for q in range(groups):
            gwr[pl.ds(k * groups + q, chans, stride=chans), :] = turned_tile[
                q * chans : (q + 1) * chans
            ]
    cut(gwr, lax.axis_index("row"), n_row, keep_out, send_out)


def right_sum(first, last, z_refs, diag_ref, acc, so_far=None):
    for step in range(first, last):
        part = lax.dot_general(
            diag_ref[step], at_step(z_refs, step)[...], NT, preferred_element_type=F32
        )
        acc[...] = part if so_far is None else so_far[...] + part
        so_far = acc


def right_first_kernel(steps, after, diag_ref, *refs):
    right_sum(0, steps, refs[:-1], diag_ref, refs[-1])


def right_kernel(dims, n_row, first, after, diag_ref, acc_first, *refs):
    chans, groups, blocks, i_rows, j_rows, step_rows, sequences = dims
    tiles = sequences * chans // LANES
    j_pad = -(-j_rows // LANES) * LANES
    z_refs, (keep_out, send_out, acc, turned, gr_all) = refs[:-5], refs[-5:]
    right_sum(first, i_rows // step_rows, z_refs, diag_ref, acc, acc_first)
    for a in range(blocks):
        at, shift = divmod(a * j_rows, LANES)
        mine = acc[:, at * LANES : at * LANES + j_pad]
        if shift:
            mine = pltpu.roll(mine, LANES - shift, axis=1)
        for b in range(groups):
            for lo in range(groups):
                first = b * sequences + lo * tiles
                turned[pl.ds(lo * chans + groups * a + b, tiles, stride=LANES), :] = mine[
                    first : first + tiles
                ]
    for t in range(tiles):
        lanes = slice(t * LANES, (t + 1) * LANES)
        gr_all[pl.ds(t, j_rows, stride=tiles), :] = turned[lanes, :].T[:j_rows]
    cut(gr_all, lax.axis_index("row"), n_row, keep_out, send_out)


def right_rows_kernel(dims, n_row, after, rj_ref, keep_ref, right_held, right_came, *refs):
    chans, groups, blocks, i_rows, j_rows, step_rows, sequences = dims
    tiles = sequences * chans // LANES
    j_pad = -(-j_rows // LANES) * LANES
    rbig, rbt_ref, flat, turned = refs
    place((right_held, right_came), lax.axis_index("row"), n_row, flat)
    for t in range(tiles):
        lanes = slice(t * LANES, (t + 1) * LANES)
        masked = flat[0:j_rows, lanes] * rj_ref[...] * keep_ref[:, lanes]
        if j_rows < j_pad:
            masked = jnp.concatenate([masked, jnp.zeros((j_pad - j_rows, LANES), F32)], axis=0)
        turned[lanes, :] = masked.T
    for a in range(blocks):
        parts = [
            turned[pl.ds(lo * chans + groups * a + b, tiles, stride=LANES), :]
            for b in range(groups)
            for lo in range(groups)
        ]
        block = jnp.concatenate(parts, axis=0)
        rbig[a * j_rows : (a + 1) * j_rows, :] = block.T[:j_rows].astype(BF16)
    rbt_ref[...] = rbig[...].T


def left_kernel(dims, n_col, after, rbt_ref, *refs):
    chans, groups, blocks, i_rows, j_rows, step_rows, sequences = dims
    tiles = sequences * chans // LANES
    z_refs, (keep_out, send_out, gl_all) = refs[:-3], refs[-3:]
    group = lane_group((sequences, LANES), chans)
    group_t = lane_group((tiles, LANES), chans)

    for step in range(i_rows // step_rows):
        z_ref = at_step(z_refs, step)
        for pair in range(0, step_rows, 2):
            part = jnp.dot(
                rbt_ref[...],
                z_ref[:, pair * LANES : (pair + 2) * LANES],
                preferred_element_type=F32,
            )
            for k in range(2):
                mine = part[:, k * LANES : (k + 1) * LANES]
                total = mine[0:sequences]
                for b in range(1, groups):
                    total = jnp.where(group == b, mine[b * sequences : (b + 1) * sequences], total)
                shift = LANES // 2
                while shift >= chans:
                    total = total + pltpu.roll(total, shift, axis=1)
                    shift //= 2
                merged = total[0:tiles]
                for lo in range(1, groups):
                    merged = jnp.where(group_t == lo, total[lo * tiles : (lo + 1) * tiles], merged)
                at = (step * step_rows + pair + k) * tiles
                gl_all[at : at + tiles, :] = merged
    cut(gl_all, lax.axis_index("col"), n_col, keep_out, send_out)


def total_of(keep_ref, came_ref, k=0):
    return keep_ref[k].astype(F32) + came_ref[k].astype(F32)


def join_kernel(after, held_ref, came_ref, out_ref):
    count = held_ref.shape[0]
    for k in range(count):
        out_ref[k] = held_ref[k]
        out_ref[count + k] = came_ref[k]


def fold_kernel(after, held_ref, came_ref, keep_out, send_out):
    for k in range(held_ref.shape[0]):
        into = send_out if k % 2 else keep_out
        into[k // 2] = total_of(held_ref, came_ref, k).astype(into.dtype)


def turn_kernel(n_col, after, held_ref, came_ref, keep_out, send_out, whole):
    whole[...] = total_of(held_ref, came_ref)
    cut(whole, lax.axis_index("col"), n_col, keep_out, send_out)


def write_rows(whole, rows, keep_ref, out_ref, tiles):
    own = out_ref.shape[0]
    for t in range(tiles):
        lanes = slice(t * LANES, (t + 1) * LANES)
        out_ref[:, lanes] = whole[pl.ds(t, own, stride=tiles), :] * (
            rows * keep_ref[:, lanes]
        )


def pair_rows(dims, step, ri_ref, y_ref, wp_ref, inv_ref, out_ref, at):
    chans, groups, blocks, i_rows, j_rows, step_rows, sequences = dims
    pairs = step_rows * j_rows
    y_flat = y_ref[step * step_rows : (step + 1) * step_rows].reshape(pairs, blocks * LANES)
    projected = jnp.dot(y_flat, wp_ref[...], preferred_element_type=F32)
    for i in range(step_rows):
        row = step * step_rows + i
        inverse = jnp.where(ri_ref[row : row + 1, :] > 0, inv_ref[...], 1.0)
        out_ref[at + i] = (projected[i * j_rows : (i + 1) * j_rows] * inverse).astype(BF16)


def pair_first_kernel(dims, steps, after, ri_ref, y_ref, wp_ref, inv_ref, out_ref):
    for step in range(steps):
        pair_rows(dims, step, ri_ref, y_ref, wp_ref, inv_ref, out_ref, step * dims[5])


def pair_kernel(dims, *refs):
    i_rows, j_rows, step_rows = dims[3:6]
    after_left, after_right, ri_ref, y_ref, wp_ref, inv_ref, early = refs[:7]
    out_ref, staged, sems = refs[7:]
    begin = early.shape[0]
    copies = [pltpu.make_async_copy(early, out_ref.at[pl.ds(0, begin)], sems.at[0])]
    copies[0].start()
    for step in range(begin // step_rows, i_rows // step_rows):
        at = step * step_rows - begin
        pair_rows(dims, step, ri_ref, y_ref, wp_ref, inv_ref, staged, at)
        copies.append(
            pltpu.make_async_copy(
                staged.at[pl.ds(at, step_rows)],
                out_ref.at[pl.ds(begin + at, step_rows)],
                sems.at[len(copies)],
            )
        )
        copies[-1].start()
    for copy in copies:
        copy.wait()


def final_kernel(dims, after, ri_ref, rj_ref, keep_ref, *refs):
    chans, groups, blocks, i_rows, j_rows, step_rows, sequences = dims
    tiles = sequences * chans // LANES
    left, right, weight = refs[0:2], refs[2:4], refs[4:6]
    gl_out, gr_out, gw_out, whole = refs[6:]
    for refs_in, out, rows_ref, axis in (
        (left, gl_out, ri_ref, "col"),
        (right, gr_out, rj_ref, "row"),
    ):
        own = out.shape[0]
        whole[0 : own * tiles, :] = total_of(*refs_in)
        first = pl.multiple_of(lax.axis_index(axis) * own, 8)
        write_rows(whole, rows_ref[pl.ds(first, own), :], keep_ref, out, tiles)
    gw_out[...] = total_of(*weight)


def swap(array, axis, n, bit):
    return lax.ppermute(array, axis, [(s, s ^ bit) for s in range(n)])


def owners_of(n):
    held, bit = [0], n // 2
    while bit > 1:
        held, bit = held + [k ^ bit for k in held], bit // 2
    return held, [k ^ 1 for k in held]


def gather(block, own, axis, n, after):
    held, sent, bit = own, block[None], n // 2
    while bit > 1:
        came = swap(sent, axis, n, bit)
        shape = (2 * held.shape[0],) + held.shape[1:]
        held = small_call(join_kernel, [pltpu.VMEM(shape, BF16)], "join")(after, held, came)[0]
        sent, bit = held, bit // 2
    return held, swap(sent, axis, n, 1)


def reduce(keep, send, axis, n, after):
    bit = 1
    while True:
        came = swap(send, axis, n, bit)
        bit *= 2
        if bit >= n:
            return keep, came
        half = (keep.shape[0] // 2,) + keep.shape[1:]
        outs = [pltpu.VMEM(half, F32), pltpu.VMEM(half, BF16)]
        keep, send = small_call(fold_kernel, outs, "fold")(after, keep, came)


def small_call(body, outs, name, scratch=()):
    def call(after, *operands):
        return pl.pallas_call(
            body,
            in_specs=[hbm()] + vmem(len(operands)),
            out_specs=vmem(len(outs)),
            out_shape=outs,
            scratch_shapes=list(scratch),
            compiler_params=params(4),
            cost_estimate=cost(1000, 1000),
            name=name,
        )(after, *operands)

    return call


def halves(rows, n):
    return [pltpu.VMEM((n // 2, rows // n, LANES), BF16)] * 2


def vmem(count=1):
    return [pl.BlockSpec(memory_space=pltpu.VMEM)] * count


def hbm():
    return pl.BlockSpec(memory_space=pl.ANY)


def in_hbm(array):
    return pltpu.with_memory_space_constraint(array, pltpu.HBM)


def shards(left_act, right_act, row_mask, res_mask, out_weight, cotangent):
    n_col = lax.axis_size("col")
    n_row = lax.axis_size("row")
    i_rows, j_rows, pair_width = cotangent.shape
    sequences = row_mask.shape[0]
    width = left_act.shape[1]
    chans = width // sequences
    groups = LANES // chans
    blocks = chans // groups
    tiles = width // LANES
    depth = groups * sequences
    inner = chans * chans
    step_rows = 16
    steps = i_rows // step_rows
    early_steps = steps // 2
    dims = (chans, groups, blocks, i_rows, j_rows, step_rows, sequences)
    j_pad = -(-j_rows // LANES) * LANES
    span = blocks * j_rows
    own_left, own_right = left_act.shape[0], right_act.shape[0]
    macs = i_rows * j_rows * inner * pair_width

    mask_row = (res_mask.reshape(1, -1), row_mask.reshape(1, -1))
    scaled, inverse, weight, keep, i_keep, j_keep, own_l, own_r, z_first = pl.pallas_call(
        functools.partial(scale_kernel, dims),
        in_specs=[hbm()] * 6,
        out_specs=vmem(9),
        out_shape=[
            pltpu.VMEM(cotangent.shape, BF16),
            pltpu.VMEM((j_rows, LANES), F32),
            pltpu.VMEM(out_weight.shape, BF16),
            pltpu.VMEM((1, width), F32),
            pltpu.VMEM((i_rows, LANES), F32),
            pltpu.VMEM((j_rows, LANES), F32),
            pltpu.VMEM((1,) + left_act.shape, BF16),
            pltpu.VMEM((1,) + right_act.shape, BF16),
            pltpu.VMEM((early_steps, span, step_rows * LANES), BF16),
        ],
        scratch_shapes=[
            pltpu.VMEM((1, res_mask.shape[0]), jnp.int32),
            pltpu.VMEM((1, sequences), jnp.int32),
            pltpu.VMEM(out_weight.shape, BF16),
            pltpu.VMEM(out_weight.shape, F32),
            pltpu.VMEM(cotangent.shape, BF16),
            pltpu.SemaphoreType.DMA((steps,)),
            pltpu.SemaphoreType.DMA((5,)),
        ],
        compiler_params=params(16),
        cost_estimate=cost(1000, 1000),
        name="scale",
    )(*map(in_hbm, (*mask_row, cotangent, out_weight, left_act, right_act)))

    lefts = gather(left_act, own_l, "col", n_col, own_l)
    rights = gather(right_act, own_r, "row", n_row, lefts[0])

    z_last = pl.pallas_call(
        functools.partial(inner_kernel, dims, early_steps),
        in_specs=[hbm()] + vmem(2),
        out_specs=vmem()[0],
        out_shape=pltpu.VMEM((steps - early_steps, span, step_rows * LANES), BF16),
        compiler_params=params(16),
        cost_estimate=cost(16 * macs, 2**20),
        name="inner",
    )(rights[0], scaled, weight)
    z = (z_first, z_last)

    rbig, right_turned = pl.pallas_call(
        functools.partial(right_rows_kernel, dims, n_row),
        in_specs=[hbm()] + vmem(4),
        out_specs=vmem(2),
        out_shape=[pltpu.VMEM((span, depth), BF16), pltpu.VMEM((depth, span), BF16)],
        scratch_shapes=[pltpu.VMEM((j_rows, width), F32), pltpu.VMEM((width, j_pad), F32)],
        compiler_params=params(12),
        cost_estimate=cost(16 * macs, 2**20),
        name="right_rows",
    )(z_last, j_keep, keep, *rights)

    gl_cut = pl.pallas_call(
        functools.partial(left_kernel, dims, n_col),
        in_specs=[hbm()] + vmem(1 + len(z)),
        out_specs=vmem(2),
        out_shape=halves(i_rows * tiles, n_col),
        scratch_shapes=[pltpu.VMEM((i_rows * tiles, LANES), F32)],
        compiler_params=params(16),
        cost_estimate=cost(16 * macs, 2**20),
        name="left",
    )(rbig, right_turned, *z)
    y, diag, *gw_cut = pl.pallas_call(
        functools.partial(outer_kernel, dims, n_row, n_col),
        in_specs=[hbm()] + vmem(6),
        out_specs=vmem(4),
        out_shape=[
            pltpu.VMEM((i_rows, j_rows, inner), BF16),
            pltpu.VMEM((steps, depth, step_rows * LANES), BF16),
        ]
        + halves(inner, n_row),
        scratch_shapes=[
            pltpu.VMEM((i_rows, width), F32),
            pltpu.VMEM((i_rows * tiles, LANES), F32),
            pltpu.VMEM((LANES, groups * LANES), BF16),
            pltpu.VMEM((pair_width, inner), F32),
            pltpu.VMEM((inner, pair_width), F32),
        ],
        compiler_params=params(16),
        cost_estimate=cost(16 * macs, 2**20),
        name="outer",
    )(gl_cut[0], i_keep, keep, scaled, rbig, *lefts)

    gl_last = reduce(*gl_cut, "col", n_col, gw_cut[0])

    right_steps = steps // 4
    acc = pl.pallas_call(
        functools.partial(right_first_kernel, right_steps),
        in_specs=[hbm()] + vmem(1 + len(z)),
        out_specs=vmem()[0],
        out_shape=pltpu.VMEM((depth, span), F32),
        compiler_params=params(16),
        cost_estimate=cost(16 * macs, 2**20),
        name="right_first",
    )(gl_last[0], diag, *z)
    gw_row = reduce(*gw_cut, "row", n_row, acc)

    gr_cut = pl.pallas_call(
        functools.partial(right_kernel, dims, n_row, right_steps),
        in_specs=[hbm()] + vmem(2 + len(z)),
        out_specs=vmem(2),
        out_shape=halves(j_rows * tiles, n_row),
        scratch_shapes=[
            pltpu.VMEM((depth, span), F32),
            pltpu.VMEM((width, j_pad), F32),
            pltpu.VMEM((j_rows * tiles, LANES), F32),
        ],
        compiler_params=params(20),
        cost_estimate=cost(16 * macs, 2**20),
        name="right",
    )(gw_row[0], diag, acc, *z)
    gw_cut = small_call(
        functools.partial(turn_kernel, n_col),
        halves(inner // n_row, n_col),
        "turn",
        [pltpu.VMEM((inner // n_row, pair_width), F32)],
    )(gr_cut[0], *gw_row)

    half = steps // 2
    early = pl.pallas_call(
        functools.partial(pair_first_kernel, dims, half),
        in_specs=[hbm()] + vmem(4),
        out_specs=vmem()[0],
        out_shape=pltpu.VMEM((half * step_rows, j_rows, pair_width), BF16),
        compiler_params=params(12),
        cost_estimate=cost(16 * macs, 2**20),
        name="pair_first",
    )(gw_cut[0], i_keep, y, weight, inverse)
    gw_last = reduce(*gw_cut, "col", n_col, early)
    gr_last = reduce(*gr_cut, "row", n_row, gw_last[0])
    pair_out = pl.pallas_call(
        functools.partial(pair_kernel, dims),
        in_specs=[hbm()] * 2 + vmem(5),
        out_specs=hbm(),
        out_shape=jax.ShapeDtypeStruct(cotangent.shape, BF16),
        scratch_shapes=[
            pltpu.VMEM((i_rows - half * step_rows, j_rows, pair_width), BF16),
            pltpu.SemaphoreType.DMA((1 + steps - half,)),
        ],
        compiler_params=params(12),
        cost_estimate=cost(16 * macs, 2**20),
        name="pair",
    )(gl_last[1], gr_last[0], i_keep, y, weight, inverse, early)

    grad_left, grad_right, grad_weight = pl.pallas_call(
        functools.partial(final_kernel, dims),
        in_specs=[hbm()] + vmem(9),
        out_specs=vmem(3),
        out_shape=[
            jax.ShapeDtypeStruct((own_left, width), F32),
            jax.ShapeDtypeStruct((own_right, width), F32),
            jax.ShapeDtypeStruct((inner // n_row // n_col, pair_width), F32),
        ],
        scratch_shapes=[pltpu.VMEM((max(own_left, own_right) * tiles, LANES), F32)],
        compiler_params=params(4),
        cost_estimate=cost(1000, 1000),
        name="final_sums",
    )(in_hbm(pair_out), i_keep, j_keep, keep, *gl_last, *gr_last, *gw_last)
    return (pair_out, grad_left, grad_right, grad_weight)


def solution(mesh):
    placed = (
        P(("grp", "row", "col"), None),
        P(("grp", "col", "row"), None),
        P("grp"),
        P("grp"),
        P(),
        P(("grp", "row"), "col", None),
    )
    return jax.shard_map(
        shards,
        mesh=mesh,
        in_specs=placed,
        out_specs=(
            P(("grp", "row"), "col", None),
            P(("grp", "row", "col"), None),
            P(("grp", "col", "row"), None),
            P(("grp", "row", "col"), None),
        ),
        check_vma=False,
    )
```

```python
import functools

import jax
import jax.numpy as jnp
from jax import lax
from jax.experimental import pallas as pl
from jax.experimental.pallas import tpu as pltpu
from jax.sharding import PartitionSpec as P

LANES = 128
CHUNK = 4
PIECE = 8
NT = (((1,), (1,)), ((), ()))
F32 = jnp.float32
BF16 = jnp.bfloat16


def params(mib):
    return pltpu.CompilerParams(vmem_limit_bytes=mib * 2**20)


def cost(flops, nbytes):
    return pl.CostEstimate(flops=int(flops), bytes_accessed=int(nbytes), transcendentals=0)


def cut(source, index, n, keep_ref, send_ref):
    rows = source.shape[0] // n
    for k in range(n):
        at = pl.multiple_of((index ^ k) * rows, rows)
        into = send_ref if k % 2 else keep_ref
        into[k // 2] = source[pl.ds(at, rows), :].astype(into.dtype)


def place(buffers, index, n, flat):
    for buffer, owners in zip(buffers, owners_of(n)):
        rows = buffer.shape[1]
        for k, owner in enumerate(owners):
            at = pl.multiple_of((index ^ owner) * rows, 8)
            flat[pl.ds(at, rows), :] = buffer[k].astype(F32)


def lane_group(shape, chans):
    return lax.broadcasted_iota(jnp.int32, shape, 1) // chans


def mask_rows(res_ref, first, count):
    shape = (count, res_ref.shape[1])
    row = lax.broadcasted_iota(jnp.int32, shape, 0) + first
    here = lax.broadcasted_iota(jnp.int32, shape, 1) == row
    chosen = jnp.where(here, res_ref[...].astype(F32), 0.0)
    return jnp.broadcast_to(jnp.sum(chosen, axis=1, keepdims=True), (count, LANES))


def scale_kernel(dims, *refs):
    chans, groups, blocks, i_rows, j_rows, step_rows, sequences = dims
    tiles = sequences * chans // LANES
    res_hbm, seq_hbm, cot_ref, w_hbm, left_hbm, right_hbm = refs[:6]
    scaled_ref, inv_ref, wp_ref, keep_ref, ri_ref, rj_ref, left_ref, right_ref, z_ref = refs[6:15]
    res_ref, seq_ref, w_ref, w32, cot, sems, more_sems = refs[15:]
    steps = i_rows // step_rows

    def fetch(piece):
        rows = pl.ds(piece * PIECE, PIECE)
        return pltpu.make_async_copy(cot_ref.at[rows], cot.at[rows], sems.at[piece])

    pairs = [
        (res_hbm, res_ref),
        (seq_hbm, seq_ref),
        (w_hbm, w_ref),
        (left_hbm, left_ref.at[0]),
        (right_hbm, right_ref.at[0]),
    ]
    more = [
        pltpu.make_async_copy(source, to, more_sems.at[k]) for k, (source, to) in enumerate(pairs)
    ]
    for copy in more[:3]:
        copy.start()
    for piece in range(i_rows // PIECE):
        fetch(piece).start()
    for copy in more[3:]:
        copy.start()
    shape = (sequences, tiles * LANES)
    own = lax.broadcasted_iota(jnp.int32, shape, 1) // chans
    repeat = (own == lax.broadcasted_iota(jnp.int32, shape, 0)).astype(F32).astype(BF16)
    more[0].wait()
    ri_ref[...] = mask_rows(res_ref, lax.axis_index("row") * i_rows, i_rows)
    rj_ref[...] = mask_rows(res_ref, lax.axis_index("col") * j_rows, j_rows)
    more[1].wait()
    seq = seq_ref[...].astype(F32)
    keep_ref[...] = jnp.dot(
        jnp.broadcast_to(seq, (8, sequences)).astype(BF16), repeat, preferred_element_type=F32
    )[0:1]
    valid = jnp.sum(seq, axis=1, keepdims=True)
    inv_ref[...] = 1.0 / jnp.maximum(valid * rj_ref[...], 1.0)
    more[2].wait()
    w32[...] = w_ref[...].astype(F32)
    for e in range(chans):
        wp_ref[e * chans : (e + 1) * chans, :] = w32[pl.ds(e, chans, stride=chans), :].astype(BF16)
    for step in range(steps):
        for at in range(step * step_rows, (step + 1) * step_rows):
            if at % PIECE == 0:
                fetch(at // PIECE).wait()
            inverse = jnp.where(ri_ref[at : at + 1, :] > 0, inv_ref[...], 1.0)
            scaled_ref[at] = (cot[at].astype(F32) * inverse).astype(BF16)
        if step < z_ref.shape[0]:
            rows = slice(step * step_rows, (step + 1) * step_rows)
            inner_rows(dims, scaled_ref[rows], wp_ref, z_ref, step)
    more[3].wait()
    more[4].wait()


def inner_rows(dims, scaled, wp_ref, z_ref, at):
    chans, groups, blocks, i_rows, j_rows, step_rows, sequences = dims
    for first in range(0, blocks, CHUNK):
        part = lax.dot_general(
            scaled.reshape(step_rows * j_rows, LANES),
            wp_ref[first * LANES : (first + CHUNK) * LANES, :],
            NT,
            preferred_element_type=F32,
        ).astype(BF16)
        for k in range(CHUNK):
            a = first + k
            for i in range(step_rows):
                z_ref[at, a * j_rows : (a + 1) * j_rows, i * LANES : (i + 1) * LANES] = part[
                    i * j_rows : (i + 1) * j_rows, k * LANES : (k + 1) * LANES
                ]


def inner_kernel(dims, first, after, scaled_ref, wp_ref, z_ref):
    step_rows = dims[5]
    for at in range(z_ref.shape[0]):
        rows = slice((first + at) * step_rows, (first + at + 1) * step_rows)
        inner_rows(dims, scaled_ref[rows], wp_ref, z_ref, at)


def at_step(refs, step):
    for ref in refs:
        if step < ref.shape[0]:
            return ref.at[step]
        step -= ref.shape[0]


def outer_kernel(dims, n_row, n_col, *refs):
    chans, groups, blocks, i_rows, j_rows, step_rows, sequences = dims
    tiles = sequences * chans // LANES
    after, ri_ref, keep_ref, scaled_ref, rbig, left_held, left_came = refs[:7]
    y_ref, diag_ref, keep_out, send_out = refs[7:11]
    flat, lsplit, expand, gwt, gwr = refs[11:]
    place((left_held, left_came), lax.axis_index("col"), n_col, flat)
    for t in range(tiles):
        lanes = slice(t * LANES, (t + 1) * LANES)
        masked = flat[0:i_rows, lanes] * ri_ref[...] * keep_ref[:, lanes]
        lsplit[pl.ds(t, i_rows, stride=tiles), :] = masked
    shape = (LANES, groups * LANES)
    source = lax.broadcasted_iota(jnp.int32, shape, 0)
    target = lax.broadcasted_iota(jnp.int32, shape, 1)
    same = (source // chans == target // LANES) & (source % chans == target % chans)
    expand[...] = same.astype(F32).astype(BF16)
    rows = step_rows * tiles
    pairs = step_rows * j_rows
    group = lane_group((tiles, LANES), chans)

    for step in range(i_rows // step_rows):
        spread = jnp.dot(
            lsplit[step * rows : (step + 1) * rows, :].astype(BF16),
            expand[...],
            preferred_element_type=F32,
        ).astype(BF16)
        for b in range(groups):
            chosen = (group == b).astype(F32).astype(BF16)
            for lo in range(groups):
                at = b * sequences + lo * tiles
                for i in range(step_rows):
                    diag_ref[step, at : at + tiles, i * LANES : (i + 1) * LANES] = (
                        spread[i * tiles : (i + 1) * tiles, lo * LANES : (lo + 1) * LANES] * chosen
                    )
        for first in range(0, step_rows, CHUNK):
            part = jnp.dot(
                rbig[...],
                diag_ref[step, :, first * LANES : (first + CHUNK) * LANES],
                preferred_element_type=F32,
            ).astype(BF16)
            for k in range(CHUNK):
                for a in range(blocks):
                    y_ref[step * step_rows + first + k, :, a * LANES : (a + 1) * LANES] = part[
                        a * j_rows : (a + 1) * j_rows, k * LANES : (k + 1) * LANES
                    ]
        block = slice(step * step_rows, (step + 1) * step_rows)
        scaled_t = scaled_ref[block].reshape(pairs, LANES).T
        y_flat = y_ref[block].reshape(pairs, blocks * LANES)
        part = jnp.dot(scaled_t, y_flat, preferred_element_type=F32)
        gwt[...] = gwt[...] + part if step else part
    for k in range(blocks):
        turned_tile = gwt[:, k * LANES : (k + 1) * LANES].T
        for q in range(groups):
            gwr[pl.ds(k * groups + q, chans, stride=chans), :] = turned_tile[
                q * chans : (q + 1) * chans
            ]
    cut(gwr, lax.axis_index("row"), n_row, keep_out, send_out)


def right_sum(first, last, z_refs, diag_ref, acc, so_far=None):
    for step in range(first, last):
        part = lax.dot_general(
            diag_ref[step], at_step(z_refs, step)[...], NT, preferred_element_type=F32
        )
        acc[...] = part if so_far is None else so_far[...] + part
        so_far = acc


def right_first_kernel(steps, after, diag_ref, *refs):
    right_sum(0, steps, refs[:-1], diag_ref, refs[-1])


def right_kernel(dims, n_row, first, after, diag_ref, acc_first, *refs):
    chans, groups, blocks, i_rows, j_rows, step_rows, sequences = dims
    tiles = sequences * chans // LANES
    j_pad = -(-j_rows // LANES) * LANES
    z_refs, (keep_out, send_out, acc, turned, gr_all) = refs[:-5], refs[-5:]
    right_sum(first, i_rows // step_rows, z_refs, diag_ref, acc, acc_first)
    for a in range(blocks):
        at, shift = divmod(a * j_rows, LANES)
        mine = acc[:, at * LANES : at * LANES + j_pad]
        if shift:
            mine = pltpu.roll(mine, LANES - shift, axis=1)
        for b in range(groups):
            for lo in range(groups):
                first = b * sequences + lo * tiles
                turned[pl.ds(lo * chans + groups * a + b, tiles, stride=LANES), :] = mine[
                    first : first + tiles
                ]
    for t in range(tiles):
        lanes = slice(t * LANES, (t + 1) * LANES)
        gr_all[pl.ds(t, j_rows, stride=tiles), :] = turned[lanes, :].T[:j_rows]
    cut(gr_all, lax.axis_index("row"), n_row, keep_out, send_out)


def right_rows_kernel(dims, n_row, after, rj_ref, keep_ref, right_held, right_came, *refs):
    chans, groups, blocks, i_rows, j_rows, step_rows, sequences = dims
    tiles = sequences * chans // LANES
    j_pad = -(-j_rows // LANES) * LANES
    rbig, rbt_ref, flat, turned = refs
    place((right_held, right_came), lax.axis_index("row"), n_row, flat)
    for t in range(tiles):
        lanes = slice(t * LANES, (t + 1) * LANES)
        masked = flat[0:j_rows, lanes] * rj_ref[...] * keep_ref[:, lanes]
        if j_rows < j_pad:
            masked = jnp.concatenate([masked, jnp.zeros((j_pad - j_rows, LANES), F32)], axis=0)
        turned[lanes, :] = masked.T
    for a in range(blocks):
        parts = [
            turned[pl.ds(lo * chans + groups * a + b, tiles, stride=LANES), :]
            for b in range(groups)
            for lo in range(groups)
        ]
        block = jnp.concatenate(parts, axis=0)
        rbig[a * j_rows : (a + 1) * j_rows, :] = block.T[:j_rows].astype(BF16)
    rbt_ref[...] = rbig[...].T


def left_kernel(dims, n_col, after, rbt_ref, *refs):
    chans, groups, blocks, i_rows, j_rows, step_rows, sequences = dims
    tiles = sequences * chans // LANES
    z_refs, (keep_out, send_out, gl_all) = refs[:-3], refs[-3:]
    group = lane_group((sequences, LANES), chans)
    group_t = lane_group((tiles, LANES), chans)

    for step in range(i_rows // step_rows):
        z_ref = at_step(z_refs, step)
        for first in range(0, step_rows, CHUNK):
            part = jnp.dot(
                rbt_ref[...],
                z_ref[:, first * LANES : (first + CHUNK) * LANES],
                preferred_element_type=F32,
            )
            for k in range(CHUNK):
                mine = part[:, k * LANES : (k + 1) * LANES]
                total = mine[0:sequences]
                for b in range(1, groups):
                    total = jnp.where(group == b, mine[b * sequences : (b + 1) * sequences], total)
                shift = LANES // 2
                while shift >= chans:
                    total = total + pltpu.roll(total, shift, axis=1)
                    shift //= 2
                merged = total[0:tiles]
                for lo in range(1, groups):
                    merged = jnp.where(group_t == lo, total[lo * tiles : (lo + 1) * tiles], merged)
                at = (step * step_rows + first + k) * tiles
                gl_all[at : at + tiles, :] = merged
    cut(gl_all, lax.axis_index("col"), n_col, keep_out, send_out)


def total_of(keep_ref, came_ref, k=0):
    return keep_ref[k].astype(F32) + came_ref[k].astype(F32)


def join_kernel(after, held_ref, came_ref, out_ref):
    count = held_ref.shape[0]
    for k in range(count):
        out_ref[k] = held_ref[k]
        out_ref[count + k] = came_ref[k]


def fold_kernel(after, held_ref, came_ref, keep_out, send_out):
    for k in range(held_ref.shape[0]):
        into = send_out if k % 2 else keep_out
        into[k // 2] = total_of(held_ref, came_ref, k).astype(into.dtype)


def turn_kernel(n_col, after, held_ref, came_ref, keep_out, send_out, whole):
    whole[...] = total_of(held_ref, came_ref)
    cut(whole, lax.axis_index("col"), n_col, keep_out, send_out)


def write_rows(whole, rows, keep_ref, out_ref, tiles):
    own = out_ref.shape[0]
    for t in range(tiles):
        lanes = slice(t * LANES, (t + 1) * LANES)
        out_ref[:, lanes] = whole[pl.ds(t, own, stride=tiles), :] * (
            rows * keep_ref[:, lanes]
        )


def pair_rows(dims, row, ri_ref, y_ref, wp_ref, inv_ref, out_ref, at):
    j_rows = dims[4]
    y_flat = y_ref[row : row + PIECE].reshape(PIECE * j_rows, y_ref.shape[2])
    projected = jnp.dot(y_flat, wp_ref[...], preferred_element_type=F32)
    for i in range(PIECE):
        inverse = jnp.where(ri_ref[row + i : row + i + 1, :] > 0, inv_ref[...], 1.0)
        out_ref[at + i] = (projected[i * j_rows : (i + 1) * j_rows] * inverse).astype(BF16)


def pair_first_kernel(dims, after, ri_ref, y_ref, wp_ref, inv_ref, out_ref):
    for row in range(0, out_ref.shape[0], PIECE):
        pair_rows(dims, row, ri_ref, y_ref, wp_ref, inv_ref, out_ref, row)


def pair_kernel(dims, *refs):
    after, ri_ref, y_ref, wp_ref, inv_ref, early, keep_ref, held, came = refs[:9]
    out_ref, gl_out, staged, whole, left, sems = refs[9:]
    begin = early.shape[0]
    copies = [pltpu.make_async_copy(early, out_ref.at[pl.ds(0, begin)], sems.at[0])]
    copies[0].start()
    own = left.shape[0]
    first = pl.multiple_of(lax.axis_index("col") * own, 8)
    whole[...] = total_of(held, came)
    write_rows(whole, ri_ref[pl.ds(first, own), :], keep_ref, left, whole.shape[0] // own)
    copies.append(pltpu.make_async_copy(left, gl_out, sems.at[1]))
    copies[1].start()
    for row in range(begin, dims[3], PIECE):
        pair_rows(dims, row, ri_ref, y_ref, wp_ref, inv_ref, staged, row - begin)
        copies.append(
            pltpu.make_async_copy(
                staged.at[pl.ds(row - begin, PIECE)],
                out_ref.at[pl.ds(row, PIECE)],
                sems.at[len(copies)],
            )
        )
        copies[-1].start()
    for copy in copies:
        copy.wait()


def final_kernel(after, rj_ref, keep_ref, *refs):
    right, weight = refs[0:2], refs[2:4]
    gr_out, gw_out, whole, rows, weight_rows, sems = refs[4:]
    weight_rows[...] = total_of(*weight)
    copies = [pltpu.make_async_copy(weight_rows, gw_out, sems.at[0])]
    copies[0].start()
    own = rows.shape[0]
    first = pl.multiple_of(lax.axis_index("row") * own, 8)
    whole[...] = total_of(*right)
    write_rows(whole, rj_ref[pl.ds(first, own), :], keep_ref, rows, whole.shape[0] // own)
    copies.append(pltpu.make_async_copy(rows, gr_out, sems.at[1]))
    copies[1].start()
    for copy in copies:
        copy.wait()


def swap(array, axis, n, bit):
    return lax.ppermute(array, axis, [(s, s ^ bit) for s in range(n)])


def owners_of(n):
    held, bit = [0], n // 2
    while bit > 1:
        held, bit = held + [k ^ bit for k in held], bit // 2
    return held, [k ^ 1 for k in held]


def gather(block, own, axis, n, after):
    held, sent, bit = own, block[None], n // 2
    while bit > 1:
        came = swap(sent, axis, n, bit)
        shape = (2 * held.shape[0],) + held.shape[1:]
        held = small_call(join_kernel, [pltpu.VMEM(shape, BF16)], "join")(after, held, came)[0]
        sent, bit = held, bit // 2
    return held, swap(sent, axis, n, 1)


def reduce(keep, send, axis, n, after):
    bit = 1
    while True:
        came = swap(send, axis, n, bit)
        bit *= 2
        if bit >= n:
            return keep, came
        half = (keep.shape[0] // 2,) + keep.shape[1:]
        outs = [pltpu.VMEM(half, F32), pltpu.VMEM(half, BF16)]
        keep, send = small_call(fold_kernel, outs, "fold")(after, keep, came)


def small_call(body, outs, name, scratch=()):
    def call(after, *operands):
        return pl.pallas_call(
            body,
            in_specs=[hbm()] + vmem(len(operands)),
            out_specs=vmem(len(outs)),
            out_shape=outs,
            scratch_shapes=list(scratch),
            compiler_params=params(4),
            cost_estimate=cost(1000, 1000),
            name=name,
        )(after, *operands)

    return call


def halves(rows, n):
    return [pltpu.VMEM((n // 2, rows // n, LANES), BF16)] * 2


def vmem(count=1):
    return [pl.BlockSpec(memory_space=pltpu.VMEM)] * count


def hbm():
    return pl.BlockSpec(memory_space=pl.ANY)


def in_hbm(array):
    return pltpu.with_memory_space_constraint(array, pltpu.HBM)


def shards(left_act, right_act, row_mask, res_mask, out_weight, cotangent):
    n_col = lax.axis_size("col")
    n_row = lax.axis_size("row")
    i_rows, j_rows, pair_width = cotangent.shape
    sequences = row_mask.shape[0]
    width = left_act.shape[1]
    chans = width // sequences
    groups = LANES // chans
    blocks = chans // groups
    tiles = width // LANES
    depth = groups * sequences
    inner = chans * chans
    step_rows = 32
    steps = i_rows // step_rows
    early_steps = steps // 2
    dims = (chans, groups, blocks, i_rows, j_rows, step_rows, sequences)
    j_pad = -(-j_rows // LANES) * LANES
    span = blocks * j_rows
    own_left, own_right = left_act.shape[0], right_act.shape[0]
    macs = i_rows * j_rows * inner * pair_width

    mask_row = (res_mask.reshape(1, -1), row_mask.reshape(1, -1))
    scaled, inverse, weight, keep, i_keep, j_keep, own_l, own_r, z_first = pl.pallas_call(
        functools.partial(scale_kernel, dims),
        in_specs=[hbm()] * 6,
        out_specs=vmem(9),
        out_shape=[
            pltpu.VMEM(cotangent.shape, BF16),
            pltpu.VMEM((j_rows, LANES), F32),
            pltpu.VMEM(out_weight.shape, BF16),
            pltpu.VMEM((1, width), F32),
            pltpu.VMEM((i_rows, LANES), F32),
            pltpu.VMEM((j_rows, LANES), F32),
            pltpu.VMEM((1,) + left_act.shape, BF16),
            pltpu.VMEM((1,) + right_act.shape, BF16),
            pltpu.VMEM((early_steps, span, step_rows * LANES), BF16),
        ],
        scratch_shapes=[
            pltpu.VMEM((1, res_mask.shape[0]), jnp.int32),
            pltpu.VMEM((1, sequences), jnp.int32),
            pltpu.VMEM(out_weight.shape, BF16),
            pltpu.VMEM(out_weight.shape, F32),
            pltpu.VMEM(cotangent.shape, BF16),
            pltpu.SemaphoreType.DMA((i_rows // PIECE,)),
            pltpu.SemaphoreType.DMA((5,)),
        ],
        compiler_params=params(16),
        cost_estimate=cost(1000, 1000),
        name="scale",
    )(*map(in_hbm, (*mask_row, cotangent, out_weight, left_act, right_act)))

    lefts = gather(left_act, own_l, "col", n_col, own_l)
    rights = gather(right_act, own_r, "row", n_row, lefts[0])

    z_last = pl.pallas_call(
        functools.partial(inner_kernel, dims, early_steps),
        in_specs=[hbm()] + vmem(2),
        out_specs=vmem()[0],
        out_shape=pltpu.VMEM((steps - early_steps, span, step_rows * LANES), BF16),
        compiler_params=params(16),
        cost_estimate=cost(16 * macs, 2**20),
        name="inner",
    )(rights[0], scaled, weight)
    z = (z_first, z_last)

    rbig, right_turned = pl.pallas_call(
        functools.partial(right_rows_kernel, dims, n_row),
        in_specs=[hbm()] + vmem(4),
        out_specs=vmem(2),
        out_shape=[pltpu.VMEM((span, depth), BF16), pltpu.VMEM((depth, span), BF16)],
        scratch_shapes=[pltpu.VMEM((j_rows, width), F32), pltpu.VMEM((width, j_pad), F32)],
        compiler_params=params(12),
        cost_estimate=cost(16 * macs, 2**20),
        name="right_rows",
    )(z_last, j_keep, keep, *rights)

    gl_cut = pl.pallas_call(
        functools.partial(left_kernel, dims, n_col),
        in_specs=[hbm()] + vmem(1 + len(z)),
        out_specs=vmem(2),
        out_shape=halves(i_rows * tiles, n_col),
        scratch_shapes=[pltpu.VMEM((i_rows * tiles, LANES), F32)],
        compiler_params=params(16),
        cost_estimate=cost(16 * macs, 2**20),
        name="left",
    )(rbig, right_turned, *z)
    y, diag, *gw_cut = pl.pallas_call(
        functools.partial(outer_kernel, dims, n_row, n_col),
        in_specs=[hbm()] + vmem(6),
        out_specs=vmem(4),
        out_shape=[
            pltpu.VMEM((i_rows, j_rows, inner), BF16),
            pltpu.VMEM((steps, depth, step_rows * LANES), BF16),
        ]
        + halves(inner, n_row),
        scratch_shapes=[
            pltpu.VMEM((i_rows, width), F32),
            pltpu.VMEM((i_rows * tiles, LANES), F32),
            pltpu.VMEM((LANES, groups * LANES), BF16),
            pltpu.VMEM((pair_width, inner), F32),
            pltpu.VMEM((inner, pair_width), F32),
        ],
        compiler_params=params(16),
        cost_estimate=cost(16 * macs, 2**20),
        name="outer",
    )(gl_cut[0], i_keep, keep, scaled, rbig, *lefts)

    gl_last = reduce(*gl_cut, "col", n_col, gw_cut[0])

    right_steps = max(1, steps // 4)
    acc = pl.pallas_call(
        functools.partial(right_first_kernel, right_steps),
        in_specs=[hbm()] + vmem(1 + len(z)),
        out_specs=vmem()[0],
        out_shape=pltpu.VMEM((depth, span), F32),
        compiler_params=params(16),
        cost_estimate=cost(16 * macs, 2**20),
        name="right_first",
    )(gl_last[0], diag, *z)
    gw_row = reduce(*gw_cut, "row", n_row, acc)

    gr_cut = pl.pallas_call(
        functools.partial(right_kernel, dims, n_row, right_steps),
        in_specs=[hbm()] + vmem(2 + len(z)),
        out_specs=vmem(2),
        out_shape=halves(j_rows * tiles, n_row),
        scratch_shapes=[
            pltpu.VMEM((depth, span), F32),
            pltpu.VMEM((width, j_pad), F32),
            pltpu.VMEM((j_rows * tiles, LANES), F32),
        ],
        compiler_params=params(20),
        cost_estimate=cost(16 * macs, 2**20),
        name="right",
    )(gw_row[0], diag, acc, *z)
    gw_cut = small_call(
        functools.partial(turn_kernel, n_col),
        halves(inner // n_row, n_col),
        "turn",
        [pltpu.VMEM((inner // n_row, pair_width), F32)],
    )(gr_cut[0], *gw_row)

    begin = i_rows // PIECE // 2 * PIECE
    early = pl.pallas_call(
        functools.partial(pair_first_kernel, dims),
        in_specs=[hbm()] + vmem(4),
        out_specs=vmem()[0],
        out_shape=pltpu.VMEM((begin, j_rows, pair_width), BF16),
        compiler_params=params(12),
        cost_estimate=cost(16 * macs, 2**20),
        name="pair_first",
    )(gw_cut[0], i_keep, y, weight, inverse)
    gw_last = reduce(*gw_cut, "col", n_col, early)
    gr_last = reduce(*gr_cut, "row", n_row, gw_last[0])
    pair_out, grad_left = pl.pallas_call(
        functools.partial(pair_kernel, dims),
        in_specs=[hbm()] + vmem(8),
        out_specs=[hbm()] * 2,
        out_shape=[
            jax.ShapeDtypeStruct(cotangent.shape, BF16),
            jax.ShapeDtypeStruct((own_left, width), F32),
        ],
        scratch_shapes=[
            pltpu.VMEM((i_rows - begin, j_rows, pair_width), BF16),
            pltpu.VMEM((own_left * tiles, LANES), F32),
            pltpu.VMEM((own_left, width), F32),
            pltpu.SemaphoreType.DMA((2 + (i_rows - begin) // PIECE,)),
        ],
        compiler_params=params(12),
        cost_estimate=cost(16 * macs, 2**20),
        name="pair",
    )(gr_last[0], i_keep, y, weight, inverse, early, keep, *gl_last)

    owned = (inner // n_row // n_col, pair_width)
    grad_right, grad_weight = pl.pallas_call(
        final_kernel,
        in_specs=[hbm()] + vmem(6),
        out_specs=[hbm()] * 2,
        out_shape=[
            jax.ShapeDtypeStruct((own_right, width), F32),
            jax.ShapeDtypeStruct(owned, F32),
        ],
        scratch_shapes=[
            pltpu.VMEM((own_right * tiles, LANES), F32),
            pltpu.VMEM((own_right, width), F32),
            pltpu.VMEM(owned, F32),
            pltpu.SemaphoreType.DMA((2,)),
        ],
        compiler_params=params(4),
        cost_estimate=cost(1000, 1000),
        name="final_sums",
    )(in_hbm(pair_out), j_keep, keep, *gr_last, *gw_last)
    return (pair_out, grad_left, grad_right, grad_weight)


def solution(mesh):
    placed = (
        P(("grp", "row", "col"), None),
        P(("grp", "col", "row"), None),
        P("grp"),
        P("grp"),
        P(),
        P(("grp", "row"), "col", None),
    )
    return jax.shard_map(
        shards,
        mesh=mesh,
        in_specs=placed,
        out_specs=(
            P(("grp", "row"), "col", None),
            P(("grp", "row", "col"), None),
            P(("grp", "col", "row"), None),
            P(("grp", "row", "col"), None),
        ),
        check_vma=False,
    )
```

```python
import functools

import jax
import jax.numpy as jnp
from jax import lax
from jax.experimental import pallas as pl
from jax.experimental.pallas import tpu as pltpu
from jax.sharding import PartitionSpec as P

LANES = 128
CHUNK = 4
PIECE = 8
NT = (((1,), (1,)), ((), ()))
F32 = jnp.float32
BF16 = jnp.bfloat16


def params(mib):
    return pltpu.CompilerParams(vmem_limit_bytes=mib * 2**20)


def cost(flops, nbytes):
    return pl.CostEstimate(flops=int(flops), bytes_accessed=int(nbytes), transcendentals=0)


def cut(source, index, n, keep_ref, send_ref):
    rows = source.shape[0] // n
    for k in range(n):
        at = pl.multiple_of((index ^ k) * rows, rows)
        into = send_ref if k % 2 else keep_ref
        into[k // 2] = source[pl.ds(at, rows), :].astype(into.dtype)


def place(buffers, index, n, flat):
    for buffer, owners in zip(buffers, owners_of(n)):
        rows = buffer.shape[1]
        for k, owner in enumerate(owners):
            at = pl.multiple_of((index ^ owner) * rows, 8)
            flat[pl.ds(at, rows), :] = buffer[k].astype(F32)


def lane_group(shape, chans):
    return lax.broadcasted_iota(jnp.int32, shape, 1) // chans


def mask_rows(res_ref, first, count):
    shape = (count, res_ref.shape[1])
    row = lax.broadcasted_iota(jnp.int32, shape, 0) + first
    here = lax.broadcasted_iota(jnp.int32, shape, 1) == row
    chosen = jnp.where(here, res_ref[...].astype(F32), 0.0)
    return jnp.broadcast_to(jnp.sum(chosen, axis=1, keepdims=True), (count, LANES))


def scale_kernel(dims, *refs):
    chans, groups, blocks, i_rows, j_rows, step_rows, sequences = dims
    tiles = sequences * chans // LANES
    res_hbm, seq_hbm, cot_ref, w_hbm, left_hbm, right_hbm = refs[:6]
    scaled_ref, inv_ref, wp_ref, keep_ref, ri_ref, rj_ref, left_ref, right_ref, z_ref = refs[6:15]
    res_ref, seq_ref, w_ref, w32, cot, sems, more_sems = refs[15:]
    steps = i_rows // step_rows

    def fetch(piece):
        rows = pl.ds(piece * PIECE, PIECE)
        return pltpu.make_async_copy(cot_ref.at[rows], cot.at[rows], sems.at[piece])

    pairs = [
        (res_hbm, res_ref),
        (seq_hbm, seq_ref),
        (w_hbm, w_ref),
        (left_hbm, left_ref.at[0]),
        (right_hbm, right_ref.at[0]),
    ]
    more = [
        pltpu.make_async_copy(source, to, more_sems.at[k]) for k, (source, to) in enumerate(pairs)
    ]
    for copy in more[:3]:
        copy.start()
    for piece in range(i_rows // PIECE):
        fetch(piece).start()
    for copy in more[3:]:
        copy.start()
    shape = (sequences, tiles * LANES)
    own = lax.broadcasted_iota(jnp.int32, shape, 1) // chans
    repeat = (own == lax.broadcasted_iota(jnp.int32, shape, 0)).astype(F32).astype(BF16)
    more[0].wait()
    ri_ref[...] = mask_rows(res_ref, lax.axis_index("row") * i_rows, i_rows)
    rj_ref[...] = mask_rows(res_ref, lax.axis_index("col") * j_rows, j_rows)
    more[1].wait()
    seq = seq_ref[...].astype(F32)
    keep_ref[...] = jnp.dot(
        jnp.broadcast_to(seq, (8, sequences)).astype(BF16), repeat, preferred_element_type=F32
    )[0:1]
    valid = jnp.sum(seq, axis=1, keepdims=True)
    inv_ref[...] = 1.0 / jnp.maximum(valid * rj_ref[...], 1.0)
    more[2].wait()
    w32[...] = w_ref[...].astype(F32)
    for e in range(chans):
        wp_ref[e * chans : (e + 1) * chans, :] = w32[pl.ds(e, chans, stride=chans), :].astype(BF16)
    for step in range(steps):
        for at in range(step * step_rows, (step + 1) * step_rows):
            if at % PIECE == 0:
                fetch(at // PIECE).wait()
            inverse = jnp.where(ri_ref[at : at + 1, :] > 0, inv_ref[...], 1.0)
            scaled_ref[at] = (cot[at].astype(F32) * inverse).astype(BF16)
        if step < z_ref.shape[0]:
            rows = slice(step * step_rows, (step + 1) * step_rows)
            inner_rows(dims, scaled_ref[rows], wp_ref, z_ref, step)
    more[3].wait()
    more[4].wait()


def inner_rows(dims, scaled, wp_ref, z_ref, at):
    chans, groups, blocks, i_rows, j_rows, step_rows, sequences = dims
    for first in range(0, blocks, CHUNK):
        part = lax.dot_general(
            scaled.reshape(step_rows * j_rows, LANES),
            wp_ref[first * LANES : (first + CHUNK) * LANES, :],
            NT,
            preferred_element_type=F32,
        ).astype(BF16)
        for k in range(CHUNK):
            a = first + k
            for i in range(step_rows):
                z_ref[at, a * j_rows : (a + 1) * j_rows, i * LANES : (i + 1) * LANES] = part[
                    i * j_rows : (i + 1) * j_rows, k * LANES : (k + 1) * LANES
                ]


def inner_kernel(dims, first, after, scaled_ref, wp_ref, z_ref):
    step_rows = dims[5]
    for at in range(z_ref.shape[0]):
        rows = slice((first + at) * step_rows, (first + at + 1) * step_rows)
        inner_rows(dims, scaled_ref[rows], wp_ref, z_ref, at)


def at_step(refs, step):
    for ref in refs:
        if step < ref.shape[0]:
            return ref.at[step]
        step -= ref.shape[0]


def outer_kernel(dims, n_row, n_col, *refs):
    chans, groups, blocks, i_rows, j_rows, step_rows, sequences = dims
    tiles = sequences * chans // LANES
    after, ri_ref, keep_ref, scaled_ref, rbig, left_held, left_came = refs[:7]
    y_ref, diag_ref, keep_out, send_out = refs[7:11]
    flat, lsplit, expand, gwt, gwr = refs[11:]
    place((left_held, left_came), lax.axis_index("col"), n_col, flat)
    for t in range(tiles):
        lanes = slice(t * LANES, (t + 1) * LANES)
        masked = flat[0:i_rows, lanes] * ri_ref[...] * keep_ref[:, lanes]
        lsplit[pl.ds(t, i_rows, stride=tiles), :] = masked
    shape = (LANES, groups * LANES)
    source = lax.broadcasted_iota(jnp.int32, shape, 0)
    target = lax.broadcasted_iota(jnp.int32, shape, 1)
    same = (source // chans == target // LANES) & (source % chans == target % chans)
    expand[...] = same.astype(F32).astype(BF16)
    rows = step_rows * tiles
    deep_rows = 2 * step_rows if i_rows % (2 * step_rows) == 0 else step_rows
    group = lane_group((tiles, LANES), chans)

    for step in range(i_rows // step_rows):
        spread = jnp.dot(
            lsplit[step * rows : (step + 1) * rows, :].astype(BF16),
            expand[...],
            preferred_element_type=F32,
        ).astype(BF16)
        for b in range(groups):
            chosen = (group == b).astype(F32).astype(BF16)
            for lo in range(groups):
                at = b * sequences + lo * tiles
                for i in range(step_rows):
                    diag_ref[step, at : at + tiles, i * LANES : (i + 1) * LANES] = (
                        spread[i * tiles : (i + 1) * tiles, lo * LANES : (lo + 1) * LANES] * chosen
                    )
        for first in range(0, step_rows, CHUNK):
            part = jnp.dot(
                rbig[...],
                diag_ref[step, :, first * LANES : (first + CHUNK) * LANES],
                preferred_element_type=F32,
            ).astype(BF16)
            for k in range(CHUNK):
                for a in range(blocks):
                    y_ref[step * step_rows + first + k, :, a * LANES : (a + 1) * LANES] = part[
                        a * j_rows : (a + 1) * j_rows, k * LANES : (k + 1) * LANES
                    ]
        if (step + 1) * step_rows % deep_rows == 0:
            block = slice((step + 1) * step_rows - deep_rows, (step + 1) * step_rows)
            scaled_t = scaled_ref[block].reshape(deep_rows * j_rows, LANES).T
            y_flat = y_ref[block].reshape(deep_rows * j_rows, blocks * LANES)
            part = jnp.dot(scaled_t, y_flat, preferred_element_type=F32)
            gwt[...] = gwt[...] + part if block.start else part
    for k in range(blocks):
        turned_tile = gwt[:, k * LANES : (k + 1) * LANES].T
        for q in range(groups):
            gwr[pl.ds(k * groups + q, chans, stride=chans), :] = turned_tile[
                q * chans : (q + 1) * chans
            ]
    cut(gwr, lax.axis_index("row"), n_row, keep_out, send_out)


def right_sum(first, last, z_refs, diag_ref, acc, so_far=None):
    for step in range(first, last):
        part = lax.dot_general(
            diag_ref[step], at_step(z_refs, step)[...], NT, preferred_element_type=F32
        )
        acc[...] = part if so_far is None else so_far[...] + part
        so_far = acc


def right_first_kernel(steps, after, diag_ref, *refs):
    right_sum(0, steps, refs[:-1], diag_ref, refs[-1])


def right_kernel(dims, n_row, first, after, diag_ref, acc_first, *refs):
    chans, groups, blocks, i_rows, j_rows, step_rows, sequences = dims
    tiles = sequences * chans // LANES
    j_pad = -(-j_rows // LANES) * LANES
    z_refs, (keep_out, send_out, acc, turned, gr_all) = refs[:-5], refs[-5:]
    right_sum(first, i_rows // step_rows, z_refs, diag_ref, acc, acc_first)
    for a in range(blocks):
        at, shift = divmod(a * j_rows, LANES)
        mine = acc[:, at * LANES : at * LANES + j_pad]
        if shift:
            mine = pltpu.roll(mine, LANES - shift, axis=1)
        for b in range(groups):
            for lo in range(groups):
                first = b * sequences + lo * tiles
                turned[pl.ds(lo * chans + groups * a + b, tiles, stride=LANES), :] = mine[
                    first : first + tiles
                ]
    for t in range(tiles):
        lanes = slice(t * LANES, (t + 1) * LANES)
        gr_all[pl.ds(t, j_rows, stride=tiles), :] = turned[lanes, :].T[:j_rows]
    cut(gr_all, lax.axis_index("row"), n_row, keep_out, send_out)


def right_rows_kernel(dims, n_row, after, rj_ref, keep_ref, right_held, right_came, *refs):
    chans, groups, blocks, i_rows, j_rows, step_rows, sequences = dims
    tiles = sequences * chans // LANES
    j_pad = -(-j_rows // LANES) * LANES
    rbig, rbt_ref, flat, turned = refs
    place((right_held, right_came), lax.axis_index("row"), n_row, flat)
    for t in range(tiles):
        lanes = slice(t * LANES, (t + 1) * LANES)
        masked = flat[0:j_rows, lanes] * rj_ref[...] * keep_ref[:, lanes]
        if j_rows < j_pad:
            masked = jnp.concatenate([masked, jnp.zeros((j_pad - j_rows, LANES), F32)], axis=0)
        turned[lanes, :] = masked.T
    for a in range(blocks):
        parts = [
            turned[pl.ds(lo * chans + groups * a + b, tiles, stride=LANES), :]
            for b in range(groups)
            for lo in range(groups)
        ]
        block = jnp.concatenate(parts, axis=0)
        rbig[a * j_rows : (a + 1) * j_rows, :] = block.T[:j_rows].astype(BF16)
    rbt_ref[...] = rbig[...].T


def left_kernel(dims, n_col, after, rbt_ref, *refs):
    chans, groups, blocks, i_rows, j_rows, step_rows, sequences = dims
    tiles = sequences * chans // LANES
    z_refs, (keep_out, send_out, gl_all) = refs[:-3], refs[-3:]
    group = lane_group((sequences, LANES), chans)
    group_t = lane_group((tiles, LANES), chans)

    for step in range(i_rows // step_rows):
        z_ref = at_step(z_refs, step)
        for first in range(0, step_rows, CHUNK):
            part = jnp.dot(
                rbt_ref[...],
                z_ref[:, first * LANES : (first + CHUNK) * LANES],
                preferred_element_type=F32,
            )
            for k in range(CHUNK):
                mine = part[:, k * LANES : (k + 1) * LANES]
                total = mine[0:sequences]
                for b in range(1, groups):
                    total = jnp.where(group == b, mine[b * sequences : (b + 1) * sequences], total)
                shift = LANES // 2
                while shift >= chans:
                    total = total + pltpu.roll(total, shift, axis=1)
                    shift //= 2
                merged = total[0:tiles]
                for lo in range(1, groups):
                    merged = jnp.where(group_t == lo, total[lo * tiles : (lo + 1) * tiles], merged)
                at = (step * step_rows + first + k) * tiles
                gl_all[at : at + tiles, :] = merged
    cut(gl_all, lax.axis_index("col"), n_col, keep_out, send_out)


def total_of(keep_ref, came_ref, k=0):
    return keep_ref[k].astype(F32) + came_ref[k].astype(F32)


def join_kernel(after, held_ref, came_ref, out_ref):
    count = held_ref.shape[0]
    for k in range(count):
        out_ref[k] = held_ref[k]
        out_ref[count + k] = came_ref[k]


def fold_kernel(after, held_ref, came_ref, keep_out, send_out):
    for k in range(held_ref.shape[0]):
        into = send_out if k % 2 else keep_out
        into[k // 2] = total_of(held_ref, came_ref, k).astype(into.dtype)


def turn_kernel(n_col, after, held_ref, came_ref, keep_out, send_out, whole):
    whole[...] = total_of(held_ref, came_ref)
    cut(whole, lax.axis_index("col"), n_col, keep_out, send_out)


def write_rows(whole, rows, keep_ref, out_ref, tiles):
    own = out_ref.shape[0]
    for t in range(tiles):
        lanes = slice(t * LANES, (t + 1) * LANES)
        out_ref[:, lanes] = whole[pl.ds(t, own, stride=tiles), :] * (
            rows * keep_ref[:, lanes]
        )


def pair_rows(dims, row, ri_ref, y_ref, wp_ref, inv_ref, out_ref, at):
    j_rows = dims[4]
    y_flat = y_ref[row : row + PIECE].reshape(PIECE * j_rows, y_ref.shape[2])
    projected = jnp.dot(y_flat, wp_ref[...], preferred_element_type=F32)
    for i in range(PIECE):
        inverse = jnp.where(ri_ref[row + i : row + i + 1, :] > 0, inv_ref[...], 1.0)
        out_ref[at + i] = (projected[i * j_rows : (i + 1) * j_rows] * inverse).astype(BF16)


def pair_first_kernel(dims, after, ri_ref, y_ref, wp_ref, inv_ref, out_ref):
    for row in range(0, out_ref.shape[0], PIECE):
        pair_rows(dims, row, ri_ref, y_ref, wp_ref, inv_ref, out_ref, row)


def pair_kernel(dims, *refs):
    after, ri_ref, y_ref, wp_ref, inv_ref, early, keep_ref = refs[:7]
    left_sums, weight_sums = refs[7:9], refs[9:11]
    out_ref, gl_out, gw_out, staged, whole, left, weight, sems = refs[11:]
    begin = early.shape[0]
    copies = [pltpu.make_async_copy(early, out_ref.at[pl.ds(0, begin)], sems.at[0])]
    copies[0].start()
    own = left.shape[0]
    first = pl.multiple_of(lax.axis_index("col") * own, 8)
    whole[...] = total_of(*left_sums)
    write_rows(whole, ri_ref[pl.ds(first, own), :], keep_ref, left, whole.shape[0] // own)
    weight[...] = total_of(*weight_sums)
    copies.append(pltpu.make_async_copy(left, gl_out, sems.at[1]))
    copies.append(pltpu.make_async_copy(weight, gw_out, sems.at[2]))
    copies[1].start()
    copies[2].start()
    for row in range(begin, dims[3], PIECE):
        pair_rows(dims, row, ri_ref, y_ref, wp_ref, inv_ref, staged, row - begin)
        copies.append(
            pltpu.make_async_copy(
                staged.at[pl.ds(row - begin, PIECE)],
                out_ref.at[pl.ds(row, PIECE)],
                sems.at[len(copies)],
            )
        )
        copies[-1].start()
    for copy in copies:
        copy.wait()


def final_kernel(after, rj_ref, keep_ref, held, came, gr_out, whole):
    own = gr_out.shape[0]
    first = pl.multiple_of(lax.axis_index("row") * own, 8)
    whole[...] = total_of(held, came)
    write_rows(whole, rj_ref[pl.ds(first, own), :], keep_ref, gr_out, whole.shape[0] // own)


def swap(array, axis, n, bit):
    return lax.ppermute(array, axis, [(s, s ^ bit) for s in range(n)])


def owners_of(n):
    held, bit = [0], n // 2
    while bit > 1:
        held, bit = held + [k ^ bit for k in held], bit // 2
    return held, [k ^ 1 for k in held]


def gather(block, own, axis, n, after):
    held, sent, bit = own, block[None], n // 2
    while bit > 1:
        came = swap(sent, axis, n, bit)
        shape = (2 * held.shape[0],) + held.shape[1:]
        held = small_call(join_kernel, [pltpu.VMEM(shape, BF16)], "join")(after, held, came)[0]
        sent, bit = held, bit // 2
    return held, swap(sent, axis, n, 1)


def reduce(keep, send, axis, n, after):
    bit = 1
    while True:
        came = swap(send, axis, n, bit)
        bit *= 2
        if bit >= n:
            return keep, came
        half = (keep.shape[0] // 2,) + keep.shape[1:]
        outs = [pltpu.VMEM(half, F32), pltpu.VMEM(half, BF16)]
        keep, send = small_call(fold_kernel, outs, "fold")(after, keep, came)


def small_call(body, outs, name, scratch=()):
    def call(after, *operands):
        return pl.pallas_call(
            body,
            in_specs=[hbm()] + vmem(len(operands)),
            out_specs=vmem(len(outs)),
            out_shape=outs,
            scratch_shapes=list(scratch),
            compiler_params=params(4),
            cost_estimate=cost(1000, 1000),
            name=name,
        )(after, *operands)

    return call


def halves(rows, n):
    return [pltpu.VMEM((n // 2, rows // n, LANES), BF16)] * 2


def vmem(count=1):
    return [pl.BlockSpec(memory_space=pltpu.VMEM)] * count


def hbm():
    return pl.BlockSpec(memory_space=pl.ANY)


def in_hbm(array):
    return pltpu.with_memory_space_constraint(array, pltpu.HBM)


def shards(left_act, right_act, row_mask, res_mask, out_weight, cotangent):
    n_col = lax.axis_size("col")
    n_row = lax.axis_size("row")
    i_rows, j_rows, pair_width = cotangent.shape
    sequences = row_mask.shape[0]
    width = left_act.shape[1]
    chans = width // sequences
    groups = LANES // chans
    blocks = chans // groups
    tiles = width // LANES
    depth = groups * sequences
    inner = chans * chans
    step_rows = 16
    steps = i_rows // step_rows
    early_steps = steps // 2
    dims = (chans, groups, blocks, i_rows, j_rows, step_rows, sequences)
    j_pad = -(-j_rows // LANES) * LANES
    span = blocks * j_rows
    own_left, own_right = left_act.shape[0], right_act.shape[0]
    macs = i_rows * j_rows * inner * pair_width

    mask_row = (res_mask.reshape(1, -1), row_mask.reshape(1, -1))
    scaled, inverse, weight, keep, i_keep, j_keep, own_l, own_r, z_first = pl.pallas_call(
        functools.partial(scale_kernel, dims),
        in_specs=[hbm()] * 6,
        out_specs=vmem(9),
        out_shape=[
            pltpu.VMEM(cotangent.shape, BF16),
            pltpu.VMEM((j_rows, LANES), F32),
            pltpu.VMEM(out_weight.shape, BF16),
            pltpu.VMEM((1, width), F32),
            pltpu.VMEM((i_rows, LANES), F32),
            pltpu.VMEM((j_rows, LANES), F32),
            pltpu.VMEM((1,) + left_act.shape, BF16),
            pltpu.VMEM((1,) + right_act.shape, BF16),
            pltpu.VMEM((early_steps, span, step_rows * LANES), BF16),
        ],
        scratch_shapes=[
            pltpu.VMEM((1, res_mask.shape[0]), jnp.int32),
            pltpu.VMEM((1, sequences), jnp.int32),
            pltpu.VMEM(out_weight.shape, BF16),
            pltpu.VMEM(out_weight.shape, F32),
            pltpu.VMEM(cotangent.shape, BF16),
            pltpu.SemaphoreType.DMA((i_rows // PIECE,)),
            pltpu.SemaphoreType.DMA((5,)),
        ],
        compiler_params=params(16),
        cost_estimate=cost(1000, 1000),
        name="scale",
    )(*map(in_hbm, (*mask_row, cotangent, out_weight, left_act, right_act)))

    lefts = gather(left_act, own_l, "col", n_col, own_l)
    rights = gather(right_act, own_r, "row", n_row, lefts[0])

    z_last = pl.pallas_call(
        functools.partial(inner_kernel, dims, early_steps),
        in_specs=[hbm()] + vmem(2),
        out_specs=vmem()[0],
        out_shape=pltpu.VMEM((steps - early_steps, span, step_rows * LANES), BF16),
        compiler_params=params(16),
        cost_estimate=cost(16 * macs, 2**20),
        name="inner",
    )(rights[0], scaled, weight)
    z = (z_first, z_last)

    rbig, right_turned = pl.pallas_call(
        functools.partial(right_rows_kernel, dims, n_row),
        in_specs=[hbm()] + vmem(4),
        out_specs=vmem(2),
        out_shape=[pltpu.VMEM((span, depth), BF16), pltpu.VMEM((depth, span), BF16)],
        scratch_shapes=[pltpu.VMEM((j_rows, width), F32), pltpu.VMEM((width, j_pad), F32)],
        compiler_params=params(12),
        cost_estimate=cost(16 * macs, 2**20),
        name="right_rows",
    )(z_last, j_keep, keep, *rights)

    gl_cut = pl.pallas_call(
        functools.partial(left_kernel, dims, n_col),
        in_specs=[hbm()] + vmem(1 + len(z)),
        out_specs=vmem(2),
        out_shape=halves(i_rows * tiles, n_col),
        scratch_shapes=[pltpu.VMEM((i_rows * tiles, LANES), F32)],
        compiler_params=params(16),
        cost_estimate=cost(16 * macs, 2**20),
        name="left",
    )(rbig, right_turned, *z)
    y, diag, *gw_cut = pl.pallas_call(
        functools.partial(outer_kernel, dims, n_row, n_col),
        in_specs=[hbm()] + vmem(6),
        out_specs=vmem(4),
        out_shape=[
            pltpu.VMEM((i_rows, j_rows, inner), BF16),
            pltpu.VMEM((steps, depth, step_rows * LANES), BF16),
        ]
        + halves(inner, n_row),
        scratch_shapes=[
            pltpu.VMEM((i_rows, width), F32),
            pltpu.VMEM((i_rows * tiles, LANES), F32),
            pltpu.VMEM((LANES, groups * LANES), BF16),
            pltpu.VMEM((pair_width, inner), F32),
            pltpu.VMEM((inner, pair_width), F32),
        ],
        compiler_params=params(16),
        cost_estimate=cost(16 * macs, 2**20),
        name="outer",
    )(gl_cut[0], i_keep, keep, scaled, rbig, *lefts)

    gw_row = reduce(*gw_cut, "row", n_row, gw_cut[0])
    gl_last = reduce(*gl_cut, "col", n_col, gw_row[0])

    right_steps = steps // 2
    acc = pl.pallas_call(
        functools.partial(right_first_kernel, right_steps),
        in_specs=[hbm()] + vmem(1 + len(z)),
        out_specs=vmem()[0],
        out_shape=pltpu.VMEM((depth, span), F32),
        compiler_params=params(16),
        cost_estimate=cost(16 * macs, 2**20),
        name="right_first",
    )(gl_last[0], diag, *z)
    gw_cut = small_call(
        functools.partial(turn_kernel, n_col),
        halves(inner // n_row, n_col),
        "turn",
        [pltpu.VMEM((inner // n_row, pair_width), F32)],
    )(acc, *gw_row)

    gr_cut = pl.pallas_call(
        functools.partial(right_kernel, dims, n_row, right_steps),
        in_specs=[hbm()] + vmem(2 + len(z)),
        out_specs=vmem(2),
        out_shape=halves(j_rows * tiles, n_row),
        scratch_shapes=[
            pltpu.VMEM((depth, span), F32),
            pltpu.VMEM((width, j_pad), F32),
            pltpu.VMEM((j_rows * tiles, LANES), F32),
        ],
        compiler_params=params(20),
        cost_estimate=cost(16 * macs, 2**20),
        name="right",
    )(gw_cut[0], diag, acc, *z)
    gw_last = reduce(*gw_cut, "col", n_col, gr_cut[0])

    begin = i_rows // PIECE // 2 * PIECE
    early = pl.pallas_call(
        functools.partial(pair_first_kernel, dims),
        in_specs=[hbm()] + vmem(4),
        out_specs=vmem()[0],
        out_shape=pltpu.VMEM((begin, j_rows, pair_width), BF16),
        compiler_params=params(12),
        cost_estimate=cost(16 * macs, 2**20),
        name="pair_first",
    )(gw_last[0], i_keep, y, weight, inverse)
    gr_last = reduce(*gr_cut, "row", n_row, early)
    owned = (inner // n_row // n_col, pair_width)
    pair_out, grad_left, grad_weight = pl.pallas_call(
        functools.partial(pair_kernel, dims),
        in_specs=[hbm()] + vmem(10),
        out_specs=[hbm()] * 3,
        out_shape=[
            jax.ShapeDtypeStruct(cotangent.shape, BF16),
            jax.ShapeDtypeStruct((own_left, width), F32),
            jax.ShapeDtypeStruct(owned, F32),
        ],
        scratch_shapes=[
            pltpu.VMEM((i_rows - begin, j_rows, pair_width), BF16),
            pltpu.VMEM((own_left * tiles, LANES), F32),
            pltpu.VMEM((own_left, width), F32),
            pltpu.VMEM(owned, F32),
            pltpu.SemaphoreType.DMA((3 + (i_rows - begin) // PIECE,)),
        ],
        compiler_params=params(12),
        cost_estimate=cost(16 * macs, 2**20),
        name="pair",
    )(gr_last[0], i_keep, y, weight, inverse, early, keep, *gl_last, *gw_last)

    grad_right = pl.pallas_call(
        final_kernel,
        in_specs=[hbm()] + vmem(4),
        out_specs=vmem()[0],
        out_shape=jax.ShapeDtypeStruct((own_right, width), F32),
        scratch_shapes=[pltpu.VMEM((own_right * tiles, LANES), F32)],
        compiler_params=params(4),
        cost_estimate=cost(1000, 1000),
        name="final_sums",
    )(in_hbm(pair_out), j_keep, keep, *gr_last)
    return (pair_out, grad_left, grad_right, grad_weight)


def solution(mesh):
    placed = (
        P(("grp", "row", "col"), None),
        P(("grp", "col", "row"), None),
        P("grp"),
        P("grp"),
        P(),
        P(("grp", "row"), "col", None),
    )
    return jax.shard_map(
        shards,
        mesh=mesh,
        in_specs=placed,
        out_specs=(
            P(("grp", "row"), "col", None),
            P(("grp", "row", "col"), None),
            P(("grp", "col", "row"), None),
            P(("grp", "row", "col"), None),
        ),
        check_vma=False,
    )
```

```python
import functools

import jax
import jax.numpy as jnp
from jax import lax
from jax.experimental import pallas as pl
from jax.experimental.pallas import tpu as pltpu
from jax.sharding import PartitionSpec as P

LANES = 128
CHUNK = 4
PIECE = 8
NT = (((1,), (1,)), ((), ()))
F32 = jnp.float32
BF16 = jnp.bfloat16


def params(mib):
    return pltpu.CompilerParams(vmem_limit_bytes=mib * 2**20)


def cost(flops, nbytes):
    return pl.CostEstimate(flops=int(flops), bytes_accessed=int(nbytes), transcendentals=0)


def cut(source, index, n, keep_ref, send_ref):
    rows = source.shape[0] // n
    for k in range(n):
        at = pl.multiple_of((index ^ k) * rows, rows)
        into = send_ref if k % 2 else keep_ref
        into[k // 2] = source[pl.ds(at, rows), :].astype(into.dtype)


def place(buffers, index, n, flat):
    for buffer, owners in zip(buffers, owners_of(n)):
        rows = buffer.shape[1]
        for k, owner in enumerate(owners):
            at = pl.multiple_of((index ^ owner) * rows, 8)
            flat[pl.ds(at, rows), :] = buffer[k].astype(F32)


def lane_group(shape, chans):
    return lax.broadcasted_iota(jnp.int32, shape, 1) // chans


def mask_rows(res_ref, first, count):
    shape = (count, res_ref.shape[1])
    row = lax.broadcasted_iota(jnp.int32, shape, 0) + first
    here = lax.broadcasted_iota(jnp.int32, shape, 1) == row
    chosen = jnp.where(here, res_ref[...].astype(F32), 0.0)
    return jnp.broadcast_to(jnp.sum(chosen, axis=1, keepdims=True), (count, LANES))


def scale_kernel(dims, *refs):
    chans, groups, blocks, i_rows, j_rows, step_rows, sequences = dims
    tiles = sequences * chans // LANES
    res_hbm, seq_hbm, cot_ref, w_hbm, left_hbm, right_hbm = refs[:6]
    scaled_ref, inv_ref, wp_ref, keep_ref, ri_ref, rj_ref, left_ref, right_ref, z_ref = refs[6:15]
    res_ref, seq_ref, w_ref, w32, cot, sems, more_sems = refs[15:]
    steps = i_rows // step_rows

    def fetch(piece):
        rows = pl.ds(piece * PIECE, PIECE)
        return pltpu.make_async_copy(cot_ref.at[rows], cot.at[rows], sems.at[piece])

    pairs = [
        (res_hbm, res_ref),
        (seq_hbm, seq_ref),
        (w_hbm, w_ref),
        (left_hbm, left_ref.at[0]),
        (right_hbm, right_ref.at[0]),
    ]
    more = [
        pltpu.make_async_copy(source, to, more_sems.at[k]) for k, (source, to) in enumerate(pairs)
    ]
    for copy in more[:3]:
        copy.start()
    for piece in range(i_rows // PIECE):
        fetch(piece).start()
    for copy in more[3:]:
        copy.start()
    shape = (sequences, tiles * LANES)
    own = lax.broadcasted_iota(jnp.int32, shape, 1) // chans
    repeat = (own == lax.broadcasted_iota(jnp.int32, shape, 0)).astype(F32).astype(BF16)
    more[0].wait()
    ri_ref[...] = mask_rows(res_ref, lax.axis_index("row") * i_rows, i_rows)
    rj_ref[...] = mask_rows(res_ref, lax.axis_index("col") * j_rows, j_rows)
    more[1].wait()
    seq = seq_ref[...].astype(F32)
    keep_ref[...] = jnp.dot(
        jnp.broadcast_to(seq, (8, sequences)).astype(BF16), repeat, preferred_element_type=F32
    )[0:1]
    valid = jnp.sum(seq, axis=1, keepdims=True)
    inv_ref[...] = 1.0 / jnp.maximum(valid * rj_ref[...], 1.0)
    more[2].wait()
    w32[...] = w_ref[...].astype(F32)
    for e in range(chans):
        wp_ref[e * chans : (e + 1) * chans, :] = w32[pl.ds(e, chans, stride=chans), :].astype(BF16)
    for step in range(steps):
        for at in range(step * step_rows, (step + 1) * step_rows):
            if at % PIECE == 0:
                fetch(at // PIECE).wait()
            inverse = jnp.where(ri_ref[at : at + 1, :] > 0, inv_ref[...], 1.0)
            scaled_ref[at] = (cot[at].astype(F32) * inverse).astype(BF16)
        if step < z_ref.shape[0]:
            rows = slice(step * step_rows, (step + 1) * step_rows)
            inner_rows(dims, scaled_ref[rows], wp_ref, z_ref, step)
    more[3].wait()
    more[4].wait()


def inner_rows(dims, scaled, wp_ref, z_ref, at):
    chans, groups, blocks, i_rows, j_rows, step_rows, sequences = dims
    for first in range(0, blocks, CHUNK):
        part = lax.dot_general(
            scaled.reshape(step_rows * j_rows, LANES),
            wp_ref[first * LANES : (first + CHUNK) * LANES, :],
            NT,
            preferred_element_type=F32,
        ).astype(BF16)
        for k in range(CHUNK):
            a = first + k
            for i in range(step_rows):
                z_ref[at, a * j_rows : (a + 1) * j_rows, i * LANES : (i + 1) * LANES] = part[
                    i * j_rows : (i + 1) * j_rows, k * LANES : (k + 1) * LANES
                ]


def inner_kernel(dims, first, after, scaled_ref, wp_ref, z_ref):
    step_rows = dims[5]
    for at in range(z_ref.shape[0]):
        rows = slice((first + at) * step_rows, (first + at + 1) * step_rows)
        inner_rows(dims, scaled_ref[rows], wp_ref, z_ref, at)


def at_step(refs, step):
    for ref in refs:
        if step < ref.shape[0]:
            return ref.at[step]
        step -= ref.shape[0]


def outer_kernel(dims, n_row, n_col, *refs):
    chans, groups, blocks, i_rows, j_rows, step_rows, sequences = dims
    tiles = sequences * chans // LANES
    after, ri_ref, keep_ref, scaled_ref, rbig, left_held, left_came = refs[:7]
    y_ref, diag_ref, keep_out, send_out = refs[7:11]
    flat, lsplit, expand, gwt, gwr = refs[11:]
    place((left_held, left_came), lax.axis_index("col"), n_col, flat)
    for t in range(tiles):
        lanes = slice(t * LANES, (t + 1) * LANES)
        masked = flat[0:i_rows, lanes] * ri_ref[...] * keep_ref[:, lanes]
        lsplit[pl.ds(t, i_rows, stride=tiles), :] = masked
    shape = (LANES, groups * LANES)
    source = lax.broadcasted_iota(jnp.int32, shape, 0)
    target = lax.broadcasted_iota(jnp.int32, shape, 1)
    same = (source // chans == target // LANES) & (source % chans == target % chans)
    expand[...] = same.astype(F32).astype(BF16)
    rows = step_rows * tiles
    deep_rows = 2 * step_rows if i_rows % (2 * step_rows) == 0 else step_rows
    group = lane_group((tiles, LANES), chans)

    for step in range(i_rows // step_rows):
        spread = jnp.dot(
            lsplit[step * rows : (step + 1) * rows, :].astype(BF16),
            expand[...],
            preferred_element_type=F32,
        ).astype(BF16)
        for b in range(groups):
            chosen = (group == b).astype(F32).astype(BF16)
            for lo in range(groups):
                at = b * sequences + lo * tiles
                for i in range(step_rows):
                    diag_ref[step, at : at + tiles, i * LANES : (i + 1) * LANES] = (
                        spread[i * tiles : (i + 1) * tiles, lo * LANES : (lo + 1) * LANES] * chosen
                    )
        for first in range(0, step_rows, CHUNK):
            part = jnp.dot(
                rbig[...],
                diag_ref[step, :, first * LANES : (first + CHUNK) * LANES],
                preferred_element_type=F32,
            ).astype(BF16)
            for k in range(CHUNK):
                for a in range(blocks):
                    y_ref[step * step_rows + first + k, :, a * LANES : (a + 1) * LANES] = part[
                        a * j_rows : (a + 1) * j_rows, k * LANES : (k + 1) * LANES
                    ]
        if (step + 1) * step_rows % deep_rows == 0:
            block = slice((step + 1) * step_rows - deep_rows, (step + 1) * step_rows)
            scaled_t = scaled_ref[block].reshape(deep_rows * j_rows, LANES).T
            y_flat = y_ref[block].reshape(deep_rows * j_rows, blocks * LANES)
            part = jnp.dot(scaled_t, y_flat, preferred_element_type=F32)
            gwt[...] = gwt[...] + part if block.start else part
    for k in range(blocks):
        turned_tile = gwt[:, k * LANES : (k + 1) * LANES].T
        for q in range(groups):
            gwr[pl.ds(k * groups + q, chans, stride=chans), :] = turned_tile[
                q * chans : (q + 1) * chans
            ]
    cut(gwr, lax.axis_index("row"), n_row, keep_out, send_out)


def right_sum(first, last, z_refs, diag_ref, acc, so_far=None):
    for step in range(first, last):
        part = lax.dot_general(
            diag_ref[step], at_step(z_refs, step)[...], NT, preferred_element_type=F32
        )
        acc[...] = part if so_far is None else so_far[...] + part
        so_far = acc


def right_first_kernel(steps, after, diag_ref, *refs):
    right_sum(0, steps, refs[:-1], diag_ref, refs[-1])


def right_kernel(dims, n_row, first, after, diag_ref, acc_first, *refs):
    chans, groups, blocks, i_rows, j_rows, step_rows, sequences = dims
    tiles = sequences * chans // LANES
    j_pad = -(-j_rows // LANES) * LANES
    z_refs, (keep_out, send_out, acc, turned, gr_all) = refs[:-5], refs[-5:]
    right_sum(first, i_rows // step_rows, z_refs, diag_ref, acc, acc_first)
    for a in range(blocks):
        at, shift = divmod(a * j_rows, LANES)
        mine = acc[:, at * LANES : at * LANES + j_pad]
        if shift:
            mine = pltpu.roll(mine, LANES - shift, axis=1)
        for b in range(groups):
            for lo in range(groups):
                first = b * sequences + lo * tiles
                turned[pl.ds(lo * chans + groups * a + b, tiles, stride=LANES), :] = mine[
                    first : first + tiles
                ]
    for t in range(tiles):
        lanes = slice(t * LANES, (t + 1) * LANES)
        gr_all[pl.ds(t, j_rows, stride=tiles), :] = turned[lanes, :].T[:j_rows]
    cut(gr_all, lax.axis_index("row"), n_row, keep_out, send_out)


def right_rows_kernel(dims, n_row, after, rj_ref, keep_ref, right_held, right_came, *refs):
    chans, groups, blocks, i_rows, j_rows, step_rows, sequences = dims
    tiles = sequences * chans // LANES
    j_pad = -(-j_rows // LANES) * LANES
    rbig, rbt_ref, flat, turned = refs
    place((right_held, right_came), lax.axis_index("row"), n_row, flat)
    for t in range(tiles):
        lanes = slice(t * LANES, (t + 1) * LANES)
        masked = flat[0:j_rows, lanes] * rj_ref[...] * keep_ref[:, lanes]
        if j_rows < j_pad:
            masked = jnp.concatenate([masked, jnp.zeros((j_pad - j_rows, LANES), F32)], axis=0)
        turned[lanes, :] = masked.T
    for a in range(blocks):
        parts = [
            turned[pl.ds(lo * chans + groups * a + b, tiles, stride=LANES), :]
            for b in range(groups)
            for lo in range(groups)
        ]
        block = jnp.concatenate(parts, axis=0)
        rbig[a * j_rows : (a + 1) * j_rows, :] = block.T[:j_rows].astype(BF16)
    rbt_ref[...] = rbig[...].T


def left_kernel(dims, n_col, after, rbt_ref, *refs):
    chans, groups, blocks, i_rows, j_rows, step_rows, sequences = dims
    tiles = sequences * chans // LANES
    z_refs, (keep_out, send_out, gl_all) = refs[:-3], refs[-3:]
    group = lane_group((sequences, LANES), chans)
    group_t = lane_group((tiles, LANES), chans)

    for step in range(i_rows // step_rows):
        z_ref = at_step(z_refs, step)
        for first in range(0, step_rows, CHUNK):
            part = jnp.dot(
                rbt_ref[...],
                z_ref[:, first * LANES : (first + CHUNK) * LANES],
                preferred_element_type=F32,
            )
            for k in range(CHUNK):
                mine = part[:, k * LANES : (k + 1) * LANES]
                total = mine[0:sequences]
                for b in range(1, groups):
                    total = jnp.where(group == b, mine[b * sequences : (b + 1) * sequences], total)
                shift = LANES // 2
                while shift >= chans:
                    total = total + pltpu.roll(total, shift, axis=1)
                    shift //= 2
                merged = total[0:tiles]
                for lo in range(1, groups):
                    merged = jnp.where(group_t == lo, total[lo * tiles : (lo + 1) * tiles], merged)
                at = (step * step_rows + first + k) * tiles
                gl_all[at : at + tiles, :] = merged
    cut(gl_all, lax.axis_index("col"), n_col, keep_out, send_out)


def total_of(keep_ref, came_ref, k=0):
    return keep_ref[k].astype(F32) + came_ref[k].astype(F32)


def join_kernel(after, held_ref, came_ref, out_ref):
    count = held_ref.shape[0]
    for k in range(count):
        out_ref[k] = held_ref[k]
        out_ref[count + k] = came_ref[k]


def fold_kernel(after, held_ref, came_ref, keep_out, send_out):
    for k in range(held_ref.shape[0]):
        into = send_out if k % 2 else keep_out
        into[k // 2] = total_of(held_ref, came_ref, k).astype(into.dtype)


def copy_kernel(after, *refs):
    count = len(refs) // 2
    for source, to in zip(refs[:count], refs[count:]):
        to[...] = source[...]


def turn_kernel(n_col, after, held_ref, came_ref, keep_out, send_out, whole):
    whole[...] = total_of(held_ref, came_ref)
    cut(whole, lax.axis_index("col"), n_col, keep_out, send_out)


def write_rows(whole, rows, keep_ref, out_ref, tiles):
    own = out_ref.shape[0]
    for t in range(tiles):
        lanes = slice(t * LANES, (t + 1) * LANES)
        out_ref[:, lanes] = whole[pl.ds(t, own, stride=tiles), :] * (
            rows * keep_ref[:, lanes]
        )


def pair_kernel(dims, *refs):
    after, ri_ref, y_ref, wp_ref, inv_ref, keep_ref, held, came = refs[:8]
    out_ref, gl_out, staged, whole, left, sems = refs[8:]
    i_rows, j_rows = dims[3:5]
    own = left.shape[0]
    first = pl.multiple_of(lax.axis_index("col") * own, 8)
    whole[...] = total_of(held, came)
    write_rows(whole, ri_ref[pl.ds(first, own), :], keep_ref, left, whole.shape[0] // own)
    copies = [pltpu.make_async_copy(left, gl_out, sems.at[0])]
    copies[0].start()
    for row in range(0, i_rows, PIECE):
        y_flat = y_ref[row : row + PIECE].reshape(PIECE * j_rows, y_ref.shape[2])
        projected = jnp.dot(y_flat, wp_ref[...], preferred_element_type=F32)
        for i in range(PIECE):
            inverse = jnp.where(ri_ref[row + i : row + i + 1, :] > 0, inv_ref[...], 1.0)
            staged[row + i] = (projected[i * j_rows : (i + 1) * j_rows] * inverse).astype(BF16)
        rows = pl.ds(row, PIECE)
        copies.append(
            pltpu.make_async_copy(staged.at[rows], out_ref.at[rows], sems.at[len(copies)])
        )
        copies[-1].start()
    for copy in copies:
        copy.wait()


def final_kernel(after, rj_ref, keep_ref, *refs):
    right, weight = refs[0:2], refs[2:4]
    gr_out, gw_out, whole, rows, weight_rows, sems = refs[4:]
    weight_rows[...] = total_of(*weight)
    copies = [pltpu.make_async_copy(weight_rows, gw_out, sems.at[0])]
    copies[0].start()
    own = rows.shape[0]
    first = pl.multiple_of(lax.axis_index("row") * own, 8)
    whole[...] = total_of(*right)
    write_rows(whole, rj_ref[pl.ds(first, own), :], keep_ref, rows, whole.shape[0] // own)
    copies.append(pltpu.make_async_copy(rows, gr_out, sems.at[1]))
    copies[1].start()
    for copy in copies:
        copy.wait()


def swap(array, axis, n, bit):
    return lax.ppermute(array, axis, [(s, s ^ bit) for s in range(n)])


def owners_of(n):
    held, bit = [0], n // 2
    while bit > 1:
        held, bit = held + [k ^ bit for k in held], bit // 2
    return held, [k ^ 1 for k in held]


def gather(block, own, axis, n, after):
    held, sent, bit = own, block[None], n // 2
    while bit > 1:
        came = swap(sent, axis, n, bit)
        shape = (2 * held.shape[0],) + held.shape[1:]
        held = small_call(join_kernel, [pltpu.VMEM(shape, BF16)], "join")(after, held, came)[0]
        sent, bit = held, bit // 2
    return held, swap(sent, axis, n, 1)


def reduce(keep, send, axis, n, after, between=None):
    bit = 1
    while True:
        came = swap(send, axis, n, bit)
        bit *= 2
        if bit >= n:
            if between is not None:
                between(keep)
            return keep, came
        half = (keep.shape[0] // 2,) + keep.shape[1:]
        outs = [pltpu.VMEM(half, F32), pltpu.VMEM(half, BF16)]
        keep, send = small_call(fold_kernel, outs, "fold")(after, keep, came)
        if between is not None:
            gate, between = between(keep), None
            keep, send = hold(gate, keep, send)


def small_call(body, outs, name, scratch=(), flops=1000):
    def call(after, *operands):
        return pl.pallas_call(
            body,
            in_specs=[hbm()] + vmem(len(operands)),
            out_specs=vmem(len(outs)),
            out_shape=outs,
            scratch_shapes=list(scratch),
            compiler_params=params(4),
            cost_estimate=cost(flops, 1000),
            name=name,
        )(after, *operands)

    return call


def hold(after, *arrays):
    outs = [pltpu.VMEM(array.shape, array.dtype) for array in arrays]
    return small_call(copy_kernel, outs, "hold", flops=10**10)(after, *arrays)


def halves(rows, n):
    return [pltpu.VMEM((n // 2, rows // n, LANES), BF16)] * 2


def vmem(count=1):
    return [pl.BlockSpec(memory_space=pltpu.VMEM)] * count


def hbm():
    return pl.BlockSpec(memory_space=pl.ANY)


def in_hbm(array):
    return pltpu.with_memory_space_constraint(array, pltpu.HBM)


def shards(left_act, right_act, row_mask, res_mask, out_weight, cotangent):
    n_col = lax.axis_size("col")
    n_row = lax.axis_size("row")
    i_rows, j_rows, pair_width = cotangent.shape
    sequences = row_mask.shape[0]
    width = left_act.shape[1]
    chans = width // sequences
    groups = LANES // chans
    blocks = chans // groups
    tiles = width // LANES
    depth = groups * sequences
    inner = chans * chans
    step_rows = 16
    steps = i_rows // step_rows
    early_steps = steps // 2
    dims = (chans, groups, blocks, i_rows, j_rows, step_rows, sequences)
    j_pad = -(-j_rows // LANES) * LANES
    span = blocks * j_rows
    own_left, own_right = left_act.shape[0], right_act.shape[0]
    macs = i_rows * j_rows * inner * pair_width

    mask_row = (res_mask.reshape(1, -1), row_mask.reshape(1, -1))
    scaled, inverse, weight, keep, i_keep, j_keep, own_l, own_r, z_first = pl.pallas_call(
        functools.partial(scale_kernel, dims),
        in_specs=[hbm()] * 6,
        out_specs=vmem(9),
        out_shape=[
            pltpu.VMEM(cotangent.shape, BF16),
            pltpu.VMEM((j_rows, LANES), F32),
            pltpu.VMEM(out_weight.shape, BF16),
            pltpu.VMEM((1, width), F32),
            pltpu.VMEM((i_rows, LANES), F32),
            pltpu.VMEM((j_rows, LANES), F32),
            pltpu.VMEM((1,) + left_act.shape, BF16),
            pltpu.VMEM((1,) + right_act.shape, BF16),
            pltpu.VMEM((early_steps, span, step_rows * LANES), BF16),
        ],
        scratch_shapes=[
            pltpu.VMEM((1, res_mask.shape[0]), jnp.int32),
            pltpu.VMEM((1, sequences), jnp.int32),
            pltpu.VMEM(out_weight.shape, BF16),
            pltpu.VMEM(out_weight.shape, F32),
            pltpu.VMEM(cotangent.shape, BF16),
            pltpu.SemaphoreType.DMA((i_rows // PIECE,)),
            pltpu.SemaphoreType.DMA((5,)),
        ],
        compiler_params=params(16),
        cost_estimate=cost(1000, 1000),
        name="scale",
    )(*map(in_hbm, (*mask_row, cotangent, out_weight, left_act, right_act)))

    lefts = gather(left_act, own_l, "col", n_col, own_l)
    rights = gather(right_act, own_r, "row", n_row, lefts[0])

    z_last = pl.pallas_call(
        functools.partial(inner_kernel, dims, early_steps),
        in_specs=[hbm()] + vmem(2),
        out_specs=vmem()[0],
        out_shape=pltpu.VMEM((steps - early_steps, span, step_rows * LANES), BF16),
        compiler_params=params(16),
        cost_estimate=cost(16 * macs, 2**20),
        name="inner",
    )(rights[0], scaled, weight)
    z = (z_first, z_last)

    rbig, right_turned = pl.pallas_call(
        functools.partial(right_rows_kernel, dims, n_row),
        in_specs=[hbm()] + vmem(4),
        out_specs=vmem(2),
        out_shape=[pltpu.VMEM((span, depth), BF16), pltpu.VMEM((depth, span), BF16)],
        scratch_shapes=[pltpu.VMEM((j_rows, width), F32), pltpu.VMEM((width, j_pad), F32)],
        compiler_params=params(12),
        cost_estimate=cost(16 * macs, 2**20),
        name="right_rows",
    )(z_last, j_keep, keep, *rights)

    gl_cut = pl.pallas_call(
        functools.partial(left_kernel, dims, n_col),
        in_specs=[hbm()] + vmem(1 + len(z)),
        out_specs=vmem(2),
        out_shape=halves(i_rows * tiles, n_col),
        scratch_shapes=[pltpu.VMEM((i_rows * tiles, LANES), F32)],
        compiler_params=params(16),
        cost_estimate=cost(16 * macs, 2**20),
        name="left",
    )(rbig, right_turned, *z)
    y, diag, *gw_cut = pl.pallas_call(
        functools.partial(outer_kernel, dims, n_row, n_col),
        in_specs=[hbm()] + vmem(6),
        out_specs=vmem(4),
        out_shape=[
            pltpu.VMEM((i_rows, j_rows, inner), BF16),
            pltpu.VMEM((steps, depth, step_rows * LANES), BF16),
        ]
        + halves(inner, n_row),
        scratch_shapes=[
            pltpu.VMEM((i_rows, width), F32),
            pltpu.VMEM((i_rows * tiles, LANES), F32),
            pltpu.VMEM((LANES, groups * LANES), BF16),
            pltpu.VMEM((pair_width, inner), F32),
            pltpu.VMEM((inner, pair_width), F32),
        ],
        compiler_params=params(16),
        cost_estimate=cost(16 * macs, 2**20),
        name="outer",
    )(gl_cut[0], i_keep, keep, scaled, rbig, *lefts)

    gw_row = []

    def weight_rounds(after):
        gw_row.extend(reduce(*gw_cut, "row", n_row, after))
        return gw_row[0]

    gl_last = reduce(*gl_cut, "col", n_col, gw_cut[0], weight_rounds)

    right_steps = steps // 2
    acc = pl.pallas_call(
        functools.partial(right_first_kernel, right_steps),
        in_specs=[hbm()] + vmem(1 + len(z)),
        out_specs=vmem()[0],
        out_shape=pltpu.VMEM((depth, span), F32),
        compiler_params=params(16),
        cost_estimate=cost(1000, 1000),
        name="right_first",
    )(gl_last[0], diag, *z)
    gw_turned = small_call(
        functools.partial(turn_kernel, n_col),
        halves(inner // n_row, n_col),
        "turn",
        [pltpu.VMEM((inner // n_row, pair_width), F32)],
    )(acc, *gw_row)

    gr_cut = pl.pallas_call(
        functools.partial(right_kernel, dims, n_row, right_steps),
        in_specs=[hbm()] + vmem(2 + len(z)),
        out_specs=vmem(2),
        out_shape=halves(j_rows * tiles, n_row),
        scratch_shapes=[
            pltpu.VMEM((depth, span), F32),
            pltpu.VMEM((width, j_pad), F32),
            pltpu.VMEM((j_rows * tiles, LANES), F32),
        ],
        compiler_params=params(20),
        cost_estimate=cost(16 * macs, 2**20),
        name="right",
    )(gw_turned[0], diag, acc, *z)
    gr_held = []

    def right_rounds(after):
        gr_held.extend(hold(after, *gr_cut))
        return gr_held[0]

    gw_last = reduce(*gw_turned, "col", n_col, gr_cut[0], right_rounds)
    gr_last = reduce(*gr_held, "row", n_row, gw_last[0])

    pair_out, grad_left = pl.pallas_call(
        functools.partial(pair_kernel, dims),
        in_specs=[hbm()] + vmem(7),
        out_specs=[hbm()] * 2,
        out_shape=[
            jax.ShapeDtypeStruct(cotangent.shape, BF16),
            jax.ShapeDtypeStruct((own_left, width), F32),
        ],
        scratch_shapes=[
            pltpu.VMEM(cotangent.shape, BF16),
            pltpu.VMEM((own_left * tiles, LANES), F32),
            pltpu.VMEM((own_left, width), F32),
            pltpu.SemaphoreType.DMA((1 + i_rows // PIECE,)),
        ],
        compiler_params=params(12),
        cost_estimate=cost(16 * macs, 2**20),
        name="pair",
    )(gr_last[0], i_keep, y, weight, inverse, keep, *gl_last)

    owned = (inner // n_row // n_col, pair_width)
    grad_right, grad_weight = pl.pallas_call(
        final_kernel,
        in_specs=[hbm()] + vmem(6),
        out_specs=[hbm()] * 2,
        out_shape=[
            jax.ShapeDtypeStruct((own_right, width), F32),
            jax.ShapeDtypeStruct(owned, F32),
        ],
        scratch_shapes=[
            pltpu.VMEM((own_right * tiles, LANES), F32),
            pltpu.VMEM((own_right, width), F32),
            pltpu.VMEM(owned, F32),
            pltpu.SemaphoreType.DMA((2,)),
        ],
        compiler_params=params(4),
        cost_estimate=cost(1000, 1000),
        name="final_sums",
    )(in_hbm(pair_out), j_keep, keep, *gr_last, *gw_last)
    return (pair_out, grad_left, grad_right, grad_weight)


def solution(mesh):
    placed = (
        P(("grp", "row", "col"), None),
        P(("grp", "col", "row"), None),
        P("grp"),
        P("grp"),
        P(),
        P(("grp", "row"), "col", None),
    )
    return jax.shard_map(
        shards,
        mesh=mesh,
        in_specs=placed,
        out_specs=(
            P(("grp", "row"), "col", None),
            P(("grp", "row", "col"), None),
            P(("grp", "col", "row"), None),
            P(("grp", "row", "col"), None),
        ),
        check_vma=False,
    )
```

```python
import functools

import jax
import jax.numpy as jnp
from jax import lax
from jax.experimental import pallas as pl
from jax.experimental.pallas import tpu as pltpu
from jax.sharding import PartitionSpec as P

LANES = 128
CHUNK = 4
PIECE = 8
NT = (((1,), (1,)), ((), ()))
F32 = jnp.float32
BF16 = jnp.bfloat16


def params(mib):
    return pltpu.CompilerParams(vmem_limit_bytes=mib * 2**20)


def cost(flops, nbytes):
    return pl.CostEstimate(flops=int(flops), bytes_accessed=int(nbytes), transcendentals=0)


def cut(source, index, n, keep_ref, send_ref):
    rows = source.shape[0] // n
    for k in range(n):
        at = pl.multiple_of((index ^ k) * rows, rows)
        into = send_ref if k % 2 else keep_ref
        into[k // 2] = source[pl.ds(at, rows), :].astype(into.dtype)


def place(buffers, index, n, flat):
    for buffer, owners in zip(buffers, owners_of(n)):
        rows = buffer.shape[1]
        for k, owner in enumerate(owners):
            at = pl.multiple_of((index ^ owner) * rows, 8)
            flat[pl.ds(at, rows), :] = buffer[k].astype(F32)


def lane_group(shape, chans):
    return lax.broadcasted_iota(jnp.int32, shape, 1) // chans


def mask_rows(res_ref, first, count):
    shape = (count, res_ref.shape[1])
    row = lax.broadcasted_iota(jnp.int32, shape, 0) + first
    here = lax.broadcasted_iota(jnp.int32, shape, 1) == row
    chosen = jnp.where(here, res_ref[...].astype(F32), 0.0)
    return jnp.broadcast_to(jnp.sum(chosen, axis=1, keepdims=True), (count, LANES))


def scale_kernel(dims, *refs):
    chans, groups, blocks, i_rows, j_rows, step_rows, sequences = dims
    tiles = sequences * chans // LANES
    res_hbm, seq_hbm, cot_ref, w_hbm, left_hbm, right_hbm = refs[:6]
    scaled_ref, inv_ref, wp_ref, keep_ref, ri_ref, rj_ref, left_ref, right_ref, z_ref = refs[6:15]
    res_ref, seq_ref, w_ref, w32, cot, sems, more_sems = refs[15:]
    steps = i_rows // step_rows

    def fetch(piece):
        rows = pl.ds(piece * step_rows, step_rows)
        return pltpu.make_async_copy(cot_ref.at[rows], cot.at[rows], sems.at[piece])

    pairs = [
        (res_hbm, res_ref),
        (seq_hbm, seq_ref),
        (w_hbm, w_ref),
        (left_hbm, left_ref.at[0]),
        (right_hbm, right_ref.at[0]),
    ]
    more = [
        pltpu.make_async_copy(source, to, more_sems.at[k]) for k, (source, to) in enumerate(pairs)
    ]
    for copy in more[:3]:
        copy.start()
    for piece in range(i_rows // step_rows):
        fetch(piece).start()
    for copy in more[3:]:
        copy.start()
    shape = (sequences, tiles * LANES)
    own = lax.broadcasted_iota(jnp.int32, shape, 1) // chans
    repeat = (own == lax.broadcasted_iota(jnp.int32, shape, 0)).astype(F32).astype(BF16)
    more[0].wait()
    ri_ref[...] = mask_rows(res_ref, lax.axis_index("row") * i_rows, i_rows)
    rj_ref[...] = mask_rows(res_ref, lax.axis_index("col") * j_rows, j_rows)
    more[1].wait()
    seq = seq_ref[...].astype(F32)
    keep_ref[...] = jnp.dot(
        jnp.broadcast_to(seq, (8, sequences)).astype(BF16), repeat, preferred_element_type=F32
    )[0:1]
    valid = jnp.sum(seq, axis=1, keepdims=True)
    inv_ref[...] = 1.0 / jnp.maximum(valid * rj_ref[...], 1.0)
    more[2].wait()
    w32[...] = w_ref[...].astype(F32)
    for e in range(chans):
        wp_ref[e * chans : (e + 1) * chans, :] = w32[pl.ds(e, chans, stride=chans), :].astype(BF16)
    for piece in range(i_rows // step_rows):
        fetch(piece).wait()
    for step in range(steps):
        for at in range(step * step_rows, (step + 1) * step_rows):
            inverse = jnp.where(ri_ref[at : at + 1, :] > 0, inv_ref[...], 1.0)
            scaled_ref[at] = (cot[at].astype(F32) * inverse).astype(BF16)
        if step < z_ref.shape[0]:
            rows = slice(step * step_rows, (step + 1) * step_rows)
            inner_rows(dims, scaled_ref[rows], wp_ref, z_ref, step)
    more[3].wait()
    more[4].wait()


def inner_rows(dims, scaled, wp_ref, z_ref, at):
    chans, groups, blocks, i_rows, j_rows, step_rows, sequences = dims
    for first in range(0, blocks, CHUNK):
        part = lax.dot_general(
            scaled.reshape(step_rows * j_rows, LANES),
            wp_ref[first * LANES : (first + CHUNK) * LANES, :],
            NT,
            preferred_element_type=F32,
        ).astype(BF16)
        for k in range(CHUNK):
            a = first + k
            for i in range(step_rows):
                z_ref[at, a * j_rows : (a + 1) * j_rows, i * LANES : (i + 1) * LANES] = part[
                    i * j_rows : (i + 1) * j_rows, k * LANES : (k + 1) * LANES
                ]


def inner_kernel(dims, first, after, scaled_ref, wp_ref, z_ref):
    step_rows = dims[5]
    for at in range(z_ref.shape[0]):
        rows = slice((first + at) * step_rows, (first + at + 1) * step_rows)
        inner_rows(dims, scaled_ref[rows], wp_ref, z_ref, at)


def at_step(refs, step):
    for ref in refs:
        if step < ref.shape[0]:
            return ref.at[step]
        step -= ref.shape[0]


def outer_kernel(dims, n_row, n_col, *refs):
    chans, groups, blocks, i_rows, j_rows, step_rows, sequences = dims
    tiles = sequences * chans // LANES
    after, ri_ref, keep_ref, scaled_ref, rbig, left_held, left_came = refs[:7]
    y_ref, diag_ref, keep_out, send_out = refs[7:11]
    flat, lsplit, expand, gwt, gwr = refs[11:]
    place((left_held, left_came), lax.axis_index("col"), n_col, flat)
    for t in range(tiles):
        lanes = slice(t * LANES, (t + 1) * LANES)
        masked = flat[0:i_rows, lanes] * ri_ref[...] * keep_ref[:, lanes]
        lsplit[pl.ds(t, i_rows, stride=tiles), :] = masked
    shape = (LANES, groups * LANES)
    source = lax.broadcasted_iota(jnp.int32, shape, 0)
    target = lax.broadcasted_iota(jnp.int32, shape, 1)
    same = (source // chans == target // LANES) & (source % chans == target % chans)
    expand[...] = same.astype(F32).astype(BF16)
    group = lane_group((tiles, LANES), chans)
    masks = [(group == b).astype(F32).astype(BF16) for b in range(groups)]
    deep_rows = 2 * step_rows if i_rows % (2 * step_rows) == 0 else step_rows

    for step in range(i_rows // step_rows):
        if step * step_rows % deep_rows == 0:
            rows = slice(step * step_rows * tiles, (step * step_rows + deep_rows) * tiles)
            spread = jnp.dot(
                lsplit[rows, :].astype(BF16), expand[...], preferred_element_type=F32
            ).astype(BF16)
            for i in range(deep_rows):
                block, at = divmod(step * step_rows + i, step_rows)
                for b in range(groups):
                    for lo in range(groups):
                        first = b * sequences + lo * tiles
                        diag_ref[
                            block, first : first + tiles, at * LANES : (at + 1) * LANES
                        ] = (
                            spread[i * tiles : (i + 1) * tiles, lo * LANES : (lo + 1) * LANES]
                            * masks[b]
                        )
        for first in range(0, step_rows, CHUNK):
            part = jnp.dot(
                rbig[...],
                diag_ref[step, :, first * LANES : (first + CHUNK) * LANES],
                preferred_element_type=F32,
            ).astype(BF16)
            for k in range(CHUNK):
                for a in range(blocks):
                    y_ref[step * step_rows + first + k, :, a * LANES : (a + 1) * LANES] = part[
                        a * j_rows : (a + 1) * j_rows, k * LANES : (k + 1) * LANES
                    ]
        if (step + 1) * step_rows % deep_rows == 0:
            block = slice((step + 1) * step_rows - deep_rows, (step + 1) * step_rows)
            scaled_t = scaled_ref[block].reshape(deep_rows * j_rows, LANES).T
            y_flat = y_ref[block].reshape(deep_rows * j_rows, blocks * LANES)
            part = jnp.dot(scaled_t, y_flat, preferred_element_type=F32)
            gwt[...] = gwt[...] + part if block.start else part
    for k in range(blocks):
        turned_tile = gwt[:, k * LANES : (k + 1) * LANES].T
        for q in range(groups):
            gwr[pl.ds(k * groups + q, chans, stride=chans), :] = turned_tile[
                q * chans : (q + 1) * chans
            ]
    cut(gwr, lax.axis_index("row"), n_row, keep_out, send_out)


def right_sum(first, last, z_refs, diag_ref, acc, so_far=None):
    for step in range(first, last):
        part = lax.dot_general(
            diag_ref[step], at_step(z_refs, step)[...], NT, preferred_element_type=F32
        )
        acc[...] = part if so_far is None else so_far[...] + part
        so_far = acc


def right_part_kernel(first, last, parts, after, diag_ref, *refs):
    right_sum(first, last, refs[:parts], diag_ref, refs[-1], *refs[parts:-1])


def right_kernel(dims, n_row, first, after, diag_ref, acc_first, *refs):
    chans, groups, blocks, i_rows, j_rows, step_rows, sequences = dims
    tiles = sequences * chans // LANES
    j_pad = -(-j_rows // LANES) * LANES
    z_refs, (keep_out, send_out, acc, turned, gr_all) = refs[:-5], refs[-5:]
    right_sum(first, i_rows // step_rows, z_refs, diag_ref, acc, acc_first)
    for a in range(blocks):
        at, shift = divmod(a * j_rows, LANES)
        mine = acc[:, at * LANES : at * LANES + j_pad]
        if shift:
            mine = pltpu.roll(mine, LANES - shift, axis=1)
        for b in range(groups):
            for lo in range(groups):
                first = b * sequences + lo * tiles
                turned[pl.ds(lo * chans + groups * a + b, tiles, stride=LANES), :] = mine[
                    first : first + tiles
                ]
    for t in range(tiles):
        lanes = slice(t * LANES, (t + 1) * LANES)
        gr_all[pl.ds(t, j_rows, stride=tiles), :] = turned[lanes, :].T[:j_rows]
    cut(gr_all, lax.axis_index("row"), n_row, keep_out, send_out)


def right_rows_kernel(dims, n_row, after, rj_ref, keep_ref, right_held, right_came, *refs):
    chans, groups, blocks, i_rows, j_rows, step_rows, sequences = dims
    tiles = sequences * chans // LANES
    j_pad = -(-j_rows // LANES) * LANES
    rbig, rbt_ref, flat, turned = refs
    place((right_held, right_came), lax.axis_index("row"), n_row, flat)
    for t in range(tiles):
        lanes = slice(t * LANES, (t + 1) * LANES)
        masked = flat[0:j_rows, lanes] * rj_ref[...] * keep_ref[:, lanes]
        if j_rows < j_pad:
            masked = jnp.concatenate([masked, jnp.zeros((j_pad - j_rows, LANES), F32)], axis=0)
        turned[lanes, :] = masked.T
    for a in range(blocks):
        parts = [
            turned[pl.ds(lo * chans + groups * a + b, tiles, stride=LANES), :]
            for b in range(groups)
            for lo in range(groups)
        ]
        block = jnp.concatenate(parts, axis=0)
        rbig[a * j_rows : (a + 1) * j_rows, :] = block.T[:j_rows].astype(BF16)
    rbt_ref[...] = rbig[...].T


def left_kernel(dims, n_col, after, rbt_ref, *refs):
    chans, groups, blocks, i_rows, j_rows, step_rows, sequences = dims
    tiles = sequences * chans // LANES
    z_refs, (keep_out, send_out, gl_all) = refs[:-3], refs[-3:]
    group = lane_group((sequences, LANES), chans)
    group_t = lane_group((tiles, LANES), chans)

    for step in range(i_rows // step_rows):
        z_ref = at_step(z_refs, step)
        for first in range(0, step_rows, CHUNK):
            part = jnp.dot(
                rbt_ref[...],
                z_ref[:, first * LANES : (first + CHUNK) * LANES],
                preferred_element_type=F32,
            )
            for k in range(CHUNK):
                mine = part[:, k * LANES : (k + 1) * LANES]
                total = mine[0:sequences]
                for b in range(1, groups):
                    total = jnp.where(group == b, mine[b * sequences : (b + 1) * sequences], total)
                shift = LANES // 2
                while shift >= chans:
                    total = total + pltpu.roll(total, shift, axis=1)
                    shift //= 2
                merged = total[0:tiles]
                for lo in range(1, groups):
                    merged = jnp.where(group_t == lo, total[lo * tiles : (lo + 1) * tiles], merged)
                at = (step * step_rows + first + k) * tiles
                gl_all[at : at + tiles, :] = merged
    cut(gl_all, lax.axis_index("col"), n_col, keep_out, send_out)


def total_of(keep_ref, came_ref, k=0):
    return keep_ref[k].astype(F32) + came_ref[k].astype(F32)


def join_kernel(after, held_ref, came_ref, out_ref):
    count = held_ref.shape[0]
    for k in range(count):
        out_ref[k] = held_ref[k]
        out_ref[count + k] = came_ref[k]


def fold_kernel(after, held_ref, came_ref, keep_out, send_out):
    for k in range(held_ref.shape[0]):
        into = send_out if k % 2 else keep_out
        into[k // 2] = total_of(held_ref, came_ref, k).astype(into.dtype)


def copy_kernel(after, *refs):
    count = len(refs) // 2
    for source, to in zip(refs[:count], refs[count:]):
        to[...] = source[...]


def turn_kernel(n_col, after, held_ref, came_ref, keep_out, send_out, whole):
    whole[...] = total_of(held_ref, came_ref)
    cut(whole, lax.axis_index("col"), n_col, keep_out, send_out)


def write_rows(whole, rows, keep_ref, out_ref, tiles):
    own = out_ref.shape[0]
    for t in range(tiles):
        lanes = slice(t * LANES, (t + 1) * LANES)
        out_ref[:, lanes] = whole[pl.ds(t, own, stride=tiles), :] * (
            rows * keep_ref[:, lanes]
        )


def pair_kernel(dims, *refs):
    after, ri_ref, y_ref, wp_ref, inv_ref, keep_ref, held, came = refs[:8]
    out_ref, gl_out, staged, whole, left, sems = refs[8:]
    i_rows, j_rows = dims[3:5]
    own = left.shape[0]
    first = pl.multiple_of(lax.axis_index("col") * own, 8)
    whole[...] = total_of(held, came)
    write_rows(whole, ri_ref[pl.ds(first, own), :], keep_ref, left, whole.shape[0] // own)
    copies = [pltpu.make_async_copy(left, gl_out, sems.at[0])]
    copies[0].start()
    for row in range(0, i_rows, PIECE):
        y_flat = y_ref[row : row + PIECE].reshape(PIECE * j_rows, y_ref.shape[2])
        projected = jnp.dot(y_flat, wp_ref[...], preferred_element_type=F32)
        for i in range(PIECE):
            inverse = jnp.where(ri_ref[row + i : row + i + 1, :] > 0, inv_ref[...], 1.0)
            staged[row + i] = (projected[i * j_rows : (i + 1) * j_rows] * inverse).astype(BF16)
        rows = pl.ds(row, PIECE)
        copies.append(
            pltpu.make_async_copy(staged.at[rows], out_ref.at[rows], sems.at[len(copies)])
        )
        copies[-1].start()
    for copy in copies:
        copy.wait()


def final_kernel(after, rj_ref, keep_ref, *refs):
    right, weight = refs[0:2], refs[2:4]
    gr_out, gw_out, whole, rows, weight_rows, sems = refs[4:]
    weight_rows[...] = total_of(*weight)
    copies = [pltpu.make_async_copy(weight_rows, gw_out, sems.at[0])]
    copies[0].start()
    own = rows.shape[0]
    first = pl.multiple_of(lax.axis_index("row") * own, 8)
    whole[...] = total_of(*right)
    write_rows(whole, rj_ref[pl.ds(first, own), :], keep_ref, rows, whole.shape[0] // own)
    copies.append(pltpu.make_async_copy(rows, gr_out, sems.at[1]))
    copies[1].start()
    for copy in copies:
        copy.wait()


def swap(array, axis, n, bit):
    return lax.ppermute(array, axis, [(s, s ^ bit) for s in range(n)])


def owners_of(n):
    held, bit = [0], n // 2
    while bit > 1:
        held, bit = held + [k ^ bit for k in held], bit // 2
    return held, [k ^ 1 for k in held]


def gather(block, own, axis, n, after):
    held, sent, bit = own, block[None], n // 2
    while bit > 1:
        came = swap(sent, axis, n, bit)
        shape = (2 * held.shape[0],) + held.shape[1:]
        held = small_call(join_kernel, [pltpu.VMEM(shape, BF16)], "join")(after, held, came)[0]
        sent, bit = held, bit // 2
    return held, swap(sent, axis, n, 1)


def reduce(keep, send, axis, n, after, between=None):
    bit = 1
    while True:
        came = swap(send, axis, n, bit)
        bit *= 2
        if bit >= n:
            if between is not None:
                between(keep)
            return keep, came
        half = (keep.shape[0] // 2,) + keep.shape[1:]
        outs = [pltpu.VMEM(half, F32), pltpu.VMEM(half, BF16)]
        keep, send = small_call(fold_kernel, outs, "fold")(after, keep, came)
        if between is not None:
            gate, between = between(keep), None
            keep, send = hold(gate, keep, send)


def small_call(body, outs, name, scratch=(), flops=1000):
    def call(after, *operands):
        return pl.pallas_call(
            body,
            in_specs=[hbm()] + vmem(len(operands)),
            out_specs=vmem(len(outs)),
            out_shape=outs,
            scratch_shapes=list(scratch),
            compiler_params=params(4),
            cost_estimate=cost(flops, 1000),
            name=name,
        )(after, *operands)

    return call


def hold(after, *arrays):
    outs = [pltpu.VMEM(array.shape, array.dtype) for array in arrays]
    return small_call(copy_kernel, outs, "hold", flops=10**10)(after, *arrays)


def halves(rows, n):
    return [pltpu.VMEM((n // 2, rows // n, LANES), BF16)] * 2


def vmem(count=1):
    return [pl.BlockSpec(memory_space=pltpu.VMEM)] * count


def hbm():
    return pl.BlockSpec(memory_space=pl.ANY)


def in_hbm(array):
    return pltpu.with_memory_space_constraint(array, pltpu.HBM)


def shards(left_act, right_act, row_mask, res_mask, out_weight, cotangent):
    n_col = lax.axis_size("col")
    n_row = lax.axis_size("row")
    i_rows, j_rows, pair_width = cotangent.shape
    sequences = row_mask.shape[0]
    width = left_act.shape[1]
    chans = width // sequences
    groups = LANES // chans
    blocks = chans // groups
    tiles = width // LANES
    depth = groups * sequences
    inner = chans * chans
    step_rows = 16
    steps = i_rows // step_rows
    early_steps = steps // 2
    dims = (chans, groups, blocks, i_rows, j_rows, step_rows, sequences)
    j_pad = -(-j_rows // LANES) * LANES
    span = blocks * j_rows
    own_left, own_right = left_act.shape[0], right_act.shape[0]
    macs = i_rows * j_rows * inner * pair_width

    mask_row = (res_mask.reshape(1, -1), row_mask.reshape(1, -1))
    scaled, inverse, weight, keep, i_keep, j_keep, own_l, own_r, z_first = pl.pallas_call(
        functools.partial(scale_kernel, dims),
        in_specs=[hbm()] * 6,
        out_specs=vmem(9),
        out_shape=[
            pltpu.VMEM(cotangent.shape, BF16),
            pltpu.VMEM((j_rows, LANES), F32),
            pltpu.VMEM(out_weight.shape, BF16),
            pltpu.VMEM((1, width), F32),
            pltpu.VMEM((i_rows, LANES), F32),
            pltpu.VMEM((j_rows, LANES), F32),
            pltpu.VMEM((1,) + left_act.shape, BF16),
            pltpu.VMEM((1,) + right_act.shape, BF16),
            pltpu.VMEM((early_steps, span, step_rows * LANES), BF16),
        ],
        scratch_shapes=[
            pltpu.VMEM((1, res_mask.shape[0]), jnp.int32),
            pltpu.VMEM((1, sequences), jnp.int32),
            pltpu.VMEM(out_weight.shape, BF16),
            pltpu.VMEM(out_weight.shape, F32),
            pltpu.VMEM(cotangent.shape, BF16),
            pltpu.SemaphoreType.DMA((steps,)),
            pltpu.SemaphoreType.DMA((5,)),
        ],
        compiler_params=params(16),
        cost_estimate=cost(1000, 1000),
        name="scale",
    )(*map(in_hbm, (*mask_row, cotangent, out_weight, left_act, right_act)))

    lefts = gather(left_act, own_l, "col", n_col, own_l)
    rights = gather(right_act, own_r, "row", n_row, lefts[0])

    z_last = pl.pallas_call(
        functools.partial(inner_kernel, dims, early_steps),
        in_specs=[hbm()] + vmem(2),
        out_specs=vmem()[0],
        out_shape=pltpu.VMEM((steps - early_steps, span, step_rows * LANES), BF16),
        compiler_params=params(16),
        cost_estimate=cost(16 * macs, 2**20),
        name="inner",
    )(rights[0], scaled, weight)
    z = (z_first, z_last)

    rbig, right_turned = pl.pallas_call(
        functools.partial(right_rows_kernel, dims, n_row),
        in_specs=[hbm()] + vmem(4),
        out_specs=vmem(2),
        out_shape=[pltpu.VMEM((span, depth), BF16), pltpu.VMEM((depth, span), BF16)],
        scratch_shapes=[pltpu.VMEM((j_rows, width), F32), pltpu.VMEM((width, j_pad), F32)],
        compiler_params=params(12),
        cost_estimate=cost(16 * macs, 2**20),
        name="right_rows",
    )(z_last, j_keep, keep, *rights)

    gl_cut = pl.pallas_call(
        functools.partial(left_kernel, dims, n_col),
        in_specs=[hbm()] + vmem(1 + len(z)),
        out_specs=vmem(2),
        out_shape=halves(i_rows * tiles, n_col),
        scratch_shapes=[pltpu.VMEM((i_rows * tiles, LANES), F32)],
        compiler_params=params(16),
        cost_estimate=cost(16 * macs, 2**20),
        name="left",
    )(rbig, right_turned, *z)
    y, diag, *gw_cut = pl.pallas_call(
        functools.partial(outer_kernel, dims, n_row, n_col),
        in_specs=[hbm()] + vmem(6),
        out_specs=vmem(4),
        out_shape=[
            pltpu.VMEM((i_rows, j_rows, inner), BF16),
            pltpu.VMEM((steps, depth, step_rows * LANES), BF16),
        ]
        + halves(inner, n_row),
        scratch_shapes=[
            pltpu.VMEM((i_rows, width), F32),
            pltpu.VMEM((i_rows * tiles, LANES), F32),
            pltpu.VMEM((LANES, groups * LANES), BF16),
            pltpu.VMEM((pair_width, inner), F32),
            pltpu.VMEM((inner, pair_width), F32),
        ],
        compiler_params=params(16),
        cost_estimate=cost(16 * macs, 2**20),
        name="outer",
    )(gl_cut[0], i_keep, keep, scaled, rbig, *lefts)

    def right_part(first, last, after, *so_far):
        return pl.pallas_call(
            functools.partial(right_part_kernel, first, last, len(z)),
            in_specs=[hbm()] + vmem(1 + len(z) + len(so_far)),
            out_specs=vmem()[0],
            out_shape=pltpu.VMEM((depth, span), F32),
            compiler_params=params(16),
            cost_estimate=cost(1000, 1000),
            name="right_part",
        )(after, diag, *z, *so_far)

    gw_row, acc = [], []
    right_steps = max(1, steps // 4)

    def weight_rounds(after):
        acc.append(right_part(0, right_steps, after))
        gw_row.extend(reduce(*gw_cut, "row", n_row, acc[0]))
        return gw_row[0]

    gl_last = reduce(*gl_cut, "col", n_col, gw_cut[0], weight_rounds)
    acc = right_part(right_steps, 2 * right_steps, gl_last[0], acc[0])
    gw_turned = small_call(
        functools.partial(turn_kernel, n_col),
        halves(inner // n_row, n_col),
        "turn",
        [pltpu.VMEM((inner // n_row, pair_width), F32)],
    )(acc, *gw_row)

    gr_cut = pl.pallas_call(
        functools.partial(right_kernel, dims, n_row, 2 * right_steps),
        in_specs=[hbm()] + vmem(2 + len(z)),
        out_specs=vmem(2),
        out_shape=halves(j_rows * tiles, n_row),
        scratch_shapes=[
            pltpu.VMEM((depth, span), F32),
            pltpu.VMEM((width, j_pad), F32),
            pltpu.VMEM((j_rows * tiles, LANES), F32),
        ],
        compiler_params=params(20),
        cost_estimate=cost(16 * macs, 2**20),
        name="right",
    )(gw_turned[0], diag, acc, *z)
    gr_held = []

    def right_rounds(after):
        gr_held.extend(hold(after, *gr_cut))
        return gr_held[0]

    gw_last = reduce(*gw_turned, "col", n_col, gr_cut[0], right_rounds)
    gr_last = reduce(*gr_held, "row", n_row, gw_last[0])

    pair_out, grad_left = pl.pallas_call(
        functools.partial(pair_kernel, dims),
        in_specs=[hbm()] + vmem(7),
        out_specs=[hbm()] * 2,
        out_shape=[
            jax.ShapeDtypeStruct(cotangent.shape, BF16),
            jax.ShapeDtypeStruct((own_left, width), F32),
        ],
        scratch_shapes=[
            pltpu.VMEM(cotangent.shape, BF16),
            pltpu.VMEM((own_left * tiles, LANES), F32),
            pltpu.VMEM((own_left, width), F32),
            pltpu.SemaphoreType.DMA((1 + i_rows // PIECE,)),
        ],
        compiler_params=params(12),
        cost_estimate=cost(16 * macs, 2**20),
        name="pair",
    )(gr_last[0], i_keep, y, weight, inverse, keep, *gl_last)

    owned = (inner // n_row // n_col, pair_width)
    grad_right, grad_weight = pl.pallas_call(
        final_kernel,
        in_specs=[hbm()] + vmem(6),
        out_specs=[hbm()] * 2,
        out_shape=[
            jax.ShapeDtypeStruct((own_right, width), F32),
            jax.ShapeDtypeStruct(owned, F32),
        ],
        scratch_shapes=[
            pltpu.VMEM((own_right * tiles, LANES), F32),
            pltpu.VMEM((own_right, width), F32),
            pltpu.VMEM(owned, F32),
            pltpu.SemaphoreType.DMA((2,)),
        ],
        compiler_params=params(4),
        cost_estimate=cost(1000, 1000),
        name="final_sums",
    )(in_hbm(pair_out), j_keep, keep, *gr_last, *gw_last)
    return (pair_out, grad_left, grad_right, grad_weight)


def solution(mesh):
    placed = (
        P(("grp", "row", "col"), None),
        P(("grp", "col", "row"), None),
        P("grp"),
        P("grp"),
        P(),
        P(("grp", "row"), "col", None),
    )
    return jax.shard_map(
        shards,
        mesh=mesh,
        in_specs=placed,
        out_specs=(
            P(("grp", "row"), "col", None),
            P(("grp", "row", "col"), None),
            P(("grp", "col", "row"), None),
            P(("grp", "row", "col"), None),
        ),
        check_vma=False,
    )
```

```python
import functools

import jax
import jax.numpy as jnp
from jax import lax
from jax.experimental import pallas as pl
from jax.experimental.pallas import tpu as pltpu
from jax.sharding import PartitionSpec as P

LANES = 128
CHUNK = 4
PIECE = 8
NT = (((1,), (1,)), ((), ()))
F32 = jnp.float32
BF16 = jnp.bfloat16


def params(mib):
    return pltpu.CompilerParams(vmem_limit_bytes=mib * 2**20)


def cost(flops, nbytes):
    return pl.CostEstimate(flops=int(flops), bytes_accessed=int(nbytes), transcendentals=0)


def cut(source, index, n, keep_ref, send_ref):
    rows = source.shape[0] // n
    for k in range(n):
        at = pl.multiple_of((index ^ k) * rows, rows)
        into = send_ref if k % 2 else keep_ref
        into[k // 2] = source[pl.ds(at, rows), :].astype(into.dtype)


def place(buffers, index, n, flat):
    for buffer, owners in zip(buffers, owners_of(n)):
        rows = buffer.shape[1]
        for k, owner in enumerate(owners):
            at = pl.multiple_of((index ^ owner) * rows, 8)
            flat[pl.ds(at, rows), :] = buffer[k].astype(F32)


def lane_group(shape, chans):
    return lax.broadcasted_iota(jnp.int32, shape, 1) // chans


def mask_rows(res_ref, first, count):
    shape = (count, res_ref.shape[1])
    row = lax.broadcasted_iota(jnp.int32, shape, 0) + first
    here = lax.broadcasted_iota(jnp.int32, shape, 1) == row
    chosen = jnp.where(here, res_ref[...].astype(F32), 0.0)
    return jnp.broadcast_to(jnp.sum(chosen, axis=1, keepdims=True), (count, LANES))


def scale_kernel(dims, *refs):
    chans, groups, blocks, i_rows, j_rows, step_rows, sequences = dims
    tiles = sequences * chans // LANES
    res_hbm, seq_hbm, cot_ref, w_hbm, left_hbm, right_hbm = refs[:6]
    scaled_ref, inv_ref, wp_ref, keep_ref, ri_ref, rj_ref, left_ref, right_ref, z_ref = refs[6:15]
    res_ref, seq_ref, w_ref, w32, cot, sems, more_sems = refs[15:]
    steps = i_rows // step_rows

    def fetch(piece):
        rows = pl.ds(piece * step_rows, step_rows)
        return pltpu.make_async_copy(cot_ref.at[rows], cot.at[rows], sems.at[piece])

    pairs = [
        (res_hbm, res_ref),
        (seq_hbm, seq_ref),
        (w_hbm, w_ref),
        (left_hbm, left_ref.at[0]),
        (right_hbm, right_ref.at[0]),
    ]
    more = [
        pltpu.make_async_copy(source, to, more_sems.at[k]) for k, (source, to) in enumerate(pairs)
    ]
    for copy in more[:3]:
        copy.start()
    for piece in range(i_rows // step_rows):
        fetch(piece).start()
    for copy in more[3:]:
        copy.start()
    shape = (sequences, tiles * LANES)
    own = lax.broadcasted_iota(jnp.int32, shape, 1) // chans
    repeat = (own == lax.broadcasted_iota(jnp.int32, shape, 0)).astype(F32).astype(BF16)
    more[0].wait()
    ri_ref[...] = mask_rows(res_ref, lax.axis_index("row") * i_rows, i_rows)
    rj_ref[...] = mask_rows(res_ref, lax.axis_index("col") * j_rows, j_rows)
    more[1].wait()
    seq = seq_ref[...].astype(F32)
    keep_ref[...] = jnp.dot(
        jnp.broadcast_to(seq, (8, sequences)).astype(BF16), repeat, preferred_element_type=F32
    )[0:1]
    valid = jnp.sum(seq, axis=1, keepdims=True)
    inv_ref[...] = 1.0 / jnp.maximum(valid * rj_ref[...], 1.0)
    more[2].wait()
    w32[...] = w_ref[...].astype(F32)
    for e in range(chans):
        wp_ref[e * chans : (e + 1) * chans, :] = w32[pl.ds(e, chans, stride=chans), :].astype(BF16)
    for piece in range(i_rows // step_rows):
        fetch(piece).wait()
    for step in range(steps):
        for at in range(step * step_rows, (step + 1) * step_rows):
            inverse = jnp.where(ri_ref[at : at + 1, :] > 0, inv_ref[...], 1.0)
            scaled_ref[at] = (cot[at].astype(F32) * inverse).astype(BF16)
        if step < z_ref.shape[0]:
            rows = slice(step * step_rows, (step + 1) * step_rows)
            inner_rows(dims, scaled_ref[rows], wp_ref, z_ref, step)
    more[3].wait()
    more[4].wait()


def inner_rows(dims, scaled, wp_ref, z_ref, at):
    chans, groups, blocks, i_rows, j_rows, step_rows, sequences = dims
    for first in range(0, blocks, CHUNK):
        part = lax.dot_general(
            scaled.reshape(step_rows * j_rows, LANES),
            wp_ref[first * LANES : (first + CHUNK) * LANES, :],
            NT,
            preferred_element_type=F32,
        ).astype(BF16)
        for k in range(CHUNK):
            a = first + k
            for i in range(step_rows):
                z_ref[at, a * j_rows : (a + 1) * j_rows, i * LANES : (i + 1) * LANES] = part[
                    i * j_rows : (i + 1) * j_rows, k * LANES : (k + 1) * LANES
                ]


def inner_kernel(dims, first, after, scaled_ref, wp_ref, z_ref):
    step_rows = dims[5]
    for at in range(z_ref.shape[0]):
        rows = slice((first + at) * step_rows, (first + at + 1) * step_rows)
        inner_rows(dims, scaled_ref[rows], wp_ref, z_ref, at)


def at_step(refs, step):
    for ref in refs:
        if step < ref.shape[0]:
            return ref.at[step]
        step -= ref.shape[0]


def outer_kernel(dims, n_row, n_col, *refs):
    chans, groups, blocks, i_rows, j_rows, step_rows, sequences = dims
    tiles = sequences * chans // LANES
    after, ri_ref, keep_ref, scaled_ref, rbig, left_held, left_came = refs[:7]
    y_ref, diag_ref, keep_out, send_out = refs[7:11]
    flat, lsplit, expand, gwt, gwr = refs[11:]
    place((left_held, left_came), lax.axis_index("col"), n_col, flat)
    for t in range(tiles):
        lanes = slice(t * LANES, (t + 1) * LANES)
        masked = flat[0:i_rows, lanes] * ri_ref[...] * keep_ref[:, lanes]
        lsplit[pl.ds(t, i_rows, stride=tiles), :] = masked
    shape = (LANES, groups * LANES)
    source = lax.broadcasted_iota(jnp.int32, shape, 0)
    target = lax.broadcasted_iota(jnp.int32, shape, 1)
    same = (source // chans == target // LANES) & (source % chans == target % chans)
    expand[...] = same.astype(F32).astype(BF16)
    group = lane_group((tiles, LANES), chans)
    masks = [(group == b).astype(F32).astype(BF16) for b in range(groups)]
    deep_rows = 2 * step_rows if i_rows % (2 * step_rows) == 0 else step_rows

    for step in range(i_rows // step_rows):
        if step * step_rows % deep_rows == 0:
            rows = slice(step * step_rows * tiles, (step * step_rows + deep_rows) * tiles)
            spread = jnp.dot(
                lsplit[rows, :].astype(BF16), expand[...], preferred_element_type=F32
            ).astype(BF16)
            for i in range(deep_rows):
                block, at = divmod(step * step_rows + i, step_rows)
                for b in range(groups):
                    for lo in range(groups):
                        first = b * sequences + lo * tiles
                        diag_ref[
                            block, first : first + tiles, at * LANES : (at + 1) * LANES
                        ] = (
                            spread[i * tiles : (i + 1) * tiles, lo * LANES : (lo + 1) * LANES]
                            * masks[b]
                        )
        for first in range(0, step_rows, CHUNK):
            part = jnp.dot(
                rbig[...],
                diag_ref[step, :, first * LANES : (first + CHUNK) * LANES],
                preferred_element_type=F32,
            ).astype(BF16)
            for k in range(CHUNK):
                for a in range(blocks):
                    y_ref[step * step_rows + first + k, :, a * LANES : (a + 1) * LANES] = part[
                        a * j_rows : (a + 1) * j_rows, k * LANES : (k + 1) * LANES
                    ]
        if (step + 1) * step_rows % deep_rows == 0:
            block = slice((step + 1) * step_rows - deep_rows, (step + 1) * step_rows)
            scaled_t = scaled_ref[block].reshape(deep_rows * j_rows, LANES).T
            y_flat = y_ref[block].reshape(deep_rows * j_rows, blocks * LANES)
            part = jnp.dot(scaled_t, y_flat, preferred_element_type=F32)
            gwt[...] = gwt[...] + part if block.start else part
    for k in range(blocks):
        turned_tile = gwt[:, k * LANES : (k + 1) * LANES].T
        for q in range(groups):
            gwr[pl.ds(k * groups + q, chans, stride=chans), :] = turned_tile[
                q * chans : (q + 1) * chans
            ]
    cut(gwr, lax.axis_index("row"), n_row, keep_out, send_out)


def right_sum(first, last, z_refs, diag_ref, acc, so_far=None):
    for step in range(first, last):
        part = lax.dot_general(
            at_step(z_refs, step)[...], diag_ref[step], NT, preferred_element_type=F32
        )
        acc[...] = part if so_far is None else so_far[...] + part
        so_far = acc


def right_part_kernel(first, last, parts, after, diag_ref, *refs):
    right_sum(first, last, refs[:parts], diag_ref, refs[-1], *refs[parts:-1])


def right_kernel(dims, n_row, first, after, diag_ref, acc_first, *refs):
    chans, groups, blocks, i_rows, j_rows, step_rows, sequences = dims
    tiles = sequences * chans // LANES
    j_pad = -(-j_rows // LANES) * LANES
    z_refs, (keep_out, send_out, acc, turned, gr_all) = refs[:-5], refs[-5:]
    right_sum(first, i_rows // step_rows, z_refs, diag_ref, acc, acc_first)
    flipped = acc[...].T
    for a in range(blocks):
        at, shift = divmod(a * j_rows, LANES)
        mine = flipped[:, at * LANES : at * LANES + j_pad]
        if shift:
            mine = pltpu.roll(mine, LANES - shift, axis=1)
        for b in range(groups):
            for lo in range(groups):
                first = b * sequences + lo * tiles
                turned[pl.ds(lo * chans + groups * a + b, tiles, stride=LANES), :] = mine[
                    first : first + tiles
                ]
    for t in range(tiles):
        lanes = slice(t * LANES, (t + 1) * LANES)
        gr_all[pl.ds(t, j_rows, stride=tiles), :] = turned[lanes, :].T[:j_rows]
    cut(gr_all, lax.axis_index("row"), n_row, keep_out, send_out)


def right_rows_kernel(dims, n_row, after, rj_ref, keep_ref, right_held, right_came, *refs):
    chans, groups, blocks, i_rows, j_rows, step_rows, sequences = dims
    tiles = sequences * chans // LANES
    j_pad = -(-j_rows // LANES) * LANES
    rbig, rbt_ref, flat, turned = refs
    place((right_held, right_came), lax.axis_index("row"), n_row, flat)
    for t in range(tiles):
        lanes = slice(t * LANES, (t + 1) * LANES)
        masked = flat[0:j_rows, lanes] * rj_ref[...] * keep_ref[:, lanes]
        if j_rows < j_pad:
            masked = jnp.concatenate([masked, jnp.zeros((j_pad - j_rows, LANES), F32)], axis=0)
        turned[lanes, :] = masked.T
    for a in range(blocks):
        parts = [
            turned[pl.ds(lo * chans + groups * a + b, tiles, stride=LANES), :]
            for b in range(groups)
            for lo in range(groups)
        ]
        block = jnp.concatenate(parts, axis=0)
        rbig[a * j_rows : (a + 1) * j_rows, :] = block.T[:j_rows].astype(BF16)
    rbt_ref[...] = rbig[...].T


def left_kernel(dims, n_col, after, rbt_ref, *refs):
    chans, groups, blocks, i_rows, j_rows, step_rows, sequences = dims
    tiles = sequences * chans // LANES
    z_refs, (keep_out, send_out, gl_all) = refs[:-3], refs[-3:]
    group = lane_group((sequences, LANES), chans)
    group_t = lane_group((tiles, LANES), chans)

    for step in range(i_rows // step_rows):
        z_ref = at_step(z_refs, step)
        for first in range(0, step_rows, CHUNK):
            part = jnp.dot(
                rbt_ref[...],
                z_ref[:, first * LANES : (first + CHUNK) * LANES],
                preferred_element_type=F32,
            )
            for k in range(CHUNK):
                mine = part[:, k * LANES : (k + 1) * LANES]
                total = mine[0:sequences]
                for b in range(1, groups):
                    total = jnp.where(group == b, mine[b * sequences : (b + 1) * sequences], total)
                shift = LANES // 2
                while shift >= chans:
                    total = total + pltpu.roll(total, shift, axis=1)
                    shift //= 2
                merged = total[0:tiles]
                for lo in range(1, groups):
                    merged = jnp.where(group_t == lo, total[lo * tiles : (lo + 1) * tiles], merged)
                at = (step * step_rows + first + k) * tiles
                gl_all[at : at + tiles, :] = merged
    cut(gl_all, lax.axis_index("col"), n_col, keep_out, send_out)


def total_of(keep_ref, came_ref, k=0):
    return keep_ref[k].astype(F32) + came_ref[k].astype(F32)


def join_kernel(after, held_ref, came_ref, out_ref):
    count = held_ref.shape[0]
    for k in range(count):
        out_ref[k] = held_ref[k]
        out_ref[count + k] = came_ref[k]


def fold_kernel(after, held_ref, came_ref, keep_out, send_out):
    for k in range(held_ref.shape[0]):
        into = send_out if k % 2 else keep_out
        into[k // 2] = total_of(held_ref, came_ref, k).astype(into.dtype)


def copy_kernel(after, *refs):
    count = len(refs) // 2
    for source, to in zip(refs[:count], refs[count:]):
        to[...] = source[...]


def turn_kernel(n_col, after, held_ref, came_ref, keep_out, send_out, whole):
    whole[...] = total_of(held_ref, came_ref)
    cut(whole, lax.axis_index("col"), n_col, keep_out, send_out)


def write_rows(whole, rows, keep_ref, out_ref, tiles):
    own = out_ref.shape[0]
    for t in range(tiles):
        lanes = slice(t * LANES, (t + 1) * LANES)
        out_ref[:, lanes] = whole[pl.ds(t, own, stride=tiles), :] * (
            rows * keep_ref[:, lanes]
        )


def pair_kernel(dims, *refs):
    after, ri_ref, y_ref, wp_ref, inv_ref, keep_ref, held, came = refs[:8]
    out_ref, gl_out, staged, whole, left, sems = refs[8:]
    i_rows, j_rows = dims[3:5]
    own = left.shape[0]
    first = pl.multiple_of(lax.axis_index("col") * own, 8)
    whole[...] = total_of(held, came)
    write_rows(whole, ri_ref[pl.ds(first, own), :], keep_ref, left, whole.shape[0] // own)
    copies = [pltpu.make_async_copy(left, gl_out, sems.at[0])]
    copies[0].start()
    for row in range(0, i_rows, PIECE):
        y_flat = y_ref[row : row + PIECE].reshape(PIECE * j_rows, y_ref.shape[2])
        projected = jnp.dot(y_flat, wp_ref[...], preferred_element_type=F32)
        for i in range(PIECE):
            inverse = jnp.where(ri_ref[row + i : row + i + 1, :] > 0, inv_ref[...], 1.0)
            staged[row + i] = (projected[i * j_rows : (i + 1) * j_rows] * inverse).astype(BF16)
        rows = pl.ds(row, PIECE)
        copies.append(
            pltpu.make_async_copy(staged.at[rows], out_ref.at[rows], sems.at[len(copies)])
        )
        copies[-1].start()
    for copy in copies:
        copy.wait()


def final_kernel(after, rj_ref, keep_ref, *refs):
    right, weight = refs[0:2], refs[2:4]
    gr_out, gw_out, whole, rows, weight_rows, sems = refs[4:]
    weight_rows[...] = total_of(*weight)
    copies = [pltpu.make_async_copy(weight_rows, gw_out, sems.at[0])]
    copies[0].start()
    own = rows.shape[0]
    first = pl.multiple_of(lax.axis_index("row") * own, 8)
    whole[...] = total_of(*right)
    write_rows(whole, rj_ref[pl.ds(first, own), :], keep_ref, rows, whole.shape[0] // own)
    copies.append(pltpu.make_async_copy(rows, gr_out, sems.at[1]))
    copies[1].start()
    for copy in copies:
        copy.wait()


def swap(array, axis, n, bit):
    return lax.ppermute(array, axis, [(s, s ^ bit) for s in range(n)])


def owners_of(n):
    held, bit = [0], n // 2
    while bit > 1:
        held, bit = held + [k ^ bit for k in held], bit // 2
    return held, [k ^ 1 for k in held]


def gather(block, own, axis, n, after):
    held, sent, bit = own, block[None], n // 2
    while bit > 1:
        came = swap(sent, axis, n, bit)
        shape = (2 * held.shape[0],) + held.shape[1:]
        held = small_call(join_kernel, [pltpu.VMEM(shape, BF16)], "join")(after, held, came)[0]
        sent, bit = held, bit // 2
    return held, swap(sent, axis, n, 1)


def reduce(keep, send, axis, n, after, between=None):
    bit = 1
    while True:
        came = swap(send, axis, n, bit)
        bit *= 2
        if bit >= n:
            if between is not None:
                between(keep)
            return keep, came
        half = (keep.shape[0] // 2,) + keep.shape[1:]
        outs = [pltpu.VMEM(half, F32), pltpu.VMEM(half, BF16)]
        keep, send = small_call(fold_kernel, outs, "fold")(after, keep, came)
        if between is not None:
            gate, between = between(keep), None
            keep, send = hold(gate, keep, send)


def small_call(body, outs, name, scratch=(), flops=1000):
    def call(after, *operands):
        return pl.pallas_call(
            body,
            in_specs=[hbm()] + vmem(len(operands)),
            out_specs=vmem(len(outs)),
            out_shape=outs,
            scratch_shapes=list(scratch),
            compiler_params=params(4),
            cost_estimate=cost(flops, 1000),
            name=name,
        )(after, *operands)

    return call


def hold(after, *arrays):
    outs = [pltpu.VMEM(array.shape, array.dtype) for array in arrays]
    return small_call(copy_kernel, outs, "hold", flops=10**10)(after, *arrays)


def halves(rows, n):
    return [pltpu.VMEM((n // 2, rows // n, LANES), BF16)] * 2


def vmem(count=1):
    return [pl.BlockSpec(memory_space=pltpu.VMEM)] * count


def hbm():
    return pl.BlockSpec(memory_space=pl.ANY)


def in_hbm(array):
    return pltpu.with_memory_space_constraint(array, pltpu.HBM)


def shards(left_act, right_act, row_mask, res_mask, out_weight, cotangent):
    n_col = lax.axis_size("col")
    n_row = lax.axis_size("row")
    i_rows, j_rows, pair_width = cotangent.shape
    sequences = row_mask.shape[0]
    width = left_act.shape[1]
    chans = width // sequences
    groups = LANES // chans
    blocks = chans // groups
    tiles = width // LANES
    depth = groups * sequences
    inner = chans * chans
    step_rows = 16
    steps = i_rows // step_rows
    early_steps = 3 * steps // 4
    dims = (chans, groups, blocks, i_rows, j_rows, step_rows, sequences)
    j_pad = -(-j_rows // LANES) * LANES
    span = blocks * j_rows
    own_left, own_right = left_act.shape[0], right_act.shape[0]
    macs = i_rows * j_rows * inner * pair_width

    mask_row = (res_mask.reshape(1, -1), row_mask.reshape(1, -1))
    scaled, inverse, weight, keep, i_keep, j_keep, own_l, own_r, z_first = pl.pallas_call(
        functools.partial(scale_kernel, dims),
        in_specs=[hbm()] * 6,
        out_specs=vmem(9),
        out_shape=[
            pltpu.VMEM(cotangent.shape, BF16),
            pltpu.VMEM((j_rows, LANES), F32),
            pltpu.VMEM(out_weight.shape, BF16),
            pltpu.VMEM((1, width), F32),
            pltpu.VMEM((i_rows, LANES), F32),
            pltpu.VMEM((j_rows, LANES), F32),
            pltpu.VMEM((1,) + left_act.shape, BF16),
            pltpu.VMEM((1,) + right_act.shape, BF16),
            pltpu.VMEM((early_steps, span, step_rows * LANES), BF16),
        ],
        scratch_shapes=[
            pltpu.VMEM((1, res_mask.shape[0]), jnp.int32),
            pltpu.VMEM((1, sequences), jnp.int32),
            pltpu.VMEM(out_weight.shape, BF16),
            pltpu.VMEM(out_weight.shape, F32),
            pltpu.VMEM(cotangent.shape, BF16),
            pltpu.SemaphoreType.DMA((steps,)),
            pltpu.SemaphoreType.DMA((5,)),
        ],
        compiler_params=params(16),
        cost_estimate=cost(1000, 1000),
        name="scale",
    )(*map(in_hbm, (*mask_row, cotangent, out_weight, left_act, right_act)))

    lefts = gather(left_act, own_l, "col", n_col, own_l)
    rights = gather(right_act, own_r, "row", n_row, lefts[0])

    z_last = pl.pallas_call(
        functools.partial(inner_kernel, dims, early_steps),
        in_specs=[hbm()] + vmem(2),
        out_specs=vmem()[0],
        out_shape=pltpu.VMEM((steps - early_steps, span, step_rows * LANES), BF16),
        compiler_params=params(16),
        cost_estimate=cost(16 * macs, 2**20),
        name="inner",
    )(rights[0], scaled, weight)
    z = (z_first, z_last)

    rbig, right_turned = pl.pallas_call(
        functools.partial(right_rows_kernel, dims, n_row),
        in_specs=[hbm()] + vmem(4),
        out_specs=vmem(2),
        out_shape=[pltpu.VMEM((span, depth), BF16), pltpu.VMEM((depth, span), BF16)],
        scratch_shapes=[pltpu.VMEM((j_rows, width), F32), pltpu.VMEM((width, j_pad), F32)],
        compiler_params=params(12),
        cost_estimate=cost(16 * macs, 2**20),
        name="right_rows",
    )(z_last, j_keep, keep, *rights)

    gl_cut = pl.pallas_call(
        functools.partial(left_kernel, dims, n_col),
        in_specs=[hbm()] + vmem(1 + len(z)),
        out_specs=vmem(2),
        out_shape=halves(i_rows * tiles, n_col),
        scratch_shapes=[pltpu.VMEM((i_rows * tiles, LANES), F32)],
        compiler_params=params(16),
        cost_estimate=cost(16 * macs, 2**20),
        name="left",
    )(rbig, right_turned, *z)
    y, diag, *gw_cut = pl.pallas_call(
        functools.partial(outer_kernel, dims, n_row, n_col),
        in_specs=[hbm()] + vmem(6),
        out_specs=vmem(4),
        out_shape=[
            pltpu.VMEM((i_rows, j_rows, inner), BF16),
            pltpu.VMEM((steps, depth, step_rows * LANES), BF16),
        ]
        + halves(inner, n_row),
        scratch_shapes=[
            pltpu.VMEM((i_rows, width), F32),
            pltpu.VMEM((i_rows * tiles, LANES), F32),
            pltpu.VMEM((LANES, groups * LANES), BF16),
            pltpu.VMEM((pair_width, inner), F32),
            pltpu.VMEM((inner, pair_width), F32),
        ],
        compiler_params=params(16),
        cost_estimate=cost(16 * macs, 2**20),
        name="outer",
    )(gl_cut[0], i_keep, keep, scaled, rbig, *lefts)

    def right_part(first, last, after, *so_far):
        return pl.pallas_call(
            functools.partial(right_part_kernel, first, last, len(z)),
            in_specs=[hbm()] + vmem(1 + len(z) + len(so_far)),
            out_specs=vmem()[0],
            out_shape=pltpu.VMEM((span, depth), F32),
            compiler_params=params(16),
            cost_estimate=cost(1000, 1000),
            name="right_part",
        )(after, diag, *z, *so_far)

    gw_row, acc = [], []
    right_steps = max(1, steps // 4)

    def weight_rounds(after):
        acc.append(right_part(0, right_steps, after))
        gw_row.extend(reduce(*gw_cut, "row", n_row, acc[0]))
        return gw_row[0]

    gl_last = reduce(*gl_cut, "col", n_col, gw_cut[0], weight_rounds)
    acc = right_part(right_steps, 2 * right_steps, gl_last[0], acc[0])
    gw_turned = small_call(
        functools.partial(turn_kernel, n_col),
        halves(inner // n_row, n_col),
        "turn",
        [pltpu.VMEM((inner // n_row, pair_width), F32)],
    )(acc, *gw_row)

    gr_cut = pl.pallas_call(
        functools.partial(right_kernel, dims, n_row, 2 * right_steps),
        in_specs=[hbm()] + vmem(2 + len(z)),
        out_specs=vmem(2),
        out_shape=halves(j_rows * tiles, n_row),
        scratch_shapes=[
            pltpu.VMEM((span, depth), F32),
            pltpu.VMEM((width, j_pad), F32),
            pltpu.VMEM((j_rows * tiles, LANES), F32),
        ],
        compiler_params=params(20),
        cost_estimate=cost(16 * macs, 2**20),
        name="right",
    )(gw_turned[0], diag, acc, *z)
    gr_held = []

    def right_rounds(after):
        gr_held.extend(hold(after, *gr_cut))
        return gr_held[0]

    gw_last = reduce(*gw_turned, "col", n_col, gr_cut[0], right_rounds)
    gr_last = reduce(*gr_held, "row", n_row, gw_last[0])

    pair_out, grad_left = pl.pallas_call(
        functools.partial(pair_kernel, dims),
        in_specs=[hbm()] + vmem(7),
        out_specs=[hbm()] * 2,
        out_shape=[
            jax.ShapeDtypeStruct(cotangent.shape, BF16),
            jax.ShapeDtypeStruct((own_left, width), F32),
        ],
        scratch_shapes=[
            pltpu.VMEM(cotangent.shape, BF16),
            pltpu.VMEM((own_left * tiles, LANES), F32),
            pltpu.VMEM((own_left, width), F32),
            pltpu.SemaphoreType.DMA((1 + i_rows // PIECE,)),
        ],
        compiler_params=params(12),
        cost_estimate=cost(16 * macs, 2**20),
        name="pair",
    )(gr_last[0], i_keep, y, weight, inverse, keep, *gl_last)

    owned = (inner // n_row // n_col, pair_width)
    grad_right, grad_weight = pl.pallas_call(
        final_kernel,
        in_specs=[hbm()] + vmem(6),
        out_specs=[hbm()] * 2,
        out_shape=[
            jax.ShapeDtypeStruct((own_right, width), F32),
            jax.ShapeDtypeStruct(owned, F32),
        ],
        scratch_shapes=[
            pltpu.VMEM((own_right * tiles, LANES), F32),
            pltpu.VMEM((own_right, width), F32),
            pltpu.VMEM(owned, F32),
            pltpu.SemaphoreType.DMA((2,)),
        ],
        compiler_params=params(4),
        cost_estimate=cost(1000, 1000),
        name="final_sums",
    )(in_hbm(pair_out), j_keep, keep, *gr_last, *gw_last)
    return (pair_out, grad_left, grad_right, grad_weight)


def solution(mesh):
    placed = (
        P(("grp", "row", "col"), None),
        P(("grp", "col", "row"), None),
        P("grp"),
        P("grp"),
        P(),
        P(("grp", "row"), "col", None),
    )
    return jax.shard_map(
        shards,
        mesh=mesh,
        in_specs=placed,
        out_specs=(
            P(("grp", "row"), "col", None),
            P(("grp", "row", "col"), None),
            P(("grp", "col", "row"), None),
            P(("grp", "row", "col"), None),
        ),
        check_vma=False,
    )
```

```python
import functools

import jax
import jax.numpy as jnp
from jax import lax
from jax.experimental import pallas as pl
from jax.experimental.pallas import tpu as pltpu
from jax.sharding import PartitionSpec as P

LANES = 128
CHUNK = 4
PIECE = 8
NT = (((1,), (1,)), ((), ()))
F32 = jnp.float32
BF16 = jnp.bfloat16


def params(mib):
    return pltpu.CompilerParams(vmem_limit_bytes=mib * 2**20)


def cost(flops, nbytes):
    return pl.CostEstimate(flops=int(flops), bytes_accessed=int(nbytes), transcendentals=0)


def cut(source, index, n, keep_ref, send_ref):
    rows = source.shape[0] // n
    for k in range(n):
        at = pl.multiple_of((index ^ k) * rows, rows)
        into = send_ref if k % 2 else keep_ref
        into[k // 2] = source[pl.ds(at, rows), :].astype(into.dtype)


def place(buffers, index, n, flat):
    for buffer, owners in zip(buffers, owners_of(n)):
        rows = buffer.shape[1]
        for k, owner in enumerate(owners):
            at = pl.multiple_of((index ^ owner) * rows, 8)
            flat[pl.ds(at, rows), :] = buffer[k].astype(F32)


def paired(j_rows):
    return 2 * j_rows == LANES


def slot_of(tile, tiles, j_rows):
    return tile % 2 * (tiles // 2) + tile // 2 if paired(j_rows) else tile


def swap_halves(low, first, second):
    half = LANES // 2
    return (
        jnp.where(low, first, pltpu.roll(second, half, axis=1)),
        jnp.where(low, pltpu.roll(first, half, axis=1), second),
    )


def lane_group(shape, chans):
    return lax.broadcasted_iota(jnp.int32, shape, 1) // chans


def mask_rows(res_ref, first, count):
    shape = (count, res_ref.shape[1])
    row = lax.broadcasted_iota(jnp.int32, shape, 0) + first
    here = lax.broadcasted_iota(jnp.int32, shape, 1) == row
    chosen = jnp.where(here, res_ref[...].astype(F32), 0.0)
    return jnp.broadcast_to(jnp.sum(chosen, axis=1, keepdims=True), (count, LANES))


def scale_kernel(dims, *refs):
    chans, groups, blocks, i_rows, j_rows, step_rows, sequences = dims
    tiles = sequences * chans // LANES
    res_hbm, seq_hbm, cot_ref, w_hbm, left_hbm, right_hbm = refs[:6]
    scaled_ref, inv_ref, wp_ref, keep_ref, ri_ref, rj_ref, left_ref, right_ref, z_ref = refs[6:15]
    res_ref, seq_ref, w_ref, w32, cot, sems, more_sems = refs[15:]
    steps = i_rows // step_rows

    def fetch(piece):
        rows = pl.ds(piece * step_rows, step_rows)
        return pltpu.make_async_copy(cot_ref.at[rows], cot.at[rows], sems.at[piece])

    pairs = [
        (res_hbm, res_ref),
        (seq_hbm, seq_ref),
        (w_hbm, w_ref),
        (left_hbm, left_ref.at[0]),
        (right_hbm, right_ref.at[0]),
    ]
    more = [
        pltpu.make_async_copy(source, to, more_sems.at[k]) for k, (source, to) in enumerate(pairs)
    ]
    for copy in more[:3]:
        copy.start()
    for piece in range(i_rows // step_rows):
        fetch(piece).start()
    for copy in more[3:]:
        copy.start()
    shape = (sequences, tiles * LANES)
    own = lax.broadcasted_iota(jnp.int32, shape, 1) // chans
    repeat = (own == lax.broadcasted_iota(jnp.int32, shape, 0)).astype(F32).astype(BF16)
    more[0].wait()
    ri_ref[...] = mask_rows(res_ref, lax.axis_index("row") * i_rows, i_rows)
    rj_ref[...] = mask_rows(res_ref, lax.axis_index("col") * j_rows, j_rows)
    more[1].wait()
    seq = seq_ref[...].astype(F32)
    keep_ref[...] = jnp.dot(
        jnp.broadcast_to(seq, (8, sequences)).astype(BF16), repeat, preferred_element_type=F32
    )[0:1]
    valid = jnp.sum(seq, axis=1, keepdims=True)
    inv_ref[...] = 1.0 / jnp.maximum(valid * rj_ref[...], 1.0)
    more[2].wait()
    w32[...] = w_ref[...].astype(F32)
    for e in range(chans):
        wp_ref[e * chans : (e + 1) * chans, :] = w32[pl.ds(e, chans, stride=chans), :].astype(BF16)
    for piece in range(i_rows // step_rows):
        fetch(piece).wait()
    for step in range(steps):
        for at in range(step * step_rows, (step + 1) * step_rows):
            inverse = jnp.where(ri_ref[at : at + 1, :] > 0, inv_ref[...], 1.0)
            scaled_ref[at] = (cot[at].astype(F32) * inverse).astype(BF16)
        if step < z_ref.shape[0]:
            rows = slice(step * step_rows, (step + 1) * step_rows)
            inner_rows(dims, scaled_ref[rows], wp_ref, z_ref, step)
    more[3].wait()
    more[4].wait()


def inner_rows(dims, scaled, wp_ref, z_ref, at):
    chans, groups, blocks, i_rows, j_rows, step_rows, sequences = dims
    for first in range(0, blocks, CHUNK):
        part = lax.dot_general(
            scaled.reshape(step_rows * j_rows, LANES),
            wp_ref[first * LANES : (first + CHUNK) * LANES, :],
            NT,
            preferred_element_type=F32,
        ).astype(BF16)
        for k in range(CHUNK):
            a = first + k
            for i in range(step_rows):
                z_ref[at, a * j_rows : (a + 1) * j_rows, i * LANES : (i + 1) * LANES] = part[
                    i * j_rows : (i + 1) * j_rows, k * LANES : (k + 1) * LANES
                ]


def inner_kernel(dims, first, after, scaled_ref, wp_ref, z_ref):
    step_rows = dims[5]
    for at in range(z_ref.shape[0]):
        rows = slice((first + at) * step_rows, (first + at + 1) * step_rows)
        inner_rows(dims, scaled_ref[rows], wp_ref, z_ref, at)


def at_step(refs, step):
    for ref in refs:
        if step < ref.shape[0]:
            return ref.at[step]
        step -= ref.shape[0]


def outer_kernel(dims, n_row, n_col, *refs):
    chans, groups, blocks, i_rows, j_rows, step_rows, sequences = dims
    tiles = sequences * chans // LANES
    after, ri_ref, keep_ref, scaled_ref, rbig, left_held, left_came = refs[:7]
    y_ref, diag_ref, keep_out, send_out = refs[7:11]
    flat, lsplit, expand, gwt, gwr = refs[11:]
    place((left_held, left_came), lax.axis_index("col"), n_col, flat)
    for t in range(tiles):
        lanes = slice(t * LANES, (t + 1) * LANES)
        masked = flat[0:i_rows, lanes] * ri_ref[...] * keep_ref[:, lanes]
        lsplit[pl.ds(slot_of(t, tiles, j_rows), i_rows, stride=tiles), :] = masked
    shape = (LANES, groups * LANES)
    source = lax.broadcasted_iota(jnp.int32, shape, 0)
    target = lax.broadcasted_iota(jnp.int32, shape, 1)
    same = (source // chans == target // LANES) & (source % chans == target % chans)
    expand[...] = same.astype(F32).astype(BF16)
    group = lane_group((tiles, LANES), chans)
    masks = [(group == b).astype(F32).astype(BF16) for b in range(groups)]
    deep_rows = 2 * step_rows if i_rows % (2 * step_rows) == 0 else step_rows

    for step in range(i_rows // step_rows):
        if step * step_rows % deep_rows == 0:
            rows = slice(step * step_rows * tiles, (step * step_rows + deep_rows) * tiles)
            spread = jnp.dot(
                lsplit[rows, :].astype(BF16), expand[...], preferred_element_type=F32
            ).astype(BF16)
            for i in range(deep_rows):
                block, at = divmod(step * step_rows + i, step_rows)
                for b in range(groups):
                    for lo in range(groups):
                        first = b * sequences + lo * tiles
                        diag_ref[
                            block, first : first + tiles, at * LANES : (at + 1) * LANES
                        ] = (
                            spread[i * tiles : (i + 1) * tiles, lo * LANES : (lo + 1) * LANES]
                            * masks[b]
                        )
        for first in range(0, step_rows, CHUNK):
            part = jnp.dot(
                rbig[...],
                diag_ref[step, :, first * LANES : (first + CHUNK) * LANES],
                preferred_element_type=F32,
            ).astype(BF16)
            for k in range(CHUNK):
                for a in range(blocks):
                    y_ref[step * step_rows + first + k, :, a * LANES : (a + 1) * LANES] = part[
                        a * j_rows : (a + 1) * j_rows, k * LANES : (k + 1) * LANES
                    ]
        if (step + 1) * step_rows % deep_rows == 0:
            block = slice((step + 1) * step_rows - deep_rows, (step + 1) * step_rows)
            scaled_t = scaled_ref[block].reshape(deep_rows * j_rows, LANES).T
            y_flat = y_ref[block].reshape(deep_rows * j_rows, blocks * LANES)
            part = jnp.dot(scaled_t, y_flat, preferred_element_type=F32)
            gwt[...] = gwt[...] + part if block.start else part
    for k in range(blocks):
        turned_tile = gwt[:, k * LANES : (k + 1) * LANES].T
        for q in range(groups):
            gwr[pl.ds(k * groups + q, chans, stride=chans), :] = turned_tile[
                q * chans : (q + 1) * chans
            ]
    cut(gwr, lax.axis_index("row"), n_row, keep_out, send_out)


def right_sum(first, last, z_refs, diag_ref, acc, so_far=None):
    for step in range(first, last):
        part = lax.dot_general(
            diag_ref[step], at_step(z_refs, step)[...], NT, preferred_element_type=F32
        )
        acc[...] = part if so_far is None else so_far[...] + part
        so_far = acc


def right_part_kernel(first, last, parts, after, diag_ref, *refs):
    right_sum(first, last, refs[:parts], diag_ref, refs[-1], *refs[parts:-1])


def right_kernel(dims, n_row, first, after, diag_ref, acc_first, *refs):
    chans, groups, blocks, i_rows, j_rows, step_rows, sequences = dims
    tiles = sequences * chans // LANES
    j_pad = -(-j_rows // LANES) * LANES
    z_refs, (keep_out, send_out, acc, turned, gr_all) = refs[:-5], refs[-5:]
    right_sum(first, i_rows // step_rows, z_refs, diag_ref, acc, acc_first)
    if paired(j_rows):
        half = tiles // 2
        low = lane_group((half, LANES), LANES // 2) == 0
        for a in range(0, blocks, 2):
            lanes = slice(a * j_rows, (a + 2) * j_rows)
            for b in range(groups):
                for lo in range(groups):
                    first = b * sequences + lo * tiles
                    both = swap_halves(
                        low,
                        acc[first : first + half, lanes],
                        acc[first + half : first + tiles, lanes],
                    )
                    at = lo * chans + groups * a + b
                    turned[pl.ds(at, half, stride=LANES), :] = both[0]
                    turned[pl.ds(at + groups, half, stride=LANES), :] = both[1]
        for pair in range(half):
            block = turned[pair * LANES : (pair + 1) * LANES, :].T
            for k in range(2):
                gr_all[pl.ds(2 * pair + k, j_rows, stride=tiles), :] = block[
                    k * j_rows : (k + 1) * j_rows
                ]
    else:
        for a in range(blocks):
            at, shift = divmod(a * j_rows, LANES)
            mine = acc[:, at * LANES : at * LANES + j_pad]
            if shift:
                mine = pltpu.roll(mine, LANES - shift, axis=1)
            for b in range(groups):
                for lo in range(groups):
                    first = b * sequences + lo * tiles
                    turned[pl.ds(lo * chans + groups * a + b, tiles, stride=LANES), :] = mine[
                        first : first + tiles
                    ]
        for t in range(tiles):
            lanes = slice(t * LANES, (t + 1) * LANES)
            gr_all[pl.ds(t, j_rows, stride=tiles), :] = turned[lanes, :].T[:j_rows]
    cut(gr_all, lax.axis_index("row"), n_row, keep_out, send_out)


def right_rows_kernel(dims, n_row, after, rj_ref, keep_ref, right_held, right_came, *refs):
    chans, groups, blocks, i_rows, j_rows, step_rows, sequences = dims
    tiles = sequences * chans // LANES
    j_pad = -(-j_rows // LANES) * LANES
    rbig, rbt_ref, flat, turned = refs
    place((right_held, right_came), lax.axis_index("row"), n_row, flat)
    if paired(j_rows):
        half = tiles // 2
        low = lane_group((half, LANES), LANES // 2) == 0
        for pair in range(half):
            rows = []
            for t in (2 * pair, 2 * pair + 1):
                lanes = slice(t * LANES, (t + 1) * LANES)
                rows.append(flat[0:j_rows, lanes] * rj_ref[...] * keep_ref[:, lanes])
            turned[pair * LANES : (pair + 1) * LANES, :] = jnp.concatenate(rows, axis=0).T
        for a in range(0, blocks, 2):
            parts = []
            for b in range(groups):
                for lo in range(groups):
                    at = lo * chans + groups * a + b
                    parts += swap_halves(
                        low,
                        turned[pl.ds(at, half, stride=LANES), :],
                        turned[pl.ds(at + groups, half, stride=LANES), :],
                    )
            block = jnp.concatenate(parts, axis=0)
            lanes = slice(a * j_rows, (a + 2) * j_rows)
            rbt_ref[:, lanes] = block.astype(BF16)
            rbig[lanes, :] = block.T.astype(BF16)
    else:
        for t in range(tiles):
            lanes = slice(t * LANES, (t + 1) * LANES)
            masked = flat[0:j_rows, lanes] * rj_ref[...] * keep_ref[:, lanes]
            if j_rows < j_pad:
                masked = jnp.concatenate([masked, jnp.zeros((j_pad - j_rows, LANES), F32)], axis=0)
            turned[lanes, :] = masked.T
        for a in range(blocks):
            parts = [
                turned[pl.ds(lo * chans + groups * a + b, tiles, stride=LANES), :]
                for b in range(groups)
                for lo in range(groups)
            ]
            block = jnp.concatenate(parts, axis=0)
            rbig[a * j_rows : (a + 1) * j_rows, :] = block.T[:j_rows].astype(BF16)
        rbt_ref[...] = rbig[...].T


def left_kernel(dims, n_col, after, rbt_ref, *refs):
    chans, groups, blocks, i_rows, j_rows, step_rows, sequences = dims
    tiles = sequences * chans // LANES
    z_refs, (keep_out, send_out, gl_all) = refs[:-3], refs[-3:]
    group = lane_group((sequences, LANES), chans)
    group_t = lane_group((tiles, LANES), chans)

    for step in range(i_rows // step_rows):
        z_ref = at_step(z_refs, step)
        for first in range(0, step_rows, CHUNK):
            part = jnp.dot(
                rbt_ref[...],
                z_ref[:, first * LANES : (first + CHUNK) * LANES],
                preferred_element_type=F32,
            )
            for k in range(CHUNK):
                mine = part[:, k * LANES : (k + 1) * LANES]
                total = mine[0:sequences]
                for b in range(1, groups):
                    total = jnp.where(group == b, mine[b * sequences : (b + 1) * sequences], total)
                shift = LANES // 2
                while shift >= chans:
                    total = total + pltpu.roll(total, shift, axis=1)
                    shift //= 2
                merged = total[0:tiles]
                for lo in range(1, groups):
                    merged = jnp.where(group_t == lo, total[lo * tiles : (lo + 1) * tiles], merged)
                at = (step * step_rows + first + k) * tiles
                gl_all[at : at + tiles, :] = merged
    cut(gl_all, lax.axis_index("col"), n_col, keep_out, send_out)


def total_of(keep_ref, came_ref, k=0):
    return keep_ref[k].astype(F32) + came_ref[k].astype(F32)


def join_kernel(after, held_ref, came_ref, out_ref):
    count = held_ref.shape[0]
    for k in range(count):
        out_ref[k] = held_ref[k]
        out_ref[count + k] = came_ref[k]


def fold_kernel(after, held_ref, came_ref, keep_out, send_out):
    for k in range(held_ref.shape[0]):
        into = send_out if k % 2 else keep_out
        into[k // 2] = total_of(held_ref, came_ref, k).astype(into.dtype)


def copy_kernel(after, *refs):
    count = len(refs) // 2
    for source, to in zip(refs[:count], refs[count:]):
        to[...] = source[...]


def turn_kernel(n_col, after, held_ref, came_ref, keep_out, send_out, whole):
    whole[...] = total_of(held_ref, came_ref)
    cut(whole, lax.axis_index("col"), n_col, keep_out, send_out)


def write_rows(whole, rows, keep_ref, out_ref, slots):
    own = out_ref.shape[0]
    tiles = len(slots)
    for t, slot in enumerate(slots):
        lanes = slice(t * LANES, (t + 1) * LANES)
        out_ref[:, lanes] = whole[pl.ds(slot, own, stride=tiles), :] * (
            rows * keep_ref[:, lanes]
        )


def pair_kernel(dims, *refs):
    after, ri_ref, y_ref, wp_ref, inv_ref, keep_ref, held, came = refs[:8]
    out_ref, gl_out, staged, whole, left, sems = refs[8:]
    i_rows, j_rows = dims[3:5]
    own = left.shape[0]
    first = pl.multiple_of(lax.axis_index("col") * own, 8)
    whole[...] = total_of(held, came)
    tiles = whole.shape[0] // own
    slots = [slot_of(t, tiles, j_rows) for t in range(tiles)]
    write_rows(whole, ri_ref[pl.ds(first, own), :], keep_ref, left, slots)
    copies = [pltpu.make_async_copy(left, gl_out, sems.at[0])]
    copies[0].start()
    for row in range(0, i_rows, PIECE):
        y_flat = y_ref[row : row + PIECE].reshape(PIECE * j_rows, y_ref.shape[2])
        projected = jnp.dot(y_flat, wp_ref[...], preferred_element_type=F32)
        for i in range(PIECE):
            inverse = jnp.where(ri_ref[row + i : row + i + 1, :] > 0, inv_ref[...], 1.0)
            staged[row + i] = (projected[i * j_rows : (i + 1) * j_rows] * inverse).astype(BF16)
        rows = pl.ds(row, PIECE)
        copies.append(
            pltpu.make_async_copy(staged.at[rows], out_ref.at[rows], sems.at[len(copies)])
        )
        copies[-1].start()
    for copy in copies:
        copy.wait()


def final_kernel(after, rj_ref, keep_ref, *refs):
    right, weight = refs[0:2], refs[2:4]
    gr_out, gw_out, whole, rows, weight_rows, sems = refs[4:]
    weight_rows[...] = total_of(*weight)
    copies = [pltpu.make_async_copy(weight_rows, gw_out, sems.at[0])]
    copies[0].start()
    own = rows.shape[0]
    first = pl.multiple_of(lax.axis_index("row") * own, 8)
    whole[...] = total_of(*right)
    slots = range(whole.shape[0] // own)
    write_rows(whole, rj_ref[pl.ds(first, own), :], keep_ref, rows, slots)
    copies.append(pltpu.make_async_copy(rows, gr_out, sems.at[1]))
    copies[1].start()
    for copy in copies:
        copy.wait()


def swap(array, axis, n, bit):
    return lax.ppermute(array, axis, [(s, s ^ bit) for s in range(n)])


def owners_of(n):
    held, bit = [0], n // 2
    while bit > 1:
        held, bit = held + [k ^ bit for k in held], bit // 2
    return held, [k ^ 1 for k in held]


def gather(block, own, axis, n, after):
    held, sent, bit = own, block[None], n // 2
    while bit > 1:
        came = swap(sent, axis, n, bit)
        shape = (2 * held.shape[0],) + held.shape[1:]
        held = small_call(join_kernel, [pltpu.VMEM(shape, BF16)], "join")(after, held, came)[0]
        sent, bit = held, bit // 2
    return held, swap(sent, axis, n, 1)


def reduce(keep, send, axis, n, after, between=None):
    bit = 1
    while True:
        came = swap(send, axis, n, bit)
        bit *= 2
        if bit >= n:
            if between is not None:
                between(keep)
            return keep, came
        half = (keep.shape[0] // 2,) + keep.shape[1:]
        outs = [pltpu.VMEM(half, F32), pltpu.VMEM(half, BF16)]
        keep, send = small_call(fold_kernel, outs, "fold")(after, keep, came)
        if between is not None:
            gate, between = between(keep), None
            keep, send = hold(gate, keep, send)


def small_call(body, outs, name, scratch=(), flops=1000):
    def call(after, *operands):
        return pl.pallas_call(
            body,
            in_specs=[hbm()] + vmem(len(operands)),
            out_specs=vmem(len(outs)),
            out_shape=outs,
            scratch_shapes=list(scratch),
            compiler_params=params(4),
            cost_estimate=cost(flops, 1000),
            name=name,
        )(after, *operands)

    return call


def hold(after, *arrays):
    outs = [pltpu.VMEM(array.shape, array.dtype) for array in arrays]
    return small_call(copy_kernel, outs, "hold", flops=10**10)(after, *arrays)


def halves(rows, n):
    return [pltpu.VMEM((n // 2, rows // n, LANES), BF16)] * 2


def vmem(count=1):
    return [pl.BlockSpec(memory_space=pltpu.VMEM)] * count


def hbm():
    return pl.BlockSpec(memory_space=pl.ANY)


def in_hbm(array):
    return pltpu.with_memory_space_constraint(array, pltpu.HBM)


def shards(left_act, right_act, row_mask, res_mask, out_weight, cotangent):
    n_col = lax.axis_size("col")
    n_row = lax.axis_size("row")
    i_rows, j_rows, pair_width = cotangent.shape
    sequences = row_mask.shape[0]
    width = left_act.shape[1]
    chans = width // sequences
    groups = LANES // chans
    blocks = chans // groups
    tiles = width // LANES
    depth = groups * sequences
    inner = chans * chans
    step_rows = 16
    steps = i_rows // step_rows
    early_steps = steps // 2
    dims = (chans, groups, blocks, i_rows, j_rows, step_rows, sequences)
    j_pad = -(-j_rows // LANES) * LANES
    span = blocks * j_rows
    own_left, own_right = left_act.shape[0], right_act.shape[0]
    macs = i_rows * j_rows * inner * pair_width

    mask_row = (res_mask.reshape(1, -1), row_mask.reshape(1, -1))
    scaled, inverse, weight, keep, i_keep, j_keep, own_l, own_r, z_first = pl.pallas_call(
        functools.partial(scale_kernel, dims),
        in_specs=[hbm()] * 6,
        out_specs=vmem(9),
        out_shape=[
            pltpu.VMEM(cotangent.shape, BF16),
            pltpu.VMEM((j_rows, LANES), F32),
            pltpu.VMEM(out_weight.shape, BF16),
            pltpu.VMEM((1, width), F32),
            pltpu.VMEM((i_rows, LANES), F32),
            pltpu.VMEM((j_rows, LANES), F32),
            pltpu.VMEM((1,) + left_act.shape, BF16),
            pltpu.VMEM((1,) + right_act.shape, BF16),
            pltpu.VMEM((early_steps, span, step_rows * LANES), BF16),
        ],
        scratch_shapes=[
            pltpu.VMEM((1, res_mask.shape[0]), jnp.int32),
            pltpu.VMEM((1, sequences), jnp.int32),
            pltpu.VMEM(out_weight.shape, BF16),
            pltpu.VMEM(out_weight.shape, F32),
            pltpu.VMEM(cotangent.shape, BF16),
            pltpu.SemaphoreType.DMA((steps,)),
            pltpu.SemaphoreType.DMA((5,)),
        ],
        compiler_params=params(16),
        cost_estimate=cost(1000, 1000),
        name="scale",
    )(*map(in_hbm, (*mask_row, cotangent, out_weight, left_act, right_act)))

    lefts = gather(left_act, own_l, "col", n_col, own_l)
    rights = gather(right_act, own_r, "row", n_row, lefts[0])

    z_last = pl.pallas_call(
        functools.partial(inner_kernel, dims, early_steps),
        in_specs=[hbm()] + vmem(2),
        out_specs=vmem()[0],
        out_shape=pltpu.VMEM((steps - early_steps, span, step_rows * LANES), BF16),
        compiler_params=params(16),
        cost_estimate=cost(16 * macs, 2**20),
        name="inner",
    )(rights[0], scaled, weight)
    z = (z_first, z_last)

    rbig, right_turned = pl.pallas_call(
        functools.partial(right_rows_kernel, dims, n_row),
        in_specs=[hbm()] + vmem(4),
        out_specs=vmem(2),
        out_shape=[pltpu.VMEM((span, depth), BF16), pltpu.VMEM((depth, span), BF16)],
        scratch_shapes=[pltpu.VMEM((j_rows, width), F32), pltpu.VMEM((width, j_pad), F32)],
        compiler_params=params(12),
        cost_estimate=cost(16 * macs, 2**20),
        name="right_rows",
    )(z_last, j_keep, keep, *rights)

    gl_cut = pl.pallas_call(
        functools.partial(left_kernel, dims, n_col),
        in_specs=[hbm()] + vmem(1 + len(z)),
        out_specs=vmem(2),
        out_shape=halves(i_rows * tiles, n_col),
        scratch_shapes=[pltpu.VMEM((i_rows * tiles, LANES), F32)],
        compiler_params=params(16),
        cost_estimate=cost(16 * macs, 2**20),
        name="left",
    )(rbig, right_turned, *z)
    y, diag, *gw_cut = pl.pallas_call(
        functools.partial(outer_kernel, dims, n_row, n_col),
        in_specs=[hbm()] + vmem(6),
        out_specs=vmem(4),
        out_shape=[
            pltpu.VMEM((i_rows, j_rows, inner), BF16),
            pltpu.VMEM((steps, depth, step_rows * LANES), BF16),
        ]
        + halves(inner, n_row),
        scratch_shapes=[
            pltpu.VMEM((i_rows, width), F32),
            pltpu.VMEM((i_rows * tiles, LANES), F32),
            pltpu.VMEM((LANES, groups * LANES), BF16),
            pltpu.VMEM((pair_width, inner), F32),
            pltpu.VMEM((inner, pair_width), F32),
        ],
        compiler_params=params(16),
        cost_estimate=cost(16 * macs, 2**20),
        name="outer",
    )(gl_cut[0], i_keep, keep, scaled, rbig, *lefts)

    def right_part(first, last, after, *so_far):
        return pl.pallas_call(
            functools.partial(right_part_kernel, first, last, len(z)),
            in_specs=[hbm()] + vmem(1 + len(z) + len(so_far)),
            out_specs=vmem()[0],
            out_shape=pltpu.VMEM((depth, span), F32),
            compiler_params=params(16),
            cost_estimate=cost(1000, 1000),
            name="right_part",
        )(after, diag, *z, *so_far)

    gw_row, acc = [], []
    right_steps = max(1, steps // 4)

    def weight_rounds(after):
        acc.append(right_part(0, right_steps, after))
        gw_row.extend(reduce(*gw_cut, "row", n_row, acc[0]))
        return gw_row[0]

    gl_last = reduce(*gl_cut, "col", n_col, gw_cut[0], weight_rounds)
    acc = right_part(right_steps, 2 * right_steps, gl_last[0], acc[0])
    gw_turned = small_call(
        functools.partial(turn_kernel, n_col),
        halves(inner // n_row, n_col),
        "turn",
        [pltpu.VMEM((inner // n_row, pair_width), F32)],
    )(acc, *gw_row)

    gr_cut = pl.pallas_call(
        functools.partial(right_kernel, dims, n_row, 2 * right_steps),
        in_specs=[hbm()] + vmem(2 + len(z)),
        out_specs=vmem(2),
        out_shape=halves(j_rows * tiles, n_row),
        scratch_shapes=[
            pltpu.VMEM((depth, span), F32),
            pltpu.VMEM((width, j_pad), F32),
            pltpu.VMEM((j_rows * tiles, LANES), F32),
        ],
        compiler_params=params(20),
        cost_estimate=cost(16 * macs, 2**20),
        name="right",
    )(gw_turned[0], diag, acc, *z)
    gr_held = []

    def right_rounds(after):
        gr_held.extend(hold(after, *gr_cut))
        return gr_held[0]

    gw_last = reduce(*gw_turned, "col", n_col, gr_cut[0], right_rounds)
    gr_last = reduce(*gr_held, "row", n_row, gw_last[0])

    pair_out, grad_left = pl.pallas_call(
        functools.partial(pair_kernel, dims),
        in_specs=[hbm()] + vmem(7),
        out_specs=[hbm()] * 2,
        out_shape=[
            jax.ShapeDtypeStruct(cotangent.shape, BF16),
            jax.ShapeDtypeStruct((own_left, width), F32),
        ],
        scratch_shapes=[
            pltpu.VMEM(cotangent.shape, BF16),
            pltpu.VMEM((own_left * tiles, LANES), F32),
            pltpu.VMEM((own_left, width), F32),
            pltpu.SemaphoreType.DMA((1 + i_rows // PIECE,)),
        ],
        compiler_params=params(12),
        cost_estimate=cost(16 * macs, 2**20),
        name="pair",
    )(gr_last[0], i_keep, y, weight, inverse, keep, *gl_last)

    owned = (inner // n_row // n_col, pair_width)
    grad_right, grad_weight = pl.pallas_call(
        final_kernel,
        in_specs=[hbm()] + vmem(6),
        out_specs=[hbm()] * 2,
        out_shape=[
            jax.ShapeDtypeStruct((own_right, width), F32),
            jax.ShapeDtypeStruct(owned, F32),
        ],
        scratch_shapes=[
            pltpu.VMEM((own_right * tiles, LANES), F32),
            pltpu.VMEM((own_right, width), F32),
            pltpu.VMEM(owned, F32),
            pltpu.SemaphoreType.DMA((2,)),
        ],
        compiler_params=params(4),
        cost_estimate=cost(1000, 1000),
        name="final_sums",
    )(in_hbm(pair_out), j_keep, keep, *gr_last, *gw_last)
    return (pair_out, grad_left, grad_right, grad_weight)


def solution(mesh):
    placed = (
        P(("grp", "row", "col"), None),
        P(("grp", "col", "row"), None),
        P("grp"),
        P("grp"),
        P(),
        P(("grp", "row"), "col", None),
    )
    return jax.shard_map(
        shards,
        mesh=mesh,
        in_specs=placed,
        out_specs=(
            P(("grp", "row"), "col", None),
            P(("grp", "row", "col"), None),
            P(("grp", "col", "row"), None),
            P(("grp", "row", "col"), None),
        ),
        check_vma=False,
    )
```

```python
import functools

import jax
import jax.numpy as jnp
from jax import lax
from jax.experimental import pallas as pl
from jax.experimental.pallas import tpu as pltpu
from jax.sharding import PartitionSpec as P

LANES = 128
CHUNK = 4
PIECE = 8
NT = (((1,), (1,)), ((), ()))
F32 = jnp.float32
BF16 = jnp.bfloat16


def params(mib):
    return pltpu.CompilerParams(vmem_limit_bytes=mib * 2**20)


def cost(flops, nbytes):
    return pl.CostEstimate(flops=int(flops), bytes_accessed=int(nbytes), transcendentals=0)


def cut(source, index, n, keep_ref, send_ref):
    rows = source.shape[0] // n
    for k in range(n):
        at = pl.multiple_of((index ^ k) * rows, rows)
        into = send_ref if k % 2 else keep_ref
        into[k // 2] = source[pl.ds(at, rows), :].astype(into.dtype)


def place(buffers, index, n, flat):
    for buffer, owners in zip(buffers, owners_of(n)):
        rows = buffer.shape[1]
        for k, owner in enumerate(owners):
            at = pl.multiple_of((index ^ owner) * rows, 8)
            flat[pl.ds(at, rows), :] = buffer[k].astype(F32)


def paired(j_rows):
    return 2 * j_rows == LANES


def slot_of(tile, tiles, j_rows):
    return tile % 2 * (tiles // 2) + tile // 2 if paired(j_rows) else tile


def swap_halves(low, first, second):
    half = LANES // 2
    return (
        jnp.where(low, first, pltpu.roll(second, half, axis=1)),
        jnp.where(low, pltpu.roll(first, half, axis=1), second),
    )


def lane_group(shape, chans):
    return lax.broadcasted_iota(jnp.int32, shape, 1) // chans


def mask_rows(res_ref, first, count):
    shape = (count, res_ref.shape[1])
    row = lax.broadcasted_iota(jnp.int32, shape, 0) + first
    here = lax.broadcasted_iota(jnp.int32, shape, 1) == row
    chosen = jnp.where(here, res_ref[...].astype(F32), 0.0)
    return jnp.broadcast_to(jnp.sum(chosen, axis=1, keepdims=True), (count, LANES))


def scale_kernel(dims, *refs):
    chans, groups, blocks, i_rows, j_rows, step_rows, sequences = dims
    tiles = sequences * chans // LANES
    res_hbm, seq_hbm, cot_ref, w_hbm, left_hbm, right_hbm = refs[:6]
    scaled_ref, inv_ref, wp_ref, keep_ref, ri_ref, rj_ref, left_ref, right_ref, z_ref = refs[6:15]
    res_ref, seq_ref, w_ref, w32, cot, sems, more_sems = refs[15:]
    steps = i_rows // step_rows

    def fetch(piece):
        rows = pl.ds(piece * step_rows, step_rows)
        return pltpu.make_async_copy(cot_ref.at[rows], cot.at[rows], sems.at[piece])

    pairs = [
        (res_hbm, res_ref),
        (seq_hbm, seq_ref),
        (w_hbm, w_ref),
        (left_hbm, left_ref.at[0]),
        (right_hbm, right_ref.at[0]),
    ]
    more = [
        pltpu.make_async_copy(source, to, more_sems.at[k]) for k, (source, to) in enumerate(pairs)
    ]
    for copy in more[:3]:
        copy.start()
    for piece in range(i_rows // step_rows):
        fetch(piece).start()
    for copy in more[3:]:
        copy.start()
    shape = (sequences, tiles * LANES)
    own = lax.broadcasted_iota(jnp.int32, shape, 1) // chans
    repeat = (own == lax.broadcasted_iota(jnp.int32, shape, 0)).astype(F32).astype(BF16)
    more[0].wait()
    ri_ref[...] = mask_rows(res_ref, lax.axis_index("row") * i_rows, i_rows)
    rj_ref[...] = mask_rows(res_ref, lax.axis_index("col") * j_rows, j_rows)
    more[1].wait()
    seq = seq_ref[...].astype(F32)
    keep_ref[...] = jnp.dot(
        jnp.broadcast_to(seq, (8, sequences)).astype(BF16), repeat, preferred_element_type=F32
    )[0:1]
    valid = jnp.sum(seq, axis=1, keepdims=True)
    inv_ref[...] = 1.0 / jnp.maximum(valid * rj_ref[...], 1.0)
    more[2].wait()
    w32[...] = w_ref[...].astype(F32)
    for e in range(chans):
        wp_ref[e * chans : (e + 1) * chans, :] = w32[pl.ds(e, chans, stride=chans), :].astype(BF16)
    for piece in range(i_rows // step_rows):
        fetch(piece).wait()
    for step in range(steps):
        for at in range(step * step_rows, (step + 1) * step_rows):
            inverse = jnp.where(ri_ref[at : at + 1, :] > 0, inv_ref[...], 1.0)
            scaled_ref[at] = (cot[at].astype(F32) * inverse).astype(BF16)
        if step < z_ref.shape[0]:
            rows = slice(step * step_rows, (step + 1) * step_rows)
            inner_rows(dims, scaled_ref[rows], wp_ref, z_ref, step)
    more[3].wait()
    more[4].wait()


def inner_rows(dims, scaled, wp_ref, z_ref, at):
    chans, groups, blocks, i_rows, j_rows, step_rows, sequences = dims
    for first in range(0, blocks, CHUNK):
        part = lax.dot_general(
            scaled.reshape(step_rows * j_rows, LANES),
            wp_ref[first * LANES : (first + CHUNK) * LANES, :],
            NT,
            preferred_element_type=F32,
        ).astype(BF16)
        for k in range(CHUNK):
            a = first + k
            for i in range(step_rows):
                z_ref[at, a * j_rows : (a + 1) * j_rows, i * LANES : (i + 1) * LANES] = part[
                    i * j_rows : (i + 1) * j_rows, k * LANES : (k + 1) * LANES
                ]


def inner_kernel(dims, first, after, scaled_ref, wp_ref, z_ref):
    step_rows = dims[5]
    for at in range(z_ref.shape[0]):
        rows = slice((first + at) * step_rows, (first + at + 1) * step_rows)
        inner_rows(dims, scaled_ref[rows], wp_ref, z_ref, at)


def at_step(refs, step):
    for ref in refs:
        if step < ref.shape[0]:
            return ref.at[step]
        step -= ref.shape[0]


def outer_kernel(dims, n_row, n_col, *refs):
    chans, groups, blocks, i_rows, j_rows, step_rows, sequences = dims
    tiles = sequences * chans // LANES
    after, ri_ref, keep_ref, scaled_ref, rbig, left_held, left_came = refs[:7]
    y_ref, diag_ref, keep_out, send_out = refs[7:11]
    flat, lsplit, expand, gwt, gwr = refs[11:]
    place((left_held, left_came), lax.axis_index("col"), n_col, flat)
    for t in range(tiles):
        lanes = slice(t * LANES, (t + 1) * LANES)
        masked = flat[0:i_rows, lanes] * ri_ref[...] * keep_ref[:, lanes]
        lsplit[pl.ds(slot_of(t, tiles, j_rows), i_rows, stride=tiles), :] = masked
    shape = (LANES, groups * LANES)
    source = lax.broadcasted_iota(jnp.int32, shape, 0)
    target = lax.broadcasted_iota(jnp.int32, shape, 1)
    same = (source // chans == target // LANES) & (source % chans == target % chans)
    expand[...] = same.astype(F32).astype(BF16)
    group = lane_group((tiles, LANES), chans)
    masks = [(group == b).astype(F32).astype(BF16) for b in range(groups)]
    deep_rows = 2 * step_rows if i_rows % (2 * step_rows) == 0 else step_rows

    for step in range(i_rows // step_rows):
        if step * step_rows % deep_rows == 0:
            rows = slice(step * step_rows * tiles, (step * step_rows + deep_rows) * tiles)
            spread = jnp.dot(
                lsplit[rows, :].astype(BF16), expand[...], preferred_element_type=F32
            ).astype(BF16)
            for i in range(deep_rows):
                block, at = divmod(step * step_rows + i, step_rows)
                for b in range(groups):
                    for lo in range(groups):
                        first = b * sequences + lo * tiles
                        diag_ref[
                            block, first : first + tiles, at * LANES : (at + 1) * LANES
                        ] = (
                            spread[i * tiles : (i + 1) * tiles, lo * LANES : (lo + 1) * LANES]
                            * masks[b]
                        )
        for first in range(0, step_rows, CHUNK):
            part = jnp.dot(
                rbig[...],
                diag_ref[step, :, first * LANES : (first + CHUNK) * LANES],
                preferred_element_type=F32,
            ).astype(BF16)
            for k in range(CHUNK):
                for a in range(blocks):
                    y_ref[step * step_rows + first + k, :, a * LANES : (a + 1) * LANES] = part[
                        a * j_rows : (a + 1) * j_rows, k * LANES : (k + 1) * LANES
                    ]
        if (step + 1) * step_rows % deep_rows == 0:
            block = slice((step + 1) * step_rows - deep_rows, (step + 1) * step_rows)
            scaled_t = scaled_ref[block].reshape(deep_rows * j_rows, LANES).T
            y_flat = y_ref[block].reshape(deep_rows * j_rows, blocks * LANES)
            part = jnp.dot(scaled_t, y_flat, preferred_element_type=F32)
            gwt[...] = gwt[...] + part if block.start else part
    for k in range(blocks):
        turned_tile = gwt[:, k * LANES : (k + 1) * LANES].T
        for q in range(groups):
            gwr[pl.ds(k * groups + q, chans, stride=chans), :] = turned_tile[
                q * chans : (q + 1) * chans
            ]
    cut(gwr, lax.axis_index("row"), n_row, keep_out, send_out)


def right_sum(first, last, z_refs, diag_ref, acc, so_far=None):
    for step in range(first, last):
        part = lax.dot_general(
            diag_ref[step], at_step(z_refs, step)[...], NT, preferred_element_type=F32
        )
        acc[...] = part if so_far is None else so_far[...] + part
        so_far = acc


def right_part_kernel(first, last, parts, after, diag_ref, *refs):
    right_sum(first, last, refs[:parts], diag_ref, refs[-1], *refs[parts:-1])


def right_kernel(dims, n_row, after, acc, keep_out, send_out, turned, gr_all):
    chans, groups, blocks, i_rows, j_rows, step_rows, sequences = dims
    tiles = sequences * chans // LANES
    j_pad = -(-j_rows // LANES) * LANES
    if paired(j_rows):
        half = tiles // 2
        low = lane_group((half, LANES), LANES // 2) == 0
        for a in range(0, blocks, 2):
            lanes = slice(a * j_rows, (a + 2) * j_rows)
            for b in range(groups):
                for lo in range(groups):
                    first = b * sequences + lo * tiles
                    both = swap_halves(
                        low,
                        acc[first : first + half, lanes],
                        acc[first + half : first + tiles, lanes],
                    )
                    at = lo * chans + groups * a + b
                    turned[pl.ds(at, half, stride=LANES), :] = both[0]
                    turned[pl.ds(at + groups, half, stride=LANES), :] = both[1]
        for pair in range(half):
            block = turned[pair * LANES : (pair + 1) * LANES, :].T
            for k in range(2):
                gr_all[pl.ds(2 * pair + k, j_rows, stride=tiles), :] = block[
                    k * j_rows : (k + 1) * j_rows
                ]
    else:
        for a in range(blocks):
            at, shift = divmod(a * j_rows, LANES)
            mine = acc[:, at * LANES : at * LANES + j_pad]
            if shift:
                mine = pltpu.roll(mine, LANES - shift, axis=1)
            for b in range(groups):
                for lo in range(groups):
                    first = b * sequences + lo * tiles
                    turned[pl.ds(lo * chans + groups * a + b, tiles, stride=LANES), :] = mine[
                        first : first + tiles
                    ]
        for t in range(tiles):
            lanes = slice(t * LANES, (t + 1) * LANES)
            gr_all[pl.ds(t, j_rows, stride=tiles), :] = turned[lanes, :].T[:j_rows]
    cut(gr_all, lax.axis_index("row"), n_row, keep_out, send_out)


def right_rows_kernel(dims, n_row, after, rj_ref, keep_ref, right_held, right_came, *refs):
    chans, groups, blocks, i_rows, j_rows, step_rows, sequences = dims
    tiles = sequences * chans // LANES
    j_pad = -(-j_rows // LANES) * LANES
    rbig, rbt_ref, flat, turned = refs
    place((right_held, right_came), lax.axis_index("row"), n_row, flat)
    if paired(j_rows):
        half = tiles // 2
        low = lane_group((half, LANES), LANES // 2) == 0
        for pair in range(half):
            rows = []
            for t in (2 * pair, 2 * pair + 1):
                lanes = slice(t * LANES, (t + 1) * LANES)
                rows.append(flat[0:j_rows, lanes] * rj_ref[...] * keep_ref[:, lanes])
            turned[pair * LANES : (pair + 1) * LANES, :] = jnp.concatenate(rows, axis=0).T
        for a in range(0, blocks, 2):
            parts = []
            for b in range(groups):
                for lo in range(groups):
                    at = lo * chans + groups * a + b
                    parts += swap_halves(
                        low,
                        turned[pl.ds(at, half, stride=LANES), :],
                        turned[pl.ds(at + groups, half, stride=LANES), :],
                    )
            block = jnp.concatenate(parts, axis=0)
            lanes = slice(a * j_rows, (a + 2) * j_rows)
            rbt_ref[:, lanes] = block.astype(BF16)
            rbig[lanes, :] = block.T.astype(BF16)
    else:
        for t in range(tiles):
            lanes = slice(t * LANES, (t + 1) * LANES)
            masked = flat[0:j_rows, lanes] * rj_ref[...] * keep_ref[:, lanes]
            if j_rows < j_pad:
                masked = jnp.concatenate([masked, jnp.zeros((j_pad - j_rows, LANES), F32)], axis=0)
            turned[lanes, :] = masked.T
        for a in range(blocks):
            parts = [
                turned[pl.ds(lo * chans + groups * a + b, tiles, stride=LANES), :]
                for b in range(groups)
                for lo in range(groups)
            ]
            block = jnp.concatenate(parts, axis=0)
            rbig[a * j_rows : (a + 1) * j_rows, :] = block.T[:j_rows].astype(BF16)
        rbt_ref[...] = rbig[...].T


def left_kernel(dims, n_col, after, rbt_ref, *refs):
    chans, groups, blocks, i_rows, j_rows, step_rows, sequences = dims
    tiles = sequences * chans // LANES
    z_refs, (keep_out, send_out, gl_all) = refs[:-3], refs[-3:]
    group = lane_group((sequences, LANES), chans)
    group_t = lane_group((tiles, LANES), chans)

    for step in range(i_rows // step_rows):
        z_ref = at_step(z_refs, step)
        for first in range(0, step_rows, CHUNK):
            part = jnp.dot(
                rbt_ref[...],
                z_ref[:, first * LANES : (first + CHUNK) * LANES],
                preferred_element_type=F32,
            )
            for k in range(CHUNK):
                mine = part[:, k * LANES : (k + 1) * LANES]
                total = mine[0:sequences]
                for b in range(1, groups):
                    total = jnp.where(group == b, mine[b * sequences : (b + 1) * sequences], total)
                shift = LANES // 2
                while shift >= chans:
                    total = total + pltpu.roll(total, shift, axis=1)
                    shift //= 2
                merged = total[0:tiles]
                for lo in range(1, groups):
                    merged = jnp.where(group_t == lo, total[lo * tiles : (lo + 1) * tiles], merged)
                at = (step * step_rows + first + k) * tiles
                gl_all[at : at + tiles, :] = merged
    cut(gl_all, lax.axis_index("col"), n_col, keep_out, send_out)


def total_of(keep_ref, came_ref, k=0):
    return keep_ref[k].astype(F32) + came_ref[k].astype(F32)


def join_kernel(after, held_ref, came_ref, out_ref):
    count = held_ref.shape[0]
    for k in range(count):
        out_ref[k] = held_ref[k]
        out_ref[count + k] = came_ref[k]


def fold_kernel(after, held_ref, came_ref, keep_out, send_out):
    for k in range(held_ref.shape[0]):
        into = send_out if k % 2 else keep_out
        into[k // 2] = total_of(held_ref, came_ref, k).astype(into.dtype)


def copy_kernel(after, *refs):
    count = len(refs) // 2
    for source, to in zip(refs[:count], refs[count:]):
        to[...] = source[...]


def turn_kernel(n_col, after, held_ref, came_ref, keep_out, send_out, whole):
    whole[...] = total_of(held_ref, came_ref)
    cut(whole, lax.axis_index("col"), n_col, keep_out, send_out)


def write_rows(whole, rows, keep_ref, out_ref, slots):
    own = out_ref.shape[0]
    tiles = len(slots)
    for t, slot in enumerate(slots):
        lanes = slice(t * LANES, (t + 1) * LANES)
        out_ref[:, lanes] = whole[pl.ds(slot, own, stride=tiles), :] * (
            rows * keep_ref[:, lanes]
        )


def pair_kernel(dims, *refs):
    after, ri_ref, y_ref, wp_ref, inv_ref, keep_ref, held, came = refs[:8]
    out_ref, gl_out, staged, whole, left, sems = refs[8:]
    i_rows, j_rows = dims[3:5]
    own = left.shape[0]
    first = pl.multiple_of(lax.axis_index("col") * own, 8)
    whole[...] = total_of(held, came)
    tiles = whole.shape[0] // own
    slots = [slot_of(t, tiles, j_rows) for t in range(tiles)]
    write_rows(whole, ri_ref[pl.ds(first, own), :], keep_ref, left, slots)
    copies = [pltpu.make_async_copy(left, gl_out, sems.at[0])]
    copies[0].start()
    for row in range(0, i_rows, PIECE):
        y_flat = y_ref[row : row + PIECE].reshape(PIECE * j_rows, y_ref.shape[2])
        projected = jnp.dot(y_flat, wp_ref[...], preferred_element_type=F32)
        for i in range(PIECE):
            inverse = jnp.where(ri_ref[row + i : row + i + 1, :] > 0, inv_ref[...], 1.0)
            staged[row + i] = (projected[i * j_rows : (i + 1) * j_rows] * inverse).astype(BF16)
        rows = pl.ds(row, PIECE)
        copies.append(
            pltpu.make_async_copy(staged.at[rows], out_ref.at[rows], sems.at[len(copies)])
        )
        copies[-1].start()
    for copy in copies:
        copy.wait()


def final_kernel(after, rj_ref, keep_ref, *refs):
    right, weight = refs[0:2], refs[2:4]
    gr_out, gw_out, whole, rows, weight_rows, sems = refs[4:]
    weight_rows[...] = total_of(*weight)
    copies = [pltpu.make_async_copy(weight_rows, gw_out, sems.at[0])]
    copies[0].start()
    own = rows.shape[0]
    first = pl.multiple_of(lax.axis_index("row") * own, 8)
    whole[...] = total_of(*right)
    slots = range(whole.shape[0] // own)
    write_rows(whole, rj_ref[pl.ds(first, own), :], keep_ref, rows, slots)
    copies.append(pltpu.make_async_copy(rows, gr_out, sems.at[1]))
    copies[1].start()
    for copy in copies:
        copy.wait()


def swap(array, axis, n, bit):
    return lax.ppermute(array, axis, [(s, s ^ bit) for s in range(n)])


def owners_of(n):
    held, bit = [0], n // 2
    while bit > 1:
        held, bit = held + [k ^ bit for k in held], bit // 2
    return held, [k ^ 1 for k in held]


def gather(block, own, axis, n, after):
    held, sent, bit = own, block[None], n // 2
    while bit > 1:
        came = swap(sent, axis, n, bit)
        shape = (2 * held.shape[0],) + held.shape[1:]
        held = small_call(join_kernel, [pltpu.VMEM(shape, BF16)], "join")(after, held, came)[0]
        sent, bit = held, bit // 2
    return held, swap(sent, axis, n, 1)


def reduce(keep, send, axis, n, after, between=None):
    bit = 1
    while True:
        came = swap(send, axis, n, bit)
        bit *= 2
        if bit >= n:
            if between is not None:
                between(keep)
            return keep, came
        half = (keep.shape[0] // 2,) + keep.shape[1:]
        outs = [pltpu.VMEM(half, F32), pltpu.VMEM(half, BF16)]
        keep, send = small_call(fold_kernel, outs, "fold")(after, keep, came)
        if between is not None:
            gate, between = between(keep), None
            keep, send = hold(gate, keep, send)


def small_call(body, outs, name, scratch=(), flops=1000):
    def call(after, *operands):
        return pl.pallas_call(
            body,
            in_specs=[hbm()] + vmem(len(operands)),
            out_specs=vmem(len(outs)),
            out_shape=outs,
            scratch_shapes=list(scratch),
            compiler_params=params(4),
            cost_estimate=cost(flops, 1000),
            name=name,
        )(after, *operands)

    return call


def hold(after, *arrays):
    outs = [pltpu.VMEM(array.shape, array.dtype) for array in arrays]
    return small_call(copy_kernel, outs, "hold", flops=10**10)(after, *arrays)


def halves(rows, n):
    return [pltpu.VMEM((n // 2, rows // n, LANES), BF16)] * 2


def vmem(count=1):
    return [pl.BlockSpec(memory_space=pltpu.VMEM)] * count


def hbm():
    return pl.BlockSpec(memory_space=pl.ANY)


def in_hbm(array):
    return pltpu.with_memory_space_constraint(array, pltpu.HBM)


def shards(left_act, right_act, row_mask, res_mask, out_weight, cotangent):
    n_col = lax.axis_size("col")
    n_row = lax.axis_size("row")
    i_rows, j_rows, pair_width = cotangent.shape
    sequences = row_mask.shape[0]
    width = left_act.shape[1]
    chans = width // sequences
    groups = LANES // chans
    blocks = chans // groups
    tiles = width // LANES
    depth = groups * sequences
    inner = chans * chans
    step_rows = 16
    steps = i_rows // step_rows
    early_steps = steps // 2
    dims = (chans, groups, blocks, i_rows, j_rows, step_rows, sequences)
    j_pad = -(-j_rows // LANES) * LANES
    span = blocks * j_rows
    own_left, own_right = left_act.shape[0], right_act.shape[0]
    macs = i_rows * j_rows * inner * pair_width

    mask_row = (res_mask.reshape(1, -1), row_mask.reshape(1, -1))
    scaled, inverse, weight, keep, i_keep, j_keep, own_l, own_r, z_first = pl.pallas_call(
        functools.partial(scale_kernel, dims),
        in_specs=[hbm()] * 6,
        out_specs=vmem(9),
        out_shape=[
            pltpu.VMEM(cotangent.shape, BF16),
            pltpu.VMEM((j_rows, LANES), F32),
            pltpu.VMEM(out_weight.shape, BF16),
            pltpu.VMEM((1, width), F32),
            pltpu.VMEM((i_rows, LANES), F32),
            pltpu.VMEM((j_rows, LANES), F32),
            pltpu.VMEM((1,) + left_act.shape, BF16),
            pltpu.VMEM((1,) + right_act.shape, BF16),
            pltpu.VMEM((early_steps, span, step_rows * LANES), BF16),
        ],
        scratch_shapes=[
            pltpu.VMEM((1, res_mask.shape[0]), jnp.int32),
            pltpu.VMEM((1, sequences), jnp.int32),
            pltpu.VMEM(out_weight.shape, BF16),
            pltpu.VMEM(out_weight.shape, F32),
            pltpu.VMEM(cotangent.shape, BF16),
            pltpu.SemaphoreType.DMA((steps,)),
            pltpu.SemaphoreType.DMA((5,)),
        ],
        compiler_params=params(16),
        cost_estimate=cost(1000, 1000),
        name="scale",
    )(*map(in_hbm, (*mask_row, cotangent, out_weight, left_act, right_act)))

    lefts = gather(left_act, own_l, "col", n_col, own_l)
    rights = gather(right_act, own_r, "row", n_row, lefts[0])

    z_last = pl.pallas_call(
        functools.partial(inner_kernel, dims, early_steps),
        in_specs=[hbm()] + vmem(2),
        out_specs=vmem()[0],
        out_shape=pltpu.VMEM((steps - early_steps, span, step_rows * LANES), BF16),
        compiler_params=params(16),
        cost_estimate=cost(16 * macs, 2**20),
        name="inner",
    )(rights[0], scaled, weight)
    z = (z_first, z_last)

    rbig, right_turned = pl.pallas_call(
        functools.partial(right_rows_kernel, dims, n_row),
        in_specs=[hbm()] + vmem(4),
        out_specs=vmem(2),
        out_shape=[pltpu.VMEM((span, depth), BF16), pltpu.VMEM((depth, span), BF16)],
        scratch_shapes=[pltpu.VMEM((j_rows, width), F32), pltpu.VMEM((width, j_pad), F32)],
        compiler_params=params(12),
        cost_estimate=cost(16 * macs, 2**20),
        name="right_rows",
    )(z_last, j_keep, keep, *rights)

    gl_cut = pl.pallas_call(
        functools.partial(left_kernel, dims, n_col),
        in_specs=[hbm()] + vmem(1 + len(z)),
        out_specs=vmem(2),
        out_shape=halves(i_rows * tiles, n_col),
        scratch_shapes=[pltpu.VMEM((i_rows * tiles, LANES), F32)],
        compiler_params=params(16),
        cost_estimate=cost(16 * macs, 2**20),
        name="left",
    )(rbig, right_turned, *z)
    y, diag, *gw_cut = pl.pallas_call(
        functools.partial(outer_kernel, dims, n_row, n_col),
        in_specs=[hbm()] + vmem(6),
        out_specs=vmem(4),
        out_shape=[
            pltpu.VMEM((i_rows, j_rows, inner), BF16),
            pltpu.VMEM((steps, depth, step_rows * LANES), BF16),
        ]
        + halves(inner, n_row),
        scratch_shapes=[
            pltpu.VMEM((i_rows, width), F32),
            pltpu.VMEM((i_rows * tiles, LANES), F32),
            pltpu.VMEM((LANES, groups * LANES), BF16),
            pltpu.VMEM((pair_width, inner), F32),
            pltpu.VMEM((inner, pair_width), F32),
        ],
        compiler_params=params(16),
        cost_estimate=cost(16 * macs, 2**20),
        name="outer",
    )(gl_cut[0], i_keep, keep, scaled, rbig, *lefts)

    def right_part(first, last, after, *so_far):
        return pl.pallas_call(
            functools.partial(right_part_kernel, first, last, len(z)),
            in_specs=[hbm()] + vmem(1 + len(z) + len(so_far)),
            out_specs=vmem()[0],
            out_shape=pltpu.VMEM((depth, span), F32),
            compiler_params=params(16),
            cost_estimate=cost(16 * macs, 1000),
            name="right_part",
        )(after, diag, *z, *so_far)

    right_steps = max(1, steps // 4)
    acc = right_part(0, right_steps, gw_cut[0])
    gw_row = reduce(*gw_cut, "row", n_row, acc)
    gl_held = hold(gw_row[0], *gl_cut)
    acc = right_part(right_steps, steps, gl_held[0], acc)
    gw_turned = small_call(
        functools.partial(turn_kernel, n_col),
        halves(inner // n_row, n_col),
        "turn",
        [pltpu.VMEM((inner // n_row, pair_width), F32)],
    )(acc, *gw_row)
    gl_last = reduce(*gl_held, "col", n_col, gw_turned[0])


    gr_cut = pl.pallas_call(
        functools.partial(right_kernel, dims, n_row),
        in_specs=[hbm()] + vmem(),
        out_specs=vmem(2),
        out_shape=halves(j_rows * tiles, n_row),
        scratch_shapes=[
            pltpu.VMEM((width, j_pad), F32),
            pltpu.VMEM((j_rows * tiles, LANES), F32),
        ],
        compiler_params=params(20),
        cost_estimate=cost(16 * macs, 2**20),
        name="right",
    )(gl_last[0], acc)
    gr_held = []

    def right_rounds(after):
        gr_held.extend(hold(after, *gr_cut))
        return gr_held[0]

    gw_last = reduce(*gw_turned, "col", n_col, gr_cut[0], right_rounds)
    gr_last = reduce(*gr_held, "row", n_row, gw_last[0])

    pair_out, grad_left = pl.pallas_call(
        functools.partial(pair_kernel, dims),
        in_specs=[hbm()] + vmem(7),
        out_specs=[hbm()] * 2,
        out_shape=[
            jax.ShapeDtypeStruct(cotangent.shape, BF16),
            jax.ShapeDtypeStruct((own_left, width), F32),
        ],
        scratch_shapes=[
            pltpu.VMEM(cotangent.shape, BF16),
            pltpu.VMEM((own_left * tiles, LANES), F32),
            pltpu.VMEM((own_left, width), F32),
            pltpu.SemaphoreType.DMA((1 + i_rows // PIECE,)),
        ],
        compiler_params=params(12),
        cost_estimate=cost(16 * macs, 2**20),
        name="pair",
    )(gr_last[0], i_keep, y, weight, inverse, keep, *gl_last)

    owned = (inner // n_row // n_col, pair_width)
    grad_right, grad_weight = pl.pallas_call(
        final_kernel,
        in_specs=[hbm()] + vmem(6),
        out_specs=[hbm()] * 2,
        out_shape=[
            jax.ShapeDtypeStruct((own_right, width), F32),
            jax.ShapeDtypeStruct(owned, F32),
        ],
        scratch_shapes=[
            pltpu.VMEM((own_right * tiles, LANES), F32),
            pltpu.VMEM((own_right, width), F32),
            pltpu.VMEM(owned, F32),
            pltpu.SemaphoreType.DMA((2,)),
        ],
        compiler_params=params(4),
        cost_estimate=cost(1000, 1000),
        name="final_sums",
    )(in_hbm(pair_out), j_keep, keep, *gr_last, *gw_last)
    return (pair_out, grad_left, grad_right, grad_weight)


def solution(mesh):
    placed = (
        P(("grp", "row", "col"), None),
        P(("grp", "col", "row"), None),
        P("grp"),
        P("grp"),
        P(),
        P(("grp", "row"), "col", None),
    )
    return jax.shard_map(
        shards,
        mesh=mesh,
        in_specs=placed,
        out_specs=(
            P(("grp", "row"), "col", None),
            P(("grp", "row", "col"), None),
            P(("grp", "col", "row"), None),
            P(("grp", "row", "col"), None),
        ),
        check_vma=False,
    )
```

```python
import functools

import jax
import jax.numpy as jnp
from jax import lax
from jax.experimental import pallas as pl
from jax.experimental.pallas import tpu as pltpu
from jax.sharding import PartitionSpec as P

LANES = 128
CHUNK = 4
PIECE = 8
NT = (((1,), (1,)), ((), ()))
F32 = jnp.float32
BF16 = jnp.bfloat16


def params(mib):
    return pltpu.CompilerParams(vmem_limit_bytes=mib * 2**20)


def cost(flops, nbytes):
    return pl.CostEstimate(flops=int(flops), bytes_accessed=int(nbytes), transcendentals=0)


def cut(source, index, n, keep_ref, send_ref):
    rows = source.shape[0] // n
    for k in range(n):
        at = pl.multiple_of((index ^ k) * rows, rows)
        into = send_ref if k % 2 else keep_ref
        into[k // 2] = source[pl.ds(at, rows), :].astype(into.dtype)


def place(buffers, index, n, flat):
    for buffer, owners in zip(buffers, owners_of(n)):
        rows = buffer.shape[1]
        for k, owner in enumerate(owners):
            at = pl.multiple_of((index ^ owner) * rows, 8)
            flat[pl.ds(at, rows), :] = buffer[k].astype(F32)


def paired(j_rows):
    return 2 * j_rows == LANES


def slot_of(tile, tiles, j_rows):
    return tile % 2 * (tiles // 2) + tile // 2 if paired(j_rows) else tile


def swap_halves(low, first, second):
    half = LANES // 2
    return (
        jnp.where(low, first, pltpu.roll(second, half, axis=1)),
        jnp.where(low, pltpu.roll(first, half, axis=1), second),
    )


def lane_group(shape, chans):
    return lax.broadcasted_iota(jnp.int32, shape, 1) // chans


def mask_rows(res_ref, first, count):
    shape = (count, res_ref.shape[1])
    row = lax.broadcasted_iota(jnp.int32, shape, 0) + first
    here = lax.broadcasted_iota(jnp.int32, shape, 1) == row
    chosen = jnp.where(here, res_ref[...].astype(F32), 0.0)
    return jnp.broadcast_to(jnp.sum(chosen, axis=1, keepdims=True), (count, LANES))


def scale_kernel(dims, *refs):
    chans, groups, blocks, i_rows, j_rows, step_rows, sequences = dims
    tiles = sequences * chans // LANES
    res_hbm, seq_hbm, cot_ref, w_hbm, left_hbm, right_hbm = refs[:6]
    scaled_ref, inv_ref, wp_ref, keep_ref, ri_ref, rj_ref, left_ref, right_ref, z_ref = refs[6:15]
    res_ref, seq_ref, w_ref, w32, cot, sems, more_sems = refs[15:]
    steps = i_rows // step_rows

    def fetch(piece):
        rows = pl.ds(piece * step_rows, step_rows)
        return pltpu.make_async_copy(cot_ref.at[rows], cot.at[rows], sems.at[piece])

    pairs = [
        (res_hbm, res_ref),
        (seq_hbm, seq_ref),
        (w_hbm, w_ref),
        (left_hbm, left_ref.at[0]),
        (right_hbm, right_ref.at[0]),
    ]
    more = [
        pltpu.make_async_copy(source, to, more_sems.at[k]) for k, (source, to) in enumerate(pairs)
    ]
    for copy in more[:3]:
        copy.start()
    for piece in range(i_rows // step_rows):
        fetch(piece).start()
    for copy in more[3:]:
        copy.start()
    shape = (sequences, tiles * LANES)
    own = lax.broadcasted_iota(jnp.int32, shape, 1) // chans
    repeat = (own == lax.broadcasted_iota(jnp.int32, shape, 0)).astype(F32).astype(BF16)
    more[0].wait()
    ri_ref[...] = mask_rows(res_ref, lax.axis_index("row") * i_rows, i_rows)
    rj_ref[...] = mask_rows(res_ref, lax.axis_index("col") * j_rows, j_rows)
    more[1].wait()
    seq = seq_ref[...].astype(F32)
    keep_ref[...] = jnp.dot(
        jnp.broadcast_to(seq, (8, sequences)).astype(BF16), repeat, preferred_element_type=F32
    )[0:1]
    valid = jnp.sum(seq, axis=1, keepdims=True)
    inv_ref[...] = 1.0 / jnp.maximum(valid * rj_ref[...], 1.0)
    more[2].wait()
    w32[...] = w_ref[...].astype(F32)
    for e in range(chans):
        wp_ref[e * chans : (e + 1) * chans, :] = w32[pl.ds(e, chans, stride=chans), :].astype(BF16)
    for piece in range(i_rows // step_rows):
        fetch(piece).wait()
    for step in range(steps):
        for at in range(step * step_rows, (step + 1) * step_rows):
            inverse = jnp.where(ri_ref[at : at + 1, :] > 0, inv_ref[...], 1.0)
            scaled_ref[at] = (cot[at].astype(F32) * inverse).astype(BF16)
        if step < z_ref.shape[0]:
            rows = slice(step * step_rows, (step + 1) * step_rows)
            inner_rows(dims, scaled_ref[rows], wp_ref, z_ref, step)
    more[3].wait()
    more[4].wait()


def inner_rows(dims, scaled, wp_ref, z_ref, at):
    chans, groups, blocks, i_rows, j_rows, step_rows, sequences = dims
    for first in range(0, blocks, CHUNK):
        part = lax.dot_general(
            scaled.reshape(step_rows * j_rows, LANES),
            wp_ref[first * LANES : (first + CHUNK) * LANES, :],
            NT,
            preferred_element_type=F32,
        ).astype(BF16)
        for k in range(CHUNK):
            a = first + k
            for i in range(step_rows):
                z_ref[at, a * j_rows : (a + 1) * j_rows, i * LANES : (i + 1) * LANES] = part[
                    i * j_rows : (i + 1) * j_rows, k * LANES : (k + 1) * LANES
                ]


def inner_kernel(dims, first, after, scaled_ref, wp_ref, z_ref):
    step_rows = dims[5]
    for at in range(z_ref.shape[0]):
        rows = slice((first + at) * step_rows, (first + at + 1) * step_rows)
        inner_rows(dims, scaled_ref[rows], wp_ref, z_ref, at)


def at_step(refs, step):
    for ref in refs:
        if step < ref.shape[0]:
            return ref.at[step]
        step -= ref.shape[0]


def outer_kernel(dims, n_row, n_col, *refs):
    chans, groups, blocks, i_rows, j_rows, step_rows, sequences = dims
    tiles = sequences * chans // LANES
    after, ri_ref, keep_ref, scaled_ref, rbig, left_held, left_came = refs[:7]
    y_ref, diag_ref, keep_out, send_out = refs[7:11]
    flat, lsplit, expand, gwt, gwr = refs[11:]
    place((left_held, left_came), lax.axis_index("col"), n_col, flat)
    for t in range(tiles):
        lanes = slice(t * LANES, (t + 1) * LANES)
        masked = flat[0:i_rows, lanes] * ri_ref[...] * keep_ref[:, lanes]
        lsplit[pl.ds(slot_of(t, tiles, j_rows), i_rows, stride=tiles), :] = masked
    shape = (LANES, groups * LANES)
    source = lax.broadcasted_iota(jnp.int32, shape, 0)
    target = lax.broadcasted_iota(jnp.int32, shape, 1)
    same = (source // chans == target // LANES) & (source % chans == target % chans)
    expand[...] = same.astype(F32).astype(BF16)
    group = lane_group((tiles, LANES), chans)
    masks = [(group == b).astype(F32).astype(BF16) for b in range(groups)]
    deep_rows = 2 * step_rows if i_rows % (2 * step_rows) == 0 else step_rows

    for step in range(i_rows // step_rows):
        if step * step_rows % deep_rows == 0:
            rows = slice(step * step_rows * tiles, (step * step_rows + deep_rows) * tiles)
            spread = jnp.dot(
                lsplit[rows, :].astype(BF16), expand[...], preferred_element_type=F32
            ).astype(BF16)
            for i in range(deep_rows):
                block, at = divmod(step * step_rows + i, step_rows)
                for b in range(groups):
                    for lo in range(groups):
                        first = b * sequences + lo * tiles
                        diag_ref[
                            block, first : first + tiles, at * LANES : (at + 1) * LANES
                        ] = (
                            spread[i * tiles : (i + 1) * tiles, lo * LANES : (lo + 1) * LANES]
                            * masks[b]
                        )
        for first in range(0, step_rows, CHUNK):
            part = jnp.dot(
                rbig[...],
                diag_ref[step, :, first * LANES : (first + CHUNK) * LANES],
                preferred_element_type=F32,
            ).astype(BF16)
            for k in range(CHUNK):
                for a in range(blocks):
                    y_ref[step * step_rows + first + k, :, a * LANES : (a + 1) * LANES] = part[
                        a * j_rows : (a + 1) * j_rows, k * LANES : (k + 1) * LANES
                    ]
        if (step + 1) * step_rows % deep_rows == 0:
            block = slice((step + 1) * step_rows - deep_rows, (step + 1) * step_rows)
            scaled_t = scaled_ref[block].reshape(deep_rows * j_rows, LANES).T
            y_flat = y_ref[block].reshape(deep_rows * j_rows, blocks * LANES)
            part = jnp.dot(scaled_t, y_flat, preferred_element_type=F32)
            gwt[...] = gwt[...] + part if block.start else part
    for k in range(blocks):
        turned_tile = gwt[:, k * LANES : (k + 1) * LANES].T
        for q in range(groups):
            gwr[pl.ds(k * groups + q, chans, stride=chans), :] = turned_tile[
                q * chans : (q + 1) * chans
            ]
    cut(gwr, lax.axis_index("row"), n_row, keep_out, send_out)


def right_sum(first, last, z_refs, diag_ref, acc, so_far=None):
    for step in range(first, last):
        part = lax.dot_general(
            diag_ref[step], at_step(z_refs, step)[...], NT, preferred_element_type=F32
        )
        acc[...] = part if so_far is None else so_far[...] + part
        so_far = acc


def right_part_kernel(first, last, parts, after, diag_ref, *refs):
    right_sum(first, last, refs[:parts], diag_ref, refs[-1], *refs[parts:-1])


def right_kernel(dims, n_row, first, after, diag_ref, acc_first, *refs):
    chans, groups, blocks, i_rows, j_rows, step_rows, sequences = dims
    tiles = sequences * chans // LANES
    j_pad = -(-j_rows // LANES) * LANES
    z_refs, (keep_out, send_out, acc, turned, gr_all) = refs[:-5], refs[-5:]
    right_sum(first, i_rows // step_rows, z_refs, diag_ref, acc, acc_first)
    if paired(j_rows):
        half = tiles // 2
        low = lane_group((half, LANES), LANES // 2) == 0
        for a in range(0, blocks, 2):
            lanes = slice(a * j_rows, (a + 2) * j_rows)
            for b in range(groups):
                for lo in range(groups):
                    first = b * sequences + lo * tiles
                    both = swap_halves(
                        low,
                        acc[first : first + half, lanes],
                        acc[first + half : first + tiles, lanes],
                    )
                    at = lo * chans + groups * a + b
                    turned[pl.ds(at, half, stride=LANES), :] = both[0]
                    turned[pl.ds(at + groups, half, stride=LANES), :] = both[1]
        for pair in range(half):
            block = turned[pair * LANES : (pair + 1) * LANES, :].T
            for k in range(2):
                gr_all[pl.ds(2 * pair + k, j_rows, stride=tiles), :] = block[
                    k * j_rows : (k + 1) * j_rows
                ]
    else:
        for a in range(blocks):
            at, shift = divmod(a * j_rows, LANES)
            mine = acc[:, at * LANES : at * LANES + j_pad]
            if shift:
                mine = pltpu.roll(mine, LANES - shift, axis=1)
            for b in range(groups):
                for lo in range(groups):
                    first = b * sequences + lo * tiles
                    turned[pl.ds(lo * chans + groups * a + b, tiles, stride=LANES), :] = mine[
                        first : first + tiles
                    ]
        for t in range(tiles):
            lanes = slice(t * LANES, (t + 1) * LANES)
            gr_all[pl.ds(t, j_rows, stride=tiles), :] = turned[lanes, :].T[:j_rows]
    cut(gr_all, lax.axis_index("row"), n_row, keep_out, send_out)


def right_rows_kernel(dims, n_row, after, rj_ref, keep_ref, right_held, right_came, *refs):
    chans, groups, blocks, i_rows, j_rows, step_rows, sequences = dims
    tiles = sequences * chans // LANES
    j_pad = -(-j_rows // LANES) * LANES
    rbig, rbt_ref, flat, turned = refs
    place((right_held, right_came), lax.axis_index("row"), n_row, flat)
    if paired(j_rows):
        half = tiles // 2
        low = lane_group((half, LANES), LANES // 2) == 0
        for pair in range(half):
            rows = []
            for t in (2 * pair, 2 * pair + 1):
                lanes = slice(t * LANES, (t + 1) * LANES)
                rows.append(flat[0:j_rows, lanes] * rj_ref[...] * keep_ref[:, lanes])
            turned[pair * LANES : (pair + 1) * LANES, :] = jnp.concatenate(rows, axis=0).T
        for a in range(0, blocks, 2):
            parts = []
            for b in range(groups):
                for lo in range(groups):
                    at = lo * chans + groups * a + b
                    parts += swap_halves(
                        low,
                        turned[pl.ds(at, half, stride=LANES), :],
                        turned[pl.ds(at + groups, half, stride=LANES), :],
                    )
            block = jnp.concatenate(parts, axis=0)
            lanes = slice(a * j_rows, (a + 2) * j_rows)
            rbt_ref[:, lanes] = block.astype(BF16)
            rbig[lanes, :] = block.T.astype(BF16)
    else:
        for t in range(tiles):
            lanes = slice(t * LANES, (t + 1) * LANES)
            masked = flat[0:j_rows, lanes] * rj_ref[...] * keep_ref[:, lanes]
            if j_rows < j_pad:
                masked = jnp.concatenate([masked, jnp.zeros((j_pad - j_rows, LANES), F32)], axis=0)
            turned[lanes, :] = masked.T
        for a in range(blocks):
            parts = [
                turned[pl.ds(lo * chans + groups * a + b, tiles, stride=LANES), :]
                for b in range(groups)
                for lo in range(groups)
            ]
            block = jnp.concatenate(parts, axis=0)
            rbig[a * j_rows : (a + 1) * j_rows, :] = block.T[:j_rows].astype(BF16)
        rbt_ref[...] = rbig[...].T


def left_kernel(dims, n_col, after, rbt_ref, *refs):
    chans, groups, blocks, i_rows, j_rows, step_rows, sequences = dims
    tiles = sequences * chans // LANES
    z_refs, (keep_out, send_out, gl_all) = refs[:-3], refs[-3:]
    group = lane_group((sequences, LANES), chans)
    group_t = lane_group((tiles, LANES), chans)

    for step in range(i_rows // step_rows):
        z_ref = at_step(z_refs, step)
        for first in range(0, step_rows, CHUNK):
            part = jnp.dot(
                rbt_ref[...],
                z_ref[:, first * LANES : (first + CHUNK) * LANES],
                preferred_element_type=F32,
            )
            for k in range(CHUNK):
                mine = part[:, k * LANES : (k + 1) * LANES]
                total = mine[0:sequences]
                for b in range(1, groups):
                    total = jnp.where(group == b, mine[b * sequences : (b + 1) * sequences], total)
                shift = LANES // 2
                while shift >= chans:
                    total = total + pltpu.roll(total, shift, axis=1)
                    shift //= 2
                merged = total[0:tiles]
                for lo in range(1, groups):
                    merged = jnp.where(group_t == lo, total[lo * tiles : (lo + 1) * tiles], merged)
                at = (step * step_rows + first + k) * tiles
                gl_all[at : at + tiles, :] = merged
    cut(gl_all, lax.axis_index("col"), n_col, keep_out, send_out)


def total_of(keep_ref, came_ref, k=0):
    return keep_ref[k].astype(F32) + came_ref[k].astype(F32)


def join_kernel(after, held_ref, came_ref, out_ref):
    count = held_ref.shape[0]
    for k in range(count):
        out_ref[k] = held_ref[k]
        out_ref[count + k] = came_ref[k]


def fold_kernel(after, held_ref, came_ref, keep_out, send_out):
    for k in range(held_ref.shape[0]):
        into = send_out if k % 2 else keep_out
        into[k // 2] = total_of(held_ref, came_ref, k).astype(into.dtype)


def copy_kernel(after, *refs):
    count = len(refs) // 2
    for source, to in zip(refs[:count], refs[count:]):
        to[...] = source[...]


def turn_kernel(n_col, after, held_ref, came_ref, keep_out, send_out, whole):
    whole[...] = total_of(held_ref, came_ref)
    cut(whole, lax.axis_index("col"), n_col, keep_out, send_out)


def write_rows(whole, rows, keep_ref, out_ref, slots):
    own = out_ref.shape[0]
    tiles = len(slots)
    for t, slot in enumerate(slots):
        lanes = slice(t * LANES, (t + 1) * LANES)
        out_ref[:, lanes] = whole[pl.ds(slot, own, stride=tiles), :] * (
            rows * keep_ref[:, lanes]
        )


def pair_kernel(dims, *refs):
    after, ri_ref, y_ref, wp_ref, inv_ref, keep_ref, held, came = refs[:8]
    out_ref, gl_out, staged, whole, left, sems = refs[8:]
    i_rows, j_rows = dims[3:5]
    own = left.shape[0]
    first = pl.multiple_of(lax.axis_index("col") * own, 8)
    whole[...] = total_of(held, came)
    tiles = whole.shape[0] // own
    slots = [slot_of(t, tiles, j_rows) for t in range(tiles)]
    write_rows(whole, ri_ref[pl.ds(first, own), :], keep_ref, left, slots)
    copies = [pltpu.make_async_copy(left, gl_out, sems.at[0])]
    copies[0].start()
    for row in range(0, i_rows, PIECE):
        y_flat = y_ref[row : row + PIECE].reshape(PIECE * j_rows, y_ref.shape[2])
        projected = jnp.dot(y_flat, wp_ref[...], preferred_element_type=F32)
        for i in range(PIECE):
            inverse = jnp.where(ri_ref[row + i : row + i + 1, :] > 0, inv_ref[...], 1.0)
            staged[row + i] = (projected[i * j_rows : (i + 1) * j_rows] * inverse).astype(BF16)
        rows = pl.ds(row, PIECE)
        copies.append(
            pltpu.make_async_copy(staged.at[rows], out_ref.at[rows], sems.at[len(copies)])
        )
        copies[-1].start()
    for copy in copies:
        copy.wait()


def final_kernel(after, rj_ref, keep_ref, *refs):
    right, weight = refs[0:2], refs[2:4]
    gr_out, gw_out, whole, rows, weight_rows, sems = refs[4:]
    weight_rows[...] = total_of(*weight)
    copies = [pltpu.make_async_copy(weight_rows, gw_out, sems.at[0])]
    copies[0].start()
    own = rows.shape[0]
    first = pl.multiple_of(lax.axis_index("row") * own, 8)
    whole[...] = total_of(*right)
    slots = range(whole.shape[0] // own)
    write_rows(whole, rj_ref[pl.ds(first, own), :], keep_ref, rows, slots)
    copies.append(pltpu.make_async_copy(rows, gr_out, sems.at[1]))
    copies[1].start()
    for copy in copies:
        copy.wait()


def swap(array, axis, n, bit):
    return lax.ppermute(array, axis, [(s, s ^ bit) for s in range(n)])


def owners_of(n):
    held, bit = [0], n // 2
    while bit > 1:
        held, bit = held + [k ^ bit for k in held], bit // 2
    return held, [k ^ 1 for k in held]


def gather(block, own, axis, n, after, flops=1000):
    held, sent, bit = own, block[None], n // 2
    while bit > 1:
        came = swap(sent, axis, n, bit)
        shape = (2 * held.shape[0],) + held.shape[1:]
        held = small_call(join_kernel, [pltpu.VMEM(shape, BF16)], "join", (), flops)(
            after, held, came
        )[0]
        sent, bit = held, bit // 2
    return held, swap(sent, axis, n, 1)


def reduce(keep, send, axis, n, after, between=None):
    bit = 1
    while True:
        came = swap(send, axis, n, bit)
        bit *= 2
        if bit >= n:
            if between is not None:
                between(keep)
            return keep, came
        half = (keep.shape[0] // 2,) + keep.shape[1:]
        outs = [pltpu.VMEM(half, F32), pltpu.VMEM(half, BF16)]
        keep, send = small_call(fold_kernel, outs, "fold")(after, keep, came)
        if between is not None:
            gate, between = between(keep), None
            keep, send = hold(gate, keep, send)


def small_call(body, outs, name, scratch=(), flops=1000):
    def call(after, *operands):
        return pl.pallas_call(
            body,
            in_specs=[hbm()] + vmem(len(operands)),
            out_specs=vmem(len(outs)),
            out_shape=outs,
            scratch_shapes=list(scratch),
            compiler_params=params(4),
            cost_estimate=cost(flops, 1000),
            name=name,
        )(after, *operands)

    return call


def hold(after, *arrays):
    outs = [pltpu.VMEM(array.shape, array.dtype) for array in arrays]
    return small_call(copy_kernel, outs, "hold", flops=10**10)(after, *arrays)


def halves(rows, n):
    return [pltpu.VMEM((n // 2, rows // n, LANES), BF16)] * 2


def vmem(count=1):
    return [pl.BlockSpec(memory_space=pltpu.VMEM)] * count


def hbm():
    return pl.BlockSpec(memory_space=pl.ANY)


def in_hbm(array):
    return pltpu.with_memory_space_constraint(array, pltpu.HBM)


def shards(left_act, right_act, row_mask, res_mask, out_weight, cotangent):
    n_col = lax.axis_size("col")
    n_row = lax.axis_size("row")
    i_rows, j_rows, pair_width = cotangent.shape
    sequences = row_mask.shape[0]
    width = left_act.shape[1]
    chans = width // sequences
    groups = LANES // chans
    blocks = chans // groups
    tiles = width // LANES
    depth = groups * sequences
    inner = chans * chans
    step_rows = 16
    steps = i_rows // step_rows
    early_steps = steps // 2
    dims = (chans, groups, blocks, i_rows, j_rows, step_rows, sequences)
    j_pad = -(-j_rows // LANES) * LANES
    span = blocks * j_rows
    own_left, own_right = left_act.shape[0], right_act.shape[0]
    macs = i_rows * j_rows * inner * pair_width

    mask_row = (res_mask.reshape(1, -1), row_mask.reshape(1, -1))
    scaled, inverse, weight, keep, i_keep, j_keep, own_l, own_r, z_first = pl.pallas_call(
        functools.partial(scale_kernel, dims),
        in_specs=[hbm()] * 6,
        out_specs=vmem(9),
        out_shape=[
            pltpu.VMEM(cotangent.shape, BF16),
            pltpu.VMEM((j_rows, LANES), F32),
            pltpu.VMEM(out_weight.shape, BF16),
            pltpu.VMEM((1, width), F32),
            pltpu.VMEM((i_rows, LANES), F32),
            pltpu.VMEM((j_rows, LANES), F32),
            pltpu.VMEM((1,) + left_act.shape, BF16),
            pltpu.VMEM((1,) + right_act.shape, BF16),
            pltpu.VMEM((early_steps, span, step_rows * LANES), BF16),
        ],
        scratch_shapes=[
            pltpu.VMEM((1, res_mask.shape[0]), jnp.int32),
            pltpu.VMEM((1, sequences), jnp.int32),
            pltpu.VMEM(out_weight.shape, BF16),
            pltpu.VMEM(out_weight.shape, F32),
            pltpu.VMEM(cotangent.shape, BF16),
            pltpu.SemaphoreType.DMA((steps,)),
            pltpu.SemaphoreType.DMA((5,)),
        ],
        compiler_params=params(16),
        cost_estimate=cost(1000, 1000),
        name="scale",
    )(*map(in_hbm, (*mask_row, cotangent, out_weight, left_act, right_act)))

    rights = gather(right_act, own_r, "row", n_row, own_r)

    z_last = pl.pallas_call(
        functools.partial(inner_kernel, dims, early_steps),
        in_specs=[hbm()] + vmem(2),
        out_specs=vmem()[0],
        out_shape=pltpu.VMEM((steps - early_steps, span, step_rows * LANES), BF16),
        compiler_params=params(16),
        cost_estimate=cost(1000, 1000),
        name="inner",
    )(rights[0], scaled, weight)
    z = (z_first, z_last)
    lefts = gather(left_act, own_l, "col", n_col, z_last, 10**10)

    rbig, right_turned = pl.pallas_call(
        functools.partial(right_rows_kernel, dims, n_row),
        in_specs=[hbm()] + vmem(4),
        out_specs=vmem(2),
        out_shape=[pltpu.VMEM((span, depth), BF16), pltpu.VMEM((depth, span), BF16)],
        scratch_shapes=[pltpu.VMEM((j_rows, width), F32), pltpu.VMEM((width, j_pad), F32)],
        compiler_params=params(12),
        cost_estimate=cost(16 * macs, 2**20),
        name="right_rows",
    )(lefts[0], j_keep, keep, *rights)

    gl_cut = pl.pallas_call(
        functools.partial(left_kernel, dims, n_col),
        in_specs=[hbm()] + vmem(1 + len(z)),
        out_specs=vmem(2),
        out_shape=halves(i_rows * tiles, n_col),
        scratch_shapes=[pltpu.VMEM((i_rows * tiles, LANES), F32)],
        compiler_params=params(16),
        cost_estimate=cost(16 * macs, 2**20),
        name="left",
    )(rbig, right_turned, *z)
    y, diag, *gw_cut = pl.pallas_call(
        functools.partial(outer_kernel, dims, n_row, n_col),
        in_specs=[hbm()] + vmem(6),
        out_specs=vmem(4),
        out_shape=[
            pltpu.VMEM((i_rows, j_rows, inner), BF16),
            pltpu.VMEM((steps, depth, step_rows * LANES), BF16),
        ]
        + halves(inner, n_row),
        scratch_shapes=[
            pltpu.VMEM((i_rows, width), F32),
            pltpu.VMEM((i_rows * tiles, LANES), F32),
            pltpu.VMEM((LANES, groups * LANES), BF16),
            pltpu.VMEM((pair_width, inner), F32),
            pltpu.VMEM((inner, pair_width), F32),
        ],
        compiler_params=params(16),
        cost_estimate=cost(16 * macs, 2**20),
        name="outer",
    )(gl_cut[0], i_keep, keep, scaled, rbig, *lefts)

    def right_part(first, last, after, *so_far):
        return pl.pallas_call(
            functools.partial(right_part_kernel, first, last, len(z)),
            in_specs=[hbm()] + vmem(1 + len(z) + len(so_far)),
            out_specs=vmem()[0],
            out_shape=pltpu.VMEM((depth, span), F32),
            compiler_params=params(16),
            cost_estimate=cost(1000, 1000),
            name="right_part",
        )(after, diag, *z, *so_far)

    gw_row, acc = [], []
    right_steps = max(1, steps // 4)

    def weight_rounds(after):
        acc.append(right_part(0, right_steps, after))
        gw_row.extend(reduce(*gw_cut, "row", n_row, acc[0]))
        return gw_row[0]

    gl_last = reduce(*gl_cut, "col", n_col, gw_cut[0], weight_rounds)
    acc = right_part(right_steps, 2 * right_steps, gl_last[0], acc[0])
    gw_turned = small_call(
        functools.partial(turn_kernel, n_col),
        halves(inner // n_row, n_col),
        "turn",
        [pltpu.VMEM((inner // n_row, pair_width), F32)],
    )(acc, *gw_row)

    gr_cut = pl.pallas_call(
        functools.partial(right_kernel, dims, n_row, 2 * right_steps),
        in_specs=[hbm()] + vmem(2 + len(z)),
        out_specs=vmem(2),
        out_shape=halves(j_rows * tiles, n_row),
        scratch_shapes=[
            pltpu.VMEM((depth, span), F32),
            pltpu.VMEM((width, j_pad), F32),
            pltpu.VMEM((j_rows * tiles, LANES), F32),
        ],
        compiler_params=params(20),
        cost_estimate=cost(16 * macs, 2**20),
        name="right",
    )(gw_turned[0], diag, acc, *z)
    gr_held = []

    def right_rounds(after):
        gr_held.extend(hold(after, *gr_cut))
        return gr_held[0]

    gw_last = reduce(*gw_turned, "col", n_col, gr_cut[0], right_rounds)
    gr_last = reduce(*gr_held, "row", n_row, gw_last[0])

    pair_out, grad_left = pl.pallas_call(
        functools.partial(pair_kernel, dims),
        in_specs=[hbm()] + vmem(7),
        out_specs=[hbm()] * 2,
        out_shape=[
            jax.ShapeDtypeStruct(cotangent.shape, BF16),
            jax.ShapeDtypeStruct((own_left, width), F32),
        ],
        scratch_shapes=[
            pltpu.VMEM(cotangent.shape, BF16),
            pltpu.VMEM((own_left * tiles, LANES), F32),
            pltpu.VMEM((own_left, width), F32),
            pltpu.SemaphoreType.DMA((1 + i_rows // PIECE,)),
        ],
        compiler_params=params(12),
        cost_estimate=cost(16 * macs, 2**20),
        name="pair",
    )(gr_last[0], i_keep, y, weight, inverse, keep, *gl_last)

    owned = (inner // n_row // n_col, pair_width)
    grad_right, grad_weight = pl.pallas_call(
        final_kernel,
        in_specs=[hbm()] + vmem(6),
        out_specs=[hbm()] * 2,
        out_shape=[
            jax.ShapeDtypeStruct((own_right, width), F32),
            jax.ShapeDtypeStruct(owned, F32),
        ],
        scratch_shapes=[
            pltpu.VMEM((own_right * tiles, LANES), F32),
            pltpu.VMEM((own_right, width), F32),
            pltpu.VMEM(owned, F32),
            pltpu.SemaphoreType.DMA((2,)),
        ],
        compiler_params=params(4),
        cost_estimate=cost(1000, 1000),
        name="final_sums",
    )(in_hbm(pair_out), j_keep, keep, *gr_last, *gw_last)
    return (pair_out, grad_left, grad_right, grad_weight)


def solution(mesh):
    placed = (
        P(("grp", "row", "col"), None),
        P(("grp", "col", "row"), None),
        P("grp"),
        P("grp"),
        P(),
        P(("grp", "row"), "col", None),
    )
    return jax.shard_map(
        shards,
        mesh=mesh,
        in_specs=placed,
        out_specs=(
            P(("grp", "row"), "col", None),
            P(("grp", "row", "col"), None),
            P(("grp", "col", "row"), None),
            P(("grp", "row", "col"), None),
        ),
        check_vma=False,
    )
```

```python
import functools

import jax
import jax.numpy as jnp
from jax import lax
from jax.experimental import pallas as pl
from jax.experimental.pallas import tpu as pltpu
from jax.sharding import PartitionSpec as P

LANES = 128
CHUNK = 4
PIECE = 8
NT = (((1,), (1,)), ((), ()))
F32 = jnp.float32
BF16 = jnp.bfloat16


def params(mib):
    return pltpu.CompilerParams(vmem_limit_bytes=mib * 2**20)


def cost(flops, nbytes):
    return pl.CostEstimate(flops=int(flops), bytes_accessed=int(nbytes), transcendentals=0)


def cut(source, index, n, keep_ref, send_ref):
    rows = source.shape[0] // n
    for k in range(n):
        at = pl.multiple_of((index ^ k) * rows, rows)
        into = send_ref if k % 2 else keep_ref
        into[k // 2] = source[pl.ds(at, rows), :].astype(into.dtype)


def place(buffers, index, n, flat):
    for buffer, owners in zip(buffers, owners_of(n)):
        rows = buffer.shape[1]
        for k, owner in enumerate(owners):
            at = pl.multiple_of((index ^ owner) * rows, 8)
            flat[pl.ds(at, rows), :] = buffer[k].astype(F32)


def paired(j_rows):
    return 2 * j_rows == LANES


def slot_of(tile, tiles, j_rows):
    return tile % 2 * (tiles // 2) + tile // 2 if paired(j_rows) else tile


def swap_halves(low, first, second):
    half = LANES // 2
    return (
        jnp.where(low, first, pltpu.roll(second, half, axis=1)),
        jnp.where(low, pltpu.roll(first, half, axis=1), second),
    )


def lane_group(shape, chans):
    return lax.broadcasted_iota(jnp.int32, shape, 1) // chans


def mask_rows(res_ref, first, count):
    shape = (count, res_ref.shape[1])
    row = lax.broadcasted_iota(jnp.int32, shape, 0) + first
    here = lax.broadcasted_iota(jnp.int32, shape, 1) == row
    chosen = jnp.where(here, res_ref[...].astype(F32), 0.0)
    return jnp.broadcast_to(jnp.sum(chosen, axis=1, keepdims=True), (count, LANES))


def scale_kernel(dims, *refs):
    chans, groups, blocks, i_rows, j_rows, step_rows, sequences = dims
    tiles = sequences * chans // LANES
    res_hbm, seq_hbm, cot_ref, w_hbm, left_hbm, right_hbm = refs[:6]
    scaled_ref, inv_ref, wp_ref, keep_ref, ri_ref, rj_ref, left_ref, right_ref, z_ref = refs[6:15]
    res_ref, seq_ref, w_ref, w32, cot, sems, more_sems = refs[15:]
    steps = i_rows // step_rows

    def fetch(piece):
        rows = pl.ds(piece * step_rows, step_rows)
        return pltpu.make_async_copy(cot_ref.at[rows], cot.at[rows], sems.at[piece])

    pairs = [
        (res_hbm, res_ref),
        (seq_hbm, seq_ref),
        (w_hbm, w_ref),
        (left_hbm, left_ref.at[0]),
        (right_hbm, right_ref.at[0]),
    ]
    more = [
        pltpu.make_async_copy(source, to, more_sems.at[k]) for k, (source, to) in enumerate(pairs)
    ]
    for copy in more[:3]:
        copy.start()
    for piece in range(i_rows // step_rows):
        fetch(piece).start()
    for copy in more[3:]:
        copy.start()
    shape = (sequences, tiles * LANES)
    own = lax.broadcasted_iota(jnp.int32, shape, 1) // chans
    repeat = (own == lax.broadcasted_iota(jnp.int32, shape, 0)).astype(F32).astype(BF16)
    more[0].wait()
    ri_ref[...] = mask_rows(res_ref, lax.axis_index("row") * i_rows, i_rows)
    rj_ref[...] = mask_rows(res_ref, lax.axis_index("col") * j_rows, j_rows)
    more[1].wait()
    seq = seq_ref[...].astype(F32)
    keep_ref[...] = jnp.dot(
        jnp.broadcast_to(seq, (8, sequences)).astype(BF16), repeat, preferred_element_type=F32
    )[0:1]
    valid = jnp.sum(seq, axis=1, keepdims=True)
    inv_ref[...] = 1.0 / jnp.maximum(valid * rj_ref[...], 1.0)
    more[2].wait()
    w32[...] = w_ref[...].astype(F32)
    for e in range(chans):
        wp_ref[e * chans : (e + 1) * chans, :] = w32[pl.ds(e, chans, stride=chans), :].astype(BF16)
    for piece in range(i_rows // step_rows):
        fetch(piece).wait()
    for step in range(steps):
        for at in range(step * step_rows, (step + 1) * step_rows):
            inverse = jnp.where(ri_ref[at : at + 1, :] > 0, inv_ref[...], 1.0)
            scaled_ref[at] = (cot[at].astype(F32) * inverse).astype(BF16)
        if step < z_ref.shape[0]:
            rows = slice(step * step_rows, (step + 1) * step_rows)
            inner_rows(dims, scaled_ref[rows], wp_ref, z_ref, step)
    more[3].wait()
    more[4].wait()


def inner_rows(dims, scaled, wp_ref, z_ref, at):
    chans, groups, blocks, i_rows, j_rows, step_rows, sequences = dims
    for first in range(0, blocks, CHUNK):
        part = lax.dot_general(
            scaled.reshape(step_rows * j_rows, LANES),
            wp_ref[first * LANES : (first + CHUNK) * LANES, :],
            NT,
            preferred_element_type=F32,
        ).astype(BF16)
        for k in range(CHUNK):
            a = first + k
            for i in range(step_rows):
                z_ref[at, a * j_rows : (a + 1) * j_rows, i * LANES : (i + 1) * LANES] = part[
                    i * j_rows : (i + 1) * j_rows, k * LANES : (k + 1) * LANES
                ]


def inner_kernel(dims, first, after, scaled_ref, wp_ref, z_ref):
    step_rows = dims[5]
    for at in range(z_ref.shape[0]):
        rows = slice((first + at) * step_rows, (first + at + 1) * step_rows)
        inner_rows(dims, scaled_ref[rows], wp_ref, z_ref, at)


def at_step(refs, step):
    for ref in refs:
        if step < ref.shape[0]:
            return ref.at[step]
        step -= ref.shape[0]


def outer_kernel(dims, n_row, n_col, *refs):
    chans, groups, blocks, i_rows, j_rows, step_rows, sequences = dims
    tiles = sequences * chans // LANES
    after, ri_ref, keep_ref, scaled_ref, rbig, left_held, left_came = refs[:7]
    y_ref, diag_ref, keep_out, send_out = refs[7:11]
    flat, lsplit, expand, gwt, gwr = refs[11:]
    place((left_held, left_came), lax.axis_index("col"), n_col, flat)
    for t in range(tiles):
        lanes = slice(t * LANES, (t + 1) * LANES)
        masked = flat[0:i_rows, lanes] * ri_ref[...] * keep_ref[:, lanes]
        lsplit[pl.ds(slot_of(t, tiles, j_rows), i_rows, stride=tiles), :] = masked
    shape = (LANES, groups * LANES)
    source = lax.broadcasted_iota(jnp.int32, shape, 0)
    target = lax.broadcasted_iota(jnp.int32, shape, 1)
    same = (source // chans == target // LANES) & (source % chans == target % chans)
    expand[...] = same.astype(F32).astype(BF16)
    group = lane_group((tiles, LANES), chans)
    masks = [(group == b).astype(F32).astype(BF16) for b in range(groups)]
    deep_rows = 2 * step_rows if i_rows % (2 * step_rows) == 0 else step_rows

    for step in range(i_rows // step_rows):
        if step * step_rows % deep_rows == 0:
            rows = slice(step * step_rows * tiles, (step * step_rows + deep_rows) * tiles)
            spread = jnp.dot(
                lsplit[rows, :].astype(BF16), expand[...], preferred_element_type=F32
            ).astype(BF16)
            for i in range(deep_rows):
                block, at = divmod(step * step_rows + i, step_rows)
                for b in range(groups):
                    for lo in range(groups):
                        first = b * sequences + lo * tiles
                        diag_ref[
                            block, first : first + tiles, at * LANES : (at + 1) * LANES
                        ] = (
                            spread[i * tiles : (i + 1) * tiles, lo * LANES : (lo + 1) * LANES]
                            * masks[b]
                        )
        for first in range(0, step_rows, CHUNK):
            part = jnp.dot(
                rbig[...],
                diag_ref[step, :, first * LANES : (first + CHUNK) * LANES],
                preferred_element_type=F32,
            ).astype(BF16)
            for k in range(CHUNK):
                for a in range(blocks):
                    y_ref[step * step_rows + first + k, :, a * LANES : (a + 1) * LANES] = part[
                        a * j_rows : (a + 1) * j_rows, k * LANES : (k + 1) * LANES
                    ]
        if (step + 1) * step_rows % deep_rows == 0:
            block = slice((step + 1) * step_rows - deep_rows, (step + 1) * step_rows)
            scaled_t = scaled_ref[block].reshape(deep_rows * j_rows, LANES).T
            y_flat = y_ref[block].reshape(deep_rows * j_rows, blocks * LANES)
            part = jnp.dot(scaled_t, y_flat, preferred_element_type=F32)
            gwt[...] = gwt[...] + part if block.start else part
    for k in range(blocks):
        turned_tile = gwt[:, k * LANES : (k + 1) * LANES].T
        for q in range(groups):
            gwr[pl.ds(k * groups + q, chans, stride=chans), :] = turned_tile[
                q * chans : (q + 1) * chans
            ]
    cut(gwr, lax.axis_index("row"), n_row, keep_out, send_out)


def right_sum(first, last, z_refs, diag_ref, acc, so_far=None):
    for step in range(first, last):
        part = lax.dot_general(
            diag_ref[step], at_step(z_refs, step)[...], NT, preferred_element_type=F32
        )
        acc[...] = part if so_far is None else so_far[...] + part
        so_far = acc


def right_part_kernel(first, last, parts, after, diag_ref, *refs):
    right_sum(first, last, refs[:parts], diag_ref, refs[-1], *refs[parts:-1])


def right_kernel(dims, n_row, first, after, diag_ref, acc_first, *refs):
    chans, groups, blocks, i_rows, j_rows, step_rows, sequences = dims
    tiles = sequences * chans // LANES
    j_pad = -(-j_rows // LANES) * LANES
    z_refs, (keep_out, send_out, acc, turned, gr_all) = refs[:-5], refs[-5:]
    right_sum(first, i_rows // step_rows, z_refs, diag_ref, acc, acc_first)
    if paired(j_rows):
        half = tiles // 2
        low = lane_group((half, LANES), LANES // 2) == 0
        for a in range(0, blocks, 2):
            lanes = slice(a * j_rows, (a + 2) * j_rows)
            for b in range(groups):
                for lo in range(groups):
                    first = b * sequences + lo * tiles
                    both = swap_halves(
                        low,
                        acc[first : first + half, lanes],
                        acc[first + half : first + tiles, lanes],
                    )
                    at = lo * chans + groups * a + b
                    turned[pl.ds(at, half, stride=LANES), :] = both[0]
                    turned[pl.ds(at + groups, half, stride=LANES), :] = both[1]
        for pair in range(half):
            block = turned[pair * LANES : (pair + 1) * LANES, :].T
            for k in range(2):
                gr_all[pl.ds(2 * pair + k, j_rows, stride=tiles), :] = block[
                    k * j_rows : (k + 1) * j_rows
                ]
    else:
        for a in range(blocks):
            at, shift = divmod(a * j_rows, LANES)
            mine = acc[:, at * LANES : at * LANES + j_pad]
            if shift:
                mine = pltpu.roll(mine, LANES - shift, axis=1)
            for b in range(groups):
                for lo in range(groups):
                    first = b * sequences + lo * tiles
                    turned[pl.ds(lo * chans + groups * a + b, tiles, stride=LANES), :] = mine[
                        first : first + tiles
                    ]
        for t in range(tiles):
            lanes = slice(t * LANES, (t + 1) * LANES)
            gr_all[pl.ds(t, j_rows, stride=tiles), :] = turned[lanes, :].T[:j_rows]
    cut(gr_all, lax.axis_index("row"), n_row, keep_out, send_out)


def right_rows_kernel(dims, n_row, after, rj_ref, keep_ref, right_held, right_came, *refs):
    chans, groups, blocks, i_rows, j_rows, step_rows, sequences = dims
    tiles = sequences * chans // LANES
    j_pad = -(-j_rows // LANES) * LANES
    rbig, rbt_ref, flat, turned = refs
    place((right_held, right_came), lax.axis_index("row"), n_row, flat)
    if paired(j_rows):
        half = tiles // 2
        low = lane_group((half, LANES), LANES // 2) == 0
        for pair in range(half):
            rows = []
            for t in (2 * pair, 2 * pair + 1):
                lanes = slice(t * LANES, (t + 1) * LANES)
                rows.append(flat[0:j_rows, lanes] * rj_ref[...] * keep_ref[:, lanes])
            turned[pair * LANES : (pair + 1) * LANES, :] = jnp.concatenate(rows, axis=0).T
        for a in range(0, blocks, 2):
            parts = []
            for b in range(groups):
                for lo in range(groups):
                    at = lo * chans + groups * a + b
                    parts += swap_halves(
                        low,
                        turned[pl.ds(at, half, stride=LANES), :],
                        turned[pl.ds(at + groups, half, stride=LANES), :],
                    )
            block = jnp.concatenate(parts, axis=0)
            lanes = slice(a * j_rows, (a + 2) * j_rows)
            rbt_ref[:, lanes] = block.astype(BF16)
            rbig[lanes, :] = block.T.astype(BF16)
    else:
        for t in range(tiles):
            lanes = slice(t * LANES, (t + 1) * LANES)
            masked = flat[0:j_rows, lanes] * rj_ref[...] * keep_ref[:, lanes]
            if j_rows < j_pad:
                masked = jnp.concatenate([masked, jnp.zeros((j_pad - j_rows, LANES), F32)], axis=0)
            turned[lanes, :] = masked.T
        for a in range(blocks):
            parts = [
                turned[pl.ds(lo * chans + groups * a + b, tiles, stride=LANES), :]
                for b in range(groups)
                for lo in range(groups)
            ]
            block = jnp.concatenate(parts, axis=0)
            rbig[a * j_rows : (a + 1) * j_rows, :] = block.T[:j_rows].astype(BF16)
        rbt_ref[...] = rbig[...].T


def left_kernel(dims, n_col, after, rbt_ref, *refs):
    chans, groups, blocks, i_rows, j_rows, step_rows, sequences = dims
    tiles = sequences * chans // LANES
    z_refs, (keep_out, send_out, gl_all) = refs[:-3], refs[-3:]
    group = lane_group((sequences, LANES), chans)
    group_t = lane_group((tiles, LANES), chans)

    for step in range(i_rows // step_rows):
        z_ref = at_step(z_refs, step)
        for first in range(0, step_rows, CHUNK):
            part = jnp.dot(
                rbt_ref[...],
                z_ref[:, first * LANES : (first + CHUNK) * LANES],
                preferred_element_type=F32,
            )
            for k in range(CHUNK):
                mine = part[:, k * LANES : (k + 1) * LANES]
                total = mine[0:sequences]
                for b in range(1, groups):
                    total = jnp.where(group == b, mine[b * sequences : (b + 1) * sequences], total)
                shift = LANES // 2
                while shift >= chans:
                    total = total + pltpu.roll(total, shift, axis=1)
                    shift //= 2
                merged = total[0:tiles]
                for lo in range(1, groups):
                    merged = jnp.where(group_t == lo, total[lo * tiles : (lo + 1) * tiles], merged)
                at = (step * step_rows + first + k) * tiles
                gl_all[at : at + tiles, :] = merged
    cut(gl_all, lax.axis_index("col"), n_col, keep_out, send_out)


def total_of(keep_ref, came_ref, k=0):
    return keep_ref[k].astype(F32) + came_ref[k].astype(F32)


def join_kernel(after, held_ref, came_ref, out_ref):
    count = held_ref.shape[0]
    for k in range(count):
        out_ref[k] = held_ref[k]
        out_ref[count + k] = came_ref[k]


def fold_kernel(after, held_ref, came_ref, keep_out, send_out):
    for k in range(held_ref.shape[0]):
        into = send_out if k % 2 else keep_out
        into[k // 2] = total_of(held_ref, came_ref, k).astype(into.dtype)


def copy_kernel(after, *refs):
    count = len(refs) // 2
    for source, to in zip(refs[:count], refs[count:]):
        to[...] = source[...]


def turn_kernel(n_col, after, held_ref, came_ref, keep_out, send_out, whole):
    whole[...] = total_of(held_ref, came_ref)
    cut(whole, lax.axis_index("col"), n_col, keep_out, send_out)


def write_rows(whole, rows, keep_ref, out_ref, slots):
    own = out_ref.shape[0]
    tiles = len(slots)
    for t, slot in enumerate(slots):
        lanes = slice(t * LANES, (t + 1) * LANES)
        out_ref[:, lanes] = whole[pl.ds(slot, own, stride=tiles), :] * (
            rows * keep_ref[:, lanes]
        )


def pair_kernel(dims, *refs):
    after, ri_ref, y_ref, wp_ref, inv_ref, keep_ref, held, came = refs[:8]
    out_ref, gl_out, staged, whole, left, sems = refs[8:]
    i_rows, j_rows = dims[3:5]
    own = left.shape[0]
    first = pl.multiple_of(lax.axis_index("col") * own, 8)
    whole[...] = total_of(held, came)
    tiles = whole.shape[0] // own
    slots = [slot_of(t, tiles, j_rows) for t in range(tiles)]
    write_rows(whole, ri_ref[pl.ds(first, own), :], keep_ref, left, slots)
    copies = [pltpu.make_async_copy(left, gl_out, sems.at[0])]
    copies[0].start()
    for row in range(0, i_rows, PIECE):
        y_flat = y_ref[row : row + PIECE].reshape(PIECE * j_rows, y_ref.shape[2])
        projected = jnp.dot(y_flat, wp_ref[...], preferred_element_type=F32)
        for i in range(PIECE):
            inverse = jnp.where(ri_ref[row + i : row + i + 1, :] > 0, inv_ref[...], 1.0)
            staged[row + i] = (projected[i * j_rows : (i + 1) * j_rows] * inverse).astype(BF16)
        rows = pl.ds(row, PIECE)
        copies.append(
            pltpu.make_async_copy(staged.at[rows], out_ref.at[rows], sems.at[len(copies)])
        )
        copies[-1].start()
    for copy in copies:
        copy.wait()


def final_kernel(after, rj_ref, keep_ref, *refs):
    right, weight = refs[0:2], refs[2:4]
    gr_out, gw_out, whole, rows, weight_rows, sems = refs[4:]
    weight_rows[...] = total_of(*weight)
    copies = [pltpu.make_async_copy(weight_rows, gw_out, sems.at[0])]
    copies[0].start()
    own = rows.shape[0]
    first = pl.multiple_of(lax.axis_index("row") * own, 8)
    whole[...] = total_of(*right)
    slots = range(whole.shape[0] // own)
    write_rows(whole, rj_ref[pl.ds(first, own), :], keep_ref, rows, slots)
    copies.append(pltpu.make_async_copy(rows, gr_out, sems.at[1]))
    copies[1].start()
    for copy in copies:
        copy.wait()


def swap(array, axis, n, bit):
    return lax.ppermute(array, axis, [(s, s ^ bit) for s in range(n)])


def owners_of(n):
    held, bit = [0], n // 2
    while bit > 1:
        held, bit = held + [k ^ bit for k in held], bit // 2
    return held, [k ^ 1 for k in held]


def gather(block, own, axis, n, after):
    held, sent, bit = own, block[None], n // 2
    while bit > 1:
        came = swap(sent, axis, n, bit)
        shape = (2 * held.shape[0],) + held.shape[1:]
        held = small_call(join_kernel, [pltpu.VMEM(shape, BF16)], "join")(after, held, came)[0]
        sent, bit = held, bit // 2
    return held, swap(sent, axis, n, 1)


def reduce(keep, send, axis, n, after, between=None):
    bit = 1
    while True:
        came = swap(send, axis, n, bit)
        bit *= 2
        if bit >= n:
            if between is not None:
                between(keep)
            return keep, came
        half = (keep.shape[0] // 2,) + keep.shape[1:]
        outs = [pltpu.VMEM(half, F32), pltpu.VMEM(half, BF16)]
        keep, send = small_call(fold_kernel, outs, "fold")(after, keep, came)
        if between is not None:
            gate, between = between(keep), None
            keep, send = hold(gate, keep, send)


def small_call(body, outs, name, scratch=(), flops=1000):
    def call(after, *operands):
        return pl.pallas_call(
            body,
            in_specs=[hbm()] + vmem(len(operands)),
            out_specs=vmem(len(outs)),
            out_shape=outs,
            scratch_shapes=list(scratch),
            compiler_params=params(4),
            cost_estimate=cost(flops, 1000),
            name=name,
        )(after, *operands)

    return call


def hold(after, *arrays):
    outs = [pltpu.VMEM(array.shape, array.dtype) for array in arrays]
    return small_call(copy_kernel, outs, "hold", flops=10**10)(after, *arrays)


def halves(rows, n):
    return [pltpu.VMEM((n // 2, rows // n, LANES), BF16)] * 2


def vmem(count=1):
    return [pl.BlockSpec(memory_space=pltpu.VMEM)] * count


def hbm():
    return pl.BlockSpec(memory_space=pl.ANY)


def in_hbm(array):
    return pltpu.with_memory_space_constraint(array, pltpu.HBM)


def shards(left_act, right_act, row_mask, res_mask, out_weight, cotangent):
    n_col = lax.axis_size("col")
    n_row = lax.axis_size("row")
    i_rows, j_rows, pair_width = cotangent.shape
    sequences = row_mask.shape[0]
    width = left_act.shape[1]
    chans = width // sequences
    groups = LANES // chans
    blocks = chans // groups
    tiles = width // LANES
    depth = groups * sequences
    inner = chans * chans
    step_rows = 16
    steps = i_rows // step_rows
    early_steps = steps // 2
    dims = (chans, groups, blocks, i_rows, j_rows, step_rows, sequences)
    j_pad = -(-j_rows // LANES) * LANES
    span = blocks * j_rows
    own_left, own_right = left_act.shape[0], right_act.shape[0]
    macs = i_rows * j_rows * inner * pair_width

    mask_row = (res_mask.reshape(1, -1), row_mask.reshape(1, -1))
    scaled, inverse, weight, keep, i_keep, j_keep, own_l, own_r, z_first = pl.pallas_call(
        functools.partial(scale_kernel, dims),
        in_specs=[hbm()] * 6,
        out_specs=vmem(9),
        out_shape=[
            pltpu.VMEM(cotangent.shape, BF16),
            pltpu.VMEM((j_rows, LANES), F32),
            pltpu.VMEM(out_weight.shape, BF16),
            pltpu.VMEM((1, width), F32),
            pltpu.VMEM((i_rows, LANES), F32),
            pltpu.VMEM((j_rows, LANES), F32),
            pltpu.VMEM((1,) + left_act.shape, BF16),
            pltpu.VMEM((1,) + right_act.shape, BF16),
            pltpu.VMEM((early_steps, span, step_rows * LANES), BF16),
        ],
        scratch_shapes=[
            pltpu.VMEM((1, res_mask.shape[0]), jnp.int32),
            pltpu.VMEM((1, sequences), jnp.int32),
            pltpu.VMEM(out_weight.shape, BF16),
            pltpu.VMEM(out_weight.shape, F32),
            pltpu.VMEM(cotangent.shape, BF16),
            pltpu.SemaphoreType.DMA((steps,)),
            pltpu.SemaphoreType.DMA((5,)),
        ],
        compiler_params=params(16),
        cost_estimate=cost(1000, 1000),
        name="scale",
    )(*map(in_hbm, (*mask_row, cotangent, out_weight, left_act, right_act)))

    lefts = gather(left_act, own_l, "col", n_col, own_l)
    rights = gather(right_act, own_r, "row", n_row, lefts[0])

    z_last = pl.pallas_call(
        functools.partial(inner_kernel, dims, early_steps),
        in_specs=[hbm()] + vmem(2),
        out_specs=vmem()[0],
        out_shape=pltpu.VMEM((steps - early_steps, span, step_rows * LANES), BF16),
        compiler_params=params(16),
        cost_estimate=cost(16 * macs, 2**20),
        name="inner",
    )(rights[0], scaled, weight)
    z = (z_first, z_last)

    rbig, right_turned = pl.pallas_call(
        functools.partial(right_rows_kernel, dims, n_row),
        in_specs=[hbm()] + vmem(4),
        out_specs=vmem(2),
        out_shape=[pltpu.VMEM((span, depth), BF16), pltpu.VMEM((depth, span), BF16)],
        scratch_shapes=[pltpu.VMEM((j_rows, width), F32), pltpu.VMEM((width, j_pad), F32)],
        compiler_params=params(12),
        cost_estimate=cost(16 * macs, 2**20),
        name="right_rows",
    )(z_last, j_keep, keep, *rights)

    gl_cut = pl.pallas_call(
        functools.partial(left_kernel, dims, n_col),
        in_specs=[hbm()] + vmem(1 + len(z)),
        out_specs=vmem(2),
        out_shape=halves(i_rows * tiles, n_col),
        scratch_shapes=[pltpu.VMEM((i_rows * tiles, LANES), F32)],
        compiler_params=params(16),
        cost_estimate=cost(16 * macs, 2**20),
        name="left",
    )(rbig, right_turned, *z)
    y, diag, *gw_cut = pl.pallas_call(
        functools.partial(outer_kernel, dims, n_row, n_col),
        in_specs=[hbm()] + vmem(6),
        out_specs=vmem(4),
        out_shape=[
            pltpu.VMEM((i_rows, j_rows, inner), BF16),
            pltpu.VMEM((steps, depth, step_rows * LANES), BF16),
        ]
        + halves(inner, n_row),
        scratch_shapes=[
            pltpu.VMEM((i_rows, width), F32),
            pltpu.VMEM((i_rows * tiles, LANES), F32),
            pltpu.VMEM((LANES, groups * LANES), BF16),
            pltpu.VMEM((pair_width, inner), F32),
            pltpu.VMEM((inner, pair_width), F32),
        ],
        compiler_params=params(16),
        cost_estimate=cost(16 * macs, 2**20),
        name="outer",
    )(gl_cut[0], i_keep, keep, scaled, rbig, *lefts)

    def right_part(first, last, after, *so_far):
        return pl.pallas_call(
            functools.partial(right_part_kernel, first, last, len(z)),
            in_specs=[hbm()] + vmem(1 + len(z) + len(so_far)),
            out_specs=vmem()[0],
            out_shape=pltpu.VMEM((depth, span), F32),
            compiler_params=params(16),
            cost_estimate=cost(1000, 1000),
            name="right_part",
        )(after, diag, *z, *so_far)

    gw_row, acc = [], []
    right_steps = max(1, steps // 4)

    def weight_rounds(after):
        acc.append(right_part(0, right_steps, after))
        gw_row.extend(reduce(*gw_cut, "row", n_row, acc[0]))
        return gw_row[0]

    gl_last = reduce(*gl_cut, "col", n_col, gw_cut[0], weight_rounds)
    acc = acc[0]
    gw_turned = small_call(
        functools.partial(turn_kernel, n_col),
        halves(inner // n_row, n_col),
        "turn",
        [pltpu.VMEM((inner // n_row, pair_width), F32)],
    )(gl_last[0], *gw_row)

    gr_cut = pl.pallas_call(
        functools.partial(right_kernel, dims, n_row, right_steps),
        in_specs=[hbm()] + vmem(2 + len(z)),
        out_specs=vmem(2),
        out_shape=halves(j_rows * tiles, n_row),
        scratch_shapes=[
            pltpu.VMEM((depth, span), F32),
            pltpu.VMEM((width, j_pad), F32),
            pltpu.VMEM((j_rows * tiles, LANES), F32),
        ],
        compiler_params=params(20),
        cost_estimate=cost(16 * macs, 2**20),
        name="right",
    )(gw_turned[0], diag, acc, *z)
    gr_held = []

    def right_rounds(after):
        gr_held.extend(hold(after, *gr_cut))
        return gr_held[0]

    gw_last = reduce(*gw_turned, "col", n_col, gr_cut[0], right_rounds)
    gr_last = reduce(*gr_held, "row", n_row, gw_last[0])

    pair_out, grad_left = pl.pallas_call(
        functools.partial(pair_kernel, dims),
        in_specs=[hbm()] + vmem(7),
        out_specs=[hbm()] * 2,
        out_shape=[
            jax.ShapeDtypeStruct(cotangent.shape, BF16),
            jax.ShapeDtypeStruct((own_left, width), F32),
        ],
        scratch_shapes=[
            pltpu.VMEM(cotangent.shape, BF16),
            pltpu.VMEM((own_left * tiles, LANES), F32),
            pltpu.VMEM((own_left, width), F32),
            pltpu.SemaphoreType.DMA((1 + i_rows // PIECE,)),
        ],
        compiler_params=params(12),
        cost_estimate=cost(16 * macs, 2**20),
        name="pair",
    )(gr_last[0], i_keep, y, weight, inverse, keep, *gl_last)

    owned = (inner // n_row // n_col, pair_width)
    grad_right, grad_weight = pl.pallas_call(
        final_kernel,
        in_specs=[hbm()] + vmem(6),
        out_specs=[hbm()] * 2,
        out_shape=[
            jax.ShapeDtypeStruct((own_right, width), F32),
            jax.ShapeDtypeStruct(owned, F32),
        ],
        scratch_shapes=[
            pltpu.VMEM((own_right * tiles, LANES), F32),
            pltpu.VMEM((own_right, width), F32),
            pltpu.VMEM(owned, F32),
            pltpu.SemaphoreType.DMA((2,)),
        ],
        compiler_params=params(4),
        cost_estimate=cost(1000, 1000),
        name="final_sums",
    )(in_hbm(pair_out), j_keep, keep, *gr_last, *gw_last)
    return (pair_out, grad_left, grad_right, grad_weight)


def solution(mesh):
    placed = (
        P(("grp", "row", "col"), None),
        P(("grp", "col", "row"), None),
        P("grp"),
        P("grp"),
        P(),
        P(("grp", "row"), "col", None),
    )
    return jax.shard_map(
        shards,
        mesh=mesh,
        in_specs=placed,
        out_specs=(
            P(("grp", "row"), "col", None),
            P(("grp", "row", "col"), None),
            P(("grp", "col", "row"), None),
            P(("grp", "row", "col"), None),
        ),
        check_vma=False,
    )
```
